32 devices in a mesh: dp: 4 (over y, x), seq: 8 (over z, core).
Axes of the slice: x: 2, y: 2, z: 4, core: 2. Of those that a mesh axis runs over, the one named last changes fastest.
Arguments:
- tokens: bfloat16 [6144, 2048], P(('dp', 'seq')), may hold values from -6 to 6
- positions: int32 [6144], P(('dp', 'seq')), may hold values from 0 to 1439, as said below
- cotangent: bfloat16 [6144, 2048], P(('dp', 'seq')), may hold values from -6 to 6
- norm_in_gain: float32 [2048], P(('dp', 'seq')), may hold values from 0.1 to 1.9
- q_down: float32 [2048, 1024], P(('dp', 'seq')), may hold values from -0.125 to 0.125
- q_gain: float32 [1024], P(('dp', 'seq')), may hold values from 0.1 to 1.9
- q_up: float32 [1024, 4096], P(('dp', 'seq')), may hold values from -0.1875 to 0.1875
- key_proj: float32 [2048, 256], P(('dp', 'seq')), may hold values from -0.125 to 0.125
- value_proj: float32 [2048, 256], P(('dp', 'seq')), may hold values from -0.125 to 0.125
- out_proj: float32 [4096, 2048], P(('dp', 'seq')), may hold values from -1 to 1
- norm_mid_gain: float32 [2048], P(('dp', 'seq')), may hold values from 0.1 to 1.9
- w_gate: float32 [2048, 5632], P(('dp', 'seq')), may hold values from -0.125 to 0.125
- w_up: float32 [2048, 5632], P(('dp', 'seq')), may hold values from -0.125 to 0.125
- w_down: float32 [5632, 2048], P(('dp', 'seq')), may hold values from -0.078125 to 0.078125
Outputs:
- output: bfloat16 [6144, 2048], P(('dp', 'seq'))
- grad_tokens: bfloat16 [6144, 2048], P(('dp', 'seq'))
- grad_norm_in_gain: float32 [2048], P(('dp', 'seq'))
- grad_q_down: float32 [2048, 1024], P(('dp', 'seq'))
- grad_q_gain: float32 [1024], P(('dp', 'seq'))
- grad_q_up: float32 [1024, 4096], P(('dp', 'seq'))
- grad_key_proj: float32 [2048, 256], P(('dp', 'seq'))
- grad_value_proj: float32 [2048, 256], P(('dp', 'seq'))
- grad_out_proj: float32 [4096, 2048], P(('dp', 'seq'))
- grad_norm_mid_gain: float32 [2048], P(('dp', 'seq'))
- grad_w_gate: float32 [2048, 5632], P(('dp', 'seq'))
- grad_w_up: float32 [2048, 5632], P(('dp', 'seq'))
- grad_w_down: float32 [5632, 2048], P(('dp', 'seq'))
The draws below stay inside these ranges and needn't reach their ends.
Inputs may be any that keep to these rules, and one draw needn't show every extreme that they name: `positions`: within each index of dp the 1536 tokens hold three whole sequences laid end to end; each entry counts from 0 at its sequence's first token. The longest of them has 1440 tokens and covers tokens of the first and of the last device of seq.
All inputs are finite; a program needn't handle non-finite values.
Results may differ from the reference program's by a relative error of at most 0.03.
Values may be sent and summed in bfloat16 or wider, within the bound.
A program may use at most 512 MiB of HBM per device.

```python
import math
import jax
import jax.numpy as jnp
from jax import lax

WIDTH = 2048
QUERY_RANK = 1024
HEADS = 16
HEAD_DIM = 256
HIDDEN_SIZE = 5632
TOK_DEV = 192
GROUP = 1536
TOKENS = 6144


def draw_positions(key, part):
    key = jax.random.fold_in(key, 11)
    short_key, order_key = jax.random.split(key)
    groups = TOKENS // GROUP
    shorts_total = TOK_DEV // 2
    first_short = jax.random.randint(short_key, (groups, 1), 1, shorts_total)
    second_short = shorts_total - first_short
    place = jax.random.randint(order_key, (groups, 1), 0, 3)
    longest = GROUP - shorts_total
    first_length = jnp.where(place == 0, longest, first_short)
    second_length = jnp.where(place == 1, longest, jnp.where(place == 0, first_short, second_short))
    boundary_one = first_length
    boundary_two = first_length + second_length
    index = jnp.arange(GROUP, dtype=jnp.int32)[None, :]
    start = jnp.where(index >= boundary_two, boundary_two, jnp.where(index >= boundary_one, boundary_one, 0))
    return (index - start).reshape(TOKENS).astype(jnp.int32)


def shard_levels(stream_key, dims, pieces, low, largest):
    def one(position, blocks):
        steps = jax.random.uniform(jax.random.fold_in(jax.random.fold_in(stream_key, 6), position), (blocks,), jnp.float32, low / len(pieces), largest / len(pieces))
        return jnp.repeat(jnp.exp(steps), dims[position] // blocks).reshape((-1,) + (1,) * (len(dims) - position - 1))

    gain = one(*pieces[0])
    for cut in pieces[1:]:
        gain = gain * one(*cut)
    return gain


def noise(rng, dims, width, most, shards=(), kind=jnp.bfloat16):
    result = width * jax.random.normal(rng, dims, jnp.float32)
    if shards:
        result = result * shard_levels(rng, dims, shards, -0.22, 0.18)
    return jnp.clip(result, -most, most).astype(kind)


def setup_inputs(seed: int = 0) -> dict:
    splits = jax.random.split(jax.random.key(seed), 15)
    tokens = noise(splits[0], (TOKENS, WIDTH), 1.0, 6.0, ((0, 32),))
    positions = draw_positions(jax.random.fold_in(splits[14], 71), 0)
    cotangent = noise(splits[2], (TOKENS, WIDTH), 1.0, 6.0, ((0, 32),))
    norm_in_gain = jnp.clip(1.0 + 0.18 * jax.random.normal(splits[3], (WIDTH,), jnp.float32), 0.1, 1.9)
    q_down = noise(splits[4], (WIDTH, QUERY_RANK), WIDTH ** -0.5, 0.125, ((0, 32),), jnp.float32)
    q_gain = jnp.clip(1.0 + 0.18 * jax.random.normal(splits[5], (QUERY_RANK,), jnp.float32), 0.1, 1.9)
    q_up = noise(splits[6], (QUERY_RANK, HEADS * HEAD_DIM), QUERY_RANK ** -0.5, 0.1875, ((0, 32),), jnp.float32)
    key_proj = noise(splits[7], (WIDTH, HEAD_DIM), WIDTH ** -0.5, 0.125, ((0, 32),), jnp.float32)
    value_proj = noise(splits[8], (WIDTH, HEAD_DIM), WIDTH ** -0.5, 0.125, ((0, 32),), jnp.float32)
    out_proj = noise(splits[9], (HEADS * HEAD_DIM, WIDTH), (max(1, HEADS * HEAD_DIM * 16 // GROUP)) ** -0.5, 1.0, ((0, 32),), jnp.float32)
    norm_mid_gain = jnp.clip(1.0 + 0.18 * jax.random.normal(splits[10], (WIDTH,), jnp.float32), 0.1, 1.9)
    w_gate = noise(splits[11], (WIDTH, HIDDEN_SIZE), WIDTH ** -0.5, 0.125, ((0, 32),), jnp.float32)
    w_up = noise(splits[12], (WIDTH, HIDDEN_SIZE), WIDTH ** -0.5, 0.125, ((0, 32),), jnp.float32)
    w_down = noise(splits[13], (HIDDEN_SIZE, WIDTH), HIDDEN_SIZE ** -0.5, 0.078125, ((0, 32),), jnp.float32)
    return dict(tokens=tokens, positions=positions, cotangent=cotangent, norm_in_gain=norm_in_gain, q_down=q_down, q_gain=q_gain, q_up=q_up, key_proj=key_proj, value_proj=value_proj, out_proj=out_proj, norm_mid_gain=norm_mid_gain, w_gate=w_gate, w_up=w_up, w_down=w_down)


@jax.custom_vjp
def low(v):
    return lax.optimization_barrier(v.astype(jnp.bfloat16)).astype(jnp.float32)

@jax.custom_vjp
def low_back(v):
    return v

def low_keep(v):
    return (low(v), None)

def low_pass(kept, grad):
    return (grad,)

def back_keep(v):
    return (v, None)

def back_low(kept, grad):
    return (low(grad),)
low.defvjp(low_keep, low_pass)
low_back.defvjp(back_keep, back_low)
epsilon = 1e-05
rope_base = 10000.0
masked_score = -1e+30

def matmul(left, right):
    return jnp.dot(left, right, precision=lax.Precision.HIGHEST)

def rms_scale(values):
    return lax.rsqrt(lax.optimization_barrier(jnp.mean(values * values, axis=-1, keepdims=True)) + epsilon)

def rotary(values, places, sign):
    half = values.shape[-1] // 2
    freqs = rope_base ** (-(2.0 * jnp.arange(half).astype(jnp.float32)) / values.shape[-1])
    angles = places.astype(jnp.float32)[:, None] * freqs[None, :]
    cosine = jnp.cos(angles)[:, None, :]
    sine = jnp.sin(angles)[:, None, :]
    first = values[..., :half]
    second = values[..., half:]
    return jnp.concatenate([first * cosine - sign * second * sine, sign * first * sine + second * cosine], axis=-1)

def layer_group(params, tokens_group, positions_group):
    in_gain, down_weight, query_gain, up_query, key_weight, value_weight, output_weight, mid_gain, gate_weight, up_weight, down_ffn = [low(param) for param in params]
    count = tokens_group.shape[0]
    normed = low(tokens_group * rms_scale(tokens_group) * in_gain)
    compressed = low_back(matmul(normed, down_weight))
    compressed_normed = low(compressed * rms_scale(compressed) * query_gain)
    queries = low_back(matmul(compressed_normed, up_query)).reshape(count, HEADS, HEAD_DIM)
    queries = low(rotary(queries, positions_group, 1.0))
    keys = low_back(matmul(normed, key_weight))
    keys = low(rotary(keys[:, None, :], positions_group, 1.0)[:, 0, :])
    values = low(low_back(matmul(normed, value_weight)))
    index = jnp.arange(count, dtype=jnp.int32)
    first = index - positions_group
    seen = (index[None, :] >= first[:, None]) & (index[None, :] <= index[:, None])
    scale = 1.0 / math.sqrt(HEAD_DIM)

    def head_output(query_head):
        raw = low_back(matmul(query_head, keys.T))
        scores = jnp.where(seen, raw * scale, masked_score)
        top = lax.optimization_barrier(jnp.max(scores, axis=-1, keepdims=True))
        weights = jnp.exp(scores - top)
        probs = low(weights / lax.optimization_barrier(jnp.sum(weights, axis=-1, keepdims=True)))
        return matmul(probs, values)
    heads_out = lax.map(jax.checkpoint(head_output), queries.transpose(1, 0, 2))
    attended = low(low_back(heads_out.transpose(1, 0, 2).reshape(count, HEADS * HEAD_DIM)))
    middle = tokens_group + low_back(matmul(attended, output_weight))
    normed_mid = low(middle * rms_scale(middle) * mid_gain)
    gate = low_back(matmul(normed_mid, gate_weight))
    upper = low_back(matmul(normed_mid, up_weight))
    hidden = low(jax.nn.silu(gate) * upper)
    return middle + matmul(hidden, down_ffn)

def reference(tokens, positions, cotangent, norm_in_gain, q_down, q_gain, q_up, key_proj, value_proj, out_proj, norm_mid_gain, w_gate, w_up, w_down):
    params = (norm_in_gain, q_down, q_gain, q_up, key_proj, value_proj, out_proj, norm_mid_gain, w_gate, w_up, w_down)
    groups = TOKENS // GROUP
    inputs = tokens.astype(jnp.float32).reshape(groups, GROUP, WIDTH)
    places = positions.reshape(groups, GROUP)

    def forward(inputs, params):

        def one_group(item):
            return layer_group(params, item[0], item[1])
        return lax.map(jax.checkpoint(one_group), (inputs, places))
    outputs, pullback = jax.vjp(forward, inputs, params)
    grad_inputs, grads = pullback(cotangent.astype(jnp.float32).reshape(groups, GROUP, WIDTH))
    return (outputs.reshape(TOKENS, WIDTH).astype(jnp.bfloat16), grad_inputs.reshape(TOKENS, WIDTH).astype(jnp.bfloat16), grads[0], grads[1], grads[2], grads[3], grads[4], grads[5], grads[6], grads[7], grads[8], grads[9], grads[10])
```

```python
import math

import jax
import jax.numpy as jnp
from jax import lax
from jax.experimental import pallas as pl
from jax.experimental.pallas import tpu as pltpu
from jax.sharding import PartitionSpec as P

HEADS = 16
HEAD_DIM = 256


epsilon = 1e-05
rope_base = 10000.0
masked_score = -1e30


def rms_scale(values):
    return lax.rsqrt(jnp.mean(values * values, axis=-1, keepdims=True) + epsilon)


def rotary(values, places, sign):
    half = values.shape[-1] // 2
    freqs = rope_base ** (-(2.0 * jnp.arange(half).astype(jnp.float32)) / values.shape[-1])
    angles = places.astype(jnp.float32)[:, None] * freqs[None, :]
    cosine = jnp.cos(angles)[:, None, :]
    sine = jnp.sin(angles)[:, None, :]
    first = values[..., :half]
    second = values[..., half:]
    return jnp.concatenate(
        [first * cosine - sign * second * sine, sign * first * sine + second * cosine], axis=-1
    )


def norm_backward(inputs, scale, gain, grad_out):
    weighted = gain * grad_out
    grad_in = scale * weighted - inputs * scale * scale * scale * jnp.mean(
        weighted * inputs, axis=-1, keepdims=True
    )
    grad_gain = jnp.sum(grad_out * inputs * scale, axis=0)
    return (grad_in, grad_gain)


def add_rows(total, block, start):
    current = lax.dynamic_slice_in_dim(total, start, block.shape[0], 0)
    return lax.dynamic_update_slice_in_dim(total, current + block, start, 0)


def local(
    tokens,
    positions,
    cotangent,
    norm_in_gain,
    q_down,
    q_gain,
    q_up,
    key_proj,
    value_proj,
    out_proj,
    norm_mid_gain,
    w_gate,
    w_up,
    w_down,
):
    width = tokens.shape[0]
    scale = 1.0 / math.sqrt(HEAD_DIM)
    attention_set = (
        lax.all_gather(norm_in_gain.astype(jnp.bfloat16), ("dp", "seq"), axis=0, tiled=True),
        lax.all_gather(q_down.astype(jnp.bfloat16), ("dp", "seq"), axis=0, tiled=True),
        lax.all_gather(q_gain.astype(jnp.bfloat16), ("dp", "seq"), axis=0, tiled=True),
        lax.all_gather(q_up.astype(jnp.bfloat16), ("dp", "seq"), axis=0, tiled=True),
        lax.all_gather(key_proj.astype(jnp.bfloat16), ("dp", "seq"), axis=0, tiled=True),
        lax.all_gather(value_proj.astype(jnp.bfloat16), ("dp", "seq"), axis=0, tiled=True),
        lax.all_gather(out_proj.astype(jnp.bfloat16), ("dp", "seq"), axis=0, tiled=True),
    )
    feed_set = (
        lax.all_gather(norm_mid_gain.astype(jnp.bfloat16), ("dp", "seq"), axis=0, tiled=True),
        lax.all_gather(w_gate.astype(jnp.bfloat16), ("dp", "seq"), axis=0, tiled=True),
        lax.all_gather(w_up.astype(jnp.bfloat16), ("dp", "seq"), axis=0, tiled=True),
        lax.all_gather(w_down.astype(jnp.bfloat16), ("dp", "seq"), axis=0, tiled=True),
    )
    in_gain = attention_set[0].astype(jnp.float32)
    query_gain = attention_set[2].astype(jnp.float32)
    inputs = tokens.astype(jnp.float32)
    in_scale = rms_scale(inputs)
    normed = (inputs * in_scale * in_gain).astype(jnp.bfloat16)
    compressed = jnp.dot(normed, attention_set[1], preferred_element_type=jnp.float32)
    query_scale = rms_scale(compressed)
    compressed_normed = (compressed * query_scale * query_gain).astype(jnp.bfloat16)
    queries_raw = jnp.dot(
        compressed_normed, attention_set[3], preferred_element_type=jnp.float32
    ).reshape(width, HEADS, HEAD_DIM)
    queries = rotary(queries_raw, positions, 1.0).astype(jnp.bfloat16)
    keys_raw = jnp.dot(normed, attention_set[4], preferred_element_type=jnp.float32)
    keys = rotary(keys_raw[:, None, :], positions, 1.0)[:, 0, :].astype(jnp.bfloat16)
    values = jnp.dot(normed, attention_set[5], preferred_element_type=jnp.float32).astype(
        jnp.bfloat16
    )
    query_index = lax.axis_index("seq") * width + jnp.arange(width, dtype=jnp.int32)
    first_index = query_index - positions

    def visibility(key_start):
        key_index = key_start + jnp.arange(width, dtype=jnp.int32)
        seen = (key_index[None, :] >= first_index[:, None]) & (
            key_index[None, :] <= query_index[:, None]
        )
        return seen[:, None, :]

    start_state = (
        jnp.full((width, HEADS), masked_score, jnp.float32),
        jnp.zeros((width, HEADS), jnp.float32),
        jnp.zeros((width, HEADS, HEAD_DIM), jnp.float32),
    )
    carry = start_state
    piece = (
        lax.all_gather(keys, "seq", axis=0, tiled=True),
        lax.all_gather(values, "seq", axis=0, tiled=True),
    )
    blocks = piece[0].shape[0] // width
    key_blocks = piece[0].reshape(blocks, width, HEAD_DIM)
    value_blocks = piece[1].reshape(blocks, width, HEAD_DIM)

    def forward_one_block(state, item):
        key_block, value_block, number = item
        key_start = number * width
        top, total, accum = state
        seen = visibility(key_start)
        scores = (
            jnp.einsum("thd,kd->thk", queries, key_block, preferred_element_type=jnp.float32)
            * scale
        )
        scores = jnp.where(seen, scores, masked_score)
        new_top = jnp.maximum(top, jnp.max(scores, axis=-1))
        weights = jnp.where(seen, jnp.exp(scores - new_top[..., None]), 0.0)
        decay = jnp.exp(top - new_top)
        total = total * decay + jnp.sum(weights, axis=-1)
        accum = accum * decay[..., None] + jnp.einsum(
            "thk,kd->thd",
            weights.astype(jnp.bfloat16),
            value_block,
            preferred_element_type=jnp.float32,
        )
        state = (new_top, total, accum)
        return (state, None)

    carry, _ = lax.scan(
        forward_one_block, carry, (key_blocks, value_blocks, jnp.arange(blocks, dtype=jnp.int32))
    )
    top, total, accum = carry
    attended_full = accum / total[..., None]
    log_total = top + jnp.log(total)
    attended = attended_full.reshape(width, HEADS * HEAD_DIM).astype(jnp.bfloat16)
    middle = inputs + jnp.dot(attended, attention_set[6], preferred_element_type=jnp.float32)
    mid_gain = feed_set[0].astype(jnp.float32)
    mid_scale = rms_scale(middle)
    normed_mid = (middle * mid_scale * mid_gain).astype(jnp.bfloat16)
    gate = jnp.dot(normed_mid, feed_set[1], preferred_element_type=jnp.float32)
    upper = jnp.dot(normed_mid, feed_set[2], preferred_element_type=jnp.float32)
    sigmoid_gate = jax.nn.sigmoid(gate)
    silu_gate = gate * sigmoid_gate
    hidden = (silu_gate * upper).astype(jnp.bfloat16)
    output = (middle + jnp.dot(hidden, feed_set[3], preferred_element_type=jnp.float32)).astype(
        jnp.bfloat16
    )
    feed_back = (
        lax.all_gather(norm_mid_gain.astype(jnp.bfloat16), ("dp", "seq"), axis=0, tiled=True),
        lax.all_gather(w_gate.astype(jnp.bfloat16), ("dp", "seq"), axis=0, tiled=True),
        lax.all_gather(w_up.astype(jnp.bfloat16), ("dp", "seq"), axis=0, tiled=True),
        lax.all_gather(w_down.astype(jnp.bfloat16), ("dp", "seq"), axis=0, tiled=True),
    )
    grad_out_full = cotangent.astype(jnp.float32)
    grad_down = jnp.einsum("tf,td->fd", hidden, cotangent, preferred_element_type=jnp.float32)
    grad_hidden = jnp.einsum(
        "td,fd->tf", cotangent, feed_back[3], preferred_element_type=jnp.float32
    )
    grad_gate = (grad_hidden * upper * sigmoid_gate * (1.0 + gate * (1.0 - sigmoid_gate))).astype(
        jnp.bfloat16
    )
    grad_upper = (grad_hidden * silu_gate).astype(jnp.bfloat16)
    grad_gate_weight = jnp.einsum(
        "td,tf->df", normed_mid, grad_gate, preferred_element_type=jnp.float32
    )
    grad_up_weight = jnp.einsum(
        "td,tf->df", normed_mid, grad_upper, preferred_element_type=jnp.float32
    )
    grad_normed_mid = jnp.einsum(
        "tf,df->td", grad_gate, feed_back[1], preferred_element_type=jnp.float32
    ) + jnp.einsum("tf,df->td", grad_upper, feed_back[2], preferred_element_type=jnp.float32)
    grad_mid_norm, grad_mid_gain = norm_backward(
        middle, mid_scale, feed_back[0].astype(jnp.float32), grad_normed_mid
    )
    grad_middle = grad_out_full + grad_mid_norm
    feed_grads = (
        lax.psum_scatter(grad_mid_gain, ("dp", "seq"), scatter_dimension=0, tiled=True),
        lax.psum_scatter(grad_gate_weight, ("dp", "seq"), scatter_dimension=0, tiled=True),
        lax.psum_scatter(grad_up_weight, ("dp", "seq"), scatter_dimension=0, tiled=True),
        lax.psum_scatter(grad_down, ("dp", "seq"), scatter_dimension=0, tiled=True),
    )
    attention_back = (
        lax.all_gather(norm_in_gain.astype(jnp.bfloat16), ("dp", "seq"), axis=0, tiled=True),
        lax.all_gather(q_down.astype(jnp.bfloat16), ("dp", "seq"), axis=0, tiled=True),
        lax.all_gather(q_gain.astype(jnp.bfloat16), ("dp", "seq"), axis=0, tiled=True),
        lax.all_gather(q_up.astype(jnp.bfloat16), ("dp", "seq"), axis=0, tiled=True),
        lax.all_gather(key_proj.astype(jnp.bfloat16), ("dp", "seq"), axis=0, tiled=True),
        lax.all_gather(value_proj.astype(jnp.bfloat16), ("dp", "seq"), axis=0, tiled=True),
        lax.all_gather(out_proj.astype(jnp.bfloat16), ("dp", "seq"), axis=0, tiled=True),
    )
    branch_grad = grad_middle.astype(jnp.bfloat16)
    grad_output_weight = jnp.einsum(
        "ta,td->ad", attended, branch_grad, preferred_element_type=jnp.float32
    )
    grad_attended = (
        jnp.einsum("td,ad->ta", branch_grad, attention_back[6], preferred_element_type=jnp.float32)
        .reshape(width, HEADS, HEAD_DIM)
        .astype(jnp.bfloat16)
    )
    delta = jnp.sum(grad_attended.astype(jnp.float32) * attended_full, axis=-1)
    group_rows = width * lax.axis_size("seq")
    back_state = (
        jnp.zeros((width, HEADS, HEAD_DIM), jnp.float32),
        jnp.zeros((group_rows, HEAD_DIM), jnp.float32),
        jnp.zeros((group_rows, HEAD_DIM), jnp.float32),
    )
    carry = back_state
    piece = (
        lax.all_gather(keys, "seq", axis=0, tiled=True),
        lax.all_gather(values, "seq", axis=0, tiled=True),
    )
    blocks = piece[0].shape[0] // width
    key_blocks = piece[0].reshape(blocks, width, HEAD_DIM)
    value_blocks = piece[1].reshape(blocks, width, HEAD_DIM)

    def backward_one_block(state, item):
        key_block, value_block, number = item
        key_start = number * width
        grad_query, grad_keys, grad_values = state
        seen = visibility(key_start)
        scores = (
            jnp.einsum("thd,kd->thk", queries, key_block, preferred_element_type=jnp.float32)
            * scale
        )
        probs = jnp.where(seen, jnp.exp(scores - log_total[..., None]), 0.0)
        grad_value_block = jnp.einsum(
            "thk,thd->kd",
            probs.astype(jnp.bfloat16),
            grad_attended,
            preferred_element_type=jnp.float32,
        )
        grad_probs = jnp.einsum(
            "thd,kd->thk", grad_attended, value_block, preferred_element_type=jnp.float32
        )
        grad_scores = (probs * (grad_probs - delta[..., None]) * scale).astype(jnp.bfloat16)
        grad_query = grad_query + jnp.einsum(
            "thk,kd->thd", grad_scores, key_block, preferred_element_type=jnp.float32
        )
        grad_key_block = jnp.einsum(
            "thk,thd->kd", grad_scores, queries, preferred_element_type=jnp.float32
        )
        state = (
            grad_query,
            add_rows(grad_keys, grad_key_block, key_start),
            add_rows(grad_values, grad_value_block, key_start),
        )
        return (state, None)

    carry, _ = lax.scan(
        backward_one_block, carry, (key_blocks, value_blocks, jnp.arange(blocks, dtype=jnp.int32))
    )
    grad_query, grad_keys, grad_values = carry
    local_key_grad, local_value_grad = (
        lax.psum_scatter(
            grad_keys.astype(jnp.bfloat16), "seq", scatter_dimension=0, tiled=True
        ).astype(jnp.float32),
        lax.psum_scatter(
            grad_values.astype(jnp.bfloat16), "seq", scatter_dimension=0, tiled=True
        ).astype(jnp.float32),
    )
    grad_key_pre = rotary(local_key_grad[:, None, :], positions, -1.0)[:, 0, :].astype(jnp.bfloat16)
    grad_value_pre = local_value_grad.astype(jnp.bfloat16)
    grad_query_pre = (
        rotary(grad_query, positions, -1.0).reshape(width, HEADS * HEAD_DIM).astype(jnp.bfloat16)
    )
    grad_up_query = jnp.einsum(
        "tr,ta->ra", compressed_normed, grad_query_pre, preferred_element_type=jnp.float32
    )
    grad_compressed_normed = jnp.einsum(
        "ta,ra->tr", grad_query_pre, attention_back[3], preferred_element_type=jnp.float32
    )
    grad_compressed, grad_query_gain = norm_backward(
        compressed, query_scale, attention_back[2].astype(jnp.float32), grad_compressed_normed
    )
    grad_compressed = grad_compressed.astype(jnp.bfloat16)
    grad_down_weight = jnp.einsum(
        "td,tr->dr", normed, grad_compressed, preferred_element_type=jnp.float32
    )
    grad_key_weight = jnp.einsum(
        "td,te->de", normed, grad_key_pre, preferred_element_type=jnp.float32
    )
    grad_value_weight = jnp.einsum(
        "td,te->de", normed, grad_value_pre, preferred_element_type=jnp.float32
    )
    grad_normed = jnp.einsum(
        "tr,dr->td", grad_compressed, attention_back[1], preferred_element_type=jnp.float32
    )
    grad_normed = grad_normed + jnp.einsum(
        "te,de->td", grad_key_pre, attention_back[4], preferred_element_type=jnp.float32
    )
    grad_normed = grad_normed + jnp.einsum(
        "te,de->td", grad_value_pre, attention_back[5], preferred_element_type=jnp.float32
    )
    grad_in_norm, grad_in_gain = norm_backward(
        inputs, in_scale, attention_back[0].astype(jnp.float32), grad_normed
    )
    grad_tokens = (grad_middle + grad_in_norm).astype(jnp.bfloat16)
    attention_grads = (
        lax.psum_scatter(grad_in_gain, ("dp", "seq"), scatter_dimension=0, tiled=True),
        lax.psum_scatter(grad_down_weight, ("dp", "seq"), scatter_dimension=0, tiled=True),
        lax.psum_scatter(grad_query_gain, ("dp", "seq"), scatter_dimension=0, tiled=True),
        lax.psum_scatter(grad_up_query, ("dp", "seq"), scatter_dimension=0, tiled=True),
        lax.psum_scatter(grad_key_weight, ("dp", "seq"), scatter_dimension=0, tiled=True),
        lax.psum_scatter(grad_value_weight, ("dp", "seq"), scatter_dimension=0, tiled=True),
        lax.psum_scatter(grad_output_weight, ("dp", "seq"), scatter_dimension=0, tiled=True),
    )
    return (
        output,
        grad_tokens,
        attention_grads[0],
        attention_grads[1],
        attention_grads[2],
        attention_grads[3],
        attention_grads[4],
        attention_grads[5],
        attention_grads[6],
        feed_grads[0],
        feed_grads[1],
        feed_grads[2],
        feed_grads[3],
    )


BITS = {"y": ("dp", 2), "x": ("dp", 1), "h": ("seq", 4), "l": ("seq", 2), "c": ("seq", 1)}
bf16 = jnp.bfloat16
f32 = jnp.float32


def swap(value, bit):
    axis, mask = BITS[bit]
    return lax.ppermute(value, axis, [(i, i ^ mask) for i in range(lax.axis_size(axis))])


def swap_many(value, mask):
    return lax.ppermute(value, ("dp", "seq"), [(i, i ^ mask) for i in range(32)])


def pick(value, index, axis=0):
    return lax.dynamic_index_in_dim(value, index, axis, keepdims=False)


def gather_plane(block):
    half = block.shape[0] // 2
    from_x = swap(block, "x")
    from_l = swap(block, "l")
    from_xl = jnp.concatenate([swap(from_x[:half], "l"), swap(from_l[half:], "x")])
    mine = [block, from_l, from_x, from_xl]
    pieces = []
    for piece in mine:
        pieces += [piece, swap(piece, "c")]
    return jnp.stack(pieces)


def scatter_plane(parts):
    half = parts.shape[1] // 2
    parts = parts.reshape((2, 2, 2) + parts.shape[1:])
    pair = parts[:, :, 0].astype(f32) + swap(parts[:, :, 1], "c").astype(f32)
    upper = pair[:, :, :half]
    lower = pair[:, :, half:]
    upper_one = upper[0] + swap(upper[1].astype(bf16), "x").astype(f32)
    lower_one = lower[:, 0] + swap(lower[:, 1].astype(bf16), "l").astype(f32)
    upper_two = upper_one[0] + swap(upper_one[1].astype(bf16), "l").astype(f32)
    lower_two = lower_one[0] + swap(lower_one[1].astype(bf16), "x").astype(f32)
    return jnp.concatenate([upper_two, lower_two])


def exchange_plane(pieces, rank):
    out = jnp.zeros_like(pieces)
    for j in range(8):
        mask = (j & 4) * 2 + (j & 3)
        piece = pick(pieces, rank ^ j)
        if mask:
            piece = swap_many(piece, mask)
        out = lax.dynamic_update_index_in_dim(out, piece, rank ^ j, 0)
    return out


def gather_rows(block, y, h):
    from_h = swap(block, "h")
    from_y = swap(block, "y")
    from_yh = swap(from_h, "y")
    out = jnp.zeros((2, block.shape[0], 2) + block.shape[1:], block.dtype)
    for piece, at_y, at_h in ((block, y, h), (from_h, y, 1 - h), (from_y, 1 - y, h), (from_yh, 1 - y, 1 - h)):
        out = lax.dynamic_update_slice(out, piece[None, :, None], (at_y, 0, at_h, 0, 0))
    return out


def scatter_rows(parts, y, h):
    kept = pick(parts, y).astype(f32) + swap(pick(parts, 1 - y), "y").astype(f32)
    return pick(kept, h, 1) + swap(pick(kept, 1 - h, 1).astype(bf16), "h").astype(f32)


MASK = {"y": 16, "x": 8, "h": 4, "l": 2, "c": 1}


def flip(number, bits):
    bit = 1
    while bit <= bits:
        if bits & bit:
            number = number + bit - 2 * bit * ((number // bit) % 2)
        bit *= 2
    return number


def coordinates():
    dp = lax.axis_index("dp")
    seq = lax.axis_index("seq")
    return dp // 2, dp % 2, seq // 4, (seq // 2) % 2, seq % 2


def partner(mask):
    return flip(lax.axis_index("dp"), mask // 8), flip(lax.axis_index("seq"), mask % 8)


def greet(masks):
    barrier = pltpu.get_barrier_semaphore()
    for mask in masks:
        pl.semaphore_signal(barrier, inc=1, device_id=partner(mask), device_id_type=pl.DeviceIdType.MESH)
    pl.semaphore_wait(barrier, len(masks))


class Wire:
    def __init__(self, send_sem, recv_sem, local_sem):
        self.send_sem, self.recv_sem, self.local_sem = send_sem, recv_sem, local_sem
        self.copies = []
        self.locals = 0

    def send(self, src, dst, mask):
        k = len(self.copies)
        copy = pltpu.make_async_remote_copy(
            src_ref=src,
            dst_ref=dst,
            send_sem=self.send_sem.at[k],
            recv_sem=self.recv_sem.at[k],
            device_id=partner(mask),
            device_id_type=pl.DeviceIdType.MESH,
        )
        copy.start()
        self.copies.append(copy)
        return copy

    def local(self, src, dst):
        copy = pltpu.make_async_copy(src, dst, self.local_sem.at[self.locals])
        self.locals += 1
        copy.start()
        return copy

    def close(self):
        for copy in self.copies:
            copy.wait_send()


def wires(remote, local):
    return [pltpu.SemaphoreType.DMA((remote,)), pltpu.SemaphoreType.DMA((remote,)), pltpu.SemaphoreType.DMA((local,))]


def arrived(copies):
    for copy in copies:
        copy.wait_recv()


ANY = pl.BlockSpec(memory_space=pl.ANY)
VMEM = pl.BlockSpec(memory_space=pltpu.VMEM)
PLANE = [j // 4 * 8 + j % 4 for j in range(1, 8)]


def moving(kernel, number, outs, operands, scratch, in_specs=None, out_specs=None, bytes_sent=1 << 20):
    return pl.pallas_call(
        kernel,
        out_shape=outs,
        in_specs=in_specs or [ANY] * len(operands),
        out_specs=out_specs or [ANY] * len(outs),
        scratch_shapes=scratch,
        compiler_params=pltpu.CompilerParams(
            collective_id=number, has_side_effects=True, vmem_limit_bytes=48 * 1024 * 1024
        ),
        cost_estimate=pl.CostEstimate(flops=0, bytes_accessed=bytes_sent, transcendentals=0),
        name=kernel.__name__,
    )(*operands)


def head_kernel(first, upq, gu, out, upq_out, gu_out, send_sem, recv_sem, local_sem):
    y, x, h, l, c = coordinates()
    rank = x * 4 + l * 2 + c
    wire = Wire(send_sem, recv_sem, local_sem)
    greet([16, 4] + PLANE)
    width = first.shape[1]
    cut = [0, width // 3 // 128 * 128, width // 3 // 128 * 256, width]
    parts = [pl.ds(cut[i], cut[i + 1] - cut[i]) for i in range(3)]
    a, b, d = parts
    mine = wire.local(first, out.at[0, 0, 0, 0, 0])
    one = [wire.send(first.at[:, p], out.at[0, 0, 1, 0, 0, :, p], 4) for p in parts]
    up_rows = upq.shape[1]
    gu_rows = gu.shape[2]
    up_place = lambda: upq_out.at[y, x, h, pl.ds((l * 2 + c) * up_rows, up_rows), :]
    gu_place = lambda: gu_out.at[:, x, pl.ds((l * 2 + c) * gu_rows, gu_rows), :]
    up_mine = wire.local(upq.at[rank], up_place())
    up_sent = [wire.send(upq.at[flip(rank, j)], up_place(), PLANE[j - 1]) for j in range(1, 8)]
    mine.wait()
    one[0].wait_recv()
    two_a = wire.send(out.at[0, 0, :, 0, 0, :, a], out.at[0, 0, :, 1, 0, :, a], 2)
    one[1].wait_recv()
    two_b = wire.send(out.at[0, 0, :, 0, 0, :, b], out.at[0, 1, :, 0, 0, :, b], 8)
    one[2].wait_recv()
    two_d = wire.send(out.at[0, 0, :, 0, 0, :, d], out.at[1, 0, :, 0, 0, :, d], 16)
    up_mine.wait()
    arrived(up_sent)
    up_h = wire.send(upq_out.at[y, :, h], upq_out.at[y, :, h], 4)
    two_a.wait_recv()
    three_a = wire.send(out.at[0, 0, :, :, 0, :, a], out.at[0, 1, :, :, 0, :, a], 8)
    two_b.wait_recv()
    three_b = wire.send(out.at[0, :, :, 0, 0, :, b], out.at[1, :, :, 0, 0, :, b], 16)
    two_d.wait_recv()
    three_d = wire.send(out.at[:, 0, :, 0, 0, :, d], out.at[:, 0, :, 1, 0, :, d], 2)
    three_a.wait_recv()
    four_a = wire.send(out.at[0, :, :, :, 0, :, a], out.at[1, :, :, :, 0, :, a], 16)
    three_b.wait_recv()
    four_b = wire.send(out.at[:, :, :, 0, 0, :, b], out.at[:, :, :, 1, 0, :, b], 2)
    three_d.wait_recv()
    four_d = wire.send(out.at[:, 0, :, :, 0, :, d], out.at[:, 1, :, :, 0, :, d], 8)
    five = [
        wire.send(out.at[0, :, :, :, 0, :, a], out.at[0, :, :, :, 1, :, a], 1),
        wire.send(out.at[:, :, :, 0, 0, :, b], out.at[:, :, :, 0, 1, :, b], 1),
        wire.send(out.at[:, 0, :, :, 0, :, d], out.at[:, 0, :, :, 1, :, d], 1),
    ]
    up_y = [wire.send(upq_out.at[y, :, h], upq_out.at[y, :, h], 16)]
    up_h.wait_recv()
    up_y += [wire.send(upq_out.at[y, :, 1 - h], upq_out.at[y, :, 1 - h], 16)]
    gu_mine = wire.local(gu.at[rank], gu_place())
    gu_sent = [wire.send(gu.at[flip(rank, j)], gu_place(), PLANE[j - 1]) for j in range(1, 8)]
    four_a.wait_recv()
    five += [wire.send(out.at[1, :, :, :, 0, :, a], out.at[1, :, :, :, 1, :, a], 1)]
    four_b.wait_recv()
    five += [wire.send(out.at[:, :, :, 1, 0, :, b], out.at[:, :, :, 1, 1, :, b], 1)]
    four_d.wait_recv()
    five += [wire.send(out.at[:, 1, :, :, 0, :, d], out.at[:, 1, :, :, 1, :, d], 1)]
    gu_mine.wait()
    arrived(five + up_y + gu_sent)
    wire.close()


def head(first, upq, gu):
    rows, width = first.shape
    outs = [
        jax.ShapeDtypeStruct((2, 2, 2, 2, 2, rows, width), bf16),
        jax.ShapeDtypeStruct((2, 2, 2, 4 * upq.shape[1], upq.shape[2]), bf16),
        jax.ShapeDtypeStruct((2, 2, 4 * gu.shape[2], gu.shape[3]), bf16),
    ]
    return moving(head_kernel, 1, outs, (first, upq, gu), wires(40, 4))


def plane_gather(wire, block, out, own):
    half = block.shape[0] // 2
    top, low = pl.ds(0, half), pl.ds(half, half)
    from_x = wire.send(block, out.at[1, 0, 0], 8)
    from_l = wire.send(block, out.at[0, 1, 0], 2)
    from_c = [wire.send(block, out.at[0, 0, 1], 1)]
    mine = wire.local(block, own) if own is not None else None

    def finish():
        from_x.wait_recv()
        second = [wire.send(out.at[1, 0, 0, top], out.at[1, 1, 0, top], 2)]
        from_l.wait_recv()
        second += [wire.send(out.at[0, 1, 0, low], out.at[1, 1, 0, low], 8)]
        cores = from_c + [wire.send(out.at[1, 0, 0], out.at[1, 0, 1], 1), wire.send(out.at[0, 1, 0], out.at[0, 1, 1], 1)]
        second[0].wait_recv()
        cores += [wire.send(out.at[1, 1, 0, top], out.at[1, 1, 1, top], 1)]
        second[1].wait_recv()
        cores += [wire.send(out.at[1, 1, 0, low], out.at[1, 1, 1, low], 1)]
        if mine is not None:
            mine.wait()
        arrived(cores)

    return finish


def spread(wire, block, place):
    y, x, h, l, c = coordinates()
    mine = wire.local(block, place(y, h))
    from_h = wire.send(block, place(y, h), 4)
    from_y = wire.send(block, place(y, h), 16)

    def second():
        from_h.wait_recv()
        last = wire.send(place(y, 1 - h), place(y, 1 - h), 16)

        def finish():
            mine.wait()
            arrived([from_y, last])

        return finish

    return second


def pack_kernel(block, out_weight, out, weight_out, weight_all, send_sem, recv_sem, local_sem):
    y, x, h, l, c = coordinates()
    wire = Wire(send_sem, recv_sem, local_sem)
    greet([16, 4, 8, 2, 1])
    near = block.shape[1]
    far = out.shape[5 - 1] - near
    columns, far_columns = pl.ds(0, near), pl.ds(near, far)
    from_h = wire.send(block.at[:, pl.ds(near - far, far)], out.at[0, 0, 0, :, far_columns], 4)
    near_out = out.at[:, :, :, :, columns]
    finish = plane_gather(wire, block, near_out, near_out.at[0, 0, 0])
    second = spread(wire, out_weight, lambda yy, hh: weight_all.at[yy, hh])
    from_h.wait_recv()
    far_out = out.at[:, :, :, :, far_columns]
    finish_far = plane_gather(wire, far_out.at[0, 0, 0], far_out, None)
    finish()
    finish_far()
    second()()
    swapped = wire.send(weight_all.at[:, 1 - c], weight_out.at[:, c], 1)
    kept = wire.local(weight_all.at[:, c], weight_out.at[:, c])
    kept.wait()
    swapped.wait_recv()
    wire.close()


def pack(block, out_weight):
    rows, near = block.shape
    outs = [
        jax.ShapeDtypeStruct((2, 2, 2, rows, near + 2 * HEAD_DIM), bf16),
        jax.ShapeDtypeStruct((2, 2) + out_weight.shape, bf16),
        jax.ShapeDtypeStruct((2, 2) + out_weight.shape, bf16),
    ]
    return moving(pack_kernel, 2, outs, (block, out_weight), wires(32, 4))[:2]


def plane_reduce(wire, parts, out, from_c, send_one, recv_one, send_two, recv_two):
    rows = parts.shape[3]
    half = rows // 2
    step = 16
    order = [(1, 1), (1, 0), (0, 1), (0, 0)]
    cores = {k: wire.send(parts.at[k[0], k[1], 1], from_c.at[k[0], k[1]], 1) for k in order}
    up = lambda ref, i: ref[pl.ds(i, step)].astype(f32)

    def pair(k, base, i):
        return up(parts.at[k[0], k[1], 0], base + i) + up(from_c.at[k[0], k[1]], base + i)

    def each(body):
        @pl.loop(0, half // step)
        def _(i):
            body(pl.multiple_of(i * step, step))

    state = {}

    def first():
        for k in order[:3]:
            cores[k].wait_recv()
            if k[0]:
                def fill(i, k=k):
                    send_one[0, k[1], pl.ds(i, step)] = pair(k, 0, i).astype(bf16)
                each(fill)
            if k[1]:
                def fill(i, k=k):
                    send_one[1, k[0], pl.ds(i, step)] = pair(k, half, i).astype(bf16)
                each(fill)
            if k == (1, 1):
                state["x1"] = wire.send(send_one.at[0, 1], recv_one.at[0, 1], 8)
                state["l1"] = wire.send(send_one.at[1, 1], recv_one.at[1, 1], 2)
            elif k == (1, 0):
                state["x0"] = wire.send(send_one.at[0, 0], recv_one.at[0, 0], 8)
            else:
                state["l0"] = wire.send(send_one.at[1, 0], recv_one.at[1, 0], 2)
        cores[(0, 0)].wait_recv()

    def middle():
        state["x1"].wait_recv()
        def fill(i):
            send_two[0, pl.ds(i, step)] = (pair((0, 1), 0, i) + up(recv_one.at[0, 1], i)).astype(bf16)
        each(fill)
        state["l2"] = wire.send(send_two.at[0], recv_two.at[0], 2)
        state["l1"].wait_recv()
        def fill(i):
            send_two[1, pl.ds(i, step)] = (pair((1, 0), half, i) + up(recv_one.at[1, 1], i)).astype(bf16)
        each(fill)
        state["x2"] = wire.send(send_two.at[1], recv_two.at[1], 8)

    def finish():
        state["x0"].wait_recv()
        state["l0"].wait_recv()
        state["l2"].wait_recv()
        def fill(i):
            out[pl.ds(i, step)] = pair((0, 0), 0, i) + up(recv_one.at[0, 0], i) + up(recv_two.at[0], i)
        each(fill)
        state["x2"].wait_recv()
        def fill(i):
            out[pl.ds(half + i, step)] = pair((0, 0), half, i) + up(recv_one.at[1, 0], i) + up(recv_two.at[1], i)
        each(fill)

    return first, middle, finish


def reduce_scratch(rows, width):
    half = rows // 2
    return [
        pltpu.VMEM((2, 2, rows, width), bf16),
        pltpu.VMEM((2, 2, half, width), bf16),
        pltpu.VMEM((2, 2, half, width), bf16),
        pltpu.VMEM((2, half, width), bf16),
        pltpu.VMEM((2, half, width), bf16),
    ]


def middle_kernel(parts, gate, out, gate_out, from_c, s1, r1, s2, r2, send_sem, recv_sem, local_sem):
    wire = Wire(send_sem, recv_sem, local_sem)
    greet([16, 4, 8, 2, 1])
    first, middle, finish = plane_reduce(wire, parts, out, from_c, s1, r1, s2, r2)
    second = spread(wire, gate, lambda yy, hh: gate_out.at[yy, :, hh])
    first()
    middle()
    last = second()
    finish()
    last()
    wire.close()


def middle_sum(parts, gate_set):
    rows, width = parts.shape[3:]
    outs = [
        jax.ShapeDtypeStruct((rows, width), f32),
        jax.ShapeDtypeStruct((2, 2, 2) + gate_set.shape[1:], bf16),
    ]
    return moving(
        middle_kernel, 3, outs, (parts, gate_set), reduce_scratch(rows, width) + wires(20, 2),
        in_specs=[VMEM, ANY], out_specs=[VMEM, ANY],
    )


def feed_kernel(block, up, out, up_out, send_sem, recv_sem, local_sem):
    wire = Wire(send_sem, recv_sem, local_sem)
    greet([16, 4, 8, 2, 1])
    finish = plane_gather(wire, block, out, out.at[0, 0, 0])
    second = spread(wire, up, lambda yy, hh: up_out.at[yy, :, hh])
    finish()
    second()()
    wire.close()


def feed_gather(block, up_set):
    outs = [
        jax.ShapeDtypeStruct((2, 2, 2) + block.shape, bf16),
        jax.ShapeDtypeStruct((2, 2, 2) + up_set.shape[1:], bf16),
    ]
    return moving(feed_kernel, 4, outs, (block, up_set), wires(16, 4))


def add_rows_into(rows, body, step=16):
    @pl.loop(0, rows // step)
    def _(i):
        body(pl.ds(pl.multiple_of(i * step, step), step))


def wide(ref, where):
    return ref[where].astype(f32)


def fold(wire, source, chunks, recv_y, send_h, recv_h, out):
    y, x, h, l, c = coordinates()
    sent = {}
    for hh, name in ((1 - h, "far"), (h, "near")):
        for i, (start, size) in enumerate(chunks):
            sent[name, i] = wire.send(source(1 - y, hh, i), recv_y.at[hh, pl.ds(start, size)], 16)
    passed = []

    def second():
        for i, (start, size) in enumerate(chunks):
            sent["far", i].wait_recv()
            mine, theirs, target = source(y, 1 - h, i), recv_y.at[1 - h, pl.ds(start, size)], send_h.at[pl.ds(start, size)]

            def body(r, mine=mine, theirs=theirs, target=target):
                target[r] = (wide(mine, r) + wide(theirs, r)).astype(bf16)

            add_rows_into(size, body)
            passed.append(wire.send(target, recv_h.at[pl.ds(start, size)], 4))

    def finish():
        for i, (start, size) in enumerate(chunks):
            sent["near", i].wait_recv()
            passed[i].wait_recv()
            mine, theirs = source(y, h, i), recv_y.at[h, pl.ds(start, size)]
            far, target = recv_h.at[pl.ds(start, size)], out.at[pl.ds(start, size)]

            def body(r, mine=mine, theirs=theirs, far=far, target=target):
                target[r] = (wide(mine, r) + wide(theirs, r) + wide(far, r)).astype(out.dtype)

            add_rows_into(size, body)

    return second, finish


def fold_scratch(rows, width):
    return [pltpu.VMEM((2, rows, width), bf16), pltpu.VMEM((rows, width), bf16), pltpu.VMEM((rows, width), bf16)]


def columns_of(grad):
    return lambda yy, hh, i: grad.at[yy, i, hh]


def rows_of(grad, chunks):
    return lambda yy, hh, i: grad.at[yy, hh, pl.ds(*chunks[i])]


def halves(rows):
    first = rows // 2 // 16 * 16 if rows % 32 == 0 else (rows // 2 + 15) // 16 * 16
    return [(0, first), (first, rows - first)]


def hand_back(wire, own, out):
    y, x, h, l, c = coordinates()
    rank = x * 4 + l * 2 + c
    rows = out.shape[1]
    piece = lambda k: own.at[pl.ds(pl.multiple_of(k * rows, rows), rows)]
    mine = wire.local(piece(rank), out.at[rank])
    sent = [wire.send(piece(flip(rank, j)), out.at[rank], PLANE[j - 1]) for j in range(1, 8)]

    def finish():
        mine.wait()
        arrived(sent)

    return finish


def mid_sum_kernel(parts, grad, out, grad_out, from_c, s1, r1, s2, r2, ry, sh, rh, send_sem, recv_sem, local_sem):
    wire = Wire(send_sem, recv_sem, local_sem)
    greet([16, 8, 4, 2, 1])
    chunks = halves(grad.shape[2])
    first, middle, finish = plane_reduce(wire, parts, out, from_c, s1, r1, s2, r2)
    second, last = fold(wire, rows_of(grad, chunks), chunks, ry, sh, rh, grad_out)
    first()
    second()
    middle()
    finish()
    last()
    wire.close()


def mid_sum(parts, grad):
    rows, width = parts.shape[3:]
    grad_rows = grad.shape[2]
    outs = [jax.ShapeDtypeStruct((rows, width), f32), jax.ShapeDtypeStruct((grad_rows, width), f32)]
    return moving(
        mid_sum_kernel, 5, outs, (parts, grad),
        reduce_scratch(rows, width) + fold_scratch(grad_rows, width) + wires(20, 1),
        in_specs=[VMEM, VMEM], out_specs=[VMEM, VMEM],
    )


def branch_kernel(block, grad, out, grad_out, ry, sh, rh, own, send_sem, recv_sem, local_sem):
    wire = Wire(send_sem, recv_sem, local_sem)
    greet([16, 4] + PLANE)
    size = grad.shape[3]
    chunks = [(0, size), (size, size)]
    finish = plane_gather(wire, block, out, out.at[0, 0, 0])
    second, last = fold(wire, columns_of(grad), chunks, ry, sh, rh, own)
    finish()
    second()
    last()
    hand_back(wire, own, grad_out)()
    wire.close()


def branch_gather(block, grad):
    outs = [
        jax.ShapeDtypeStruct((2, 2, 2) + block.shape, bf16),
        jax.ShapeDtypeStruct((8, grad.shape[3] // 4, grad.shape[4]), bf16),
    ]
    own = (2 * grad.shape[3], grad.shape[4])
    return moving(
        branch_kernel, 6, outs, (block, grad), fold_scratch(*own) + [pltpu.VMEM(own, bf16)] + wires(40, 4),
        in_specs=[ANY, VMEM],
    )


def back_sum_kernel(parts, grad, out, grad_out, from_c, s1, r1, s2, r2, ry, sh, rh, own, send_sem, recv_sem, local_sem):
    wire = Wire(send_sem, recv_sem, local_sem)
    greet([16, 4] + PLANE)
    size = grad.shape[3]
    chunks = [(0, size), (size, size)]
    first, middle, finish = plane_reduce(wire, parts, out, from_c, s1, r1, s2, r2)
    second, last = fold(wire, columns_of(grad), chunks, ry, sh, rh, own)
    first()
    second()
    middle()
    finish()
    last()
    hand_back(wire, own, grad_out)()
    wire.close()


def back_sum(parts, grad):
    rows, width = parts.shape[3:]
    own = (2 * grad.shape[3], grad.shape[4])
    outs = [
        jax.ShapeDtypeStruct((rows, width), f32),
        jax.ShapeDtypeStruct((8, grad.shape[3] // 4, grad.shape[4]), bf16),
    ]
    return moving(
        back_sum_kernel, 7, outs, (parts, grad),
        reduce_scratch(rows, width) + fold_scratch(*own) + [pltpu.VMEM(own, bf16)] + wires(40, 4),
        in_specs=[VMEM, VMEM], out_specs=[VMEM, ANY],
    )


def tail_kernel(parts, up_grad, out_grad, out, up_out, out_out, acc, recv, from_c, uy, us, ur, up_own, oy, os, orr, oc, out_sum, send_sem, recv_sem, local_sem):
    y, x, h, l, c = coordinates()
    wire = Wire(send_sem, recv_sem, local_sem)
    greet([16, 4] + PLANE)
    rows, width = out.shape
    third = width // 3 // 128 * 128
    cut = [(0, third), (third, third), (2 * third, width - 2 * third)]
    columns = [pl.ds(*k) for k in cut]
    bit_of = {"y": 0, "x": 1, "h": 2, "l": 3}
    orders = ["yxlh", "lyxh", "xlyh"]

    def where(fixed):
        return tuple(fixed.get(k, slice(None)) for k in "yxhl")

    swapped = wire.send(out_grad.at[:, 1 - c], oc.at[:, c], 1)
    cores = []
    for p in range(3):
        pair = []
        for side in (1, 0):
            place = where({orders[p][0]: side})
            pair.append(wire.send(parts.at[place + (1, slice(None), columns[p])], from_c.at[place + (slice(None), columns[p])], 1))
        cores.append(pair)
    chunks = [(0, up_grad.shape[3]), (up_grad.shape[3], up_grad.shape[3])]
    up_second, up_last = fold(wire, columns_of(up_grad), chunks, uy, us, ur, up_own)

    def every(fixed, body):
        free = [k for k in "yxhl" if k not in fixed]
        count = 2 ** len(free)

        @pl.loop(0, count * (rows // 16))
        def _(i):
            block = i // (rows // 16)
            r = pl.ds(pl.multiple_of((i % (rows // 16)) * 16, 16), 16)
            at = dict(fixed)
            for position, k in enumerate(reversed(free)):
                at[k] = (block // 2**position) % 2
            body(tuple(at[k] for k in "yxhl"), r)

    for side in (1, 0):
        for p in range(3):
            cores[p][1 - side].wait_recv()

            def body(at, r, p=p):
                total = wide(parts, at + (0, r, columns[p])) + wide(from_c, at + (r, columns[p]))
                acc[at + (r, columns[p])] = total.astype(bf16)

            every({orders[p][0]: side}, body)
            if side == 1:
                place = where({orders[p][0]: 1}) + (slice(None), columns[p])
                sent = wire.send(acc.at[place], recv.at[place], MASK[orders[p][0]])
                cores[p].append(sent)
    up_second()
    swapped.wait_recv()
    out_chunks = halves(out_grad.shape[2])

    kept = wire.local(out_grad.at[:, c], oc.at[:, c])
    kept.wait()
    out_source = lambda yy, hh, i: oc.at[yy, hh, pl.ds(*out_chunks[i])]
    out_second, out_last = fold(wire, out_source, out_chunks, oy, os, orr, out_sum)
    for step in range(4):
        for p in range(3):
            order = orders[p]
            fixed = {k: 0 for k in order[:step]}
            cores[p][-1].wait_recv()
            far = where({**fixed, order[step]: 1})

            def body(at, r, p=p, bit=order[step]):
                other = tuple(1 if k == bit else v for k, v in zip("yxhl", at))
                total = wide(acc, at + (r, columns[p])) + wide(recv, other + (r, columns[p]))
                if step == 3:
                    out[r, columns[p]] = total
                else:
                    acc[at + (r, columns[p])] = total.astype(bf16)

            every({**fixed, order[step]: 0}, body)
            if step < 3:
                place = where({**fixed, order[step]: 0, order[step + 1]: 1}) + (slice(None), columns[p])
                cores[p].append(wire.send(acc.at[place], recv.at[place], MASK[order[step + 1]]))
        if step == 0:
            out_second()
            up_last()
            up_back = hand_back(wire, up_own, up_out)
    out_last()

    def body(r):
        out_out[r] = out_sum[r]

    add_rows_into(out_sum.shape[0], body)
    up_back()
    wire.close()


def tail(parts, up_grad, out_grad):
    rows, width = parts.shape[5:]
    own = (2 * up_grad.shape[3], up_grad.shape[4])
    out_rows, out_width = out_grad.shape[2:]
    outs = [
        jax.ShapeDtypeStruct((rows, width), f32),
        jax.ShapeDtypeStruct((8, up_grad.shape[3] // 4, up_grad.shape[4]), bf16),
        jax.ShapeDtypeStruct((out_rows, out_width), f32),
    ]
    blocks = (2, 2, 2, 2, rows, width)
    scratch = [pltpu.VMEM(blocks, bf16)] * 3 + fold_scratch(*own) + [pltpu.VMEM(own, bf16)]
    scratch += fold_scratch(out_rows, out_width)
    scratch += [pltpu.VMEM((2, 2, out_rows, out_width), bf16), pltpu.VMEM((out_rows, out_width), f32)]
    return moving(
        tail_kernel, 8, outs, (parts, up_grad, out_grad), scratch + wires(60, 4),
        in_specs=[VMEM, VMEM, VMEM], out_specs=[VMEM, ANY, VMEM],
    )


def rope_table(places):
    half = HEAD_DIM // 2
    freqs = rope_base ** (-(2.0 * jnp.arange(half).astype(f32)) / HEAD_DIM)
    angles = places.astype(f32)[:, None] * freqs[None, :]
    return jnp.cos(angles), jnp.sin(angles)


def turn(values, cosine, sine, sign):
    half = HEAD_DIM // 2
    first = values[..., :half]
    second = values[..., half:]
    return jnp.concatenate([first * cosine - sign * second * sine, sign * first * sine + second * cosine], axis=-1)


QUERY_BLOCK = 384


def attend_kernel(q_ref, k_ref, v_ref, kidx_ref, qidx_ref, first_ref, o_ref, lse_ref):
    scores = lax.dot_general(q_ref[...], k_ref[...], (((1,), (1,)), ((), ())), preferred_element_type=f32)
    keys = kidx_ref[...]
    seen = (keys >= first_ref[...]) & (keys <= qidx_ref[...])
    scores = jnp.where(seen, scores * (1.0 / math.sqrt(HEAD_DIM)), masked_score)
    top = jnp.max(scores, axis=-1, keepdims=True)
    weights = jnp.exp(scores - top)
    total = jnp.sum(weights, axis=-1, keepdims=True)
    out = jnp.dot(weights.astype(bf16), v_ref[...], preferred_element_type=f32)
    o_ref[...] = out / total
    lse_ref[...] = top + jnp.log(total)


def attend(queries, keys, values, key_index, query_index, first_index):
    tokens = queries.shape[0]
    group = keys.shape[1]
    blocks = tokens // 2 // QUERY_BLOCK
    row = lambda g, a, i: (g * blocks + i, 0)
    head = lambda g, a, i: (g * blocks + i, a)
    whole = lambda g, a, i: (g, 0, 0)
    return pl.pallas_call(
        attend_kernel,
        grid=(2, 2, blocks),
        in_specs=[
            pl.BlockSpec((QUERY_BLOCK, HEAD_DIM), head),
            pl.BlockSpec((None, group, HEAD_DIM), whole),
            pl.BlockSpec((None, group, HEAD_DIM), whole),
            pl.BlockSpec((None, 1, group), whole),
            pl.BlockSpec((QUERY_BLOCK, 1), row),
            pl.BlockSpec((QUERY_BLOCK, 1), row),
        ],
        out_specs=[
            pl.BlockSpec((QUERY_BLOCK, HEAD_DIM), head),
            pl.BlockSpec((None, QUERY_BLOCK, 1), lambda g, a, i: (a, g * blocks + i, 0)),
        ],
        out_shape=[
            jax.ShapeDtypeStruct((tokens, 2 * HEAD_DIM), f32),
            jax.ShapeDtypeStruct((2, tokens, 1), f32),
        ],
        compiler_params=pltpu.CompilerParams(vmem_limit_bytes=48 * 1024 * 1024),
        cost_estimate=pl.CostEstimate(flops=4 * 2 * tokens * group * HEAD_DIM, bytes_accessed=12_000_000, transcendentals=2 * tokens * group),
        name="attend",
    )(queries, keys, values, key_index, query_index, first_index)


def attend_back_kernel(q_ref, do_ref, k_ref, v_ref, kidx_ref, qidx_ref, first_ref, lse_ref, delta_ref, dq_ref, dk_ref, dv_ref):
    scale = 1.0 / math.sqrt(HEAD_DIM)

    @pl.when((pl.program_id(1) == 0) & (pl.program_id(2) == 0))
    def _():
        dk_ref[...] = jnp.zeros_like(dk_ref)
        dv_ref[...] = jnp.zeros_like(dv_ref)

    queries = q_ref[...]
    grad = do_ref[...]
    keys = k_ref[...]
    scores = lax.dot_general(keys, queries, (((1,), (1,)), ((), ())), preferred_element_type=f32)
    index = kidx_ref[...]
    seen = (index >= first_ref[...]) & (index <= qidx_ref[...])
    probs = jnp.where(seen, jnp.exp(scores * scale - lse_ref[...]), 0.0)
    dv_ref[...] += jnp.dot(probs.astype(bf16), grad, preferred_element_type=f32)
    grad_probs = lax.dot_general(v_ref[...], grad, (((1,), (1,)), ((), ())), preferred_element_type=f32)
    grad_scores = (probs * (grad_probs - delta_ref[...]) * scale).astype(bf16)
    dk_ref[...] += jnp.dot(grad_scores, queries, preferred_element_type=f32)
    dq_ref[...] = lax.dot_general(grad_scores, keys, (((0,), (0,)), ((), ())), preferred_element_type=f32)


def attend_back(queries, grads, keys, values, key_index, query_index, first_index, lse, delta):
    tokens = queries.shape[0]
    group = keys.shape[1]
    blocks = tokens // 2 // QUERY_BLOCK
    row = lambda g, a, i: (0, g * blocks + i)
    head = lambda g, a, i: (g * blocks + i, a)
    whole = lambda g, a, i: (g, 0, 0)
    stat = lambda g, a, i: (a, 0, g * blocks + i)
    return pl.pallas_call(
        attend_back_kernel,
        grid=(2, 2, blocks),
        in_specs=[
            pl.BlockSpec((QUERY_BLOCK, HEAD_DIM), head),
            pl.BlockSpec((QUERY_BLOCK, HEAD_DIM), head),
            pl.BlockSpec((None, group, HEAD_DIM), whole),
            pl.BlockSpec((None, group, HEAD_DIM), whole),
            pl.BlockSpec((None, group, 1), whole),
            pl.BlockSpec((1, QUERY_BLOCK), row),
            pl.BlockSpec((1, QUERY_BLOCK), row),
            pl.BlockSpec((None, 1, QUERY_BLOCK), stat),
            pl.BlockSpec((None, 1, QUERY_BLOCK), stat),
        ],
        out_specs=[
            pl.BlockSpec((QUERY_BLOCK, HEAD_DIM), head),
            pl.BlockSpec((None, group, HEAD_DIM), whole),
            pl.BlockSpec((None, group, HEAD_DIM), whole),
        ],
        out_shape=[
            jax.ShapeDtypeStruct((tokens, 2 * HEAD_DIM), f32),
            jax.ShapeDtypeStruct((2, group, HEAD_DIM), f32),
            jax.ShapeDtypeStruct((2, group, HEAD_DIM), f32),
        ],
        compiler_params=pltpu.CompilerParams(vmem_limit_bytes=48 * 1024 * 1024),
        cost_estimate=pl.CostEstimate(flops=10 * 2 * tokens * group * HEAD_DIM, bytes_accessed=18_000_000, transcendentals=2 * tokens * group),
        name="attend_back",
    )(queries, grads, keys, values, key_index, query_index, first_index, lse, delta)


def plane_local(
    tokens,
    positions,
    cotangent,
    norm_in_gain,
    q_down,
    q_gain,
    q_up,
    key_proj,
    value_proj,
    out_proj,
    norm_mid_gain,
    w_gate,
    w_up,
    w_down,
):
    rows, width = tokens.shape
    rank_dim = q_down.shape[1]
    hidden_size = w_gate.shape[1]
    dp = lax.axis_index("dp")
    seq = lax.axis_index("seq")
    y, x = dp // 2, dp % 2
    h, l, c = seq // 4, (seq // 2) % 2, seq % 2
    device = dp * 8 + seq
    rank = x * 4 + l * 2 + c

    d_rows = q_down.shape[0]
    gain_rows = lambda gain: jnp.pad(gain, (0, d_rows - gain.shape[0]))
    gains = jnp.stack([norm_in_gain, gain_rows(q_gain), norm_mid_gain], axis=1)
    gains = jnp.pad(gains, ((0, 0), (0, 125)))
    first_set = jnp.concatenate([q_down, key_proj, value_proj, gains], axis=1).astype(bf16)
    split = rank_dim + 2 * HEAD_DIM

    place = jnp.arange(32, dtype=jnp.int32)
    block_order = place ^ device
    order = (block_order[:, None] * d_rows + jnp.arange(d_rows, dtype=jnp.int32)[None, :]).reshape(-1)
    permute = (jnp.arange(width, dtype=jnp.int32)[:, None] == order[None, :]).astype(bf16)
    block_permute = (place[:, None] == block_order[None, :]).astype(f32)
    exact = lax.Precision.HIGHEST

    places = gather_small(positions)
    blocks = jnp.arange(8, dtype=jnp.int32) ^ rank
    in_group = h * (4 * rows) + (blocks % 4)[:, None] * rows + jnp.arange(rows, dtype=jnp.int32)[None, :]
    query_index = in_group.reshape(-1)
    first_index = (in_group - places).reshape(-1)
    own_keys = in_group.reshape(2, 4 * rows)
    far_keys = own_keys + (1 - 2 * h) * (4 * rows)
    key_index = jnp.concatenate([own_keys, far_keys], axis=1)
    cosine, sine = rope_table(places.reshape(-1))

    up_query_pieces = (
        q_up.astype(bf16)
        .reshape(-1, 2, 2, 2, 2, HEAD_DIM)
        .transpose(2, 4, 3, 0, 1, 5)
        .reshape(8, -1, 2 * HEAD_DIM)
    )
    slice_size = hidden_size // 8
    piece_size = hidden_size // 32

    def hidden_pieces(weight):
        return (
            weight.reshape(-1, 2, 2, 2, 4, piece_size)
            .transpose(2, 4, 0, 1, 3, 5)
            .reshape(8, -1, slice_size)
        )

    gate_up_pieces = jnp.stack([hidden_pieces(w_gate.astype(bf16)), hidden_pieces(w_up.astype(bf16))], 1)
    first_set, up_query, gate_up_set = head(first_set, up_query_pieces, gate_up_pieces)
    first_set = first_set.reshape(width, -1)
    first_weight = first_set[:, :split]
    up_query = up_query.reshape(rank_dim, 2 * HEAD_DIM)
    out_rows = out_proj.shape[0]
    down_weight = gather_rows(w_down.astype(bf16)[None], y, h).reshape(slice_size, width)

    inputs = tokens.astype(f32)
    inputs_rel = jnp.dot(tokens, permute, preferred_element_type=f32)
    in_scale = rms_scale(inputs)
    in_gain = first_set[:, split].astype(f32)
    gain_blocks = first_set.reshape(32, d_rows, -1)
    query_gain = jnp.dot(block_permute, gain_blocks[:, : q_gain.shape[0], split + 1].astype(f32), precision=exact).reshape(-1)
    mid_gain = jnp.dot(block_permute, gain_blocks[:, :, split + 2].astype(f32), precision=exact).reshape(-1)
    normed = (inputs_rel * in_scale * in_gain).astype(bf16)
    mixed = jnp.dot(normed, first_weight, preferred_element_type=f32)
    compressed = mixed[:, :rank_dim]
    query_scale = rms_scale(compressed)
    compressed_normed = (compressed * query_scale * query_gain).astype(bf16)
    own_cosine, own_sine = cosine[:rows], sine[:rows]
    keys = turn(mixed[:, rank_dim : rank_dim + HEAD_DIM], own_cosine, own_sine, 1.0).astype(bf16)
    values = mixed[:, rank_dim + HEAD_DIM :].astype(bf16)
    plane_set, out_weight = pack(
        jnp.concatenate([compressed_normed, keys, values], axis=1), out_proj.astype(bf16)
    )
    out_weight = out_weight.reshape(2 * HEAD_DIM, width)
    plane_set = plane_set.reshape(2, 4 * rows, -1)
    plane_normed = plane_set.reshape(8 * rows, -1)[:, :rank_dim]
    own_kv, far_kv = plane_set[..., rank_dim:split], plane_set[..., split:]
    group_kv = jnp.concatenate([own_kv, far_kv], axis=1)
    group_keys, group_values = group_kv[..., :HEAD_DIM], group_kv[..., HEAD_DIM:]

    queries = jnp.dot(plane_normed, up_query, preferred_element_type=f32).reshape(8 * rows, 2, HEAD_DIM)
    queries = turn(queries, cosine[:, None], sine[:, None], 1.0).astype(bf16).reshape(8 * rows, 2 * HEAD_DIM)
    attended_full, log_total = attend(
        queries, group_keys, group_values, key_index[:, None, :], query_index[:, None], first_index[:, None]
    )
    attended = attended_full.astype(bf16)
    out_parts = jnp.dot(attended, out_weight, preferred_element_type=f32).astype(bf16)
    attention_sum, gate_weight = middle_sum(out_parts.reshape(2, 2, 2, rows, width), gate_up_set[0])
    middle = inputs + attention_sum
    gate_weight = gate_weight.reshape(width, slice_size)

    mid_scale = rms_scale(middle)
    normed_mid = (middle * mid_scale * mid_gain).astype(bf16)
    plane_cotangent = gather_plane(cotangent).reshape(8 * rows, width)
    plane_mid, up_weight = feed_gather(normed_mid, gate_up_set[1])
    plane_mid = plane_mid.reshape(8 * rows, width)
    up_weight = up_weight.reshape(width, slice_size)
    gate = jnp.dot(plane_mid, gate_weight, preferred_element_type=f32)
    upper = jnp.dot(plane_mid, up_weight, preferred_element_type=f32)
    sigmoid_gate = jax.nn.sigmoid(gate)
    silu_gate = gate * sigmoid_gate
    hidden = (silu_gate * upper).astype(bf16)
    grad_hidden = lax.dot_general(plane_cotangent, down_weight, (((1,), (1,)), ((), ())), preferred_element_type=f32)
    grad_gate = (grad_hidden * upper * sigmoid_gate * (1.0 + gate * (1.0 - sigmoid_gate))).astype(bf16)
    grad_upper = (grad_hidden * silu_gate).astype(bf16)
    mid_parts = lax.dot_general(grad_gate, gate_weight, (((1,), (1,)), ((), ())), preferred_element_type=f32)
    mid_parts = mid_parts + lax.dot_general(grad_upper, up_weight, (((1,), (1,)), ((), ())), preferred_element_type=f32)
    final_parts = jnp.dot(hidden, down_weight, preferred_element_type=f32).astype(bf16)
    output = (middle + scatter_plane(final_parts.reshape(8, rows, width))).astype(bf16)

    def over_tokens(left, right):
        return lax.dot_general(left, right, (((0,), (0,)), ((), ())), preferred_element_type=f32)

    grad_down = over_tokens(hidden, plane_cotangent).astype(bf16).reshape(2, 2, piece_size, width)
    grad_normed_mid, grad_down = mid_sum(mid_parts.astype(bf16).reshape(2, 2, 2, rows, width), grad_down)

    def hidden_whole(pieces):
        return (
            pieces.reshape(2, 4, -1, 2, 2, piece_size)
            .transpose(2, 3, 0, 4, 1, 5)
            .reshape(-1, hidden_size)
            .astype(f32)
        )

    by_rows = lambda grad: grad.astype(bf16).reshape(2, 2, 2, -1, grad.shape[-1])
    grad_gate_weight = by_rows(over_tokens(plane_mid, grad_gate))
    grad_up_weight = by_rows(over_tokens(plane_mid, grad_upper))

    grad_mid_norm, grad_mid_gain = norm_backward(middle, mid_scale, mid_gain, grad_normed_mid)
    grad_middle = cotangent.astype(f32) + grad_mid_norm
    branch_grad = grad_middle.astype(bf16)
    plane_branch, grad_gate_weight = branch_gather(branch_grad, grad_gate_weight)
    plane_branch = plane_branch.reshape(8 * rows, width)
    grad_gate_weight = hidden_whole(grad_gate_weight)
    grad_out = over_tokens(attended, plane_branch).astype(bf16).reshape(2, 2, out_rows, width)

    grad_attended = lax.dot_general(plane_branch, out_weight, (((1,), (1,)), ((), ())), preferred_element_type=f32)
    grad_attended = grad_attended.astype(bf16)
    delta = jnp.sum((grad_attended.astype(f32) * attended_full).reshape(8 * rows, 2, HEAD_DIM), axis=-1)
    grad_query, grad_keys, grad_values = attend_back(
        queries,
        grad_attended,
        group_keys,
        group_values,
        key_index[:, :, None],
        query_index[None, :],
        first_index[None, :],
        log_total.reshape(2, 1, 8 * rows),
        delta.T.reshape(2, 1, 8 * rows),
    )
    grad_query_pre = turn(grad_query.reshape(8 * rows, 2, HEAD_DIM), cosine[:, None], sine[:, None], -1.0)
    grad_query_pre = grad_query_pre.reshape(8 * rows, 2 * HEAD_DIM).astype(bf16)
    grad_up_query = by_rows(over_tokens(plane_normed, grad_query_pre))
    normed_parts = lax.dot_general(grad_query_pre, up_query, (((1,), (1,)), ((), ())), preferred_element_type=f32)
    key_value_parts = jnp.concatenate([grad_keys, grad_values], axis=-1).astype(bf16)
    key_value_parts = key_value_parts.reshape(2, 2, 4, rows, 2 * HEAD_DIM)
    back_set = jnp.concatenate(
        [
            normed_parts.astype(bf16).reshape(8, rows, rank_dim),
            key_value_parts[:, 0].reshape(8, rows, -1),
            key_value_parts[:, 1].reshape(8, rows, -1),
        ],
        axis=-1,
    )
    back_total, grad_up_weight = back_sum(back_set.reshape(2, 2, 2, rows, 2 * rank_dim), grad_up_weight)
    grad_up_weight = hidden_whole(grad_up_weight)
    grad_compressed_normed = back_total[:, :rank_dim]
    kv_grad = back_total[:, rank_dim:split] + swap(back_total[:, split:].astype(bf16), "h").astype(f32)
    grad_key_pre = turn(kv_grad[:, :HEAD_DIM], own_cosine, own_sine, -1.0).astype(bf16)
    grad_value_pre = kv_grad[:, HEAD_DIM:].astype(bf16)
    grad_compressed, grad_query_gain = norm_backward(compressed, query_scale, query_gain, grad_compressed_normed)
    mixed_grad = jnp.concatenate([grad_compressed.astype(bf16), grad_key_pre, grad_value_pre], axis=1)
    grad_normed = lax.dot_general(mixed_grad, first_weight, (((1,), (1,)), ((), ())), preferred_element_type=f32)
    grad_in_norm, grad_in_gain = norm_backward(inputs_rel, in_scale, in_gain, grad_normed)
    grad_in_norm = lax.dot_general(grad_in_norm.astype(bf16), permute, (((1,), (1,)), ((), ())), preferred_element_type=f32)
    grad_tokens = (grad_middle + grad_in_norm).astype(bf16)

    to_relative = lambda gain: lax.dot_general(
        block_permute, gain.reshape(32, -1), (((0,), (0,)), ((), ())), precision=exact
    )
    grad_gains = jnp.stack(
        [
            grad_in_gain.reshape(32, d_rows),
            jnp.pad(to_relative(grad_query_gain), ((0, 0), (0, d_rows - q_gain.shape[0]))),
            to_relative(grad_mid_gain),
        ],
        axis=-1,
    ).reshape(width, 3)
    first_grad = over_tokens(normed, mixed_grad).astype(bf16)
    first_grad = jnp.concatenate([first_grad, jnp.pad(grad_gains, ((0, 0), (0, 125))).astype(bf16)], axis=1)
    total, grad_up_query, grad_output_weight = tail(
        first_grad.reshape(2, 2, 2, 2, 2, d_rows, -1), grad_up_query, grad_out
    )
    grad_up_query = (
        grad_up_query.reshape(2, 2, 2, -1, 2, HEAD_DIM)
        .transpose(3, 4, 0, 2, 1, 5)
        .reshape(q_up.shape)
        .astype(f32)
    )
    return (
        output,
        grad_tokens,
        total[:, split],
        total[:, :rank_dim],
        total[: q_gain.shape[0], split + 1],
        grad_up_query,
        total[:, rank_dim : rank_dim + HEAD_DIM],
        total[:, rank_dim + HEAD_DIM : split],
        grad_output_weight,
        total[:, split + 2],
        grad_gate_weight,
        grad_up_weight,
        grad_down,
    )


def gather_small(value):
    value = value[None]
    for bit in "clx":
        value = jnp.concatenate([value, swap(value, bit)])
    return value


def solution(mesh):
    return jax.shard_map(
        plane_local if dict(mesh.shape) == {"dp": 4, "seq": 8} else local,
        mesh=mesh,
        in_specs=(
            P(("dp", "seq"), None),
            P(("dp", "seq")),
            P(("dp", "seq"), None),
            P(("dp", "seq")),
            P(("dp", "seq"), None),
            P(("dp", "seq")),
            P(("dp", "seq"), None),
            P(("dp", "seq"), None),
            P(("dp", "seq"), None),
            P(("dp", "seq"), None),
            P(("dp", "seq")),
            P(("dp", "seq"), None),
            P(("dp", "seq"), None),
            P(("dp", "seq"), None),
        ),
        out_specs=(
            P(("dp", "seq"), None),
            P(("dp", "seq"), None),
            P(("dp", "seq")),
            P(("dp", "seq"), None),
            P(("dp", "seq")),
            P(("dp", "seq"), None),
            P(("dp", "seq"), None),
            P(("dp", "seq"), None),
            P(("dp", "seq"), None),
            P(("dp", "seq")),
            P(("dp", "seq"), None),
            P(("dp", "seq"), None),
            P(("dp", "seq"), None),
        ),
        check_vma=False,
    )
```

```python
import math

import jax
import jax.numpy as jnp
from jax import lax
from jax.experimental import pallas as pl
from jax.experimental.pallas import tpu as pltpu
from jax.sharding import PartitionSpec as P

HEADS = 16
HEAD_DIM = 256


epsilon = 1e-05
rope_base = 10000.0
masked_score = -1e30


def rms_scale(values):
    return lax.rsqrt(jnp.mean(values * values, axis=-1, keepdims=True) + epsilon)


def rotary(values, places, sign):
    half = values.shape[-1] // 2
    freqs = rope_base ** (-(2.0 * jnp.arange(half).astype(jnp.float32)) / values.shape[-1])
    angles = places.astype(jnp.float32)[:, None] * freqs[None, :]
    cosine = jnp.cos(angles)[:, None, :]
    sine = jnp.sin(angles)[:, None, :]
    first = values[..., :half]
    second = values[..., half:]
    return jnp.concatenate(
        [first * cosine - sign * second * sine, sign * first * sine + second * cosine], axis=-1
    )


def norm_backward(inputs, scale, gain, grad_out):
    weighted = gain * grad_out
    grad_in = scale * weighted - inputs * scale * scale * scale * jnp.mean(
        weighted * inputs, axis=-1, keepdims=True
    )
    grad_gain = jnp.sum(grad_out * inputs * scale, axis=0)
    return (grad_in, grad_gain)


def add_rows(total, block, start):
    current = lax.dynamic_slice_in_dim(total, start, block.shape[0], 0)
    return lax.dynamic_update_slice_in_dim(total, current + block, start, 0)


def local(
    tokens,
    positions,
    cotangent,
    norm_in_gain,
    q_down,
    q_gain,
    q_up,
    key_proj,
    value_proj,
    out_proj,
    norm_mid_gain,
    w_gate,
    w_up,
    w_down,
):
    width = tokens.shape[0]
    scale = 1.0 / math.sqrt(HEAD_DIM)
    attention_set = (
        lax.all_gather(norm_in_gain.astype(jnp.bfloat16), ("dp", "seq"), axis=0, tiled=True),
        lax.all_gather(q_down.astype(jnp.bfloat16), ("dp", "seq"), axis=0, tiled=True),
        lax.all_gather(q_gain.astype(jnp.bfloat16), ("dp", "seq"), axis=0, tiled=True),
        lax.all_gather(q_up.astype(jnp.bfloat16), ("dp", "seq"), axis=0, tiled=True),
        lax.all_gather(key_proj.astype(jnp.bfloat16), ("dp", "seq"), axis=0, tiled=True),
        lax.all_gather(value_proj.astype(jnp.bfloat16), ("dp", "seq"), axis=0, tiled=True),
        lax.all_gather(out_proj.astype(jnp.bfloat16), ("dp", "seq"), axis=0, tiled=True),
    )
    feed_set = (
        lax.all_gather(norm_mid_gain.astype(jnp.bfloat16), ("dp", "seq"), axis=0, tiled=True),
        lax.all_gather(w_gate.astype(jnp.bfloat16), ("dp", "seq"), axis=0, tiled=True),
        lax.all_gather(w_up.astype(jnp.bfloat16), ("dp", "seq"), axis=0, tiled=True),
        lax.all_gather(w_down.astype(jnp.bfloat16), ("dp", "seq"), axis=0, tiled=True),
    )
    in_gain = attention_set[0].astype(jnp.float32)
    query_gain = attention_set[2].astype(jnp.float32)
    inputs = tokens.astype(jnp.float32)
    in_scale = rms_scale(inputs)
    normed = (inputs * in_scale * in_gain).astype(jnp.bfloat16)
    compressed = jnp.dot(normed, attention_set[1], preferred_element_type=jnp.float32)
    query_scale = rms_scale(compressed)
    compressed_normed = (compressed * query_scale * query_gain).astype(jnp.bfloat16)
    queries_raw = jnp.dot(
        compressed_normed, attention_set[3], preferred_element_type=jnp.float32
    ).reshape(width, HEADS, HEAD_DIM)
    queries = rotary(queries_raw, positions, 1.0).astype(jnp.bfloat16)
    keys_raw = jnp.dot(normed, attention_set[4], preferred_element_type=jnp.float32)
    keys = rotary(keys_raw[:, None, :], positions, 1.0)[:, 0, :].astype(jnp.bfloat16)
    values = jnp.dot(normed, attention_set[5], preferred_element_type=jnp.float32).astype(
        jnp.bfloat16
    )
    query_index = lax.axis_index("seq") * width + jnp.arange(width, dtype=jnp.int32)
    first_index = query_index - positions

    def visibility(key_start):
        key_index = key_start + jnp.arange(width, dtype=jnp.int32)
        seen = (key_index[None, :] >= first_index[:, None]) & (
            key_index[None, :] <= query_index[:, None]
        )
        return seen[:, None, :]

    start_state = (
        jnp.full((width, HEADS), masked_score, jnp.float32),
        jnp.zeros((width, HEADS), jnp.float32),
        jnp.zeros((width, HEADS, HEAD_DIM), jnp.float32),
    )
    carry = start_state
    piece = (
        lax.all_gather(keys, "seq", axis=0, tiled=True),
        lax.all_gather(values, "seq", axis=0, tiled=True),
    )
    blocks = piece[0].shape[0] // width
    key_blocks = piece[0].reshape(blocks, width, HEAD_DIM)
    value_blocks = piece[1].reshape(blocks, width, HEAD_DIM)

    def forward_one_block(state, item):
        key_block, value_block, number = item
        key_start = number * width
        top, total, accum = state
        seen = visibility(key_start)
        scores = (
            jnp.einsum("thd,kd->thk", queries, key_block, preferred_element_type=jnp.float32)
            * scale
        )
        scores = jnp.where(seen, scores, masked_score)
        new_top = jnp.maximum(top, jnp.max(scores, axis=-1))
        weights = jnp.where(seen, jnp.exp(scores - new_top[..., None]), 0.0)
        decay = jnp.exp(top - new_top)
        total = total * decay + jnp.sum(weights, axis=-1)
        accum = accum * decay[..., None] + jnp.einsum(
            "thk,kd->thd",
            weights.astype(jnp.bfloat16),
            value_block,
            preferred_element_type=jnp.float32,
        )
        state = (new_top, total, accum)
        return (state, None)

    carry, _ = lax.scan(
        forward_one_block, carry, (key_blocks, value_blocks, jnp.arange(blocks, dtype=jnp.int32))
    )
    top, total, accum = carry
    attended_full = accum / total[..., None]
    log_total = top + jnp.log(total)
    attended = attended_full.reshape(width, HEADS * HEAD_DIM).astype(jnp.bfloat16)
    middle = inputs + jnp.dot(attended, attention_set[6], preferred_element_type=jnp.float32)
    mid_gain = feed_set[0].astype(jnp.float32)
    mid_scale = rms_scale(middle)
    normed_mid = (middle * mid_scale * mid_gain).astype(jnp.bfloat16)
    gate = jnp.dot(normed_mid, feed_set[1], preferred_element_type=jnp.float32)
    upper = jnp.dot(normed_mid, feed_set[2], preferred_element_type=jnp.float32)
    sigmoid_gate = jax.nn.sigmoid(gate)
    silu_gate = gate * sigmoid_gate
    hidden = (silu_gate * upper).astype(jnp.bfloat16)
    output = (middle + jnp.dot(hidden, feed_set[3], preferred_element_type=jnp.float32)).astype(
        jnp.bfloat16
    )
    feed_back = (
        lax.all_gather(norm_mid_gain.astype(jnp.bfloat16), ("dp", "seq"), axis=0, tiled=True),
        lax.all_gather(w_gate.astype(jnp.bfloat16), ("dp", "seq"), axis=0, tiled=True),
        lax.all_gather(w_up.astype(jnp.bfloat16), ("dp", "seq"), axis=0, tiled=True),
        lax.all_gather(w_down.astype(jnp.bfloat16), ("dp", "seq"), axis=0, tiled=True),
    )
    grad_out_full = cotangent.astype(jnp.float32)
    grad_down = jnp.einsum("tf,td->fd", hidden, cotangent, preferred_element_type=jnp.float32)
    grad_hidden = jnp.einsum(
        "td,fd->tf", cotangent, feed_back[3], preferred_element_type=jnp.float32
    )
    grad_gate = (grad_hidden * upper * sigmoid_gate * (1.0 + gate * (1.0 - sigmoid_gate))).astype(
        jnp.bfloat16
    )
    grad_upper = (grad_hidden * silu_gate).astype(jnp.bfloat16)
    grad_gate_weight = jnp.einsum(
        "td,tf->df", normed_mid, grad_gate, preferred_element_type=jnp.float32
    )
    grad_up_weight = jnp.einsum(
        "td,tf->df", normed_mid, grad_upper, preferred_element_type=jnp.float32
    )
    grad_normed_mid = jnp.einsum(
        "tf,df->td", grad_gate, feed_back[1], preferred_element_type=jnp.float32
    ) + jnp.einsum("tf,df->td", grad_upper, feed_back[2], preferred_element_type=jnp.float32)
    grad_mid_norm, grad_mid_gain = norm_backward(
        middle, mid_scale, feed_back[0].astype(jnp.float32), grad_normed_mid
    )
    grad_middle = grad_out_full + grad_mid_norm
    feed_grads = (
        lax.psum_scatter(grad_mid_gain, ("dp", "seq"), scatter_dimension=0, tiled=True),
        lax.psum_scatter(grad_gate_weight, ("dp", "seq"), scatter_dimension=0, tiled=True),
        lax.psum_scatter(grad_up_weight, ("dp", "seq"), scatter_dimension=0, tiled=True),
        lax.psum_scatter(grad_down, ("dp", "seq"), scatter_dimension=0, tiled=True),
    )
    attention_back = (
        lax.all_gather(norm_in_gain.astype(jnp.bfloat16), ("dp", "seq"), axis=0, tiled=True),
        lax.all_gather(q_down.astype(jnp.bfloat16), ("dp", "seq"), axis=0, tiled=True),
        lax.all_gather(q_gain.astype(jnp.bfloat16), ("dp", "seq"), axis=0, tiled=True),
        lax.all_gather(q_up.astype(jnp.bfloat16), ("dp", "seq"), axis=0, tiled=True),
        lax.all_gather(key_proj.astype(jnp.bfloat16), ("dp", "seq"), axis=0, tiled=True),
        lax.all_gather(value_proj.astype(jnp.bfloat16), ("dp", "seq"), axis=0, tiled=True),
        lax.all_gather(out_proj.astype(jnp.bfloat16), ("dp", "seq"), axis=0, tiled=True),
    )
    branch_grad = grad_middle.astype(jnp.bfloat16)
    grad_output_weight = jnp.einsum(
        "ta,td->ad", attended, branch_grad, preferred_element_type=jnp.float32
    )
    grad_attended = (
        jnp.einsum("td,ad->ta", branch_grad, attention_back[6], preferred_element_type=jnp.float32)
        .reshape(width, HEADS, HEAD_DIM)
        .astype(jnp.bfloat16)
    )
    delta = jnp.sum(grad_attended.astype(jnp.float32) * attended_full, axis=-1)
    group_rows = width * lax.axis_size("seq")
    back_state = (
        jnp.zeros((width, HEADS, HEAD_DIM), jnp.float32),
        jnp.zeros((group_rows, HEAD_DIM), jnp.float32),
        jnp.zeros((group_rows, HEAD_DIM), jnp.float32),
    )
    carry = back_state
    piece = (
        lax.all_gather(keys, "seq", axis=0, tiled=True),
        lax.all_gather(values, "seq", axis=0, tiled=True),
    )
    blocks = piece[0].shape[0] // width
    key_blocks = piece[0].reshape(blocks, width, HEAD_DIM)
    value_blocks = piece[1].reshape(blocks, width, HEAD_DIM)

    def backward_one_block(state, item):
        key_block, value_block, number = item
        key_start = number * width
        grad_query, grad_keys, grad_values = state
        seen = visibility(key_start)
        scores = (
            jnp.einsum("thd,kd->thk", queries, key_block, preferred_element_type=jnp.float32)
            * scale
        )
        probs = jnp.where(seen, jnp.exp(scores - log_total[..., None]), 0.0)
        grad_value_block = jnp.einsum(
            "thk,thd->kd",
            probs.astype(jnp.bfloat16),
            grad_attended,
            preferred_element_type=jnp.float32,
        )
        grad_probs = jnp.einsum(
            "thd,kd->thk", grad_attended, value_block, preferred_element_type=jnp.float32
        )
        grad_scores = (probs * (grad_probs - delta[..., None]) * scale).astype(jnp.bfloat16)
        grad_query = grad_query + jnp.einsum(
            "thk,kd->thd", grad_scores, key_block, preferred_element_type=jnp.float32
        )
        grad_key_block = jnp.einsum(
            "thk,thd->kd", grad_scores, queries, preferred_element_type=jnp.float32
        )
        state = (
            grad_query,
            add_rows(grad_keys, grad_key_block, key_start),
            add_rows(grad_values, grad_value_block, key_start),
        )
        return (state, None)

    carry, _ = lax.scan(
        backward_one_block, carry, (key_blocks, value_blocks, jnp.arange(blocks, dtype=jnp.int32))
    )
    grad_query, grad_keys, grad_values = carry
    local_key_grad, local_value_grad = (
        lax.psum_scatter(
            grad_keys.astype(jnp.bfloat16), "seq", scatter_dimension=0, tiled=True
        ).astype(jnp.float32),
        lax.psum_scatter(
            grad_values.astype(jnp.bfloat16), "seq", scatter_dimension=0, tiled=True
        ).astype(jnp.float32),
    )
    grad_key_pre = rotary(local_key_grad[:, None, :], positions, -1.0)[:, 0, :].astype(jnp.bfloat16)
    grad_value_pre = local_value_grad.astype(jnp.bfloat16)
    grad_query_pre = (
        rotary(grad_query, positions, -1.0).reshape(width, HEADS * HEAD_DIM).astype(jnp.bfloat16)
    )
    grad_up_query = jnp.einsum(
        "tr,ta->ra", compressed_normed, grad_query_pre, preferred_element_type=jnp.float32
    )
    grad_compressed_normed = jnp.einsum(
        "ta,ra->tr", grad_query_pre, attention_back[3], preferred_element_type=jnp.float32
    )
    grad_compressed, grad_query_gain = norm_backward(
        compressed, query_scale, attention_back[2].astype(jnp.float32), grad_compressed_normed
    )
    grad_compressed = grad_compressed.astype(jnp.bfloat16)
    grad_down_weight = jnp.einsum(
        "td,tr->dr", normed, grad_compressed, preferred_element_type=jnp.float32
    )
    grad_key_weight = jnp.einsum(
        "td,te->de", normed, grad_key_pre, preferred_element_type=jnp.float32
    )
    grad_value_weight = jnp.einsum(
        "td,te->de", normed, grad_value_pre, preferred_element_type=jnp.float32
    )
    grad_normed = jnp.einsum(
        "tr,dr->td", grad_compressed, attention_back[1], preferred_element_type=jnp.float32
    )
    grad_normed = grad_normed + jnp.einsum(
        "te,de->td", grad_key_pre, attention_back[4], preferred_element_type=jnp.float32
    )
    grad_normed = grad_normed + jnp.einsum(
        "te,de->td", grad_value_pre, attention_back[5], preferred_element_type=jnp.float32
    )
    grad_in_norm, grad_in_gain = norm_backward(
        inputs, in_scale, attention_back[0].astype(jnp.float32), grad_normed
    )
    grad_tokens = (grad_middle + grad_in_norm).astype(jnp.bfloat16)
    attention_grads = (
        lax.psum_scatter(grad_in_gain, ("dp", "seq"), scatter_dimension=0, tiled=True),
        lax.psum_scatter(grad_down_weight, ("dp", "seq"), scatter_dimension=0, tiled=True),
        lax.psum_scatter(grad_query_gain, ("dp", "seq"), scatter_dimension=0, tiled=True),
        lax.psum_scatter(grad_up_query, ("dp", "seq"), scatter_dimension=0, tiled=True),
        lax.psum_scatter(grad_key_weight, ("dp", "seq"), scatter_dimension=0, tiled=True),
        lax.psum_scatter(grad_value_weight, ("dp", "seq"), scatter_dimension=0, tiled=True),
        lax.psum_scatter(grad_output_weight, ("dp", "seq"), scatter_dimension=0, tiled=True),
    )
    return (
        output,
        grad_tokens,
        attention_grads[0],
        attention_grads[1],
        attention_grads[2],
        attention_grads[3],
        attention_grads[4],
        attention_grads[5],
        attention_grads[6],
        feed_grads[0],
        feed_grads[1],
        feed_grads[2],
        feed_grads[3],
    )


bf16 = jnp.bfloat16
f32 = jnp.float32
ANY = pl.BlockSpec(memory_space=pl.ANY)
VMEM = pl.BlockSpec(memory_space=pltpu.VMEM)
PLANE = [j // 4 * 8 + j % 4 for j in range(1, 8)]
LINKS = [16, 8, 4, 2, 1]


def flip(number, bits):
    bit = 1
    while bit <= bits:
        if bits & bit:
            number = number + bit - 2 * bit * ((number // bit) % 2)
        bit *= 2
    return number


def coordinates():
    dp = lax.axis_index("dp")
    seq = lax.axis_index("seq")
    return dp // 2, dp % 2, seq // 4, (seq // 2) % 2, seq % 2


def partner(mask):
    return flip(lax.axis_index("dp"), mask // 8), flip(lax.axis_index("seq"), mask % 8)


def greet(masks):
    barrier = pltpu.get_barrier_semaphore()
    for mask in masks:
        pl.semaphore_signal(barrier, inc=1, device_id=partner(mask), device_id_type=pl.DeviceIdType.MESH)
    pl.semaphore_wait(barrier, len(masks))


class Wire:
    def __init__(self, send_sem, recv_sem, local_sem):
        self.send_sem, self.recv_sem, self.local_sem = send_sem, recv_sem, local_sem
        self.copies = []
        self.locals = 0

    def send(self, src, dst, mask):
        k = len(self.copies)
        copy = pltpu.make_async_remote_copy(
            src_ref=src,
            dst_ref=dst,
            send_sem=self.send_sem.at[k],
            recv_sem=self.recv_sem.at[k],
            device_id=partner(mask),
            device_id_type=pl.DeviceIdType.MESH,
        )
        copy.start()
        self.copies.append(copy)
        return copy

    def local(self, src, dst):
        copy = pltpu.make_async_copy(src, dst, self.local_sem.at[self.locals])
        self.locals += 1
        copy.start()
        return copy

    def close(self):
        for copy in self.copies:
            copy.wait_send()


def wires(remote, local):
    return [pltpu.SemaphoreType.DMA((remote,)), pltpu.SemaphoreType.DMA((remote,)), pltpu.SemaphoreType.DMA((local,))]


def arrived(copies):
    for copy in copies:
        copy.wait_recv()


def landed(copies):
    for copy in copies:
        copy.wait()


def moving(kernel, number, outs, operands, scratch, in_specs=None, out_specs=None, limit=56):
    return pl.pallas_call(
        kernel,
        out_shape=outs,
        in_specs=in_specs or [ANY] * len(operands),
        out_specs=out_specs or [ANY] * len(outs),
        scratch_shapes=scratch,
        compiler_params=pltpu.CompilerParams(
            collective_id=number, has_side_effects=True, vmem_limit_bytes=limit * 1024 * 1024
        ),
        cost_estimate=pl.CostEstimate(flops=0, bytes_accessed=100_000_000, transcendentals=0),
        name=kernel.__name__,
    )(*operands)


def shaped(shape, dtype=bf16):
    return jax.ShapeDtypeStruct(tuple(shape), dtype)


def each_rows(rows, body, step=16):
    @pl.loop(0, rows // step)
    def _(i):
        body(pl.ds(pl.multiple_of(i * step, step), step))


def wide(ref, where):
    return ref[where].astype(f32)


def plane_gather(wire, block, out, own):
    half = block.shape[0] // 2
    top, low = pl.ds(0, half), pl.ds(half, half)
    from_x = wire.send(block, out.at[1, 0, 0], 8)
    from_l = wire.send(block, out.at[0, 1, 0], 2)
    cores = [wire.send(block, out.at[0, 0, 1], 1)]
    mine = wire.local(block, own) if own is not None else None

    def second():
        from_x.wait_recv()
        diagonal = [wire.send(out.at[1, 0, 0, top], out.at[1, 1, 0, top], 2)]
        from_l.wait_recv()
        diagonal += [wire.send(out.at[0, 1, 0, low], out.at[1, 1, 0, low], 8)]
        cores.append(wire.send(out.at[1, 0, 0], out.at[1, 0, 1], 1))
        cores.append(wire.send(out.at[0, 1, 0], out.at[0, 1, 1], 1))

        def finish():
            diagonal[0].wait_recv()
            cores.append(wire.send(out.at[1, 1, 0, top], out.at[1, 1, 1, top], 1))
            diagonal[1].wait_recv()
            cores.append(wire.send(out.at[1, 1, 0, low], out.at[1, 1, 1, low], 1))
            if mine is not None:
                mine.wait()
            arrived(cores)

        return finish

    return second


def plane_reduce(wire, parts, out, kept, from_c, send_one, recv_one, send_two, recv_two):
    half = kept.shape[2] // 2
    order = [(1, 1), (1, 0), (0, 1), (0, 0)]
    cores = {k: wire.send(parts.at[k[0], k[1], 1], from_c.at[k[0], k[1]], 1) for k in order}
    loads = {k: wire.local(parts.at[k[0], k[1], 0], kept.at[k[0], k[1]]) for k in order}

    def pair(k, r):
        return wide(kept.at[k[0], k[1]], r) + wide(from_c.at[k[0], k[1]], r)

    def below(r):
        return pl.ds(half + r.start, r.size)

    state = {}

    def first():
        for k in order[:3]:
            loads[k].wait()
            cores[k].wait_recv()
            if k[0]:

                def fill(r, k=k):
                    send_one[0, k[1], r] = pair(k, r).astype(bf16)

                each_rows(half, fill)
                state["x", k[1]] = wire.send(send_one.at[0, k[1]], recv_one.at[0, k[1]], 8)
            if k[1]:

                def fill(r, k=k):
                    send_one[1, k[0], r] = pair(k, below(r)).astype(bf16)

                each_rows(half, fill)
                state["l", k[0]] = wire.send(send_one.at[1, k[0]], recv_one.at[1, k[0]], 2)
        loads[0, 0].wait()
        cores[0, 0].wait_recv()

    def middle():
        state["x", 1].wait_recv()

        def fill(r):
            send_two[0, r] = (pair((0, 1), r) + wide(recv_one.at[0, 1], r)).astype(bf16)

        each_rows(half, fill)
        state["l2"] = wire.send(send_two.at[0], recv_two.at[0], 2)
        state["l", 1].wait_recv()

        def fill(r):
            send_two[1, r] = (pair((1, 0), below(r)) + wide(recv_one.at[1, 1], r)).astype(bf16)

        each_rows(half, fill)
        state["x2"] = wire.send(send_two.at[1], recv_two.at[1], 8)

    def finish():
        state["x", 0].wait_recv()
        state["l2"].wait_recv()

        def fill(r):
            out[r] = pair((0, 0), r) + wide(recv_one.at[0, 0], r) + wide(recv_two.at[0], r)

        each_rows(half, fill)
        state["l", 0].wait_recv()
        state["x2"].wait_recv()

        def fill(r):
            out[below(r)] = pair((0, 0), below(r)) + wide(recv_one.at[1, 0], r) + wide(recv_two.at[1], r)

        each_rows(half, fill)

    return first, middle, finish


def reduce_scratch(rows, width):
    half = rows // 2
    return [
        pltpu.VMEM((2, 2, rows, width), bf16),
        pltpu.VMEM((2, 2, rows, width), bf16),
        pltpu.VMEM((2, 2, half, width), bf16),
        pltpu.VMEM((2, 2, half, width), bf16),
        pltpu.VMEM((2, half, width), bf16),
        pltpu.VMEM((2, half, width), bf16),
    ]


def over_y(wire, own, far, place):
    y, x, h, l, c = coordinates()
    mine = [wire.local(own, place(y, h)), wire.local(far, place(y, 1 - h))]
    sent = [wire.send(own, place(y, h), 16), wire.send(far, place(y, 1 - h), 16)]

    def finish():
        landed(mine)
        arrived(sent)

    return finish


def head_kernel(
    q_down, key, value, gains, q_up, gate, up, out_proj, w_down, places,
    first_out, upq_out, gu_out, wo_out, wo_far, wd_out, gains_out, places_out,
    first, upq, gu, staged, send_sem, recv_sem, local_sem,
):
    y, x, h, l, c = coordinates()
    rank = x * 4 + l * 2 + c
    wire = Wire(send_sem, recv_sem, local_sem)
    greet([16, 4] + PLANE)
    r1, r2 = q_down.shape[1], q_down.shape[1] + key.shape[1]
    first[:, :r1] = q_down[...].astype(bf16)
    first[:, r1:r2] = key[...].astype(bf16)
    first[:, r2:] = value[...].astype(bf16)
    width = first.shape[1]
    third = width // 3
    a, b, d = (pl.ds(i * third, third) for i in range(3))
    mine = [wire.local(first, first_out.at[y, x, h, l, c]), wire.local(gains, gains_out.at[y, x, h, l, c])]
    one = [wire.send(first.at[:, p], first_out.at[y, x, h, l, c, :, p], 4) for p in (a, b, d)]
    gain = wire.send(gains, gains_out.at[y, x, h, l, c], 4)
    place = [wire.send(places, places_out.at[j], PLANE[j - 1]) for j in range(1, 8)]
    place_mine = wire.local(places, places_out.at[0])
    heads = q_up.shape[1] // HEAD_DIM
    for head in range(heads):
        hy, hx, hh, hl = head // 8, head // 4 % 2, head // 2 % 2, head % 2
        target = hx * 4 + hl * 2 + hh
        upq[target, :, hy * HEAD_DIM : (hy + 1) * HEAD_DIM] = q_up[:, head * HEAD_DIM : (head + 1) * HEAD_DIM].astype(bf16)
    up_rows = upq.shape[1]
    up_place = lambda: upq_out.at[y, x, h, pl.ds((l * 2 + c) * up_rows, up_rows), :]
    up_mine = wire.local(upq.at[rank], up_place())
    up_sent = [wire.send(upq.at[flip(rank, j)], up_place(), PLANE[j - 1]) for j in range(1, 8)]
    wo_out[...] = out_proj[...].astype(bf16)
    wo_sent = wire.send(wo_out, wo_far, 4)
    piece = gate.shape[1] // 32
    size = 4 * piece
    main = size // 128 * 128
    for target in range(8):
        for where, weight in ((0, gate), (1, up)):
            for q in range(4):
                n = q // 2 * 16 + target // 4 * 8 + q % 2 * 4 + target % 4
                staged[where, :, q * piece : (q + 1) * piece] = weight[:, n * piece : (n + 1) * piece]
        gu[target, :, :main] = staged[0, :, :main].astype(bf16)
        rest = size - main
        both = jnp.concatenate([staged[0, :, main : main + rest], staged[1, :, main : main + rest]], axis=1)
        gu[target, :, main : main + 2 * rest] = both.astype(bf16)
        gu[target, :, main + 2 * rest :] = staged[1, :, :main].astype(bf16)
    gu_rows = gu.shape[1]
    gu_place = lambda: gu_out.at[x, pl.ds((l * 2 + c) * gu_rows, gu_rows), :]
    gu_mine = wire.local(gu.at[rank], gu_place())
    gu_sent = [wire.send(gu.at[flip(rank, j)], gu_place(), PLANE[j - 1]) for j in range(1, 8)]
    wd_out[...] = w_down[...].astype(bf16)
    landed(mine)

    every = slice(None)

    def step(held, columns, mask):
        at = tuple(every if k in held else v for k, v in zip("yxhlc", (y, x, h, l, c)))
        if columns is None:
            return wire.send(gains_out.at[at], gains_out.at[at], mask)
        place = first_out.at[at + (every, columns)]
        return wire.send(place, place, mask)

    one[0].wait_recv()
    two_a = step("h", a, 2)
    one[1].wait_recv()
    two_b = step("h", b, 8)
    one[2].wait_recv()
    two_d = step("h", d, 16)
    gain.wait_recv()
    gain = step("h", None, 2)
    up_mine.wait()
    arrived(up_sent)
    up_h = wire.send(upq_out.at[y, :, h], upq_out.at[y, :, h], 4)
    two_a.wait_recv()
    three_a = step("hl", a, 8)
    two_b.wait_recv()
    three_b = step("hx", b, 16)
    two_d.wait_recv()
    three_d = step("hy", d, 2)
    gain.wait_recv()
    gain = step("hl", None, 8)
    up_y = [wire.send(upq_out.at[y, :, h], upq_out.at[y, :, h], 16)]
    three_a.wait_recv()
    four_a = step("hlx", a, 16)
    three_b.wait_recv()
    four_b = step("hxy", b, 2)
    three_d.wait_recv()
    four_d = step("hyl", d, 8)
    five = [step("hlx", a, 1), step("hxy", b, 1), step("hyl", d, 1)]
    gain.wait_recv()
    gain = step("hlx", None, 16)
    up_h.wait_recv()
    up_y += [wire.send(upq_out.at[y, :, 1 - h], upq_out.at[y, :, 1 - h], 16)]

    def last(held, bit, columns):
        at = {k: every if k in held else v for k, v in zip("yxhlc", (y, x, h, l, c))}
        at[bit] = 1 - dict(zip("yxhlc", (y, x, h, l, c)))[bit]
        place = first_out.at[tuple(at[k] for k in "yxhlc") + (every, columns)]
        return wire.send(place, place, 1)

    four_a.wait_recv()
    five += [last("hlx", "y", a)]
    four_b.wait_recv()
    five += [last("hxy", "l", b)]
    gain.wait_recv()
    five += [step("hlxy", None, 1)]
    four_d.wait_recv()
    five += [last("hyl", "x", d)]
    gu_mine.wait()
    place_mine.wait()
    arrived(five + up_y + gu_sent + place + [wo_sent])
    wire.close()


def head(q_down, key, value, gains, q_up, gate, up, out_proj, w_down, places):
    rows = q_down.shape[0]
    width = q_down.shape[1] + 2 * key.shape[1]
    columns = gate.shape[1] // 4
    slice_size = gate.shape[1] // 8
    outs = [
        shaped((2, 2, 2, 2, 2, rows, width)),
        shaped((2, 2, 2, 4 * q_up.shape[0], 2 * HEAD_DIM)),
        shaped((2, 4 * rows, columns)),
        shaped(out_proj.shape),
        shaped(out_proj.shape),
        shaped(w_down.shape),
        shaped((2, 2, 2, 2, 2) + gains.shape, f32),
        shaped((8,) + places.shape, jnp.int32),
    ]
    scratch = [
        pltpu.VMEM((rows, width), bf16),
        pltpu.VMEM((8, q_up.shape[0], 2 * HEAD_DIM), bf16),
        pltpu.VMEM((8, rows, columns), bf16),
        pltpu.VMEM((2, rows, slice_size), f32),
    ]
    operands = (q_down, key, value, gains, q_up, gate, up, out_proj, w_down, places)
    return moving(
        head_kernel, 1, outs, operands, scratch + wires(60, 8),
        in_specs=[VMEM] * len(operands),
        out_specs=[ANY, ANY, ANY, VMEM, ANY, VMEM, ANY, ANY],
    )


def turned(values, cosine, sine, sign):
    half = HEAD_DIM // 2
    out = []
    for start in range(0, values.shape[1], HEAD_DIM):
        one, two = values[:, start : start + half], values[:, start + half : start + HEAD_DIM]
        out += [one * cosine - sign * two * sine, sign * one * sine + two * cosine]
    return jnp.concatenate(out, axis=1)


def row_scale(values):
    return lax.rsqrt(jnp.mean(values * values, axis=-1, keepdims=True) + epsilon)


def pack_kernel(
    tokens, gain_in, gain_q, first_weight, cosine, sine, wo_own, wo_far, gu_set,
    out, weight_out, gu_far, normed, compressed,
    weight, block, weight_all, send_sem, recv_sem, local_sem,
):
    y, x, h, l, c = coordinates()
    wire = Wire(send_sem, recv_sem, local_sem)
    load = wire.local(first_weight, weight)
    greet(LINKS)
    weight_done = over_y(wire, wo_own, wo_far, lambda yy, hh: weight_all.at[yy, hh])
    gu_sent = wire.send(gu_set, gu_far, 4)
    inputs = tokens[...].astype(f32)
    normed[...] = (inputs * row_scale(inputs) * gain_in[...]).astype(bf16)
    load.wait()
    mixed = jnp.dot(normed[...], weight[...], preferred_element_type=f32)
    rank_dim = compressed.shape[1]
    query = mixed[:, :rank_dim]
    compressed[...] = query
    block[:, :rank_dim] = (query * row_scale(query) * gain_q[...]).astype(bf16)
    block[:, rank_dim : rank_dim + HEAD_DIM] = turned(
        mixed[:, rank_dim : rank_dim + HEAD_DIM], cosine[...], sine[...], 1.0
    ).astype(bf16)
    block[:, rank_dim + HEAD_DIM :] = mixed[:, rank_dim + HEAD_DIM :].astype(bf16)
    near = block.shape[1]
    far = 2 * HEAD_DIM
    columns, far_columns = pl.ds(0, near), pl.ds(near, far)
    from_h = wire.send(block.at[:, pl.ds(near - far, far)], out.at[0, 0, 0, :, far_columns], 4)
    near_out = out.at[:, :, :, :, columns]
    second = plane_gather(wire, block, near_out, near_out.at[0, 0, 0])
    from_h.wait_recv()
    far_out = out.at[:, :, :, :, far_columns]
    second_far = plane_gather(wire, far_out.at[0, 0, 0], far_out, None)
    finish = second()
    finish_far = second_far()
    weight_done()
    swapped = wire.send(weight_all.at[:, 1 - c], weight_out.at[:, c], 1)
    kept = wire.local(weight_all.at[:, c], weight_out.at[:, c])
    finish()
    finish_far()
    kept.wait()
    arrived([swapped, gu_sent])
    wire.close()


def pack(tokens, gain_in, gain_q, first_weight, cosine, sine, wo_own, wo_far, gu_set):
    rows, width = tokens.shape
    near = first_weight.shape[1]
    rank_dim = near - 2 * HEAD_DIM
    outs = [
        shaped((2, 2, 2, rows, near + 2 * HEAD_DIM)),
        shaped((2, 2) + wo_own.shape),
        shaped(gu_set.shape),
        shaped((rows, width)),
        shaped((rows, rank_dim), f32),
    ]
    operands = (tokens, gain_in, gain_q, first_weight, cosine, sine, wo_own, wo_far, gu_set)
    return moving(
        pack_kernel, 2, outs, operands,
        [pltpu.VMEM(first_weight.shape, bf16), pltpu.VMEM((rows, near), bf16), pltpu.VMEM((2, 2) + wo_own.shape, bf16)]
        + wires(32, 8),
        in_specs=[VMEM, VMEM, VMEM, ANY, VMEM, VMEM, VMEM, VMEM, ANY],
        out_specs=[ANY, VMEM, ANY, VMEM, VMEM],
    )


def scores_of(keys, queries, index, first, last):
    scores = lax.dot_general(keys, queries, (((1,), (1,)), ((), ())), preferred_element_type=f32)
    seen = (index >= first) & (index <= last)
    return scores * (1.0 / math.sqrt(HEAD_DIM)), seen


def attend_kernel(
    plane_set, wq, wo, cosine, sine, key_index, query_index, first_index, cotangent, gu_own, gu_far, gu_next,
    queries_out, attended, lse, parts, cotangents, gu_out, gu_far_next,
    kv, normed, staged, load_sem, send_sem, recv_sem, local_sem,
):
    wire = Wire(send_sem, recv_sem, local_sem)
    rank_dim = wq.shape[0]
    loads = [
        pltpu.make_async_copy(plane_set.at[:, :, :, :, pl.ds(rank_dim, 4 * HEAD_DIM)], kv, load_sem.at[0]),
        pltpu.make_async_copy(plane_set.at[:, :, :, :, pl.ds(0, rank_dim)], normed, load_sem.at[1]),
    ]
    for load in loads:
        load.start()
    greet(LINKS)
    second = plane_gather(wire, cotangent, cotangents, cotangents.at[0, 0, 0])
    gu_done = over_y(wire, gu_own, gu_far, lambda yy, hh: gu_out.at[yy, hh])
    gu_sent = wire.send(gu_next, gu_far_next, 4)
    landed(loads)
    rows = kv.shape[3]
    block = 2 * rows

    def one(g, i):
        start = pl.multiple_of((g * 2 + i) * block, block)
        place = pl.ds(start, block)
        raw = jnp.dot(normed[g, i].reshape(block, rank_dim), wq[...], preferred_element_type=f32)
        queries = turned(raw, cosine[place], sine[place], 1.0).astype(bf16)
        queries_out[place] = queries
        keys = jnp.concatenate(
            [kv[g, :, :, :, :HEAD_DIM].reshape(2 * block, HEAD_DIM), kv[g, :, :, :, 2 * HEAD_DIM : 3 * HEAD_DIM].reshape(2 * block, HEAD_DIM)]
        )
        values = jnp.concatenate(
            [kv[g, :, :, :, HEAD_DIM : 2 * HEAD_DIM].reshape(2 * block, HEAD_DIM), kv[g, :, :, :, 3 * HEAD_DIM :].reshape(2 * block, HEAD_DIM)]
        )
        merged = []
        for a in range(2):
            scores, seen = scores_of(
                keys, queries[:, a * HEAD_DIM : (a + 1) * HEAD_DIM], key_index[...], first_index[:, place], query_index[:, place]
            )
            scores = jnp.where(seen, scores, masked_score)
            top = jnp.max(scores, axis=0, keepdims=True)
            weights = jnp.exp(scores - top)
            total = jnp.sum(weights, axis=0, keepdims=True)
            lse[a, :, place] = top + jnp.log(total)
            probs = (weights * (1.0 / total)).astype(bf16)
            merged.append(lax.dot_general(probs, values, (((0,), (0,)), ((), ())), preferred_element_type=f32).astype(bf16))
        merged = jnp.concatenate(merged, axis=1)
        attended[place] = merged
        staged[g, i] = jnp.dot(merged, wo[...], preferred_element_type=f32).astype(bf16).reshape(2, rows, -1)
        pltpu.make_async_copy(staged.at[g, i], parts.at[g, i], load_sem.at[2 + g * 2 + i]).start()

    @pl.loop(0, 2)
    def _(k):
        one(0, k)

    finish = second()

    @pl.loop(0, 2)
    def _(k):
        one(1, k)

    for k in range(4):
        pltpu.make_async_copy(staged.at[k // 2, k % 2], parts.at[k // 2, k % 2], load_sem.at[2 + k]).wait()
    finish()
    gu_done()
    gu_sent.wait_recv()
    wire.close()


def attend(plane_set, wq, wo, cosine, sine, key_index, query_index, first_index, cotangent, gu_own, gu_far, gu_next):
    rows = plane_set.shape[3]
    tokens = 8 * rows
    width = wo.shape[1]
    rank_dim = wq.shape[0]
    outs = [
        shaped((tokens, 2 * HEAD_DIM)),
        shaped((tokens, 2 * HEAD_DIM)),
        shaped((2, 1, tokens), f32),
        shaped((2, 2, 2, rows, width)),
        shaped((2, 2, 2, rows, width)),
        shaped((2, 2) + gu_own.shape),
        shaped(gu_next.shape),
    ]
    scratch = [
        pltpu.VMEM((2, 2, 2, rows, 4 * HEAD_DIM), bf16),
        pltpu.VMEM((2, 2, 2, rows, rank_dim), bf16),
        pltpu.VMEM((2, 2, 2, rows, width), bf16),
        pltpu.SemaphoreType.DMA((6,)),
    ]
    operands = (plane_set, wq, wo, cosine, sine, key_index, query_index, first_index, cotangent, gu_own, gu_far, gu_next)
    return moving(
        attend_kernel, 3, outs, operands, scratch + wires(20, 8),
        in_specs=[ANY] + [VMEM] * 10 + [ANY],
        out_specs=[VMEM, VMEM, VMEM, ANY, ANY, ANY, ANY],
    )


def middle_kernel(
    parts, tokens, gain, gu_own, gu_far, wd_own,
    middle, plane_mid, gu_out, wd_out,
    kept, from_c, s1, r1, s2, r2, normed, wd_far, send_sem, recv_sem, local_sem,
):
    wire = Wire(send_sem, recv_sem, local_sem)
    greet(LINKS)
    first, then, finish = plane_reduce(wire, parts, middle, kept, from_c, s1, r1, s2, r2)
    wd_sent = wire.send(wd_own, wd_far, 4)
    gu_done = over_y(wire, gu_own, gu_far, lambda yy, hh: gu_out.at[yy, hh])
    first()
    then()
    finish()

    def norm(r):
        value = tokens[r].astype(f32) + middle[r]
        middle[r] = value
        normed[r] = (value * row_scale(value) * gain[...]).astype(bf16)

    each_rows(normed.shape[0], norm)
    second = plane_gather(wire, normed, plane_mid, plane_mid.at[0, 0, 0])
    wd_sent.wait_recv()
    wd_done = over_y(wire, wd_own, wd_far, lambda yy, hh: wd_out.at[yy, hh])
    second()()
    gu_done()
    wd_done()
    wire.close()


def middle_step(parts, tokens, gain, gu_own, gu_far, wd_own):
    rows, width = tokens.shape
    outs = [
        shaped((rows, width), f32),
        shaped(parts.shape),
        shaped((2, 2) + gu_own.shape),
        shaped((2, 2) + wd_own.shape),
    ]
    operands = (parts, tokens, gain, gu_own, gu_far, wd_own)
    return moving(
        middle_kernel, 4, outs, operands,
        reduce_scratch(rows, width) + [pltpu.VMEM((rows, width), bf16), pltpu.VMEM(wd_own.shape, bf16)] + wires(40, 12),
        in_specs=[ANY, VMEM, VMEM, VMEM, VMEM, VMEM],
        out_specs=[VMEM, ANY, ANY, ANY],
    )


def feed_kernel(mid, cotangent, gu_one, gu_two, down, hidden, grads, mid_parts, final_parts, gu, wd, sems):
    main = gu.shape[4] // 2 // 128 * 128
    units = down.shape[2] * 4
    padded = wd.shape[0]
    columns = gu.shape[4]

    @pl.when(pl.program_id(0) == 0)
    def _():
        copies = [
            pltpu.make_async_copy(gu_one, gu.at[:, 0], sems.at[0]),
            pltpu.make_async_copy(gu_two, gu.at[:, 1], sems.at[1]),
        ]
        size = down.shape[2]
        for k in range(4):
            copies.append(pltpu.make_async_copy(down.at[k // 2, k % 2], wd.at[pl.ds(k * size, size)], sems.at[2 + k]))
        for copy in copies:
            copy.start()
        wd[units:] = jnp.zeros((padded - units, wd.shape[1]), bf16)
        landed(copies)

    weight = gu[...].reshape(-1, columns)
    both = jnp.dot(mid[...], weight, preferred_element_type=f32)
    gate = both[:, : main + 128]
    upper = jnp.concatenate([both[:, main + 128 :], pltpu.roll(both[:, main : main + 128], 64, 1)], axis=1)
    grad = lax.dot_general(cotangent[...], wd[...], (((1,), (1,)), ((), ())), preferred_element_type=f32)
    sigmoid = 1.0 / (1.0 + jnp.exp(-gate))
    silu = gate * sigmoid
    hid = (silu * upper).astype(bf16)
    hidden[...] = hid[:, :units]
    final_parts[...] = jnp.dot(hid, wd[...], preferred_element_type=f32).astype(bf16)
    grad_gate = grad * upper * sigmoid * (1.0 + gate * (1.0 - sigmoid))
    grad_upper = grad * silu
    joint = grad_gate[:, main:] + pltpu.roll(grad_upper[:, main:], 64, 1)
    out = jnp.concatenate([grad_gate[:, :main], joint, grad_upper[:, :main]], axis=1).astype(bf16)
    grads[...] = out
    mid_parts[...] = lax.dot_general(out, weight, (((1,), (1,)), ((), ())), preferred_element_type=f32).astype(bf16)


def feed(mid, cotangent, gu_one, gu_two, down, block=384):
    tokens, width = mid.shape
    columns = gu_one.shape[-1]
    units = 4 * down.shape[2]
    padded = (units + 127) // 128 * 128
    by_block = lambda n: pl.BlockSpec((block, n), lambda i: (i, 0))
    return pl.pallas_call(
        feed_kernel,
        grid=(tokens // block,),
        in_specs=[by_block(width), by_block(width), ANY, ANY, ANY],
        out_specs=[by_block(units), by_block(columns), by_block(width), by_block(width)],
        out_shape=[shaped((tokens, units)), shaped((tokens, columns)), shaped((tokens, width)), shaped((tokens, width))],
        scratch_shapes=[
            pltpu.VMEM((2, 2, 2) + gu_one.shape[2:], bf16),
            pltpu.VMEM((padded, width), bf16),
            pltpu.SemaphoreType.DMA((6,)),
        ],
        compiler_params=pltpu.CompilerParams(vmem_limit_bytes=56 * 1024 * 1024),
        cost_estimate=pl.CostEstimate(flops=12 * tokens * width * units, bytes_accessed=40_000_000, transcendentals=0),
        name="feed",
    )(mid, cotangent, gu_one, gu_two, down)


def fold_y(wire, source, mine, recv, passed, kept):
    y, x, h, l, c = coordinates()
    sent = [wire.send(source(1 - y, hh), recv.at[hh], 16) for hh in (1 - h, h)]
    loads = [wire.local(source(y, hh), mine.at[hh]) for hh in (1 - h, h)]

    def finish():
        for k, hh, target in ((0, 1 - h, passed), (1, h, kept)):
            loads[k].wait()
            sent[k].wait_recv()

            def body(r, hh=hh, target=target):
                target[r] = (wide(mine.at[hh], r) + wide(recv.at[hh], r)).astype(target.dtype)

            each_rows(target.shape[0], body)

    return finish


def fold_scratch(rows, width):
    return [pltpu.VMEM((2, rows, width), bf16), pltpu.VMEM((2, rows, width), bf16)]


def fold_h(wire, passed, kept, recv, out):
    sent = wire.send(passed, recv, 4)

    def finish():
        sent.wait_recv()

        def body(r):
            out[r] = (wide(kept, r) + wide(recv, r)).astype(out.dtype)

        each_rows(out.shape[0], body)

    return finish


def hand_back(wire, own, out):
    y, x, h, l, c = coordinates()
    rank = x * 4 + l * 2 + c
    mine = wire.local(own(rank), out.at[rank])
    sent = [wire.send(own(flip(rank, j)), out.at[rank], PLANE[j - 1]) for j in range(1, 8)]

    def finish():
        mine.wait()
        arrived(sent)

    return finish


def norm_back(value, gain, grad):
    scale = row_scale(value)
    weighted = gain * grad
    inner = scale * weighted - value * scale * scale * scale * jnp.mean(weighted * value, axis=-1, keepdims=True)
    return inner, grad * value * scale


def branch_kernel(
    parts, middle, cotangent, gain, down_grad, gu_grad,
    grad_middle, gain_grad, plane_branch, down_out, gu_passed, gu_kept,
    kept, from_c, s1, r1, s2, r2, normed_grad, branch, wd_mine, wd_recv, wd_passed, wd_kept, wd_far, gu_mine, gu_recv,
    send_sem, recv_sem, local_sem,
):
    wire = Wire(send_sem, recv_sem, local_sem)
    greet(LINKS)
    first, then, finish = plane_reduce(wire, parts, normed_grad, kept, from_c, s1, r1, s2, r2)
    down_y = fold_y(wire, lambda yy, hh: down_grad.at[yy, hh], wd_mine, wd_recv, wd_passed, wd_kept)
    first()
    then()
    gain_grad[...] = jnp.zeros_like(gain_grad)
    finish()

    def norm(r):
        inner, outer = norm_back(middle[r], gain[...], normed_grad[r])
        value = cotangent[r].astype(f32) + inner
        grad_middle[r] = value
        branch[r] = value.astype(bf16)
        gain_grad[...] += jnp.sum(outer, axis=0, keepdims=True)

    each_rows(branch.shape[0], norm)
    second = plane_gather(wire, branch, plane_branch, plane_branch.at[0, 0, 0])
    down_y()
    down_h = fold_h(wire, wd_passed, wd_kept, wd_far, down_out)
    gu_y = fold_y(wire, lambda yy, hh: gu_grad.at[yy, 0, hh], gu_mine, gu_recv, gu_passed, gu_kept)
    second()()
    gu_y()
    down_h()
    wire.close()


def branch_step(parts, middle, cotangent, gain, down_grad, gu_grad):
    rows, width = middle.shape
    down = down_grad.shape[2:]
    gu = gu_grad.shape[3:]
    outs = [
        shaped((rows, width), f32),
        shaped((1, width), f32),
        shaped(parts.shape),
        shaped(down, f32),
        shaped(gu),
        shaped(gu),
    ]
    scratch = reduce_scratch(rows, width) + [pltpu.VMEM((rows, width), f32), pltpu.VMEM((rows, width), bf16)]
    scratch += fold_scratch(*down) + [pltpu.VMEM(down, bf16), pltpu.VMEM(down, bf16), pltpu.VMEM(down, bf16)]
    scratch += fold_scratch(*gu)
    operands = (parts, middle, cotangent, gain, down_grad, gu_grad)
    return moving(
        branch_kernel, 5, outs, operands, scratch + wires(40, 16),
        in_specs=[ANY, VMEM, VMEM, VMEM, ANY, ANY],
        out_specs=[VMEM, VMEM, ANY, VMEM, VMEM, VMEM],
    )


def attend_back_kernel(
    plane_set, plane_branch, queries, attended, lse, wq, wo, cosine, sine, key_index, query_index, first_index,
    final_parts, middle, gu_passed, gu_kept, gu_grad,
    query_grad, parts, output, gu_out, gu_passed_next, gu_kept_next,
    kv, branch, staged, grad_keys, grad_values, kept, from_c, s1, r1, s2, r2, total, gu_recv, gu_mine, gu_recv_y,
    load_sem, send_sem, recv_sem, local_sem,
):
    wire = Wire(send_sem, recv_sem, local_sem)
    rank_dim = wq.shape[0]
    rows = kv.shape[3]
    block = 2 * rows
    load_kv = pltpu.make_async_copy(plane_set.at[:, :, :, :, pl.ds(rank_dim, 4 * HEAD_DIM)], kv, load_sem.at[0])
    load_kv.start()

    def load_branch(k):
        return pltpu.make_async_copy(plane_branch.at[k // 2, k % 2], branch.at[k % 2], load_sem.at[1 + k % 2])

    load_branch(0).start()
    greet(LINKS)
    first, then, finish = plane_reduce(wire, final_parts, total, kept, from_c, s1, r1, s2, r2)
    gu_h = fold_h(wire, gu_passed, gu_kept, gu_recv, gu_out)
    gu_y = fold_y(wire, lambda yy, hh: gu_grad.at[yy, 1, hh], gu_mine, gu_recv_y, gu_passed_next, gu_kept_next)
    load_kv.wait()
    scale = 1.0 / math.sqrt(HEAD_DIM)

    def one(k):
        g = k // 2
        i = k % 2
        load_branch(k).wait()

        @pl.when(k < 3)
        def _():
            load_branch(k + 1).start()

        @pl.when(i == 0)
        def _():
            grad_keys[...] = jnp.zeros_like(grad_keys)
            grad_values[...] = jnp.zeros_like(grad_values)

        start = pl.multiple_of(k * block, block)
        place = pl.ds(start, block)
        grads = lax.dot_general(
            branch[i].reshape(block, -1), wo[...], (((1,), (1,)), ((), ())), preferred_element_type=f32
        ).astype(bf16)
        keys = jnp.concatenate(
            [kv[g, :, :, :, :HEAD_DIM].reshape(2 * block, HEAD_DIM), kv[g, :, :, :, 2 * HEAD_DIM : 3 * HEAD_DIM].reshape(2 * block, HEAD_DIM)]
        )
        values = jnp.concatenate(
            [kv[g, :, :, :, HEAD_DIM : 2 * HEAD_DIM].reshape(2 * block, HEAD_DIM), kv[g, :, :, :, 3 * HEAD_DIM :].reshape(2 * block, HEAD_DIM)]
        )
        query_parts = []
        for a in range(2):
            span = slice(a * HEAD_DIM, (a + 1) * HEAD_DIM)
            query, grad = queries[place, span], grads[:, span]
            product = grad.astype(f32) * attended[place, span].astype(f32)
            delta = lax.dot_general(
                jnp.ones((8, HEAD_DIM), f32), product, (((1,), (1,)), ((), ())),
                precision=lax.Precision.HIGHEST, preferred_element_type=f32,
            )[:1]
            scores, seen = scores_of(keys, query, key_index[...], first_index[:, place], query_index[:, place])
            probs = jnp.where(seen, jnp.exp(scores - lse[a, :, place]), 0.0)
            grad_values[...] += jnp.dot(probs.astype(bf16), grad, preferred_element_type=f32)
            grad_probs = lax.dot_general(values, grad, (((1,), (1,)), ((), ())), preferred_element_type=f32)
            grad_scores = (probs * (grad_probs - delta) * scale).astype(bf16)
            grad_keys[...] += jnp.dot(grad_scores, query, preferred_element_type=f32)
            query_parts.append(
                lax.dot_general(grad_scores, keys, (((0,), (0,)), ((), ())), preferred_element_type=f32)
            )
        query_sum = turned(jnp.concatenate(query_parts, axis=1), cosine[place], sine[place], -1.0).astype(bf16)
        query_grad[place] = query_sum
        normed = lax.dot_general(query_sum, wq[...], (((1,), (1,)), ((), ())), preferred_element_type=f32)
        staged[g, i, :, :, :rank_dim] = normed.astype(bf16).reshape(2, rows, rank_dim)

        @pl.when(i == 1)
        def _():
            for number, (source, side) in enumerate(
                ((grad_keys, 0), (grad_values, 0), (grad_keys, 1), (grad_values, 1))
            ):
                column = rank_dim + number * HEAD_DIM
                half = source[side * 2 * block : (side + 1) * 2 * block].astype(bf16)
                staged[g, :, :, :, column : column + HEAD_DIM] = half.reshape(2, 2, rows, HEAD_DIM)
            pltpu.make_async_copy(staged.at[g], parts.at[g], load_sem.at[3 + g]).start()

    def steps(a, b):
        @pl.loop(a, b)
        def _(k):
            one(k)

    steps(0, 1)
    first()
    steps(1, 3)
    then()
    gu_h()
    steps(3, 4)
    finish()

    def emit(r):
        output[r] = (middle[r] + total[r]).astype(bf16)

    each_rows(output.shape[0], emit)
    for g in range(2):
        pltpu.make_async_copy(staged.at[g], parts.at[g], load_sem.at[3 + g]).wait()
    gu_y()
    wire.close()


def attend_back(
    plane_set, plane_branch, queries, attended, lse, wq, wo, cosine, sine, key_index, query_index, first_index,
    final_parts, middle, gu_passed, gu_kept, gu_grad,
):
    rows, width = middle.shape
    tokens = 8 * rows
    gu = gu_passed.shape
    outs = [
        shaped((tokens, 2 * HEAD_DIM)),
        shaped((2, 2, 2, rows, wq.shape[0] + 4 * HEAD_DIM)),
        shaped((rows, width)),
        shaped(gu),
        shaped(gu),
        shaped(gu),
    ]
    scratch = [
        pltpu.VMEM((2, 2, 2, rows, 4 * HEAD_DIM), bf16),
        pltpu.VMEM((2, 2, rows, width), bf16),
        pltpu.VMEM((2, 2, 2, rows, wq.shape[0] + 4 * HEAD_DIM), bf16),
        pltpu.VMEM((8 * rows, HEAD_DIM), f32),
        pltpu.VMEM((8 * rows, HEAD_DIM), f32),
    ]
    scratch += reduce_scratch(rows, width) + [pltpu.VMEM((rows, width), f32), pltpu.VMEM(gu, bf16)]
    scratch += fold_scratch(*gu) + [pltpu.SemaphoreType.DMA((5,))]
    operands = (
        plane_set, plane_branch, queries, attended, lse, wq, wo, cosine, sine, key_index, query_index, first_index,
        final_parts, middle, gu_passed, gu_kept, gu_grad,
    )
    return moving(
        attend_back_kernel, 6, outs, operands, scratch + wires(30, 12),
        in_specs=[ANY, ANY] + [VMEM] * 10 + [ANY, VMEM, ANY, VMEM, ANY],
        out_specs=[VMEM, ANY, VMEM, VMEM, VMEM, VMEM],
        limit=62,
    )


def tail_kernel(
    parts, normed, compressed, tokens, grad_middle, first_weight, gain_in, gain_q, gain_mid_grad, cosine, sine,
    gu_total, gu_passed, gu_kept, up_grad, out_grad,
    grad_tokens, down_out, key_out, value_out, gains_out, gate_out, up_out, q_up_out, out_out,
    kept, from_c, s1, r1, s2, r2, back, kv_send, kv_recv, weight, mixed, normed_grad, gain_rows,
    blocks, acc, recv, core, gains, gains_recv,
    gu_far, gu_own, gu_back, gu_wide, up_mine, up_recv, up_passed, up_kept, up_far, up_own, up_back,
    heads, o_mine, o_recv, o_passed, o_kept, o_far,
    send_sem, recv_sem, local_sem,
):
    y, x, h, l, c = coordinates()
    own = dict(zip("yxhlc", (y, x, h, l, c)))
    every = slice(None)
    wire = Wire(send_sem, recv_sem, local_sem)
    load = wire.local(first_weight, weight)
    greet([16, 4] + PLANE)
    first, then, finish = plane_reduce(wire, parts, back, kept, from_c, s1, r1, s2, r2)
    gu_h = fold_h(wire, gu_passed, gu_kept, gu_far, gu_own)
    swapped = wire.send(out_grad.at[:, 1 - c], heads.at[:, c], 1)
    stayed = wire.local(out_grad.at[:, c], heads.at[:, c])
    first()
    stayed.wait()
    swapped.wait_recv()
    o_y = fold_y(wire, lambda yy, hh: heads.at[yy, hh], o_mine, o_recv, o_passed, o_kept)
    up_y = [
        fold_y(wire, lambda yy, hh, k=k: up_grad.at[yy, k, hh], up_mine.at[k], up_recv.at[k], up_passed.at[k], up_kept.at[k])
        for k in range(2)
    ]
    then()
    finish()
    rows = back.shape[0]
    rank_dim = compressed.shape[1]
    split = rank_dim + 2 * HEAD_DIM
    kv_send[...] = back[:, split:].astype(bf16)
    far = wire.send(kv_send, kv_recv, 4)
    inner, outer = norm_back(compressed[...], gain_q[...], back[:, :rank_dim])
    mixed[:, :rank_dim] = inner.astype(bf16)
    gain_rows[1:2, :rank_dim] = jnp.sum(outer, axis=0, keepdims=True)
    gain_rows[2:3, :] = gain_mid_grad[...]
    gu_h()
    piece_rows = gu_back.shape[2]
    piece = lambda k: pl.ds(pl.multiple_of((k % 4) * piece_rows, piece_rows), piece_rows)

    both = [wire.local(gu_total, gu_wide.at[0]), wire.local(gu_own, gu_wide.at[1])]
    landed(both)
    gu_done = hand_back(wire, lambda k: gu_wide.at[k // 4, piece(k)], gu_back.at[0])
    far.wait_recv()
    kv = back[:, rank_dim:split] + kv_recv[...].astype(f32)
    mixed[:, rank_dim : rank_dim + HEAD_DIM] = turned(kv[:, :HEAD_DIM], cosine[...], sine[...], -1.0).astype(bf16)
    mixed[:, rank_dim + HEAD_DIM :] = kv[:, HEAD_DIM:].astype(bf16)
    size = normed.shape[1] // 8
    cores = []
    for k in range(8):
        at = (k // 4, k // 2 % 2, k % 2)
        grad = lax.dot_general(
            normed[:, k * size : (k + 1) * size], mixed[...], (((0,), (0,)), ((), ())), preferred_element_type=f32
        )
        blocks[at] = grad.astype(bf16).reshape(blocks.shape[3:])
        cores.append(wire.send(blocks.at[at + (every, 1 - c)], core.at[at], 1))
    o_y()
    o_h = fold_h(wire, o_passed, o_kept, o_far, out_out)
    for k in range(2):
        up_y[k]()
    up_h = [fold_h(wire, up_passed.at[k], up_kept.at[k], up_far.at[k], up_own.at[k]) for k in range(2)]
    span = blocks.shape[5]
    width = blocks.shape[6]
    third = width // 3
    columns = [pl.ds(i * third, third) for i in range(3)]
    orders = ["yxlh", "lyxh", "xlyh"]
    sent = [None] * 3

    def index(fixed, block):
        free = [k for k in "yxhl" if k not in fixed]
        at = dict(fixed)
        for position, k in enumerate(reversed(free)):
            at[k] = (block // 2**position) % 2
        return tuple(at[k] for k in "yxhl")

    def over(fixed, body):
        count = 2 ** (4 - len(fixed))

        @pl.loop(0, count * (span // 16))
        def _(i):
            r = pl.ds(pl.multiple_of((i % (span // 16)) * 16, 16), 16)
            body(index(fixed, i // (span // 16)), r)

    def pass_on(p, step):
        order = orders[p]
        fixed = {k: own[k] for k in order[:step]}
        bit = order[step]
        src = {**fixed, bit: 1 - own[bit]}
        dst = {**fixed, bit: own[bit]}
        place = lambda at: tuple(at.get(k, every) for k in "yxhl") + (every, columns[p])
        mask = {"y": 16, "x": 8, "h": 4, "l": 2}[bit]
        sent[p] = wire.send(acc.at[place(src)], recv.at[place(dst)], mask)

    arrived(cores)
    for first_side in (True, False):
        for p in range(3):
            bit = orders[p][0]

            def body(at, r, p=p):
                value = wide(blocks, at + (c, r, columns[p])) + wide(core, at + (r, columns[p]))
                acc[at + (r, columns[p])] = value.astype(bf16)

            over({bit: 1 - own[bit] if first_side else own[bit]}, body)
            if first_side:
                pass_on(p, 0)
    load.wait()
    normed_grad[...] = lax.dot_general(mixed[...], weight[...], (((1,), (1,)), ((), ())), preferred_element_type=f32)
    gain_rows[0:1, :] = jnp.zeros((1, gain_rows.shape[1]), f32)

    def norm(r):
        inner, outer = norm_back(tokens[r].astype(f32), gain_in[...], normed_grad[r])
        grad_tokens[r] = (grad_middle[r] + inner).astype(bf16)
        gain_rows[0:1, :] += jnp.sum(outer, axis=0, keepdims=True)

    each_rows(rows, norm)
    q_span = rank_dim // 32
    gains[...] = jnp.zeros_like(gains)
    for n in range(32):
        at = (n // 16, n // 8 % 2, n // 4 % 2, n // 2 % 2, n % 2, 0)
        gains[at + (slice(0, 128),)] = jnp.concatenate(
            [gain_rows[0, n * span : (n + 1) * span], gain_rows[2, n * span : (n + 1) * span]], axis=0
        )
        gains[at + (slice(128, 128 + q_span),)] = gain_rows[1, n * q_span : (n + 1) * q_span]

    def pass_gains(order, step):
        fixed = {k: own[k] for k in order[:step]}
        bit = order[step]
        place = lambda at: tuple(at.get(k, every) for k in "yxhlc")
        mask = {"y": 16, "x": 8, "h": 4, "l": 2, "c": 1}[bit]
        return wire.send(gains.at[place({**fixed, bit: 1 - own[bit]})], gains_recv.at[place({**fixed, bit: own[bit]})], mask)

    def add_gains(order, step):
        fixed = {k: own[k] for k in order[:step]}
        bit = order[step]
        place = lambda at: tuple(at.get(k, every) for k in "yxhlc")
        mine = place({**fixed, bit: own[bit]})
        gains[mine] = gains[mine] + gains_recv[place({**fixed, bit: 1 - own[bit]})]

    gain_order = "cyxlh"
    gain_sent = pass_gains(gain_order, 0)
    gain_step = 0
    for step in range(4):
        for p in range(3):
            order = orders[p]
            fixed = {k: own[k] for k in order[:step]}
            bit = order[step]
            sent[p].wait_recv()

            def body(at, r, p=p, bit=bit, last=step == 3):
                other = tuple(1 - own[k] if k == bit else v for k, v in zip("yxhl", at))
                value = wide(acc, at + (r, columns[p])) + wide(recv, other + (r, columns[p]))
                if last:
                    back[r, columns[p]] = value
                else:
                    acc[at + (r, columns[p])] = value.astype(bf16)

            if step < 3:
                over({**fixed, bit: own[bit], order[step + 1]: 1 - own[order[step + 1]]}, body)
                pass_on(p, step + 1)
                over({**fixed, bit: own[bit], order[step + 1]: own[order[step + 1]]}, body)
            else:
                over({**fixed, bit: own[bit]}, body)
        if gain_step < 5:
            gain_sent.wait_recv()
            add_gains(gain_order, gain_step)
            gain_step += 1
            if gain_step < 5:
                gain_sent = pass_gains(gain_order, gain_step)
        if step == 0:
            for k in range(2):
                up_h[k]()
            up_rows = up_back.shape[1]
            up_piece = lambda k: up_own.at[k // 4, pl.ds(pl.multiple_of((k % 4) * up_rows, up_rows), up_rows)]
            up_done = hand_back(wire, up_piece, up_back)
            gu_done()
            unit = gate_out.shape[1] // 32
            units = 4 * unit
            main = units // 128 * 128
            rest = units - main
            for source in range(8):
                tile = gu_back[0, source].astype(f32)
                halves = (
                    tile[:, : main + rest],
                    jnp.concatenate([tile[:, main + 2 * rest :], tile[:, main + rest : main + 2 * rest]], axis=1),
                )
                for half, target in zip(halves, (gate_out, up_out)):
                    for q in range(4):
                        n = q // 2 * 16 + source // 4 * 8 + q % 2 * 4 + source % 4
                        target[:, n * unit : (n + 1) * unit] = half[:, q * unit : (q + 1) * unit]
        if step == 1:
            o_h()
            up_done()
            for head in range(q_up_out.shape[1] // HEAD_DIM):
                hy, hx, hh, hl = head // 8, head // 4 % 2, head // 2 % 2, head % 2
                source = hx * 4 + hl * 2 + hh
                q_up_out[:, head * HEAD_DIM : (head + 1) * HEAD_DIM] = up_back[
                    source, :, hy * HEAD_DIM : (hy + 1) * HEAD_DIM
                ].astype(f32)
    while gain_step < 5:
        gain_sent.wait_recv()
        add_gains(gain_order, gain_step)
        gain_step += 1
        if gain_step < 5:
            gain_sent = pass_gains(gain_order, gain_step)
    gains_out[...] = gains[y, x, h, l, c]
    down_out[...] = back[:span, :rank_dim]
    key_out[...] = back[:span, rank_dim : rank_dim + HEAD_DIM]
    value_out[...] = back[:span, rank_dim + HEAD_DIM : split]
    wire.close()


def tail(
    parts, normed, compressed, tokens, grad_middle, first_weight, gain_in, gain_q, gain_mid_grad, cosine, sine,
    gu_total, gu_passed, gu_kept, up_grad, out_grad,
):
    rows, width = tokens.shape
    rank_dim = compressed.shape[1]
    near = first_weight.shape[1]
    span = width // 32
    gu = gu_total.shape
    units = gu[1] * 4
    up = up_grad.shape[3:]
    heads = out_grad.shape[2:]
    outs = [
        shaped((rows, width)),
        shaped((span, rank_dim), f32),
        shaped((span, HEAD_DIM), f32),
        shaped((span, HEAD_DIM), f32),
        shaped((1, 256), f32),
        shaped((span, units), f32),
        shaped((span, units), f32),
        shaped((up[0] // 4, 8 * up[1]), f32),
        shaped(heads, f32),
    ]
    sums = (2, 2, 2, 2, span, near)
    scratch = reduce_scratch(rows, width) + [
        pltpu.VMEM((rows, width), f32),
        pltpu.VMEM((rows, 2 * HEAD_DIM), bf16),
        pltpu.VMEM((rows, 2 * HEAD_DIM), bf16),
        pltpu.VMEM(first_weight.shape, bf16),
        pltpu.VMEM((rows, near), bf16),
        pltpu.VMEM((rows, width), f32),
        pltpu.VMEM((8, width), f32),
        pltpu.VMEM((2, 2, 2, 2, 2, span, near), bf16),
        pltpu.VMEM(sums, bf16),
        pltpu.VMEM(sums, bf16),
        pltpu.VMEM(sums, bf16),
        pltpu.VMEM((2, 2, 2, 2, 2, 1, 256), f32),
        pltpu.VMEM((2, 2, 2, 2, 2, 1, 256), f32),
        pltpu.VMEM(gu, bf16),
        pltpu.VMEM(gu, bf16),
        pltpu.VMEM((1, 8, span, gu[1]), bf16),
        pltpu.VMEM((2,) + gu, bf16),
        pltpu.VMEM((2, 2) + up, bf16),
        pltpu.VMEM((2, 2) + up, bf16),
        pltpu.VMEM((2,) + up, bf16),
        pltpu.VMEM((2,) + up, bf16),
        pltpu.VMEM((2,) + up, bf16),
        pltpu.VMEM((2,) + up, bf16),
        pltpu.VMEM((8, up[0] // 4, up[1]), bf16),
        pltpu.VMEM((2, 2) + heads, bf16),
        pltpu.VMEM((2,) + heads, bf16),
        pltpu.VMEM((2,) + heads, bf16),
        pltpu.VMEM(heads, bf16),
        pltpu.VMEM(heads, bf16),
        pltpu.VMEM(heads, bf16),
    ]
    operands = (
        parts, normed, compressed, tokens, grad_middle, first_weight, gain_in, gain_q, gain_mid_grad, cosine, sine,
        gu_total, gu_passed, gu_kept, up_grad, out_grad,
    )
    return moving(
        tail_kernel, 7, outs, operands, scratch + wires(80, 24),
        in_specs=[ANY] + [VMEM] * 4 + [ANY] + [VMEM] * 5 + [ANY, ANY, VMEM, ANY, ANY],
        out_specs=[VMEM] * 9,
        limit=62,
    )


def rope_table(places):
    half = HEAD_DIM // 2
    freqs = rope_base ** (-(2.0 * jnp.arange(half).astype(f32)) / HEAD_DIM)
    angles = places.astype(f32)[:, None] * freqs[None, :]
    return jnp.cos(angles), jnp.sin(angles)


def plane_local(
    tokens,
    positions,
    cotangent,
    norm_in_gain,
    q_down,
    q_gain,
    q_up,
    key_proj,
    value_proj,
    out_proj,
    norm_mid_gain,
    w_gate,
    w_up,
    w_down,
):
    rows, width = tokens.shape
    rank_dim = q_down.shape[1]
    seq = lax.axis_index("seq")
    h, l, c = seq // 4, (seq // 2) % 2, seq % 2
    span, q_span = norm_in_gain.shape[0], q_gain.shape[0]

    gains = jnp.concatenate([norm_in_gain, norm_mid_gain, q_gain, jnp.zeros((256 - 2 * span - q_span,), f32)])
    gains = lax.reduce_precision(gains, 8, 7).reshape(1, 256)
    first_weight, up_query, gu_set, wo_own, wo_far, wd_own, gains, places = head(
        q_down, key_proj, value_proj, gains, q_up, w_gate, w_up, out_proj, w_down, positions.reshape(1, rows)
    )
    first_weight = first_weight.reshape(width, rank_dim + 2 * HEAD_DIM)
    up_query = up_query.reshape(rank_dim, 2 * HEAD_DIM)
    gains = gains.reshape(32, 256)
    in_gain = gains[:, :span].reshape(1, width)
    mid_gain = gains[:, span : 2 * span].reshape(1, width)
    query_gain = gains[:, 2 * span : 2 * span + q_span].reshape(1, rank_dim)

    blocks = jnp.arange(4, dtype=jnp.int32) ^ (l * 2 + c)
    in_half = (blocks[:, None] * rows + jnp.arange(rows, dtype=jnp.int32)[None, :]).reshape(-1)
    own_index = h * (4 * rows) + in_half
    query_index = jnp.concatenate([own_index, own_index]).reshape(1, 8 * rows)
    places = places.reshape(1, 8 * rows)
    first_index = query_index - places
    key_index = jnp.concatenate([own_index, (1 - h) * (4 * rows) + in_half]).reshape(8 * rows, 1)
    cosine, sine = rope_table(places.reshape(-1))

    plane_set, out_weight, gu_far, normed, compressed = pack(
        tokens, in_gain, query_gain, first_weight, cosine[:rows], sine[:rows], wo_own, wo_far, gu_set[0]
    )
    out_weight = out_weight.reshape(2 * HEAD_DIM, width)
    queries, attended, lse, out_parts, plane_cotangent, gu_one, gu_far = attend(
        plane_set, up_query, out_weight, cosine, sine, key_index, query_index, first_index, cotangent,
        gu_set[0], gu_far, gu_set[1],
    )
    middle, plane_mid, gu_two, down_weight = middle_step(out_parts, tokens, mid_gain, gu_set[1], gu_far, wd_own)
    plane_mid = plane_mid.reshape(8 * rows, width)
    plane_cotangent = plane_cotangent.reshape(8 * rows, width)
    hidden, gu_grads, mid_parts, final_parts = feed(plane_mid, plane_cotangent, gu_one, gu_two, down_weight)

    def over_tokens(left, right):
        grad = lax.dot_general(left, right, (((0,), (0,)), ((), ())), preferred_element_type=f32)
        return grad.astype(bf16)

    by_rows = lambda grad: grad.reshape(2, 2, 2, -1, grad.shape[-1])
    by_plane = lambda parts: parts.reshape(2, 2, 2, rows, -1)
    down_grad = over_tokens(hidden, plane_cotangent).reshape(2, 2, -1, width)
    gu_grad = by_rows(over_tokens(plane_mid, gu_grads))
    grad_middle, mid_gain_grad, plane_branch, grad_down, gu_passed, gu_kept = branch_step(
        by_plane(mid_parts), middle, cotangent, mid_gain, down_grad, gu_grad
    )
    query_grad, back_parts, output, gu_total, gu_passed, gu_kept = attend_back(
        plane_set, plane_branch, queries, attended, lse, up_query, out_weight, cosine, sine,
        key_index, query_index, first_index, by_plane(final_parts), middle, gu_passed, gu_kept, gu_grad,
    )
    out_grad = over_tokens(attended, plane_branch.reshape(8 * rows, width)).reshape(2, 2, -1, width)
    up_grad = by_rows(over_tokens(plane_set.reshape(8 * rows, -1)[:, :rank_dim], query_grad))
    grad_tokens, grad_q_down, grad_key, grad_value, grad_gains, grad_gate, grad_up, grad_q_up, grad_out = tail(
        back_parts, normed, compressed, tokens, grad_middle, first_weight, in_gain, query_gain, mid_gain_grad,
        cosine[:rows], sine[:rows], gu_total, gu_passed, gu_kept, up_grad, out_grad,
    )
    return (
        output,
        grad_tokens,
        grad_gains[0, :span],
        grad_q_down,
        grad_gains[0, 2 * span : 2 * span + q_span],
        grad_q_up,
        grad_key,
        grad_value,
        grad_out,
        grad_gains[0, span : 2 * span],
        grad_gate,
        grad_up,
        grad_down,
    )


def solution(mesh):
    return jax.shard_map(
        plane_local if dict(mesh.shape) == {"dp": 4, "seq": 8} else local,
        mesh=mesh,
        in_specs=(
            P(("dp", "seq"), None),
            P(("dp", "seq")),
            P(("dp", "seq"), None),
            P(("dp", "seq")),
            P(("dp", "seq"), None),
            P(("dp", "seq")),
            P(("dp", "seq"), None),
            P(("dp", "seq"), None),
            P(("dp", "seq"), None),
            P(("dp", "seq"), None),
            P(("dp", "seq")),
            P(("dp", "seq"), None),
            P(("dp", "seq"), None),
            P(("dp", "seq"), None),
        ),
        out_specs=(
            P(("dp", "seq"), None),
            P(("dp", "seq"), None),
            P(("dp", "seq")),
            P(("dp", "seq"), None),
            P(("dp", "seq")),
            P(("dp", "seq"), None),
            P(("dp", "seq"), None),
            P(("dp", "seq"), None),
            P(("dp", "seq"), None),
            P(("dp", "seq")),
            P(("dp", "seq"), None),
            P(("dp", "seq"), None),
            P(("dp", "seq"), None),
        ),
        check_vma=False,
    )
```

```python
import math

import jax
import jax.numpy as jnp
from jax import lax
from jax.experimental import pallas as pl
from jax.experimental.pallas import tpu as pltpu
from jax.sharding import PartitionSpec as P

HEADS = 16
HEAD_DIM = 256


epsilon = 1e-05
rope_base = 10000.0
masked_score = -1e30


def rms_scale(values):
    return lax.rsqrt(jnp.mean(values * values, axis=-1, keepdims=True) + epsilon)


def rotary(values, places, sign):
    half = values.shape[-1] // 2
    freqs = rope_base ** (-(2.0 * jnp.arange(half).astype(jnp.float32)) / values.shape[-1])
    angles = places.astype(jnp.float32)[:, None] * freqs[None, :]
    cosine = jnp.cos(angles)[:, None, :]
    sine = jnp.sin(angles)[:, None, :]
    first = values[..., :half]
    second = values[..., half:]
    return jnp.concatenate(
        [first * cosine - sign * second * sine, sign * first * sine + second * cosine], axis=-1
    )


def norm_backward(inputs, scale, gain, grad_out):
    weighted = gain * grad_out
    grad_in = scale * weighted - inputs * scale * scale * scale * jnp.mean(
        weighted * inputs, axis=-1, keepdims=True
    )
    grad_gain = jnp.sum(grad_out * inputs * scale, axis=0)
    return (grad_in, grad_gain)


def add_rows(total, block, start):
    current = lax.dynamic_slice_in_dim(total, start, block.shape[0], 0)
    return lax.dynamic_update_slice_in_dim(total, current + block, start, 0)


def local(
    tokens,
    positions,
    cotangent,
    norm_in_gain,
    q_down,
    q_gain,
    q_up,
    key_proj,
    value_proj,
    out_proj,
    norm_mid_gain,
    w_gate,
    w_up,
    w_down,
):
    width = tokens.shape[0]
    scale = 1.0 / math.sqrt(HEAD_DIM)
    attention_set = (
        lax.all_gather(norm_in_gain.astype(jnp.bfloat16), ("dp", "seq"), axis=0, tiled=True),
        lax.all_gather(q_down.astype(jnp.bfloat16), ("dp", "seq"), axis=0, tiled=True),
        lax.all_gather(q_gain.astype(jnp.bfloat16), ("dp", "seq"), axis=0, tiled=True),
        lax.all_gather(q_up.astype(jnp.bfloat16), ("dp", "seq"), axis=0, tiled=True),
        lax.all_gather(key_proj.astype(jnp.bfloat16), ("dp", "seq"), axis=0, tiled=True),
        lax.all_gather(value_proj.astype(jnp.bfloat16), ("dp", "seq"), axis=0, tiled=True),
        lax.all_gather(out_proj.astype(jnp.bfloat16), ("dp", "seq"), axis=0, tiled=True),
    )
    feed_set = (
        lax.all_gather(norm_mid_gain.astype(jnp.bfloat16), ("dp", "seq"), axis=0, tiled=True),
        lax.all_gather(w_gate.astype(jnp.bfloat16), ("dp", "seq"), axis=0, tiled=True),
        lax.all_gather(w_up.astype(jnp.bfloat16), ("dp", "seq"), axis=0, tiled=True),
        lax.all_gather(w_down.astype(jnp.bfloat16), ("dp", "seq"), axis=0, tiled=True),
    )
    in_gain = attention_set[0].astype(jnp.float32)
    query_gain = attention_set[2].astype(jnp.float32)
    inputs = tokens.astype(jnp.float32)
    in_scale = rms_scale(inputs)
    normed = (inputs * in_scale * in_gain).astype(jnp.bfloat16)
    compressed = jnp.dot(normed, attention_set[1], preferred_element_type=jnp.float32)
    query_scale = rms_scale(compressed)
    compressed_normed = (compressed * query_scale * query_gain).astype(jnp.bfloat16)
    queries_raw = jnp.dot(
        compressed_normed, attention_set[3], preferred_element_type=jnp.float32
    ).reshape(width, HEADS, HEAD_DIM)
    queries = rotary(queries_raw, positions, 1.0).astype(jnp.bfloat16)
    keys_raw = jnp.dot(normed, attention_set[4], preferred_element_type=jnp.float32)
    keys = rotary(keys_raw[:, None, :], positions, 1.0)[:, 0, :].astype(jnp.bfloat16)
    values = jnp.dot(normed, attention_set[5], preferred_element_type=jnp.float32).astype(
        jnp.bfloat16
    )
    query_index = lax.axis_index("seq") * width + jnp.arange(width, dtype=jnp.int32)
    first_index = query_index - positions

    def visibility(key_start):
        key_index = key_start + jnp.arange(width, dtype=jnp.int32)
        seen = (key_index[None, :] >= first_index[:, None]) & (
            key_index[None, :] <= query_index[:, None]
        )
        return seen[:, None, :]

    start_state = (
        jnp.full((width, HEADS), masked_score, jnp.float32),
        jnp.zeros((width, HEADS), jnp.float32),
        jnp.zeros((width, HEADS, HEAD_DIM), jnp.float32),
    )
    carry = start_state
    piece = (
        lax.all_gather(keys, "seq", axis=0, tiled=True),
        lax.all_gather(values, "seq", axis=0, tiled=True),
    )
    blocks = piece[0].shape[0] // width
    key_blocks = piece[0].reshape(blocks, width, HEAD_DIM)
    value_blocks = piece[1].reshape(blocks, width, HEAD_DIM)

    def forward_one_block(state, item):
        key_block, value_block, number = item
        key_start = number * width
        top, total, accum = state
        seen = visibility(key_start)
        scores = (
            jnp.einsum("thd,kd->thk", queries, key_block, preferred_element_type=jnp.float32)
            * scale
        )
        scores = jnp.where(seen, scores, masked_score)
        new_top = jnp.maximum(top, jnp.max(scores, axis=-1))
        weights = jnp.where(seen, jnp.exp(scores - new_top[..., None]), 0.0)
        decay = jnp.exp(top - new_top)
        total = total * decay + jnp.sum(weights, axis=-1)
        accum = accum * decay[..., None] + jnp.einsum(
            "thk,kd->thd",
            weights.astype(jnp.bfloat16),
            value_block,
            preferred_element_type=jnp.float32,
        )
        state = (new_top, total, accum)
        return (state, None)

    carry, _ = lax.scan(
        forward_one_block, carry, (key_blocks, value_blocks, jnp.arange(blocks, dtype=jnp.int32))
    )
    top, total, accum = carry
    attended_full = accum / total[..., None]
    log_total = top + jnp.log(total)
    attended = attended_full.reshape(width, HEADS * HEAD_DIM).astype(jnp.bfloat16)
    middle = inputs + jnp.dot(attended, attention_set[6], preferred_element_type=jnp.float32)
    mid_gain = feed_set[0].astype(jnp.float32)
    mid_scale = rms_scale(middle)
    normed_mid = (middle * mid_scale * mid_gain).astype(jnp.bfloat16)
    gate = jnp.dot(normed_mid, feed_set[1], preferred_element_type=jnp.float32)
    upper = jnp.dot(normed_mid, feed_set[2], preferred_element_type=jnp.float32)
    sigmoid_gate = jax.nn.sigmoid(gate)
    silu_gate = gate * sigmoid_gate
    hidden = (silu_gate * upper).astype(jnp.bfloat16)
    output = (middle + jnp.dot(hidden, feed_set[3], preferred_element_type=jnp.float32)).astype(
        jnp.bfloat16
    )
    feed_back = (
        lax.all_gather(norm_mid_gain.astype(jnp.bfloat16), ("dp", "seq"), axis=0, tiled=True),
        lax.all_gather(w_gate.astype(jnp.bfloat16), ("dp", "seq"), axis=0, tiled=True),
        lax.all_gather(w_up.astype(jnp.bfloat16), ("dp", "seq"), axis=0, tiled=True),
        lax.all_gather(w_down.astype(jnp.bfloat16), ("dp", "seq"), axis=0, tiled=True),
    )
    grad_out_full = cotangent.astype(jnp.float32)
    grad_down = jnp.einsum("tf,td->fd", hidden, cotangent, preferred_element_type=jnp.float32)
    grad_hidden = jnp.einsum(
        "td,fd->tf", cotangent, feed_back[3], preferred_element_type=jnp.float32
    )
    grad_gate = (grad_hidden * upper * sigmoid_gate * (1.0 + gate * (1.0 - sigmoid_gate))).astype(
        jnp.bfloat16
    )
    grad_upper = (grad_hidden * silu_gate).astype(jnp.bfloat16)
    grad_gate_weight = jnp.einsum(
        "td,tf->df", normed_mid, grad_gate, preferred_element_type=jnp.float32
    )
    grad_up_weight = jnp.einsum(
        "td,tf->df", normed_mid, grad_upper, preferred_element_type=jnp.float32
    )
    grad_normed_mid = jnp.einsum(
        "tf,df->td", grad_gate, feed_back[1], preferred_element_type=jnp.float32
    ) + jnp.einsum("tf,df->td", grad_upper, feed_back[2], preferred_element_type=jnp.float32)
    grad_mid_norm, grad_mid_gain = norm_backward(
        middle, mid_scale, feed_back[0].astype(jnp.float32), grad_normed_mid
    )
    grad_middle = grad_out_full + grad_mid_norm
    feed_grads = (
        lax.psum_scatter(grad_mid_gain, ("dp", "seq"), scatter_dimension=0, tiled=True),
        lax.psum_scatter(grad_gate_weight, ("dp", "seq"), scatter_dimension=0, tiled=True),
        lax.psum_scatter(grad_up_weight, ("dp", "seq"), scatter_dimension=0, tiled=True),
        lax.psum_scatter(grad_down, ("dp", "seq"), scatter_dimension=0, tiled=True),
    )
    attention_back = (
        lax.all_gather(norm_in_gain.astype(jnp.bfloat16), ("dp", "seq"), axis=0, tiled=True),
        lax.all_gather(q_down.astype(jnp.bfloat16), ("dp", "seq"), axis=0, tiled=True),
        lax.all_gather(q_gain.astype(jnp.bfloat16), ("dp", "seq"), axis=0, tiled=True),
        lax.all_gather(q_up.astype(jnp.bfloat16), ("dp", "seq"), axis=0, tiled=True),
        lax.all_gather(key_proj.astype(jnp.bfloat16), ("dp", "seq"), axis=0, tiled=True),
        lax.all_gather(value_proj.astype(jnp.bfloat16), ("dp", "seq"), axis=0, tiled=True),
        lax.all_gather(out_proj.astype(jnp.bfloat16), ("dp", "seq"), axis=0, tiled=True),
    )
    branch_grad = grad_middle.astype(jnp.bfloat16)
    grad_output_weight = jnp.einsum(
        "ta,td->ad", attended, branch_grad, preferred_element_type=jnp.float32
    )
    grad_attended = (
        jnp.einsum("td,ad->ta", branch_grad, attention_back[6], preferred_element_type=jnp.float32)
        .reshape(width, HEADS, HEAD_DIM)
        .astype(jnp.bfloat16)
    )
    delta = jnp.sum(grad_attended.astype(jnp.float32) * attended_full, axis=-1)
    group_rows = width * lax.axis_size("seq")
    back_state = (
        jnp.zeros((width, HEADS, HEAD_DIM), jnp.float32),
        jnp.zeros((group_rows, HEAD_DIM), jnp.float32),
        jnp.zeros((group_rows, HEAD_DIM), jnp.float32),
    )
    carry = back_state
    piece = (
        lax.all_gather(keys, "seq", axis=0, tiled=True),
        lax.all_gather(values, "seq", axis=0, tiled=True),
    )
    blocks = piece[0].shape[0] // width
    key_blocks = piece[0].reshape(blocks, width, HEAD_DIM)
    value_blocks = piece[1].reshape(blocks, width, HEAD_DIM)

    def backward_one_block(state, item):
        key_block, value_block, number = item
        key_start = number * width
        grad_query, grad_keys, grad_values = state
        seen = visibility(key_start)
        scores = (
            jnp.einsum("thd,kd->thk", queries, key_block, preferred_element_type=jnp.float32)
            * scale
        )
        probs = jnp.where(seen, jnp.exp(scores - log_total[..., None]), 0.0)
        grad_value_block = jnp.einsum(
            "thk,thd->kd",
            probs.astype(jnp.bfloat16),
            grad_attended,
            preferred_element_type=jnp.float32,
        )
        grad_probs = jnp.einsum(
            "thd,kd->thk", grad_attended, value_block, preferred_element_type=jnp.float32
        )
        grad_scores = (probs * (grad_probs - delta[..., None]) * scale).astype(jnp.bfloat16)
        grad_query = grad_query + jnp.einsum(
            "thk,kd->thd", grad_scores, key_block, preferred_element_type=jnp.float32
        )
        grad_key_block = jnp.einsum(
            "thk,thd->kd", grad_scores, queries, preferred_element_type=jnp.float32
        )
        state = (
            grad_query,
            add_rows(grad_keys, grad_key_block, key_start),
            add_rows(grad_values, grad_value_block, key_start),
        )
        return (state, None)

    carry, _ = lax.scan(
        backward_one_block, carry, (key_blocks, value_blocks, jnp.arange(blocks, dtype=jnp.int32))
    )
    grad_query, grad_keys, grad_values = carry
    local_key_grad, local_value_grad = (
        lax.psum_scatter(
            grad_keys.astype(jnp.bfloat16), "seq", scatter_dimension=0, tiled=True
        ).astype(jnp.float32),
        lax.psum_scatter(
            grad_values.astype(jnp.bfloat16), "seq", scatter_dimension=0, tiled=True
        ).astype(jnp.float32),
    )
    grad_key_pre = rotary(local_key_grad[:, None, :], positions, -1.0)[:, 0, :].astype(jnp.bfloat16)
    grad_value_pre = local_value_grad.astype(jnp.bfloat16)
    grad_query_pre = (
        rotary(grad_query, positions, -1.0).reshape(width, HEADS * HEAD_DIM).astype(jnp.bfloat16)
    )
    grad_up_query = jnp.einsum(
        "tr,ta->ra", compressed_normed, grad_query_pre, preferred_element_type=jnp.float32
    )
    grad_compressed_normed = jnp.einsum(
        "ta,ra->tr", grad_query_pre, attention_back[3], preferred_element_type=jnp.float32
    )
    grad_compressed, grad_query_gain = norm_backward(
        compressed, query_scale, attention_back[2].astype(jnp.float32), grad_compressed_normed
    )
    grad_compressed = grad_compressed.astype(jnp.bfloat16)
    grad_down_weight = jnp.einsum(
        "td,tr->dr", normed, grad_compressed, preferred_element_type=jnp.float32
    )
    grad_key_weight = jnp.einsum(
        "td,te->de", normed, grad_key_pre, preferred_element_type=jnp.float32
    )
    grad_value_weight = jnp.einsum(
        "td,te->de", normed, grad_value_pre, preferred_element_type=jnp.float32
    )
    grad_normed = jnp.einsum(
        "tr,dr->td", grad_compressed, attention_back[1], preferred_element_type=jnp.float32
    )
    grad_normed = grad_normed + jnp.einsum(
        "te,de->td", grad_key_pre, attention_back[4], preferred_element_type=jnp.float32
    )
    grad_normed = grad_normed + jnp.einsum(
        "te,de->td", grad_value_pre, attention_back[5], preferred_element_type=jnp.float32
    )
    grad_in_norm, grad_in_gain = norm_backward(
        inputs, in_scale, attention_back[0].astype(jnp.float32), grad_normed
    )
    grad_tokens = (grad_middle + grad_in_norm).astype(jnp.bfloat16)
    attention_grads = (
        lax.psum_scatter(grad_in_gain, ("dp", "seq"), scatter_dimension=0, tiled=True),
        lax.psum_scatter(grad_down_weight, ("dp", "seq"), scatter_dimension=0, tiled=True),
        lax.psum_scatter(grad_query_gain, ("dp", "seq"), scatter_dimension=0, tiled=True),
        lax.psum_scatter(grad_up_query, ("dp", "seq"), scatter_dimension=0, tiled=True),
        lax.psum_scatter(grad_key_weight, ("dp", "seq"), scatter_dimension=0, tiled=True),
        lax.psum_scatter(grad_value_weight, ("dp", "seq"), scatter_dimension=0, tiled=True),
        lax.psum_scatter(grad_output_weight, ("dp", "seq"), scatter_dimension=0, tiled=True),
    )
    return (
        output,
        grad_tokens,
        attention_grads[0],
        attention_grads[1],
        attention_grads[2],
        attention_grads[3],
        attention_grads[4],
        attention_grads[5],
        attention_grads[6],
        feed_grads[0],
        feed_grads[1],
        feed_grads[2],
        feed_grads[3],
    )


bf16 = jnp.bfloat16
f32 = jnp.float32
ANY = pl.BlockSpec(memory_space=pl.ANY)
VMEM = pl.BlockSpec(memory_space=pltpu.VMEM)
PLANE = [j // 4 * 8 + j % 4 for j in range(1, 8)]
LINKS = [16, 8, 4, 2, 1]


def flip(number, bits):
    bit = 1
    while bit <= bits:
        if bits & bit:
            number = number + bit - 2 * bit * ((number // bit) % 2)
        bit *= 2
    return number


def coordinates():
    dp = lax.axis_index("dp")
    seq = lax.axis_index("seq")
    return dp // 2, dp % 2, seq // 4, (seq // 2) % 2, seq % 2


def partner(mask):
    return flip(lax.axis_index("dp"), mask // 8), flip(lax.axis_index("seq"), mask % 8)


def greet(masks):
    barrier = pltpu.get_barrier_semaphore()
    for mask in masks:
        pl.semaphore_signal(barrier, inc=1, device_id=partner(mask), device_id_type=pl.DeviceIdType.MESH)
    pl.semaphore_wait(barrier, len(masks))


class Wire:
    def __init__(self, send_sem, recv_sem, local_sem):
        self.send_sem, self.recv_sem, self.local_sem = send_sem, recv_sem, local_sem
        self.copies = []
        self.locals = 0

    def send(self, src, dst, mask):
        k = len(self.copies)
        copy = pltpu.make_async_remote_copy(
            src_ref=src,
            dst_ref=dst,
            send_sem=self.send_sem.at[k],
            recv_sem=self.recv_sem.at[k],
            device_id=partner(mask),
            device_id_type=pl.DeviceIdType.MESH,
        )
        copy.start()
        self.copies.append(copy)
        return copy

    def local(self, src, dst):
        copy = pltpu.make_async_copy(src, dst, self.local_sem.at[self.locals])
        self.locals += 1
        copy.start()
        return copy

    def close(self):
        for copy in self.copies:
            copy.wait_send()


def wires(remote, local):
    return [pltpu.SemaphoreType.DMA((remote,)), pltpu.SemaphoreType.DMA((remote,)), pltpu.SemaphoreType.DMA((local,))]


def arrived(copies):
    for copy in copies:
        copy.wait_recv()


def landed(copies):
    for copy in copies:
        copy.wait()


def moving(kernel, number, outs, operands, scratch, in_specs=None, out_specs=None, limit=56):
    return pl.pallas_call(
        kernel,
        out_shape=outs,
        in_specs=in_specs or [ANY] * len(operands),
        out_specs=out_specs or [ANY] * len(outs),
        scratch_shapes=scratch,
        compiler_params=pltpu.CompilerParams(
            collective_id=number, has_side_effects=True, vmem_limit_bytes=limit * 1024 * 1024
        ),
        cost_estimate=pl.CostEstimate(flops=0, bytes_accessed=100_000_000, transcendentals=0),
        name=kernel.__name__,
    )(*operands)


def shaped(shape, dtype=bf16):
    return jax.ShapeDtypeStruct(tuple(shape), dtype)


def each_rows(rows, body, step=16):
    @pl.loop(0, rows // step)
    def _(i):
        body(pl.ds(pl.multiple_of(i * step, step), step))


def wide(ref, where):
    return ref[where].astype(f32)


def routes(rows, pieces, direct):
    size = rows // pieces
    return [(pl.ds(i * size, size), "xl" if i < direct else "lx") for i in range(pieces)]


def plane_gather(wire, block, out, own, ways):
    links = {"x": (out.at[1, 0, 0], out.at[1, 0, 1], 8), "l": (out.at[0, 1, 0], out.at[0, 1, 1], 2)}
    far, far_core = out.at[1, 1, 0], out.at[1, 1, 1]
    ordered = [k for k in range(len(ways)) if ways[k][1] == "xl"] + [k for k in range(len(ways)) if ways[k][1] == "lx"]
    came = {}
    for turn in (0, 1):
        for k in ordered:
            rows, way = ways[k]
            target, _, mask = links[way[turn]]
            came[way[turn], k] = wire.send(block.at[rows], target.at[rows], mask)
    cores = [wire.send(block, out.at[0, 0, 1], 1)]
    mine = wire.local(block, own) if own is not None else None
    diagonal = {}

    def step(k):
        rows, way = ways[k]
        target, core, _ = links[way[0]]
        came[way[0], k].wait_recv()
        diagonal[k] = wire.send(target.at[rows], far.at[rows], links[way[1]][2])
        cores.append(wire.send(target.at[rows], core.at[rows], 1))

    def finish():
        for k in ordered:
            rows, way = ways[k]
            target, core, _ = links[way[1]]
            came[way[1], k].wait_recv()
            cores.append(wire.send(target.at[rows], core.at[rows], 1))
        for k in ordered:
            rows, way = ways[k]
            diagonal[k].wait_recv()
            cores.append(wire.send(far.at[rows], far_core.at[rows], 1))
        if mine is not None:
            mine.wait()
        arrived(cores)

    return [lambda k=k: step(k) for k in ordered], finish


ARRIVAL = [(1, 1), (1, 0), (0, 1), (0, 0)]


def plane_reduce(wire, parts, out, kept, from_c, send_one, recv_one, send_two, recv_two, ways, load=True):
    cores = {}
    loads = {}
    masks = {"x": 8, "l": 2}
    beside = {"xl": (1, 0), "lx": (0, 1)}
    after = {"xl": (0, 1), "lx": (1, 0)}
    came = {}
    passed = {}

    def give(k):
        cores[k] = wire.send(parts.at[k[0], k[1], 1], from_c.at[k[0], k[1]], 1)
        if load:
            loads[k] = wire.local(parts.at[k[0], k[1], 0], kept.at[k[0], k[1]])

    def pair(k, r):
        return wide(kept.at[k[0], k[1]], r) + wide(from_c.at[k[0], k[1]], r)

    def within(rows, body):
        @pl.loop(0, rows.size // 16)
        def _(i):
            body(pl.ds(pl.multiple_of(rows.start + i * 16, 16), 16))

    def put(slot, k, j):
        rows, way = ways[j]

        def fill(r):
            send_one[slot, r] = pair(k, r).astype(bf16)

        within(rows, fill)
        came[slot, j] = wire.send(send_one.at[slot, rows], recv_one.at[slot, rows], masks[way[0]])

    def arrive(k):
        if load:
            loads[k].wait()
        cores[k].wait_recv()
        for j in range(len(ways)):
            if k == (1, 1):
                put(0, k, j)
            elif beside[ways[j][1]] == k:
                put(1, k, j)

    def step(j):
        rows, way = ways[j]
        came[0, j].wait_recv()

        def fill(r):
            send_two[r] = (pair(after[way], r) + wide(recv_one.at[0], r)).astype(bf16)

        within(rows, fill)
        passed[j] = wire.send(send_two.at[rows], recv_two.at[rows], masks[way[1]])

    def finish():
        for j, (rows, way) in enumerate(ways):
            came[1, j].wait_recv()
            passed[j].wait_recv()

            def fill(r):
                out[r] = pair((0, 0), r) + wide(recv_one.at[1], r) + wide(recv_two, r)

            within(rows, fill)

    return give, arrive, [lambda j=j: step(j) for j in range(len(ways))], finish


def each(action, items=ARRIVAL):
    for item in items:
        action(item)


def do(steps):
    for step in steps:
        step()


def reduce_scratch(rows, width):
    return [
        pltpu.VMEM((2, 2, rows, width), bf16),
        pltpu.VMEM((2, 2, rows, width), bf16),
        pltpu.VMEM((2, rows, width), bf16),
        pltpu.VMEM((2, rows, width), bf16),
        pltpu.VMEM((rows, width), bf16),
        pltpu.VMEM((rows, width), bf16),
    ]


def over_y(wire, block, place, side):
    y, x, h, l, c = coordinates()
    hh = h if side == 0 else 1 - h
    mine = wire.local(block, place(y, hh))
    sent = wire.send(block, place(y, hh), 16)

    def finish():
        mine.wait()
        sent.wait_recv()

    return finish


def thirds(width):
    main = (width * 5 // 12) // 128 * 128
    return [pl.ds(0, main), pl.ds(main, main), pl.ds(2 * main, width - 2 * main)]


def head_kernel(
    q_down, key, value, gains, q_up, gate, up, out_proj, w_down, places,
    first_out, upq_out, gu, wo_out, wo_far, wd_out, in_gain, mid_gain, q_gain, place_row,
    first, upq, staged, gains_out, places_out, send_sem, recv_sem, local_sem,
):
    y, x, h, l, c = coordinates()
    rank = x * 4 + l * 2 + c
    wire = Wire(send_sem, recv_sem, local_sem)
    greet([16, 4] + PLANE)
    r1, r2 = q_down.shape[1], q_down.shape[1] + key.shape[1]
    first[:, :r1] = q_down[...].astype(bf16)
    first[:, r1:r2] = key[...].astype(bf16)
    first[:, r2:] = value[...].astype(bf16)
    width = first.shape[1]
    a, b, d = thirds(width)
    mine = [wire.local(first, first_out.at[y, x, h, l, c]), wire.local(gains, gains_out.at[y, x, h, l, c])]
    one = [wire.send(first.at[:, p], first_out.at[y, x, h, l, c, :, p], 4) for p in (a, b, d)]
    gain = wire.send(gains, gains_out.at[y, x, h, l, c], 4)
    place = [wire.send(places, places_out.at[j], PLANE[j - 1]) for j in range(1, 8)]
    place_mine = wire.local(places, places_out.at[0])
    heads = q_up.shape[1] // HEAD_DIM
    for head in range(heads):
        hy, hx, hh, hl = head // 8, head // 4 % 2, head // 2 % 2, head % 2
        target = hx * 4 + hl * 2 + hh
        upq[target, :, hy * HEAD_DIM : (hy + 1) * HEAD_DIM] = q_up[:, head * HEAD_DIM : (head + 1) * HEAD_DIM].astype(bf16)
    up_rows = upq.shape[1]
    up_place = lambda: upq_out.at[y, x, h, pl.ds((l * 2 + c) * up_rows, up_rows), :]
    up_mine = wire.local(upq.at[rank], up_place())
    up_sent = [wire.send(upq.at[flip(rank, j)], up_place(), PLANE[j - 1]) for j in range(1, 8)]
    wo_out[...] = out_proj[...].astype(bf16)
    piece = gate.shape[1] // 32
    size = 4 * piece
    main = size // 128 * 128
    for target in range(8):
        for where, weight in ((0, gate), (1, up)):
            for q in range(4):
                n = q // 2 * 16 + target // 4 * 8 + q % 2 * 4 + target % 4
                staged[where, :, q * piece : (q + 1) * piece] = weight[:, n * piece : (n + 1) * piece]
        gu[target, :, :main] = staged[0, :, :main].astype(bf16)
        rest = size - main
        both = jnp.concatenate([staged[0, :, main : main + rest], staged[1, :, main : main + rest]], axis=1)
        gu[target, :, main : main + 2 * rest] = both.astype(bf16)
        gu[target, :, main + 2 * rest :] = staged[1, :, :main].astype(bf16)
    wd_out[...] = w_down[...].astype(bf16)
    landed(mine)

    every = slice(None)

    def step(held, columns, mask):
        at = tuple(every if k in held else v for k, v in zip("yxhlc", (y, x, h, l, c)))
        if columns is None:
            return wire.send(gains_out.at[at], gains_out.at[at], mask)
        place = first_out.at[at + (every, columns)]
        return wire.send(place, place, mask)

    def last(held, bit, columns):
        at = {k: every if k in held else v for k, v in zip("yxhlc", (y, x, h, l, c))}
        at[bit] = 1 - dict(zip("yxhlc", (y, x, h, l, c)))[bit]
        place = first_out.at[tuple(at[k] for k in "yxhlc") + (every, columns)]
        return wire.send(place, place, 1)

    bits = {"y": 16, "x": 8, "h": 4, "l": 2}
    orders = [("hlxy", a), ("hlyx", b), ("hxyl", d)]
    sent = one
    for k in range(1, 4):
        following = []
        for (order, columns), copy in zip(orders, sent):
            copy.wait_recv()
            following.append(step(order[:k], columns, bits[order[k]]))
        sent = following
        gain.wait_recv()
        gain = step("hlxy"[:k], None, bits["hlxy"[k]])
        if k == 1:
            up_mine.wait()
            arrived(up_sent)
            up_h = wire.send(upq_out.at[y, :, h], upq_out.at[y, :, h], 4)
            up_y = [wire.send(upq_out.at[y, :, h], upq_out.at[y, :, h], 16)]
            wo_sent = wire.send(wo_out, wo_far, 4)
        if k == 3:
            five = [step(order[:3], columns, 1) for order, columns in orders]
    up_h.wait_recv()
    up_y += [wire.send(upq_out.at[y, :, 1 - h], upq_out.at[y, :, 1 - h], 16)]
    gain.wait_recv()
    gain = step("hlxy", None, 1)
    for (order, columns), copy in zip(orders, sent):
        copy.wait_recv()
        five.append(last(order[:3], order[3], columns))
    place_mine.wait()
    arrived(place)
    rows = places.shape[1]
    first_rows = jnp.concatenate([places_out[j] for j in range(8)], axis=1)
    place_row[...] = first_rows
    gain.wait_recv()
    span, q_span = in_gain.shape[1] // 32, q_gain.shape[1] // 32
    for n in range(32):
        row = gains_out[n // 16, n // 8 % 2, n // 4 % 2, n // 2 % 2, n % 2]
        in_gain[:, n * span : (n + 1) * span] = row[:, :span]
        mid_gain[:, n * span : (n + 1) * span] = row[:, span : 2 * span]
        q_gain[:, n * q_span : (n + 1) * q_span] = row[:, 2 * span : 2 * span + q_span]
    arrived(five + up_y + [wo_sent])
    wire.close()


def head(q_down, key, value, gains, q_up, gate, up, out_proj, w_down, places):
    rows = q_down.shape[0]
    width = q_down.shape[1] + 2 * key.shape[1]
    columns = gate.shape[1] // 4
    slice_size = gate.shape[1] // 8
    outs = [
        shaped((2, 2, 2, 2, 2, rows, width)),
        shaped((2, 2, 2, 4 * q_up.shape[0], 2 * HEAD_DIM)),
        shaped((8, rows, columns)),
        shaped(out_proj.shape),
        shaped(out_proj.shape),
        shaped(w_down.shape),
        shaped((1, 32 * rows), f32),
        shaped((1, 32 * rows), f32),
        shaped((1, q_down.shape[1]), f32),
        shaped((1, 8 * places.shape[1]), jnp.int32),
    ]
    scratch = [
        pltpu.VMEM((rows, width), bf16),
        pltpu.VMEM((8, q_up.shape[0], 2 * HEAD_DIM), bf16),
        pltpu.VMEM((2, rows, slice_size), f32),
        pltpu.VMEM((2, 2, 2, 2, 2) + gains.shape, f32),
        pltpu.VMEM((8,) + places.shape, jnp.int32),
    ]
    operands = (q_down, key, value, gains, q_up, gate, up, out_proj, w_down, places)
    return moving(
        head_kernel, 1, outs, operands, scratch + wires(100, 8),
        in_specs=[VMEM] * len(operands),
        out_specs=[ANY, ANY, VMEM, VMEM, ANY, VMEM, VMEM, VMEM, VMEM, VMEM],
    )


def turned(values, cosine, sine, sign):
    half = HEAD_DIM // 2
    out = []
    for start in range(0, values.shape[1], HEAD_DIM):
        one, two = values[:, start : start + half], values[:, start + half : start + HEAD_DIM]
        out += [one * cosine - sign * two * sine, sign * one * sine + two * cosine]
    return jnp.concatenate(out, axis=1)


def row_scale(values):
    return lax.rsqrt(jnp.mean(values * values, axis=-1, keepdims=True) + epsilon)


def pack_kernel(
    tokens, gain_in, gain_q, first_weight, cosine, sine, wo_own, wo_far, gu, wd_own,
    out, weight_out, gu_out, wd_far, normed, compressed,
    weight, block, weight_all, send_sem, recv_sem, local_sem,
):
    y, x, h, l, c = coordinates()
    wire = Wire(send_sem, recv_sem, local_sem)
    load = wire.local(first_weight, weight)
    greet([16, 4] + PLANE)
    rank = x * 4 + l * 2 + c
    gu_rows = gu.shape[1]
    gu_place = gu_out.at[x, pl.ds((l * 2 + c) * gu_rows, gu_rows), :]
    gu_mine = wire.local(gu.at[rank], gu_place)
    gu_sent = [wire.send(gu.at[flip(rank, j)], gu_place, PLANE[j - 1]) for j in range(1, 8)]
    weight_done = [over_y(wire, ref, lambda yy, hh: weight_all.at[yy, hh], k) for k, ref in enumerate((wo_own, wo_far))]
    inputs = tokens[...].astype(f32)
    normed[...] = (inputs * row_scale(inputs) * gain_in[...]).astype(bf16)
    load.wait()
    mixed = jnp.dot(normed[...], weight[...], preferred_element_type=f32)
    rank_dim = compressed.shape[1]
    query = mixed[:, :rank_dim]
    compressed[...] = query
    block[:, :rank_dim] = (query * row_scale(query) * gain_q[...]).astype(bf16)
    block[:, rank_dim : rank_dim + HEAD_DIM] = turned(
        mixed[:, rank_dim : rank_dim + HEAD_DIM], cosine[...], sine[...], 1.0
    ).astype(bf16)
    block[:, rank_dim + HEAD_DIM :] = mixed[:, rank_dim + HEAD_DIM :].astype(bf16)
    near = block.shape[1]
    far = 2 * HEAD_DIM
    columns, far_columns = pl.ds(0, near), pl.ds(near, far)
    from_h = wire.send(block.at[:, pl.ds(near - far, far)], out.at[0, 0, 0, :, far_columns], 4)
    wd_sent = wire.send(wd_own, wd_far, 4)
    near_out = out.at[:, :, :, :, columns]
    size = block.shape[0]
    steps, finish = plane_gather(wire, block, near_out, near_out.at[0, 0, 0], routes(size, 4, 1))
    from_h.wait_recv()
    far_out = out.at[:, :, :, :, far_columns]
    far_steps, far_finish = plane_gather(wire, far_out.at[0, 0, 0], far_out, None, routes(size, 2, 1))
    do(steps)
    do(far_steps)
    do(weight_done)
    swapped = wire.send(weight_all.at[:, 1 - c], weight_out.at[:, c], 1)
    kept = wire.local(weight_all.at[:, c], weight_out.at[:, c])
    finish()
    far_finish()
    kept.wait()
    gu_mine.wait()
    arrived([swapped, wd_sent] + gu_sent)
    wire.close()


def pack(tokens, gain_in, gain_q, first_weight, cosine, sine, wo_own, wo_far, gu, wd_own):
    rows, width = tokens.shape
    near = first_weight.shape[1]
    rank_dim = near - 2 * HEAD_DIM
    outs = [
        shaped((2, 2, 2, rows, near + 2 * HEAD_DIM)),
        shaped((2, 2) + wo_own.shape),
        shaped((2, 4 * gu.shape[1], gu.shape[2])),
        shaped(wd_own.shape),
        shaped((rows, width)),
        shaped((rows, rank_dim), f32),
    ]
    operands = (tokens, gain_in, gain_q, first_weight, cosine, sine, wo_own, wo_far, gu, wd_own)
    return moving(
        pack_kernel, 2, outs, operands,
        [pltpu.VMEM(first_weight.shape, bf16), pltpu.VMEM((rows, near), bf16), pltpu.VMEM((2, 2) + wo_own.shape, bf16)]
        + wires(60, 12),
        in_specs=[VMEM, VMEM, VMEM, ANY, VMEM, VMEM, VMEM, VMEM, VMEM, VMEM],
        out_specs=[ANY, VMEM, ANY, ANY, VMEM, VMEM],
    )


def mask_of(index, first, last):
    return jnp.where((index >= first) & (index <= last), 0.0, masked_score)


def scores_of(keys, queries):
    return lax.dot_general(keys, queries, (((1,), (1,)), ((), ())), preferred_element_type=f32)


def attend_kernel(
    plane_set, wq, wo, cosine, sine, key_index, query_index, first_index, tokens, gain, cotangent, gu_set, wd_own, wd_far,
    queries_out, attended, lse, middle, plane_mid, cotangents, gu_zero, gu_one, wd_out,
    kv, normed, staged, mask, from_c, s1, r1, s2, r2, mid, gu_far, gu_next, load_sem, send_sem, recv_sem, local_sem,
):
    wire = Wire(send_sem, recv_sem, local_sem)
    rank_dim = wq.shape[0]
    loads = [
        pltpu.make_async_copy(plane_set.at[:, :, :, :, pl.ds(rank_dim, 4 * HEAD_DIM)], kv, load_sem.at[0]),
        pltpu.make_async_copy(plane_set.at[:, :, :, :, pl.ds(0, rank_dim)], normed, load_sem.at[1]),
    ]
    for load in loads:
        load.start()
    greet(LINKS)
    places = [lambda yy, hh: gu_zero.at[yy, hh], lambda yy, hh: gu_one.at[yy, hh]]
    passing, gathered = plane_gather(
        wire, cotangent, cotangents, cotangents.at[0, 0, 0], routes(cotangent.shape[0], 4, 1)
    )
    far_sent = wire.send(gu_set.at[0], gu_far, 4)
    gu_done = [over_y(wire, ref, lambda yy, hh: wd_out.at[yy, hh], k) for k, ref in enumerate((wd_own, wd_far))]
    landed(loads)
    rows = kv.shape[3]
    block = 2 * rows

    def one(g, i):
        start = (g * 2 + i) * block
        place = pl.ds(start, block)
        raw = jnp.dot(normed[g, i].reshape(block, rank_dim), wq[...], preferred_element_type=f32)
        queries = (turned(raw, cosine[place], sine[place], 1.0) * (1.0 / math.sqrt(HEAD_DIM))).astype(bf16)
        queries_out[place] = queries
        mask[...] = mask_of(key_index[...], first_index[:, place], query_index[:, place])
        keys = jnp.concatenate(
            [kv[g, :, :, :, :HEAD_DIM].reshape(2 * block, HEAD_DIM), kv[g, :, :, :, 2 * HEAD_DIM : 3 * HEAD_DIM].reshape(2 * block, HEAD_DIM)]
        )
        values = jnp.concatenate(
            [kv[g, :, :, :, HEAD_DIM : 2 * HEAD_DIM].reshape(2 * block, HEAD_DIM), kv[g, :, :, :, 3 * HEAD_DIM :].reshape(2 * block, HEAD_DIM)]
        )
        merged = []
        for a in range(2):
            scores = scores_of(keys, queries[:, a * HEAD_DIM : (a + 1) * HEAD_DIM]) + mask[...]
            top = jnp.max(scores, axis=0, keepdims=True)
            weights = jnp.exp(scores - top)
            total = jnp.sum(weights, axis=0, keepdims=True)
            lse[a, :, place] = top + jnp.log(total)
            probs = (weights * (1.0 / total)).astype(bf16)
            merged.append(lax.dot_general(probs, values, (((0,), (0,)), ((), ())), preferred_element_type=f32).astype(bf16))
        merged = jnp.concatenate(merged, axis=1)
        attended[place] = merged
        staged[g, i] = jnp.dot(merged, wo[...], preferred_element_type=f32).astype(bf16).reshape(2, rows, -1)

    give, arrive, steps, finish = plane_reduce(
        wire, staged, middle, staged.at[:, :, 0], from_c, s1, r1, s2, r2, routes(rows, 4, 3), load=False
    )
    for number, k in enumerate(ARRIVAL):
        one(*k)
        give(k)
        if number == 0:
            arrive(k)
        elif number > 1:
            arrive(ARRIVAL[number - 1])
        if number == 1:
            do(passing[:2])
        if number == 2:
            do(passing[2:])
    arrive((0, 0))
    gu_done += [over_y(wire, gu_set.at[k], places[k], 0) for k in range(2)]
    do(steps)
    far_sent.wait_recv()
    next_sent = wire.send(gu_set.at[1], gu_next, 4)
    gu_done.append(over_y(wire, gu_far, places[0], 1))
    gathered()
    finish()

    def norm(r):
        value = tokens[r].astype(f32) + middle[r]
        middle[r] = value
        mid[r] = (value * row_scale(value) * gain[...]).astype(bf16)

    each_rows(rows, norm)
    steps, finish = plane_gather(wire, mid, plane_mid, plane_mid.at[0, 0, 0], routes(rows, 4, 2))
    do(steps)
    next_sent.wait_recv()
    gu_done.append(over_y(wire, gu_next, places[1], 1))
    finish()
    do(gu_done)
    wire.close()


def attend(plane_set, wq, wo, cosine, sine, key_index, query_index, first_index, tokens, gain, cotangent, gu_set, wd_own, wd_far):
    rows, width = tokens.shape
    count = 8 * rows
    rank_dim = wq.shape[0]
    gu = gu_set.shape[1:]
    outs = [
        shaped((count, 2 * HEAD_DIM)),
        shaped((count, 2 * HEAD_DIM)),
        shaped((2, 1, count), f32),
        shaped((rows, width), f32),
        shaped((2, 2, 2, rows, width)),
        shaped((2, 2, 2, rows, width)),
        shaped((2, 2) + gu),
        shaped((2, 2) + gu),
        shaped((2, 2) + wd_own.shape),
    ]
    scratch = [
        pltpu.VMEM((2, 2, 2, rows, 4 * HEAD_DIM), bf16),
        pltpu.VMEM((2, 2, 2, rows, rank_dim), bf16),
        pltpu.VMEM((2, 2, 2, rows, width), bf16),
        pltpu.VMEM((count, 2 * rows), f32),
    ]
    scratch += reduce_scratch(rows, width)[1:]
    scratch += [pltpu.VMEM((rows, width), bf16), pltpu.VMEM(gu, bf16), pltpu.VMEM(gu, bf16), pltpu.SemaphoreType.DMA((2,))]
    operands = (
        plane_set, wq, wo, cosine, sine, key_index, query_index, first_index, tokens, gain, cotangent, gu_set, wd_own, wd_far,
    )
    return moving(
        attend_kernel, 3, outs, operands, scratch + wires(80, 16),
        in_specs=[ANY] + [VMEM] * 13,
        out_specs=[VMEM, VMEM, VMEM, VMEM, ANY, ANY, ANY, ANY, ANY],
        limit=62,
    )


def feed_kernel(mid, cotangent, gu_zero, gu_one, down, hidden, grads, mid_parts, final_parts, gu, wd, sems):
    main = gu.shape[4] // 2 // 128 * 128
    units = down.shape[2] * 4
    padded = wd.shape[0]
    columns = gu.shape[4]

    @pl.when(pl.program_id(0) == 0)
    def _():
        copies = [
            pltpu.make_async_copy(gu_zero, gu.at[:, 0], sems.at[0]),
            pltpu.make_async_copy(gu_one, gu.at[:, 1], sems.at[1]),
        ]
        size = down.shape[2]
        for k in range(4):
            copies.append(pltpu.make_async_copy(down.at[k // 2, k % 2], wd.at[pl.ds(k * size, size)], sems.at[2 + k]))
        for copy in copies:
            copy.start()
        wd[units:] = jnp.zeros((padded - units, wd.shape[1]), bf16)
        landed(copies)

    weight = gu[...].reshape(-1, columns)
    both = jnp.dot(mid[...], weight, preferred_element_type=f32)
    gate = both[:, : main + 128]
    upper = jnp.concatenate([both[:, main + 128 :], pltpu.roll(both[:, main : main + 128], 64, 1)], axis=1)
    grad = lax.dot_general(cotangent[...], wd[...], (((1,), (1,)), ((), ())), preferred_element_type=f32)
    sigmoid = 1.0 / (1.0 + jnp.exp(-gate))
    silu = gate * sigmoid
    hid = (silu * upper).astype(bf16)
    hidden[...] = hid[:, :units]
    final_parts[...] = jnp.dot(hid, wd[...], preferred_element_type=f32).astype(bf16)
    grad_gate = grad * upper * sigmoid * (1.0 + gate * (1.0 - sigmoid))
    grad_upper = grad * silu
    joint = grad_gate[:, main:] + pltpu.roll(grad_upper[:, main:], 64, 1)
    out = jnp.concatenate([grad_gate[:, :main], joint, grad_upper[:, :main]], axis=1).astype(bf16)
    grads[...] = out
    mid_parts[...] = lax.dot_general(out, weight, (((1,), (1,)), ((), ())), preferred_element_type=f32).astype(bf16)


def feed(mid, cotangent, gu_zero, gu_one, down, block=384):
    tokens, width = mid.shape
    columns = gu_zero.shape[-1]
    units = 4 * down.shape[2]
    padded = (units + 127) // 128 * 128
    by_block = lambda n: pl.BlockSpec((block, n), lambda i: (i, 0))
    return pl.pallas_call(
        feed_kernel,
        grid=(tokens // block,),
        in_specs=[by_block(width), by_block(width), ANY, ANY, ANY],
        out_specs=[by_block(units), by_block(columns), by_block(width), by_block(width)],
        out_shape=[shaped((tokens, units)), shaped((tokens, columns)), shaped((tokens, width)), shaped((tokens, width))],
        scratch_shapes=[
            pltpu.VMEM((2, 2, 2) + gu_zero.shape[2:], bf16),
            pltpu.VMEM((padded, width), bf16),
            pltpu.SemaphoreType.DMA((6,)),
        ],
        compiler_params=pltpu.CompilerParams(vmem_limit_bytes=56 * 1024 * 1024),
        cost_estimate=pl.CostEstimate(flops=12 * tokens * width * units, bytes_accessed=40_000_000, transcendentals=0),
        name="feed",
    )(mid, cotangent, gu_zero, gu_one, down)


def fold_y(wire, source, recv, passed, kept):
    y, x, h, l, c = coordinates()
    sent = [wire.send(source(1 - y, hh), recv.at[hh], 16) for hh in (1 - h, h)]

    def half(k, hh, target):
        sent[k].wait_recv()
        mine = source(y, hh)

        def body(r):
            target[r] = (wide(mine, r) + wide(recv.at[hh], r)).astype(target.dtype)

        each_rows(target.shape[0], body)

    return lambda: half(0, 1 - h, passed), lambda: half(1, h, kept)


def fold_h(wire, passed, kept, recv, out):
    sent = wire.send(passed, recv, 4)

    def finish():
        sent.wait_recv()

        def body(r):
            out[r] = (wide(kept, r) + wide(recv, r)).astype(out.dtype)

        each_rows(out.shape[0], body)

    return finish


def hand_back(wire, own, out):
    y, x, h, l, c = coordinates()
    rank = x * 4 + l * 2 + c
    mine = wire.local(own(rank), out.at[rank])
    sent = [wire.send(own(flip(rank, j)), out.at[rank], PLANE[j - 1]) for j in range(1, 8)]

    def finish():
        mine.wait()
        arrived(sent)

    return finish


def norm_back(value, gain, grad):
    scale = row_scale(value)
    weighted = gain * grad
    inner = scale * weighted - value * scale * scale * scale * jnp.mean(weighted * value, axis=-1, keepdims=True)
    return inner, grad * value * scale


def over_tokens(left, right):
    return lax.dot_general(left, right, (((0,), (0,)), ((), ())), preferred_element_type=f32).astype(bf16)


def branch_kernel(
    parts, middle, cotangent, gain, mid, hidden, gu_grads, cotangents,
    grad_middle, gain_grad, plane_branch, down_out, gu_passed, gu_kept, gu_one,
    kept, from_c, s1, r1, s2, r2, normed_grad, branch, wd_grad, wd_recv, wd_passed, wd_kept, wd_far, gu_zero, gu_recv,
    mid_v, hidden_v, gu_v, cotangents_v, load_sem, send_sem, recv_sem, local_sem,
):
    wire = Wire(send_sem, recv_sem, local_sem)
    loads = [
        pltpu.make_async_copy(source, target, load_sem.at[k])
        for k, (source, target) in enumerate(
            ((hidden, hidden_v), (cotangents, cotangents_v), (gu_grads, gu_v), (mid, mid_v))
        )
    ]
    greet(LINKS)
    size = middle.shape[0]
    give, arrive, steps, finish = plane_reduce(
        wire, parts, normed_grad, kept, from_c, s1, r1, s2, r2, routes(size, 4, 3)
    )
    each(give)
    for load in loads:
        load.start()
    each(arrive)
    landed(loads[:2])
    down_rows = wd_grad.shape[2]
    for k in range(4):
        wd_grad[k // 2, k % 2] = over_tokens(hidden_v[:, k * down_rows : (k + 1) * down_rows], cotangents_v[...])
    down_passed, down_kept = fold_y(wire, lambda yy, hh: wd_grad.at[yy, hh], wd_recv, wd_passed, wd_kept)
    landed(loads[2:])
    gu_rows = gu_one.shape[2]

    def columns(yy, xx, hh):
        start = (yy * 4 + xx * 2 + hh) * gu_rows
        return over_tokens(mid_v[:, start : start + gu_rows], gu_v[...])

    for k in range(4):
        gu_zero[k // 2, k % 2] = columns(k // 2, 0, k % 2)
        steps[k]()
    down_passed()
    down_h = fold_h(wire, wd_passed, wd_kept, wd_far, down_out)
    gain_grad[...] = jnp.zeros_like(gain_grad)
    finish()

    def norm(r):
        inner, outer = norm_back(middle[r], gain[...], normed_grad[r])
        value = cotangent[r].astype(f32) + inner
        grad_middle[r] = value
        branch[r] = value.astype(bf16)
        gain_grad[...] += jnp.sum(outer, axis=0, keepdims=True)

    each_rows(size, norm)
    steps, finish = plane_gather(wire, branch, plane_branch, plane_branch.at[0, 0, 0], routes(size, 4, 2))
    gu_sums = fold_y(wire, lambda yy, hh: gu_zero.at[yy, hh], gu_recv, gu_passed, gu_kept)
    for k in range(4):
        gu_one[k // 2, k % 2] = columns(k // 2, 1, k % 2)
        steps[k]()
    down_kept()
    finish()
    do(gu_sums)
    down_h()
    wire.close()


def branch_step(parts, middle, cotangent, gain, mid, hidden, gu_grads, cotangents):
    rows, width = middle.shape
    columns = gu_grads.shape[1]
    down = (hidden.shape[1] // 4, width)
    gu = (width // 8, columns)
    outs = [
        shaped((rows, width), f32),
        shaped((1, width), f32),
        shaped(parts.shape),
        shaped(down, f32),
        shaped(gu),
        shaped(gu),
        shaped((2, 2) + gu),
    ]
    scratch = reduce_scratch(rows, width) + [pltpu.VMEM((rows, width), f32), pltpu.VMEM((rows, width), bf16)]
    scratch += [pltpu.VMEM((2, 2) + down, bf16), pltpu.VMEM((2,) + down, bf16)] + [pltpu.VMEM(down, bf16)] * 3
    scratch += [pltpu.VMEM((2, 2) + gu, bf16), pltpu.VMEM((2,) + gu, bf16)]
    scratch += [pltpu.VMEM(v.shape, bf16) for v in (mid, hidden, gu_grads, cotangents)]
    operands = (parts, middle, cotangent, gain, mid, hidden, gu_grads, cotangents)
    return moving(
        branch_kernel, 4, outs, operands, scratch + [pltpu.SemaphoreType.DMA((4,))] + wires(60, 16),
        in_specs=[ANY, VMEM, VMEM, VMEM, ANY, ANY, ANY, ANY],
        out_specs=[VMEM, VMEM, ANY, VMEM, VMEM, VMEM, VMEM],
        limit=62,
    )


def attend_back_kernel(
    plane_set, plane_branch, queries, attended, lse, wq, wo, cosine, sine, key_index, query_index, first_index,
    final_parts, middle, gu_passed, gu_kept, gu_one,
    query_grad, parts, output, gu_out, gu_passed_next, gu_kept_next,
    kv, branch, staged, grad_keys, grad_values, kept, from_c, s1, r1, s2, r2, total, gu_recv, gu_recv_y, mask,
    load_sem, send_sem, recv_sem, local_sem,
):
    wire = Wire(send_sem, recv_sem, local_sem)
    rank_dim = wq.shape[0]
    rows = kv.shape[3]
    block = 2 * rows
    load_kv = pltpu.make_async_copy(plane_set.at[:, :, :, :, pl.ds(rank_dim, 4 * HEAD_DIM)], kv, load_sem.at[0])
    load_kv.start()

    def load_branch(k):
        return pltpu.make_async_copy(plane_branch.at[k // 2, k % 2], branch.at[k % 2], load_sem.at[1 + k % 2])

    load_branch(0).start()
    greet(LINKS)
    give, arrive, passing, finish = plane_reduce(
        wire, final_parts, total, kept, from_c, s1, r1, s2, r2, routes(middle.shape[0], 4, 3)
    )
    each(give)
    gu_h = fold_h(wire, gu_passed, gu_kept, gu_recv, gu_out)
    gu_sums = fold_y(wire, lambda yy, hh: gu_one.at[yy, hh], gu_recv_y, gu_passed_next, gu_kept_next)
    load_kv.wait()
    def one(k):
        g = k // 2
        i = k % 2
        load_branch(k).wait()

        @pl.when(k < 3)
        def _():
            load_branch(k + 1).start()

        @pl.when(i == 0)
        def _():
            grad_keys[...] = jnp.zeros_like(grad_keys)
            grad_values[...] = jnp.zeros_like(grad_values)

        start = pl.multiple_of(k * block, block)
        place = pl.ds(start, block)
        grads = lax.dot_general(
            branch[i].reshape(block, -1), wo[...], (((1,), (1,)), ((), ())), preferred_element_type=f32
        ).astype(bf16)
        keys = jnp.concatenate(
            [kv[g, :, :, :, :HEAD_DIM].reshape(2 * block, HEAD_DIM), kv[g, :, :, :, 2 * HEAD_DIM : 3 * HEAD_DIM].reshape(2 * block, HEAD_DIM)]
        )
        values = jnp.concatenate(
            [kv[g, :, :, :, HEAD_DIM : 2 * HEAD_DIM].reshape(2 * block, HEAD_DIM), kv[g, :, :, :, 3 * HEAD_DIM :].reshape(2 * block, HEAD_DIM)]
        )
        query_parts = []
        mask[...] = mask_of(key_index[...], first_index[:, place], query_index[:, place])
        for a in range(2):
            span = slice(a * HEAD_DIM, (a + 1) * HEAD_DIM)
            query, grad = queries[place, span], grads[:, span]
            product = grad.astype(f32) * attended[place, span].astype(f32)
            delta = lax.dot_general(
                jnp.ones((8, HEAD_DIM), f32), product, (((1,), (1,)), ((), ())),
                precision=lax.Precision.HIGHEST, preferred_element_type=f32,
            )[:1]
            probs = jnp.exp(scores_of(keys, query) + mask[...] - lse[a, :, place])
            grad_values[...] += jnp.dot(probs.astype(bf16), grad, preferred_element_type=f32)
            grad_probs = lax.dot_general(values, grad, (((1,), (1,)), ((), ())), preferred_element_type=f32)
            grad_scores = (probs * (grad_probs - delta)).astype(bf16)
            grad_keys[...] += jnp.dot(grad_scores, query, preferred_element_type=f32)
            query_parts.append(
                lax.dot_general(grad_scores, keys, (((0,), (0,)), ((), ())), preferred_element_type=f32)
            )
        query_sum = turned(jnp.concatenate(query_parts, axis=1), cosine[place], sine[place], -1.0)
        query_sum = (query_sum * (1.0 / math.sqrt(HEAD_DIM))).astype(bf16)
        query_grad[place] = query_sum
        normed = lax.dot_general(query_sum, wq[...], (((1,), (1,)), ((), ())), preferred_element_type=f32)
        staged[g, i, :, :, :rank_dim] = normed.astype(bf16).reshape(2, rows, rank_dim)

        @pl.when(i == 1)
        def _():
            for number, (source, side) in enumerate(
                ((grad_keys, 0), (grad_values, 0), (grad_keys, 1), (grad_values, 1))
            ):
                column = rank_dim + number * HEAD_DIM
                half = source[side * 2 * block : (side + 1) * 2 * block].astype(bf16)
                staged[g, :, :, :, column : column + HEAD_DIM] = half.reshape(2, 2, rows, HEAD_DIM)
            pltpu.make_async_copy(staged.at[g], parts.at[g], load_sem.at[3 + g]).start()

    def steps(a, b):
        @pl.loop(a, b)
        def _(k):
            one(k)

    each(arrive)
    steps(0, 1)
    do(passing[:1])
    steps(1, 2)
    do(passing[1:3])
    steps(2, 3)
    do(passing[3:])
    gu_h()
    steps(3, 4)
    finish()

    def emit(r):
        output[r] = (middle[r] + total[r]).astype(bf16)

    each_rows(output.shape[0], emit)
    for g in range(2):
        pltpu.make_async_copy(staged.at[g], parts.at[g], load_sem.at[3 + g]).wait()
    do(gu_sums)
    wire.close()


def attend_back(
    plane_set, plane_branch, queries, attended, lse, wq, wo, cosine, sine, key_index, query_index, first_index,
    final_parts, middle, gu_passed, gu_kept, gu_one,
):
    rows, width = middle.shape
    tokens = 8 * rows
    gu = gu_passed.shape
    outs = [
        shaped((tokens, 2 * HEAD_DIM)),
        shaped((2, 2, 2, rows, wq.shape[0] + 4 * HEAD_DIM)),
        shaped((rows, width)),
        shaped(gu),
        shaped(gu),
        shaped(gu),
    ]
    scratch = [
        pltpu.VMEM((2, 2, 2, rows, 4 * HEAD_DIM), bf16),
        pltpu.VMEM((2, 2, rows, width), bf16),
        pltpu.VMEM((2, 2, 2, rows, wq.shape[0] + 4 * HEAD_DIM), bf16),
        pltpu.VMEM((8 * rows, HEAD_DIM), f32),
        pltpu.VMEM((8 * rows, HEAD_DIM), f32),
    ]
    scratch += reduce_scratch(rows, width) + [pltpu.VMEM((rows, width), f32), pltpu.VMEM(gu, bf16)]
    scratch += [pltpu.VMEM((2,) + gu, bf16), pltpu.VMEM((tokens, 2 * rows), f32), pltpu.SemaphoreType.DMA((5,))]
    operands = (
        plane_set, plane_branch, queries, attended, lse, wq, wo, cosine, sine, key_index, query_index, first_index,
        final_parts, middle, gu_passed, gu_kept, gu_one,
    )
    return moving(
        attend_back_kernel, 5, outs, operands, scratch + wires(60, 12),
        in_specs=[ANY, ANY] + [VMEM] * 10 + [ANY, VMEM, ANY, VMEM, VMEM],
        out_specs=[VMEM, ANY, VMEM, VMEM, VMEM, VMEM],
        limit=62,
    )


def tail_kernel(
    parts, normed, compressed, tokens, grad_middle, first_weight, gain_in, gain_q, gain_mid_grad, cosine, sine,
    gu_total, gu_passed, gu_kept, up_grad, out_grad,
    grad_tokens, down_out, key_out, value_out, gains_out, gate_out, up_out, q_up_out, out_out,
    kept, from_c, s1, r1, s2, r2, back, kv_send, kv_recv, weight, mixed, normed_grad, gain_rows,
    blocks, acc, recv, core, gains, gains_recv,
    gu_far, gu_own, gu_back, gu_wide, up_recv, up_passed, up_kept, up_far, up_own, up_back,
    heads, o_recv, o_passed, o_kept, o_far,
    send_sem, recv_sem, local_sem,
):
    y, x, h, l, c = coordinates()
    own = dict(zip("yxhlc", (y, x, h, l, c)))
    every = slice(None)
    wire = Wire(send_sem, recv_sem, local_sem)
    load = wire.local(first_weight, weight)
    greet([16, 4] + PLANE)
    rows = back.shape[0]
    rank_dim = compressed.shape[1]
    split = rank_dim + 2 * HEAD_DIM
    buffers = (parts, back, kept, from_c, s1, r1, s2, r2)
    of = lambda columns: [ref.at[(every,) * (len(ref.shape) - 1) + (columns,)] for ref in buffers]
    far_columns = pl.ds(split, back.shape[1] - split)
    far_give, far_arrive, far_steps, far_finish = plane_reduce(wire, *of(far_columns), routes(rows, 2, 1))
    give, arrive, steps, finish = plane_reduce(wire, *of(pl.ds(0, split)), routes(rows, 4, 3))
    each(far_give)
    each(give)
    each(far_arrive)
    gu_h = fold_h(wire, gu_passed, gu_kept, gu_far, gu_own)
    swapped = wire.send(out_grad.at[:, 1 - c], heads.at[:, c], 1)
    stayed = wire.local(out_grad.at[:, c], heads.at[:, c])
    each(arrive)
    stayed.wait()
    swapped.wait_recv()
    o_sums = fold_y(wire, lambda yy, hh: heads.at[yy, hh], o_recv, o_passed, o_kept)
    up_sums = [
        fold_y(wire, lambda yy, hh, k=k: up_grad.at[yy, k, hh], up_recv.at[k], up_passed.at[k], up_kept.at[k])
        for k in range(2)
    ]
    do(far_steps)
    far_finish()
    kv_send[...] = back[:, split:].astype(bf16)
    far = wire.send(kv_send, kv_recv, 4)
    do(steps)
    finish()
    inner, outer = norm_back(compressed[...], gain_q[...], back[:, :rank_dim])
    mixed[:, :rank_dim] = inner.astype(bf16)
    gain_rows[1:2, :rank_dim] = jnp.sum(outer, axis=0, keepdims=True)
    gain_rows[2:3, :] = gain_mid_grad[...]
    gu_h()
    piece_rows = gu_back.shape[2]
    piece = lambda k: pl.ds(pl.multiple_of((k % 4) * piece_rows, piece_rows), piece_rows)

    both = [wire.local(gu_total, gu_wide.at[0]), wire.local(gu_own, gu_wide.at[1])]
    landed(both)
    gu_done = hand_back(wire, lambda k: gu_wide.at[k // 4, piece(k)], gu_back.at[0])
    far.wait_recv()
    kv = back[:, rank_dim:split] + kv_recv[...].astype(f32)
    mixed[:, rank_dim : rank_dim + HEAD_DIM] = turned(kv[:, :HEAD_DIM], cosine[...], sine[...], -1.0).astype(bf16)
    mixed[:, rank_dim + HEAD_DIM :] = kv[:, HEAD_DIM:].astype(bf16)
    size = normed.shape[1] // 8
    cores = []
    for k in range(8):
        at = (k // 4, k // 2 % 2, k % 2)
        grad = lax.dot_general(
            normed[:, k * size : (k + 1) * size], mixed[...], (((0,), (0,)), ((), ())), preferred_element_type=f32
        )
        blocks[at] = grad.astype(bf16).reshape(blocks.shape[3:])
        cores.append(wire.send(blocks.at[at + (every, 1 - c)], core.at[at], 1))
    do(o_sums)
    o_h = fold_h(wire, o_passed, o_kept, o_far, out_out)
    for k in range(2):
        do(up_sums[k])
    up_h = [fold_h(wire, up_passed.at[k], up_kept.at[k], up_far.at[k], up_own.at[k]) for k in range(2)]
    span = blocks.shape[5]
    width = blocks.shape[6]
    columns = thirds(width)
    orders = ["yxlh", "xylh", "lyxh"]
    sent = [None] * 3

    def index(fixed, block):
        free = [k for k in "yxhl" if k not in fixed]
        at = dict(fixed)
        for position, k in enumerate(reversed(free)):
            at[k] = (block // 2**position) % 2
        return tuple(at[k] for k in "yxhl")

    def over(fixed, body):
        @pl.loop(0, 2 ** (4 - len(fixed)))
        def _(i):
            body(index(fixed, i))

    def pass_on(p, step):
        order = orders[p]
        fixed = {k: own[k] for k in order[:step]}
        bit = order[step]
        src = {**fixed, bit: 1 - own[bit]}
        dst = {**fixed, bit: own[bit]}
        place = lambda at: tuple(at.get(k, every) for k in "yxhl") + (every, columns[p])
        mask = {"y": 16, "x": 8, "h": 4, "l": 2}[bit]
        sent[p] = wire.send(acc.at[place(src)], recv.at[place(dst)], mask)

    arrived(cores)
    for first_side in (True, False):
        for p in range(3):
            bit = orders[p][0]

            def body(at, p=p):
                value = wide(blocks, at + (c, every, columns[p])) + wide(core, at + (every, columns[p]))
                acc[at + (every, columns[p])] = value.astype(bf16)

            over({bit: 1 - own[bit] if first_side else own[bit]}, body)
            if first_side:
                pass_on(p, 0)
    load.wait()
    normed_grad[...] = lax.dot_general(mixed[...], weight[...], (((1,), (1,)), ((), ())), preferred_element_type=f32)
    gain_rows[0:1, :] = jnp.zeros((1, gain_rows.shape[1]), f32)

    def norm(r):
        inner, outer = norm_back(tokens[r].astype(f32), gain_in[...], normed_grad[r])
        grad_tokens[r] = (grad_middle[r] + inner).astype(bf16)
        gain_rows[0:1, :] += jnp.sum(outer, axis=0, keepdims=True)

    each_rows(rows, norm)
    q_span = rank_dim // 32
    gains[...] = jnp.zeros_like(gains)
    for n in range(32):
        at = (n // 16, n // 8 % 2, n // 4 % 2, n // 2 % 2, n % 2, 0)
        gains[at + (slice(0, 128),)] = jnp.concatenate(
            [gain_rows[0, n * span : (n + 1) * span], gain_rows[2, n * span : (n + 1) * span]], axis=0
        )
        gains[at + (slice(128, 128 + q_span),)] = gain_rows[1, n * q_span : (n + 1) * q_span]

    def pass_gains(order, step):
        fixed = {k: own[k] for k in order[:step]}
        bit = order[step]
        place = lambda at: tuple(at.get(k, every) for k in "yxhlc")
        mask = {"y": 16, "x": 8, "h": 4, "l": 2, "c": 1}[bit]
        return wire.send(gains.at[place({**fixed, bit: 1 - own[bit]})], gains_recv.at[place({**fixed, bit: own[bit]})], mask)

    def add_gains(order, step):
        fixed = {k: own[k] for k in order[:step]}
        bit = order[step]
        place = lambda at: tuple(at.get(k, every) for k in "yxhlc")
        mine = place({**fixed, bit: own[bit]})
        gains[mine] = gains[mine] + gains_recv[place({**fixed, bit: 1 - own[bit]})]

    gain_order = "cyxlh"
    gain_sent = pass_gains(gain_order, 0)
    gain_step = 0
    for step in range(4):
        for p in range(3):
            order = orders[p]
            fixed = {k: own[k] for k in order[:step]}
            bit = order[step]
            sent[p].wait_recv()

            def body(at, p=p, bit=bit, last=step == 3):
                other = tuple(1 - own[k] if k == bit else v for k, v in zip("yxhl", at))
                value = wide(acc, at + (every, columns[p])) + wide(recv, other + (every, columns[p]))
                if last:
                    back[:span, columns[p]] = value
                else:
                    acc[at + (every, columns[p])] = value.astype(bf16)

            if step < 3:
                over({**fixed, bit: own[bit], order[step + 1]: 1 - own[order[step + 1]]}, body)
                pass_on(p, step + 1)
                over({**fixed, bit: own[bit], order[step + 1]: own[order[step + 1]]}, body)
            else:
                over({**fixed, bit: own[bit]}, body)
        if gain_step < 5:
            gain_sent.wait_recv()
            add_gains(gain_order, gain_step)
            gain_step += 1
            if gain_step < 5:
                gain_sent = pass_gains(gain_order, gain_step)
        if step == 0:
            for k in range(2):
                up_h[k]()
            up_rows = up_back.shape[1]
            up_piece = lambda k: up_own.at[k // 4, pl.ds(pl.multiple_of((k % 4) * up_rows, up_rows), up_rows)]
            up_done = hand_back(wire, up_piece, up_back)
            gu_done()
            unit = gate_out.shape[1] // 32
            units = 4 * unit
            main = units // 128 * 128
            rest = units - main
            for source in range(8):
                tile = gu_back[0, source].astype(f32)
                halves = (
                    tile[:, : main + rest],
                    jnp.concatenate([tile[:, main + 2 * rest :], tile[:, main + rest : main + 2 * rest]], axis=1),
                )
                for half, target in zip(halves, (gate_out, up_out)):
                    for q in range(4):
                        n = q // 2 * 16 + source // 4 * 8 + q % 2 * 4 + source % 4
                        target[:, n * unit : (n + 1) * unit] = half[:, q * unit : (q + 1) * unit]
        if step == 1:
            o_h()
            up_done()
            for head in range(q_up_out.shape[1] // HEAD_DIM):
                hy, hx, hh, hl = head // 8, head // 4 % 2, head // 2 % 2, head % 2
                source = hx * 4 + hl * 2 + hh
                q_up_out[:, head * HEAD_DIM : (head + 1) * HEAD_DIM] = up_back[
                    source, :, hy * HEAD_DIM : (hy + 1) * HEAD_DIM
                ].astype(f32)
    while gain_step < 5:
        gain_sent.wait_recv()
        add_gains(gain_order, gain_step)
        gain_step += 1
        if gain_step < 5:
            gain_sent = pass_gains(gain_order, gain_step)
    gains_out[...] = gains[y, x, h, l, c]
    down_out[...] = back[:span, :rank_dim]
    key_out[...] = back[:span, rank_dim : rank_dim + HEAD_DIM]
    value_out[...] = back[:span, rank_dim + HEAD_DIM : split]
    wire.close()


def tail(
    parts, normed, compressed, tokens, grad_middle, first_weight, gain_in, gain_q, gain_mid_grad, cosine, sine,
    gu_total, gu_passed, gu_kept, up_grad, out_grad,
):
    rows, width = tokens.shape
    rank_dim = compressed.shape[1]
    near = first_weight.shape[1]
    span = width // 32
    gu = gu_total.shape
    units = gu[1] * 4
    up = up_grad.shape[3:]
    heads = out_grad.shape[2:]
    outs = [
        shaped((rows, width)),
        shaped((span, rank_dim), f32),
        shaped((span, HEAD_DIM), f32),
        shaped((span, HEAD_DIM), f32),
        shaped((1, 256), f32),
        shaped((span, units), f32),
        shaped((span, units), f32),
        shaped((up[0] // 4, 8 * up[1]), f32),
        shaped(heads, f32),
    ]
    sums = (2, 2, 2, 2, span, near)
    scratch = reduce_scratch(rows, width) + [
        pltpu.VMEM((rows, width), f32),
        pltpu.VMEM((rows, 2 * HEAD_DIM), bf16),
        pltpu.VMEM((rows, 2 * HEAD_DIM), bf16),
        pltpu.VMEM(first_weight.shape, bf16),
        pltpu.VMEM((rows, near), bf16),
        pltpu.VMEM((rows, width), f32),
        pltpu.VMEM((8, width), f32),
        pltpu.VMEM((2, 2, 2, 2, 2, span, near), bf16),
        pltpu.VMEM(sums, bf16),
        pltpu.VMEM(sums, bf16),
        pltpu.VMEM(sums, bf16),
        pltpu.VMEM((2, 2, 2, 2, 2, 1, 256), f32),
        pltpu.VMEM((2, 2, 2, 2, 2, 1, 256), f32),
        pltpu.VMEM(gu, bf16),
        pltpu.VMEM(gu, bf16),
        pltpu.VMEM((1, 8, span, gu[1]), bf16),
        pltpu.VMEM((2,) + gu, bf16),
        pltpu.VMEM((2, 2) + up, bf16),
        pltpu.VMEM((2,) + up, bf16),
        pltpu.VMEM((2,) + up, bf16),
        pltpu.VMEM((2,) + up, bf16),
        pltpu.VMEM((2,) + up, bf16),
        pltpu.VMEM((8, up[0] // 4, up[1]), bf16),
        pltpu.VMEM((2, 2) + heads, bf16),
        pltpu.VMEM((2,) + heads, bf16),
        pltpu.VMEM(heads, bf16),
        pltpu.VMEM(heads, bf16),
        pltpu.VMEM(heads, bf16),
    ]
    operands = (
        parts, normed, compressed, tokens, grad_middle, first_weight, gain_in, gain_q, gain_mid_grad, cosine, sine,
        gu_total, gu_passed, gu_kept, up_grad, out_grad,
    )
    return moving(
        tail_kernel, 6, outs, operands, scratch + wires(100, 24),
        in_specs=[ANY] + [VMEM] * 4 + [ANY] + [VMEM] * 5 + [ANY, ANY, VMEM, VMEM, ANY],
        out_specs=[VMEM] * 9,
        limit=62,
    )


def rope_table(places):
    half = HEAD_DIM // 2
    freqs = rope_base ** (-(2.0 * jnp.arange(half).astype(f32)) / HEAD_DIM)
    angles = places.astype(f32)[:, None] * freqs[None, :]
    return jnp.cos(angles), jnp.sin(angles)


def plane_local(
    tokens,
    positions,
    cotangent,
    norm_in_gain,
    q_down,
    q_gain,
    q_up,
    key_proj,
    value_proj,
    out_proj,
    norm_mid_gain,
    w_gate,
    w_up,
    w_down,
):
    rows, width = tokens.shape
    rank_dim = q_down.shape[1]
    seq = lax.axis_index("seq")
    h, l, c = seq // 4, (seq // 2) % 2, seq % 2
    span, q_span = norm_in_gain.shape[0], q_gain.shape[0]

    gains = jnp.concatenate([norm_in_gain, norm_mid_gain, q_gain, jnp.zeros((256 - 2 * span - q_span,), f32)])
    gains = lax.reduce_precision(gains, 8, 7).reshape(1, 256)
    first_weight, up_query, gu_pieces, wo_own, wo_far, wd_own, in_gain, mid_gain, query_gain, places = head(
        q_down, key_proj, value_proj, gains, q_up, w_gate, w_up, out_proj, w_down, positions.reshape(1, rows)
    )
    first_weight = first_weight.reshape(width, rank_dim + 2 * HEAD_DIM)
    up_query = up_query.reshape(rank_dim, 2 * HEAD_DIM)

    blocks = jnp.arange(4, dtype=jnp.int32) ^ (l * 2 + c)
    in_half = (blocks[:, None] * rows + jnp.arange(rows, dtype=jnp.int32)[None, :]).reshape(-1)
    own_index = h * (4 * rows) + in_half
    query_index = jnp.concatenate([own_index, own_index]).reshape(1, 8 * rows)
    first_index = query_index - places
    key_index = jnp.concatenate([own_index, (1 - h) * (4 * rows) + in_half]).reshape(8 * rows, 1)
    cosine, sine = rope_table(places.reshape(-1))

    plane_set, out_weight, gu_set, wd_far, normed, compressed = pack(
        tokens, in_gain, query_gain, first_weight, cosine[:rows], sine[:rows], wo_own, wo_far, gu_pieces, wd_own
    )
    out_weight = out_weight.reshape(2 * HEAD_DIM, width)
    queries, attended, lse, middle, plane_mid, plane_cotangent, gu_zero, gu_one, down_weight = attend(
        plane_set, up_query, out_weight, cosine, sine, key_index, query_index, first_index, tokens, mid_gain, cotangent,
        gu_set, wd_own, wd_far,
    )
    plane_mid = plane_mid.reshape(8 * rows, width)
    plane_cotangent = plane_cotangent.reshape(8 * rows, width)
    hidden, gu_grads, mid_parts, final_parts = feed(plane_mid, plane_cotangent, gu_zero, gu_one, down_weight)

    by_plane = lambda parts: parts.reshape(2, 2, 2, rows, -1)
    grad_middle, mid_gain_grad, plane_branch, grad_down, gu_passed, gu_kept, gu_one_grad = branch_step(
        by_plane(mid_parts), middle, cotangent, mid_gain, plane_mid, hidden, gu_grads, plane_cotangent
    )
    query_grad, back_parts, output, gu_total, gu_passed, gu_kept = attend_back(
        plane_set, plane_branch, queries, attended, lse, up_query, out_weight, cosine, sine,
        key_index, query_index, first_index, by_plane(final_parts), middle, gu_passed, gu_kept, gu_one_grad,
    )
    out_grad = over_tokens(attended, plane_branch.reshape(8 * rows, width)).reshape(2, 2, -1, width)
    up_grad = over_tokens(plane_set.reshape(8 * rows, -1)[:, :rank_dim], query_grad).reshape(2, 2, 2, -1, 2 * HEAD_DIM)
    grad_tokens, grad_q_down, grad_key, grad_value, grad_gains, grad_gate, grad_up, grad_q_up, grad_out = tail(
        back_parts, normed, compressed, tokens, grad_middle, first_weight, in_gain, query_gain, mid_gain_grad,
        cosine[:rows], sine[:rows], gu_total, gu_passed, gu_kept, up_grad, out_grad,
    )
    return (
        output,
        grad_tokens,
        grad_gains[0, :span],
        grad_q_down,
        grad_gains[0, 2 * span : 2 * span + q_span],
        grad_q_up,
        grad_key,
        grad_value,
        grad_out,
        grad_gains[0, span : 2 * span],
        grad_gate,
        grad_up,
        grad_down,
    )


def solution(mesh):
    return jax.shard_map(
        plane_local if dict(mesh.shape) == {"dp": 4, "seq": 8} else local,
        mesh=mesh,
        in_specs=(
            P(("dp", "seq"), None),
            P(("dp", "seq")),
            P(("dp", "seq"), None),
            P(("dp", "seq")),
            P(("dp", "seq"), None),
            P(("dp", "seq")),
            P(("dp", "seq"), None),
            P(("dp", "seq"), None),
            P(("dp", "seq"), None),
            P(("dp", "seq"), None),
            P(("dp", "seq")),
            P(("dp", "seq"), None),
            P(("dp", "seq"), None),
            P(("dp", "seq"), None),
        ),
        out_specs=(
            P(("dp", "seq"), None),
            P(("dp", "seq"), None),
            P(("dp", "seq")),
            P(("dp", "seq"), None),
            P(("dp", "seq")),
            P(("dp", "seq"), None),
            P(("dp", "seq"), None),
            P(("dp", "seq"), None),
            P(("dp", "seq"), None),
            P(("dp", "seq")),
            P(("dp", "seq"), None),
            P(("dp", "seq"), None),
            P(("dp", "seq"), None),
        ),
        check_vma=False,
    )
```

```python
import math

import jax
import jax.numpy as jnp
from jax import lax
from jax.experimental import pallas as pl
from jax.experimental.pallas import tpu as pltpu
from jax.sharding import PartitionSpec as P

HEADS = 16
HEAD_DIM = 256


epsilon = 1e-05
rope_base = 10000.0
masked_score = -1e30


def rms_scale(values):
    return lax.rsqrt(jnp.mean(values * values, axis=-1, keepdims=True) + epsilon)


def rotary(values, places, sign):
    half = values.shape[-1] // 2
    freqs = rope_base ** (-(2.0 * jnp.arange(half).astype(jnp.float32)) / values.shape[-1])
    angles = places.astype(jnp.float32)[:, None] * freqs[None, :]
    cosine = jnp.cos(angles)[:, None, :]
    sine = jnp.sin(angles)[:, None, :]
    first = values[..., :half]
    second = values[..., half:]
    return jnp.concatenate(
        [first * cosine - sign * second * sine, sign * first * sine + second * cosine], axis=-1
    )


def norm_backward(inputs, scale, gain, grad_out):
    weighted = gain * grad_out
    grad_in = scale * weighted - inputs * scale * scale * scale * jnp.mean(
        weighted * inputs, axis=-1, keepdims=True
    )
    grad_gain = jnp.sum(grad_out * inputs * scale, axis=0)
    return (grad_in, grad_gain)


def add_rows(total, block, start):
    current = lax.dynamic_slice_in_dim(total, start, block.shape[0], 0)
    return lax.dynamic_update_slice_in_dim(total, current + block, start, 0)


def local(
    tokens,
    positions,
    cotangent,
    norm_in_gain,
    q_down,
    q_gain,
    q_up,
    key_proj,
    value_proj,
    out_proj,
    norm_mid_gain,
    w_gate,
    w_up,
    w_down,
):
    width = tokens.shape[0]
    scale = 1.0 / math.sqrt(HEAD_DIM)
    attention_set = (
        lax.all_gather(norm_in_gain.astype(jnp.bfloat16), ("dp", "seq"), axis=0, tiled=True),
        lax.all_gather(q_down.astype(jnp.bfloat16), ("dp", "seq"), axis=0, tiled=True),
        lax.all_gather(q_gain.astype(jnp.bfloat16), ("dp", "seq"), axis=0, tiled=True),
        lax.all_gather(q_up.astype(jnp.bfloat16), ("dp", "seq"), axis=0, tiled=True),
        lax.all_gather(key_proj.astype(jnp.bfloat16), ("dp", "seq"), axis=0, tiled=True),
        lax.all_gather(value_proj.astype(jnp.bfloat16), ("dp", "seq"), axis=0, tiled=True),
        lax.all_gather(out_proj.astype(jnp.bfloat16), ("dp", "seq"), axis=0, tiled=True),
    )
    feed_set = (
        lax.all_gather(norm_mid_gain.astype(jnp.bfloat16), ("dp", "seq"), axis=0, tiled=True),
        lax.all_gather(w_gate.astype(jnp.bfloat16), ("dp", "seq"), axis=0, tiled=True),
        lax.all_gather(w_up.astype(jnp.bfloat16), ("dp", "seq"), axis=0, tiled=True),
        lax.all_gather(w_down.astype(jnp.bfloat16), ("dp", "seq"), axis=0, tiled=True),
    )
    in_gain = attention_set[0].astype(jnp.float32)
    query_gain = attention_set[2].astype(jnp.float32)
    inputs = tokens.astype(jnp.float32)
    in_scale = rms_scale(inputs)
    normed = (inputs * in_scale * in_gain).astype(jnp.bfloat16)
    compressed = jnp.dot(normed, attention_set[1], preferred_element_type=jnp.float32)
    query_scale = rms_scale(compressed)
    compressed_normed = (compressed * query_scale * query_gain).astype(jnp.bfloat16)
    queries_raw = jnp.dot(
        compressed_normed, attention_set[3], preferred_element_type=jnp.float32
    ).reshape(width, HEADS, HEAD_DIM)
    queries = rotary(queries_raw, positions, 1.0).astype(jnp.bfloat16)
    keys_raw = jnp.dot(normed, attention_set[4], preferred_element_type=jnp.float32)
    keys = rotary(keys_raw[:, None, :], positions, 1.0)[:, 0, :].astype(jnp.bfloat16)
    values = jnp.dot(normed, attention_set[5], preferred_element_type=jnp.float32).astype(
        jnp.bfloat16
    )
    query_index = lax.axis_index("seq") * width + jnp.arange(width, dtype=jnp.int32)
    first_index = query_index - positions

    def visibility(key_start):
        key_index = key_start + jnp.arange(width, dtype=jnp.int32)
        seen = (key_index[None, :] >= first_index[:, None]) & (
            key_index[None, :] <= query_index[:, None]
        )
        return seen[:, None, :]

    start_state = (
        jnp.full((width, HEADS), masked_score, jnp.float32),
        jnp.zeros((width, HEADS), jnp.float32),
        jnp.zeros((width, HEADS, HEAD_DIM), jnp.float32),
    )
    carry = start_state
    piece = (
        lax.all_gather(keys, "seq", axis=0, tiled=True),
        lax.all_gather(values, "seq", axis=0, tiled=True),
    )
    blocks = piece[0].shape[0] // width
    key_blocks = piece[0].reshape(blocks, width, HEAD_DIM)
    value_blocks = piece[1].reshape(blocks, width, HEAD_DIM)

    def forward_one_block(state, item):
        key_block, value_block, number = item
        key_start = number * width
        top, total, accum = state
        seen = visibility(key_start)
        scores = (
            jnp.einsum("thd,kd->thk", queries, key_block, preferred_element_type=jnp.float32)
            * scale
        )
        scores = jnp.where(seen, scores, masked_score)
        new_top = jnp.maximum(top, jnp.max(scores, axis=-1))
        weights = jnp.where(seen, jnp.exp(scores - new_top[..., None]), 0.0)
        decay = jnp.exp(top - new_top)
        total = total * decay + jnp.sum(weights, axis=-1)
        accum = accum * decay[..., None] + jnp.einsum(
            "thk,kd->thd",
            weights.astype(jnp.bfloat16),
            value_block,
            preferred_element_type=jnp.float32,
        )
        state = (new_top, total, accum)
        return (state, None)

    carry, _ = lax.scan(
        forward_one_block, carry, (key_blocks, value_blocks, jnp.arange(blocks, dtype=jnp.int32))
    )
    top, total, accum = carry
    attended_full = accum / total[..., None]
    log_total = top + jnp.log(total)
    attended = attended_full.reshape(width, HEADS * HEAD_DIM).astype(jnp.bfloat16)
    middle = inputs + jnp.dot(attended, attention_set[6], preferred_element_type=jnp.float32)
    mid_gain = feed_set[0].astype(jnp.float32)
    mid_scale = rms_scale(middle)
    normed_mid = (middle * mid_scale * mid_gain).astype(jnp.bfloat16)
    gate = jnp.dot(normed_mid, feed_set[1], preferred_element_type=jnp.float32)
    upper = jnp.dot(normed_mid, feed_set[2], preferred_element_type=jnp.float32)
    sigmoid_gate = jax.nn.sigmoid(gate)
    silu_gate = gate * sigmoid_gate
    hidden = (silu_gate * upper).astype(jnp.bfloat16)
    output = (middle + jnp.dot(hidden, feed_set[3], preferred_element_type=jnp.float32)).astype(
        jnp.bfloat16
    )
    feed_back = (
        lax.all_gather(norm_mid_gain.astype(jnp.bfloat16), ("dp", "seq"), axis=0, tiled=True),
        lax.all_gather(w_gate.astype(jnp.bfloat16), ("dp", "seq"), axis=0, tiled=True),
        lax.all_gather(w_up.astype(jnp.bfloat16), ("dp", "seq"), axis=0, tiled=True),
        lax.all_gather(w_down.astype(jnp.bfloat16), ("dp", "seq"), axis=0, tiled=True),
    )
    grad_out_full = cotangent.astype(jnp.float32)
    grad_down = jnp.einsum("tf,td->fd", hidden, cotangent, preferred_element_type=jnp.float32)
    grad_hidden = jnp.einsum(
        "td,fd->tf", cotangent, feed_back[3], preferred_element_type=jnp.float32
    )
    grad_gate = (grad_hidden * upper * sigmoid_gate * (1.0 + gate * (1.0 - sigmoid_gate))).astype(
        jnp.bfloat16
    )
    grad_upper = (grad_hidden * silu_gate).astype(jnp.bfloat16)
    grad_gate_weight = jnp.einsum(
        "td,tf->df", normed_mid, grad_gate, preferred_element_type=jnp.float32
    )
    grad_up_weight = jnp.einsum(
        "td,tf->df", normed_mid, grad_upper, preferred_element_type=jnp.float32
    )
    grad_normed_mid = jnp.einsum(
        "tf,df->td", grad_gate, feed_back[1], preferred_element_type=jnp.float32
    ) + jnp.einsum("tf,df->td", grad_upper, feed_back[2], preferred_element_type=jnp.float32)
    grad_mid_norm, grad_mid_gain = norm_backward(
        middle, mid_scale, feed_back[0].astype(jnp.float32), grad_normed_mid
    )
    grad_middle = grad_out_full + grad_mid_norm
    feed_grads = (
        lax.psum_scatter(grad_mid_gain, ("dp", "seq"), scatter_dimension=0, tiled=True),
        lax.psum_scatter(grad_gate_weight, ("dp", "seq"), scatter_dimension=0, tiled=True),
        lax.psum_scatter(grad_up_weight, ("dp", "seq"), scatter_dimension=0, tiled=True),
        lax.psum_scatter(grad_down, ("dp", "seq"), scatter_dimension=0, tiled=True),
    )
    attention_back = (
        lax.all_gather(norm_in_gain.astype(jnp.bfloat16), ("dp", "seq"), axis=0, tiled=True),
        lax.all_gather(q_down.astype(jnp.bfloat16), ("dp", "seq"), axis=0, tiled=True),
        lax.all_gather(q_gain.astype(jnp.bfloat16), ("dp", "seq"), axis=0, tiled=True),
        lax.all_gather(q_up.astype(jnp.bfloat16), ("dp", "seq"), axis=0, tiled=True),
        lax.all_gather(key_proj.astype(jnp.bfloat16), ("dp", "seq"), axis=0, tiled=True),
        lax.all_gather(value_proj.astype(jnp.bfloat16), ("dp", "seq"), axis=0, tiled=True),
        lax.all_gather(out_proj.astype(jnp.bfloat16), ("dp", "seq"), axis=0, tiled=True),
    )
    branch_grad = grad_middle.astype(jnp.bfloat16)
    grad_output_weight = jnp.einsum(
        "ta,td->ad", attended, branch_grad, preferred_element_type=jnp.float32
    )
    grad_attended = (
        jnp.einsum("td,ad->ta", branch_grad, attention_back[6], preferred_element_type=jnp.float32)
        .reshape(width, HEADS, HEAD_DIM)
        .astype(jnp.bfloat16)
    )
    delta = jnp.sum(grad_attended.astype(jnp.float32) * attended_full, axis=-1)
    group_rows = width * lax.axis_size("seq")
    back_state = (
        jnp.zeros((width, HEADS, HEAD_DIM), jnp.float32),
        jnp.zeros((group_rows, HEAD_DIM), jnp.float32),
        jnp.zeros((group_rows, HEAD_DIM), jnp.float32),
    )
    carry = back_state
    piece = (
        lax.all_gather(keys, "seq", axis=0, tiled=True),
        lax.all_gather(values, "seq", axis=0, tiled=True),
    )
    blocks = piece[0].shape[0] // width
    key_blocks = piece[0].reshape(blocks, width, HEAD_DIM)
    value_blocks = piece[1].reshape(blocks, width, HEAD_DIM)

    def backward_one_block(state, item):
        key_block, value_block, number = item
        key_start = number * width
        grad_query, grad_keys, grad_values = state
        seen = visibility(key_start)
        scores = (
            jnp.einsum("thd,kd->thk", queries, key_block, preferred_element_type=jnp.float32)
            * scale
        )
        probs = jnp.where(seen, jnp.exp(scores - log_total[..., None]), 0.0)
        grad_value_block = jnp.einsum(
            "thk,thd->kd",
            probs.astype(jnp.bfloat16),
            grad_attended,
            preferred_element_type=jnp.float32,
        )
        grad_probs = jnp.einsum(
            "thd,kd->thk", grad_attended, value_block, preferred_element_type=jnp.float32
        )
        grad_scores = (probs * (grad_probs - delta[..., None]) * scale).astype(jnp.bfloat16)
        grad_query = grad_query + jnp.einsum(
            "thk,kd->thd", grad_scores, key_block, preferred_element_type=jnp.float32
        )
        grad_key_block = jnp.einsum(
            "thk,thd->kd", grad_scores, queries, preferred_element_type=jnp.float32
        )
        state = (
            grad_query,
            add_rows(grad_keys, grad_key_block, key_start),
            add_rows(grad_values, grad_value_block, key_start),
        )
        return (state, None)

    carry, _ = lax.scan(
        backward_one_block, carry, (key_blocks, value_blocks, jnp.arange(blocks, dtype=jnp.int32))
    )
    grad_query, grad_keys, grad_values = carry
    local_key_grad, local_value_grad = (
        lax.psum_scatter(
            grad_keys.astype(jnp.bfloat16), "seq", scatter_dimension=0, tiled=True
        ).astype(jnp.float32),
        lax.psum_scatter(
            grad_values.astype(jnp.bfloat16), "seq", scatter_dimension=0, tiled=True
        ).astype(jnp.float32),
    )
    grad_key_pre = rotary(local_key_grad[:, None, :], positions, -1.0)[:, 0, :].astype(jnp.bfloat16)
    grad_value_pre = local_value_grad.astype(jnp.bfloat16)
    grad_query_pre = (
        rotary(grad_query, positions, -1.0).reshape(width, HEADS * HEAD_DIM).astype(jnp.bfloat16)
    )
    grad_up_query = jnp.einsum(
        "tr,ta->ra", compressed_normed, grad_query_pre, preferred_element_type=jnp.float32
    )
    grad_compressed_normed = jnp.einsum(
        "ta,ra->tr", grad_query_pre, attention_back[3], preferred_element_type=jnp.float32
    )
    grad_compressed, grad_query_gain = norm_backward(
        compressed, query_scale, attention_back[2].astype(jnp.float32), grad_compressed_normed
    )
    grad_compressed = grad_compressed.astype(jnp.bfloat16)
    grad_down_weight = jnp.einsum(
        "td,tr->dr", normed, grad_compressed, preferred_element_type=jnp.float32
    )
    grad_key_weight = jnp.einsum(
        "td,te->de", normed, grad_key_pre, preferred_element_type=jnp.float32
    )
    grad_value_weight = jnp.einsum(
        "td,te->de", normed, grad_value_pre, preferred_element_type=jnp.float32
    )
    grad_normed = jnp.einsum(
        "tr,dr->td", grad_compressed, attention_back[1], preferred_element_type=jnp.float32
    )
    grad_normed = grad_normed + jnp.einsum(
        "te,de->td", grad_key_pre, attention_back[4], preferred_element_type=jnp.float32
    )
    grad_normed = grad_normed + jnp.einsum(
        "te,de->td", grad_value_pre, attention_back[5], preferred_element_type=jnp.float32
    )
    grad_in_norm, grad_in_gain = norm_backward(
        inputs, in_scale, attention_back[0].astype(jnp.float32), grad_normed
    )
    grad_tokens = (grad_middle + grad_in_norm).astype(jnp.bfloat16)
    attention_grads = (
        lax.psum_scatter(grad_in_gain, ("dp", "seq"), scatter_dimension=0, tiled=True),
        lax.psum_scatter(grad_down_weight, ("dp", "seq"), scatter_dimension=0, tiled=True),
        lax.psum_scatter(grad_query_gain, ("dp", "seq"), scatter_dimension=0, tiled=True),
        lax.psum_scatter(grad_up_query, ("dp", "seq"), scatter_dimension=0, tiled=True),
        lax.psum_scatter(grad_key_weight, ("dp", "seq"), scatter_dimension=0, tiled=True),
        lax.psum_scatter(grad_value_weight, ("dp", "seq"), scatter_dimension=0, tiled=True),
        lax.psum_scatter(grad_output_weight, ("dp", "seq"), scatter_dimension=0, tiled=True),
    )
    return (
        output,
        grad_tokens,
        attention_grads[0],
        attention_grads[1],
        attention_grads[2],
        attention_grads[3],
        attention_grads[4],
        attention_grads[5],
        attention_grads[6],
        feed_grads[0],
        feed_grads[1],
        feed_grads[2],
        feed_grads[3],
    )


bf16 = jnp.bfloat16
f32 = jnp.float32
ANY = pl.BlockSpec(memory_space=pl.ANY)
VMEM = pl.BlockSpec(memory_space=pltpu.VMEM)
PLANE = [j // 4 * 8 + j % 4 for j in range(1, 8)]
LINKS = [16, 8, 4, 2, 1]


def flip(number, bits):
    bit = 1
    while bit <= bits:
        if bits & bit:
            number = number + bit - 2 * bit * ((number // bit) % 2)
        bit *= 2
    return number


def coordinates():
    dp = lax.axis_index("dp")
    seq = lax.axis_index("seq")
    return dp // 2, dp % 2, seq // 4, (seq // 2) % 2, seq % 2


def partner(mask):
    return flip(lax.axis_index("dp"), mask // 8), flip(lax.axis_index("seq"), mask % 8)


def greet(masks):
    barrier = pltpu.get_barrier_semaphore()
    for mask in masks:
        pl.semaphore_signal(barrier, inc=1, device_id=partner(mask), device_id_type=pl.DeviceIdType.MESH)
    pl.semaphore_wait(barrier, len(masks))


class Wire:
    def __init__(self, send_sem, recv_sem, local_sem):
        self.send_sem, self.recv_sem, self.local_sem = send_sem, recv_sem, local_sem
        self.copies = []
        self.gone = []
        self.locals = 0

    def send(self, src, dst, mask):
        copy = self.later(src, dst, mask)
        copy.start()
        return copy

    def later(self, src, dst, mask):
        k = len(self.copies)
        copy = pltpu.make_async_remote_copy(
            src_ref=src,
            dst_ref=dst,
            send_sem=self.send_sem.at[k],
            recv_sem=self.recv_sem.at[k],
            device_id=partner(mask),
            device_id_type=pl.DeviceIdType.MESH,
        )
        self.copies.append(copy)
        return copy

    def local(self, src, dst):
        copy = self.later_local(src, dst)
        copy.start()
        return copy

    def later_local(self, src, dst):
        copy = pltpu.make_async_copy(src, dst, self.local_sem.at[self.locals])
        self.locals += 1
        return copy

    def left(self, copies):
        for copy in copies:
            copy.wait_send()
        self.gone += copies

    def close(self):
        for copy in self.copies:
            if not any(copy is other for other in self.gone):
                copy.wait_send()


def wires(remote, local):
    return [pltpu.SemaphoreType.DMA((remote,)), pltpu.SemaphoreType.DMA((remote,)), pltpu.SemaphoreType.DMA((local,))]


def arrived(copies):
    for copy in copies:
        copy.wait_recv()


def landed(copies):
    for copy in copies:
        copy.wait()


def moving(kernel, number, outs, operands, scratch, in_specs=None, out_specs=None, limit=56):
    return pl.pallas_call(
        kernel,
        out_shape=outs,
        in_specs=in_specs or [ANY] * len(operands),
        out_specs=out_specs or [ANY] * len(outs),
        scratch_shapes=scratch,
        compiler_params=pltpu.CompilerParams(
            collective_id=number, has_side_effects=True, vmem_limit_bytes=limit * 1024 * 1024
        ),
        cost_estimate=pl.CostEstimate(flops=0, bytes_accessed=100_000_000, transcendentals=0),
        name=kernel.__name__,
    )(*operands)


def shaped(shape, dtype=bf16):
    return jax.ShapeDtypeStruct(tuple(shape), dtype)


def each_rows(rows, body, step=16):
    @pl.loop(0, rows // step)
    def _(i):
        body(pl.ds(pl.multiple_of(i * step, step), step))


def wide(ref, where):
    return ref[where].astype(f32)


def routes(rows, pieces, direct):
    size = rows // pieces
    return [(pl.ds(i * size, size), "xl" if i < direct else "lx") for i in range(pieces)]


def plane_gather(wire, block, out, own, ways):
    links = {"x": (out.at[1, 0, 0], out.at[1, 0, 1], 8), "l": (out.at[0, 1, 0], out.at[0, 1, 1], 2)}
    far, far_core = out.at[1, 1, 0], out.at[1, 1, 1]
    ordered = [k for k in range(len(ways)) if ways[k][1] == "xl"] + [k for k in range(len(ways)) if ways[k][1] == "lx"]
    came = {}
    for turn in (0, 1):
        for k in ordered:
            rows, way = ways[k]
            target, _, mask = links[way[turn]]
            came[way[turn], k] = wire.send(block.at[rows], target.at[rows], mask)
    cores = [wire.send(block, out.at[0, 0, 1], 1)]
    mine = wire.local(block, own) if own is not None else None
    diagonal = {}

    def step(k):
        rows, way = ways[k]
        target, core, _ = links[way[0]]
        came[way[0], k].wait_recv()
        diagonal[k] = wire.send(target.at[rows], far.at[rows], links[way[1]][2])
        cores.append(wire.send(target.at[rows], core.at[rows], 1))

    def finish():
        for k in ordered:
            rows, way = ways[k]
            target, core, _ = links[way[1]]
            came[way[1], k].wait_recv()
            cores.append(wire.send(target.at[rows], core.at[rows], 1))
        for k in ordered:
            rows, way = ways[k]
            diagonal[k].wait_recv()
            cores.append(wire.send(far.at[rows], far_core.at[rows], 1))
        if mine is not None:
            mine.wait()
        arrived(cores)

    return [lambda k=k: step(k) for k in ordered], finish


ARRIVAL = [(1, 1), (1, 0), (0, 1), (0, 0)]


def plane_reduce(wire, parts, out, kept, from_c, send_one, recv_one, send_two, recv_two, ways, load=True):
    cores = {}
    loads = {}
    masks = {"x": 8, "l": 2}
    beside = {"xl": (1, 0), "lx": (0, 1)}
    after = {"xl": (0, 1), "lx": (1, 0)}
    came = {}
    passed = {}

    def give(k):
        cores[k] = wire.send(parts.at[k[0], k[1], 1], from_c.at[k[0], k[1]], 1)
        if load:
            loads[k] = wire.local(parts.at[k[0], k[1], 0], kept.at[k[0], k[1]])

    def pair(k, r):
        return wide(kept.at[k[0], k[1]], r) + wide(from_c.at[k[0], k[1]], r)

    def within(rows, body):
        @pl.loop(0, rows.size // 16)
        def _(i):
            body(pl.ds(pl.multiple_of(rows.start + i * 16, 16), 16))

    def put(slot, k, j):
        rows, way = ways[j]

        def fill(r):
            send_one[slot, r] = pair(k, r).astype(bf16)

        within(rows, fill)
        came[slot, j] = wire.send(send_one.at[slot, rows], recv_one.at[slot, rows], masks[way[0]])

    def arrive(k):
        if load:
            loads[k].wait()
        cores[k].wait_recv()
        for j in range(len(ways)):
            if k == (1, 1):
                put(0, k, j)
            elif beside[ways[j][1]] == k:
                put(1, k, j)

    def step(j):
        rows, way = ways[j]
        came[0, j].wait_recv()

        def fill(r):
            send_two[r] = (pair(after[way], r) + wide(recv_one.at[0], r)).astype(bf16)

        within(rows, fill)
        passed[j] = wire.send(send_two.at[rows], recv_two.at[rows], masks[way[1]])

    def finish():
        for j, (rows, way) in enumerate(ways):
            came[1, j].wait_recv()
            passed[j].wait_recv()

            def fill(r):
                out[r] = pair((0, 0), r) + wide(recv_one.at[1], r) + wide(recv_two, r)

            within(rows, fill)

    return give, arrive, [lambda j=j: step(j) for j in range(len(ways))], finish


def each(action, items=ARRIVAL):
    for item in items:
        action(item)


def do(steps):
    for step in steps:
        step()


def reduce_scratch(rows, width):
    return [
        pltpu.VMEM((2, 2, rows, width), bf16),
        pltpu.VMEM((2, 2, rows, width), bf16),
        pltpu.VMEM((2, rows, width), bf16),
        pltpu.VMEM((2, rows, width), bf16),
        pltpu.VMEM((rows, width), bf16),
        pltpu.VMEM((rows, width), bf16),
    ]


def over_y(wire, block, place, side):
    y, x, h, l, c = coordinates()
    hh = h if side == 0 else 1 - h
    mine = wire.local(block, place(y, hh))
    sent = wire.send(block, place(y, hh), 16)

    def finish():
        mine.wait()
        sent.wait_recv()

    return finish


def thirds(width):
    main = (width * 5 // 12) // 128 * 128
    return [pl.ds(0, main), pl.ds(main, main), pl.ds(2 * main, width - 2 * main)]


def head_kernel(
    q_down, key, value, gains, q_up, gate, up, out_proj, w_down, places,
    first_out, upq_out, gu, wo_out, wo_far, wd_out, in_gain, mid_gain, q_gain, first_index, query_index, key_index,
    cosine, sine, first, upq, staged, gains_out, places_out, send_sem, recv_sem, local_sem,
):
    y, x, h, l, c = coordinates()
    rank = x * 4 + l * 2 + c
    wire = Wire(send_sem, recv_sem, local_sem)
    greet([16, 4] + PLANE)
    r1, r2 = q_down.shape[1], q_down.shape[1] + key.shape[1]
    first[:, :r1] = q_down[...].astype(bf16)
    first[:, r1:r2] = key[...].astype(bf16)
    first[:, r2:] = value[...].astype(bf16)
    width = first.shape[1]
    a, b, d = thirds(width)
    mine = [wire.local(first, first_out.at[y, x, h, l, c]), wire.local(gains, gains_out.at[y, x, h, l, c])]
    one = [wire.send(first.at[:, p], first_out.at[y, x, h, l, c, :, p], 4) for p in (a, b, d)]
    gain = wire.send(gains, gains_out.at[y, x, h, l, c], 4)
    place = [wire.send(places, places_out.at[j], PLANE[j - 1]) for j in range(1, 8)]
    place_mine = wire.local(places, places_out.at[0])
    heads = q_up.shape[1] // HEAD_DIM
    for head in range(heads):
        hy, hx, hh, hl = head // 8, head // 4 % 2, head // 2 % 2, head % 2
        target = hx * 4 + hl * 2 + hh
        upq[target, :, hy * HEAD_DIM : (hy + 1) * HEAD_DIM] = q_up[:, head * HEAD_DIM : (head + 1) * HEAD_DIM].astype(bf16)
    up_rows = upq.shape[1]
    up_place = lambda: upq_out.at[y, x, h, pl.ds((l * 2 + c) * up_rows, up_rows), :]
    up_mine = wire.local(upq.at[rank], up_place())
    up_sent = [wire.send(upq.at[flip(rank, j)], up_place(), PLANE[j - 1]) for j in range(1, 8)]
    wo_out[...] = out_proj[...].astype(bf16)
    piece = gate.shape[1] // 32
    size = 4 * piece
    main = size // 128 * 128
    for target in range(8):
        for where, weight in ((0, gate), (1, up)):
            for q in range(4):
                n = q // 2 * 16 + target // 4 * 8 + q % 2 * 4 + target % 4
                staged[where, :, q * piece : (q + 1) * piece] = weight[:, n * piece : (n + 1) * piece]
        gu[target, :, :main] = staged[0, :, :main].astype(bf16)
        rest = size - main
        both = jnp.concatenate([staged[0, :, main : main + rest], staged[1, :, main : main + rest]], axis=1)
        gu[target, :, main : main + 2 * rest] = both.astype(bf16)
        gu[target, :, main + 2 * rest :] = staged[1, :, :main].astype(bf16)
    wd_out[...] = w_down[...].astype(bf16)
    landed(mine)

    every = slice(None)

    def step(held, columns, mask):
        at = tuple(every if k in held else v for k, v in zip("yxhlc", (y, x, h, l, c)))
        if columns is None:
            return wire.send(gains_out.at[at], gains_out.at[at], mask)
        place = first_out.at[at + (every, columns)]
        return wire.send(place, place, mask)

    def last(held, bit, columns):
        at = {k: every if k in held else v for k, v in zip("yxhlc", (y, x, h, l, c))}
        at[bit] = 1 - dict(zip("yxhlc", (y, x, h, l, c)))[bit]
        place = first_out.at[tuple(at[k] for k in "yxhlc") + (every, columns)]
        return wire.send(place, place, 1)

    bits = {"y": 16, "x": 8, "h": 4, "l": 2}
    orders = [("hlxy", a), ("hlyx", b), ("hxyl", d)]
    sent = one
    for k in range(1, 4):
        following = []
        for (order, columns), copy in zip(orders, sent):
            copy.wait_recv()
            following.append(step(order[:k], columns, bits[order[k]]))
        sent = following
        gain.wait_recv()
        gain = step("hlxy"[:k], None, bits["hlxy"[k]])
        if k == 1:
            up_mine.wait()
            arrived(up_sent)
            up_h = wire.send(upq_out.at[y, :, h], upq_out.at[y, :, h], 4)
            up_y = [wire.send(upq_out.at[y, :, h], upq_out.at[y, :, h], 16)]
            wo_sent = wire.send(wo_out, wo_far, 4)
        if k == 3:
            five = [step(order[:3], columns, 1) for order, columns in orders]
    up_h.wait_recv()
    up_y += [wire.send(upq_out.at[y, :, 1 - h], upq_out.at[y, :, 1 - h], 16)]
    gain.wait_recv()
    gain = step("hlxy", None, 1)
    for (order, columns), copy in zip(orders, sent):
        copy.wait_recv()
        five.append(last(order[:3], order[3], columns))
    place_mine.wait()
    arrived(place)
    rows = places.shape[1]
    half = HEAD_DIM // 2
    powers = lax.broadcasted_iota(jnp.int32, (rows, half), 1).astype(f32)
    freqs = jnp.exp(powers * (-2.0 / HEAD_DIM * math.log(rope_base)))
    eye = lax.broadcasted_iota(jnp.int32, (rows, rows), 0) == lax.broadcasted_iota(jnp.int32, (rows, rows), 1)
    index = []
    for j in range(8):
        place = jnp.sum(jnp.where(eye, places_out[j].astype(f32), 0.0), axis=1, keepdims=True)
        angles = place * freqs
        cosine[j * rows : (j + 1) * rows] = jnp.cos(angles)
        sine[j * rows : (j + 1) * rows] = jnp.sin(angles)
        b, d = j // 2 % 2, j % 2
        block = (l + b - 2 * l * b) * 2 + (c + d - 2 * c * d)
        start = (h * 4 + block) * rows
        index.append(start + lax.broadcasted_iota(jnp.int32, (1, rows), 1))
        side = h if j < 4 else 1 - h
        key_index[j * rows : (j + 1) * rows] = (side * 4 + block) * rows + lax.broadcasted_iota(jnp.int32, (rows, 1), 0)
    index = jnp.concatenate(index, axis=1)
    query_index[...] = index
    first_index[...] = index - jnp.concatenate([places_out[j] for j in range(8)], axis=1)
    gain.wait_recv()
    span, q_span = in_gain.shape[1] // 32, q_gain.shape[1] // 32
    for n in range(32):
        row = gains_out[n // 16, n // 8 % 2, n // 4 % 2, n // 2 % 2, n % 2]
        in_gain[:, n * span : (n + 1) * span] = row[:, :span]
        mid_gain[:, n * span : (n + 1) * span] = row[:, span : 2 * span]
        q_gain[:, n * q_span : (n + 1) * q_span] = row[:, 2 * span : 2 * span + q_span]
    arrived(five + up_y + [wo_sent])
    wire.close()


def head(q_down, key, value, gains, q_up, gate, up, out_proj, w_down, places):
    rows = q_down.shape[0]
    count = 8 * places.shape[1]
    width = q_down.shape[1] + 2 * key.shape[1]
    columns = gate.shape[1] // 4
    slice_size = gate.shape[1] // 8
    outs = [
        shaped((2, 2, 2, 2, 2, rows, width)),
        shaped((2, 2, 2, 4 * q_up.shape[0], 2 * HEAD_DIM)),
        shaped((8, rows, columns)),
        shaped(out_proj.shape),
        shaped(out_proj.shape),
        shaped(w_down.shape),
        shaped((1, 32 * rows), f32),
        shaped((1, 32 * rows), f32),
        shaped((1, q_down.shape[1]), f32),
        shaped((1, count), jnp.int32),
        shaped((1, count), jnp.int32),
        shaped((count, 1), jnp.int32),
        shaped((count, HEAD_DIM // 2), f32),
        shaped((count, HEAD_DIM // 2), f32),
    ]
    scratch = [
        pltpu.VMEM((rows, width), bf16),
        pltpu.VMEM((8, q_up.shape[0], 2 * HEAD_DIM), bf16),
        pltpu.VMEM((2, rows, slice_size), f32),
        pltpu.VMEM((2, 2, 2, 2, 2) + gains.shape, f32),
        pltpu.VMEM((8,) + places.shape, jnp.int32),
    ]
    operands = (q_down, key, value, gains, q_up, gate, up, out_proj, w_down, places)
    return moving(
        head_kernel, 1, outs, operands, scratch + wires(100, 8),
        in_specs=[VMEM] * len(operands),
        out_specs=[ANY, ANY, VMEM, VMEM, ANY] + [VMEM] * 9,
    )


def turned(values, cosine, sine, sign):
    half = HEAD_DIM // 2
    out = []
    for start in range(0, values.shape[1], HEAD_DIM):
        one, two = values[:, start : start + half], values[:, start + half : start + HEAD_DIM]
        out += [one * cosine - sign * two * sine, sign * one * sine + two * cosine]
    return jnp.concatenate(out, axis=1)


def row_scale(values):
    return lax.rsqrt(jnp.mean(values * values, axis=-1, keepdims=True) + epsilon)


def pack_kernel(
    tokens, gain_in, gain_q, first_weight, cosine, sine, wo_own, wo_far, gu, wd_own,
    out, weight_out, gu_out, wd_far, normed, compressed,
    weight, block, weight_all, send_sem, recv_sem, local_sem,
):
    y, x, h, l, c = coordinates()
    wire = Wire(send_sem, recv_sem, local_sem)
    load = wire.local(first_weight, weight)
    greet([16, 4] + PLANE)
    rank = x * 4 + l * 2 + c
    gu_rows = gu.shape[1]
    gu_place = gu_out.at[x, pl.ds((l * 2 + c) * gu_rows, gu_rows), :]
    gu_mine = wire.local(gu.at[rank], gu_place)
    gu_sent = [wire.send(gu.at[flip(rank, j)], gu_place, PLANE[j - 1]) for j in range(1, 8)]
    weight_done = [over_y(wire, ref, lambda yy, hh: weight_all.at[yy, hh], k) for k, ref in enumerate((wo_own, wo_far))]
    rows = tokens.shape[0]
    inputs = tokens[...].astype(f32)
    normed[...] = (inputs * row_scale(inputs) * gain_in[...]).astype(bf16)
    load.wait()
    mixed = jnp.dot(normed[...], weight[...], preferred_element_type=f32)
    rank_dim = compressed.shape[1]
    query = mixed[:, :rank_dim]
    compressed[...] = query
    block[:, :rank_dim] = (query * row_scale(query) * gain_q[...]).astype(bf16)
    block[:, rank_dim : rank_dim + HEAD_DIM] = turned(
        mixed[:, rank_dim : rank_dim + HEAD_DIM], cosine[:rows], sine[:rows], 1.0
    ).astype(bf16)
    block[:, rank_dim + HEAD_DIM :] = mixed[:, rank_dim + HEAD_DIM :].astype(bf16)
    near = block.shape[1]
    far = 2 * HEAD_DIM
    columns, far_columns = pl.ds(0, near), pl.ds(near, far)
    from_h = wire.send(block.at[:, pl.ds(near - far, far)], out.at[0, 0, 0, :, far_columns], 4)
    near_out = out.at[:, :, :, :, columns]
    size = block.shape[0]
    steps, finish = plane_gather(wire, block, near_out, near_out.at[0, 0, 0], routes(size, 4, 1))
    from_h.wait_recv()
    wd_sent = wire.send(wd_own, wd_far, 4)
    far_out = out.at[:, :, :, :, far_columns]
    far_steps, far_finish = plane_gather(wire, far_out.at[0, 0, 0], far_out, None, routes(size, 2, 1))
    do(steps)
    do(far_steps)
    do(weight_done)
    swapped = wire.send(weight_all.at[:, 1 - c], weight_out.at[:, c], 1)
    kept = wire.local(weight_all.at[:, c], weight_out.at[:, c])
    finish()
    far_finish()
    kept.wait()
    gu_mine.wait()
    arrived([swapped, wd_sent] + gu_sent)
    wire.close()


def pack(tokens, gain_in, gain_q, first_weight, cosine, sine, wo_own, wo_far, gu, wd_own):
    rows, width = tokens.shape
    near = first_weight.shape[1]
    rank_dim = near - 2 * HEAD_DIM
    outs = [
        shaped((2, 2, 2, rows, near + 2 * HEAD_DIM)),
        shaped((2, 2) + wo_own.shape),
        shaped((2, 4 * gu.shape[1], gu.shape[2])),
        shaped(wd_own.shape),
        shaped((rows, width)),
        shaped((rows, rank_dim), f32),
    ]
    operands = (tokens, gain_in, gain_q, first_weight, cosine, sine, wo_own, wo_far, gu, wd_own)
    return moving(
        pack_kernel, 2, outs, operands,
        [pltpu.VMEM(first_weight.shape, bf16), pltpu.VMEM((rows, near), bf16), pltpu.VMEM((2, 2) + wo_own.shape, bf16)]
        + wires(60, 12),
        in_specs=[VMEM, VMEM, VMEM, ANY, VMEM, VMEM, VMEM, VMEM, VMEM, VMEM],
        out_specs=[ANY, VMEM, ANY, ANY, VMEM, VMEM],
    )


def mask_of(index, first, last):
    return jnp.where((index >= first) & (index <= last), 0.0, masked_score)


def scores_of(keys, queries):
    return lax.dot_general(keys, queries, (((1,), (1,)), ((), ())), preferred_element_type=f32)


def attend_kernel(
    plane_set, wq, wo, cosine, sine, key_index, query_index, first_index, tokens, gain, cotangent, gu_set, wd_own, wd_far,
    queries_out, attended, lse, middle, plane_mid, cotangents, gu_zero, gu_one, wd_out,
    kv, normed, staged, mask, from_c, s1, r1, s2, r2, mid, gu_far, gu_next, load_sem, send_sem, recv_sem, local_sem,
):
    wire = Wire(send_sem, recv_sem, local_sem)
    rank_dim = wq.shape[0]
    loads = [
        pltpu.make_async_copy(plane_set.at[:, :, :, :, pl.ds(rank_dim, 4 * HEAD_DIM)], kv, load_sem.at[0]),
        pltpu.make_async_copy(plane_set.at[:, :, :, :, pl.ds(0, rank_dim)], normed, load_sem.at[1]),
    ]
    for load in loads:
        load.start()
    greet(LINKS)
    places = [lambda yy, hh: gu_zero.at[yy, hh], lambda yy, hh: gu_one.at[yy, hh]]
    passing, gathered = plane_gather(
        wire, cotangent, cotangents, cotangents.at[0, 0, 0], routes(cotangent.shape[0], 4, 1)
    )
    far_sent = wire.send(gu_set.at[0], gu_far, 4)
    gu_done = [over_y(wire, ref, lambda yy, hh: wd_out.at[yy, hh], k) for k, ref in enumerate((wd_own, wd_far))]
    landed(loads)
    rows = kv.shape[3]
    block = 2 * rows

    def one(g, i):
        start = (g * 2 + i) * block
        place = pl.ds(start, block)
        raw = jnp.dot(normed[g, i].reshape(block, rank_dim), wq[...], preferred_element_type=f32)
        queries = (turned(raw, cosine[place], sine[place], 1.0) * (1.0 / math.sqrt(HEAD_DIM))).astype(bf16)
        queries_out[place] = queries
        mask[...] = mask_of(key_index[...], first_index[:, place], query_index[:, place])
        keys = jnp.concatenate(
            [kv[g, :, :, :, :HEAD_DIM].reshape(2 * block, HEAD_DIM), kv[g, :, :, :, 2 * HEAD_DIM : 3 * HEAD_DIM].reshape(2 * block, HEAD_DIM)]
        )
        values = jnp.concatenate(
            [kv[g, :, :, :, HEAD_DIM : 2 * HEAD_DIM].reshape(2 * block, HEAD_DIM), kv[g, :, :, :, 3 * HEAD_DIM :].reshape(2 * block, HEAD_DIM)]
        )
        merged = []
        for a in range(2):
            scores = scores_of(keys, queries[:, a * HEAD_DIM : (a + 1) * HEAD_DIM]) + mask[...]
            top = jnp.max(scores, axis=0, keepdims=True)
            weights = jnp.exp(scores - top)
            total = jnp.sum(weights, axis=0, keepdims=True)
            lse[a, :, place] = top + jnp.log(total)
            probs = (weights * (1.0 / total)).astype(bf16)
            merged.append(lax.dot_general(probs, values, (((0,), (0,)), ((), ())), preferred_element_type=f32).astype(bf16))
        merged = jnp.concatenate(merged, axis=1)
        attended[place] = merged
        staged[g, i] = jnp.dot(merged, wo[...], preferred_element_type=f32).astype(bf16).reshape(2, rows, -1)

    give, arrive, steps, finish = plane_reduce(
        wire, staged, middle, staged.at[:, :, 0], from_c, s1, r1, s2, r2, routes(rows, 4, 3), load=False
    )
    for number, k in enumerate(ARRIVAL):
        one(*k)
        give(k)
        if number == 0:
            arrive(k)
        elif number > 1:
            arrive(ARRIVAL[number - 1])
        if number == 1:
            do(passing[:2])
        if number == 2:
            do(passing[2:])
    arrive((0, 0))
    gu_done += [over_y(wire, gu_set.at[k], places[k], 0) for k in range(2)]
    do(steps)
    far_sent.wait_recv()
    next_sent = wire.send(gu_set.at[1], gu_next, 4)
    gu_done.append(over_y(wire, gu_far, places[0], 1))
    gathered()
    finish()

    def norm(r):
        value = tokens[r].astype(f32) + middle[r]
        middle[r] = value
        mid[r] = (value * row_scale(value) * gain[...]).astype(bf16)

    each_rows(rows, norm)
    steps, finish = plane_gather(wire, mid, plane_mid, plane_mid.at[0, 0, 0], routes(rows, 4, 2))
    do(steps)
    next_sent.wait_recv()
    gu_done.append(over_y(wire, gu_next, places[1], 1))
    finish()
    do(gu_done)
    wire.close()


def attend(plane_set, wq, wo, cosine, sine, key_index, query_index, first_index, tokens, gain, cotangent, gu_set, wd_own, wd_far):
    rows, width = tokens.shape
    count = 8 * rows
    rank_dim = wq.shape[0]
    gu = gu_set.shape[1:]
    outs = [
        shaped((count, 2 * HEAD_DIM)),
        shaped((count, 2 * HEAD_DIM)),
        shaped((2, 1, count), f32),
        shaped((rows, width), f32),
        shaped((2, 2, 2, rows, width)),
        shaped((2, 2, 2, rows, width)),
        shaped((2, 2) + gu),
        shaped((2, 2) + gu),
        shaped((2, 2) + wd_own.shape),
    ]
    scratch = [
        pltpu.VMEM((2, 2, 2, rows, 4 * HEAD_DIM), bf16),
        pltpu.VMEM((2, 2, 2, rows, rank_dim), bf16),
        pltpu.VMEM((2, 2, 2, rows, width), bf16),
        pltpu.VMEM((count, 2 * rows), f32),
    ]
    scratch += reduce_scratch(rows, width)[1:]
    scratch += [pltpu.VMEM((rows, width), bf16), pltpu.VMEM(gu, bf16), pltpu.VMEM(gu, bf16), pltpu.SemaphoreType.DMA((2,))]
    operands = (
        plane_set, wq, wo, cosine, sine, key_index, query_index, first_index, tokens, gain, cotangent, gu_set, wd_own, wd_far,
    )
    return moving(
        attend_kernel, 3, outs, operands, scratch + wires(80, 16),
        in_specs=[ANY] + [VMEM] * 13,
        out_specs=[VMEM, VMEM, VMEM, VMEM, ANY, ANY, ANY, ANY, ANY],
        limit=62,
    )


def feed_kernel(
    mid, cotangents, gu_zero, gu_one, down,
    hidden, grads, final_parts, normed_grad,
    gu, wd, mid_v, cot_v, hid_v, grads_v, final_v, staged, from_c, s1, r1, s2, r2,
    weight_sem, load_sem, store_sem, send_sem, recv_sem, local_sem,
):
    wire = Wire(send_sem, recv_sem, local_sem)
    main = gu.shape[4] // 2 // 128 * 128
    size = down.shape[2]
    units = 4 * size
    rows = staged.shape[3]
    block = 2 * rows
    copies = [
        pltpu.make_async_copy(gu_zero, gu.at[:, 0], weight_sem.at[0]),
        pltpu.make_async_copy(gu_one, gu.at[:, 1], weight_sem.at[1]),
    ]
    for k in range(4):
        copies.append(pltpu.make_async_copy(down.at[k // 2, k % 2], wd.at[pl.ds(k * size, size)], weight_sem.at[2 + k]))
    for copy in copies:
        copy.start()

    def load(n):
        k = ARRIVAL[n]
        pairs = [(mid.at[k[0], k[1]], mid_v.at[n % 2]), (cotangents.at[k[0], k[1]], cot_v.at[n % 2])]
        moves = [pltpu.make_async_copy(src, dst, load_sem.at[2 * (n % 2) + q]) for q, (src, dst) in enumerate(pairs)]
        for move in moves:
            move.start()
        return moves

    def store(n):
        k = ARRIVAL[n]
        place = pl.ds((k[0] * 2 + k[1]) * block, block)
        pairs = [(hid_v, hidden.at[place]), (grads_v, grads.at[place]), (final_v, final_parts.at[place])]
        moves = [
            pltpu.make_async_copy(src.at[n % 2], dst, store_sem.at[3 * (n % 2) + q]) for q, (src, dst) in enumerate(pairs)
        ]
        for move in moves:
            move.start()
        return moves

    moves = [load(0)]
    greet(LINKS)
    wd[units:] = jnp.zeros((wd.shape[0] - units, wd.shape[1]), bf16)
    landed(copies)
    give, arrive, steps, finish = plane_reduce(
        wire, staged, normed_grad, staged.at[:, :, 0], from_c, s1, r1, s2, r2, routes(rows, 4, 2), load=False
    )
    weight = lambda: gu[...].reshape(-1, gu.shape[4])
    stores = []
    for n, k in enumerate(ARRIVAL):
        landed(moves[n])
        if n < 3:
            moves.append(load(n + 1))
        if n > 1:
            landed(stores[n - 2])
        slot = n % 2
        both = jnp.dot(mid_v[slot].reshape(block, -1), weight(), preferred_element_type=f32)
        if n > 0:
            arrive(ARRIVAL[n - 1])
        if n > 2:
            do(steps)
        gate = both[:, : main + 128]
        upper = jnp.concatenate([both[:, main + 128 :], pltpu.roll(both[:, main : main + 128], 64, 1)], axis=1)
        cotangent = cot_v[slot].reshape(block, -1)
        grad = lax.dot_general(cotangent, wd[...], (((1,), (1,)), ((), ())), preferred_element_type=f32)
        sigmoid = 1.0 / (1.0 + jnp.exp(-gate))
        silu = gate * sigmoid
        hid = (silu * upper).astype(bf16)
        hid_v[slot] = hid[:, :units]
        grad_gate = grad * upper * sigmoid * (1.0 + gate * (1.0 - sigmoid))
        grad_upper = grad * silu
        joint = grad_gate[:, main:] + pltpu.roll(grad_upper[:, main:], 64, 1)
        out = jnp.concatenate([grad_gate[:, :main], joint, grad_upper[:, :main]], axis=1).astype(bf16)
        grads_v[slot] = out
        mid_grad = lax.dot_general(out, weight(), (((1,), (1,)), ((), ())), preferred_element_type=f32)
        staged[k] = mid_grad.astype(bf16).reshape(2, rows, -1)
        give(k)
        final_v[slot] = jnp.dot(hid, wd[...], preferred_element_type=f32).astype(bf16)
        stores.append(store(n))
    arrive((0, 0))
    finish()
    landed(stores[2] + stores[3])
    wire.close()


def feed(mid, cotangents, gu_zero, gu_one, down):
    rows, width = mid.shape[3:]
    count = 8 * rows
    columns = gu_zero.shape[-1]
    units = 4 * down.shape[2]
    padded = (units + 127) // 128 * 128
    block = 2 * rows
    outs = [shaped((count, units)), shaped((count, columns)), shaped((count, width)), shaped((rows, width), f32)]
    scratch = [
        pltpu.VMEM((2, 2, 2) + gu_one.shape[2:], bf16),
        pltpu.VMEM((padded, width), bf16),
        pltpu.VMEM((2, 2, rows, width), bf16),
        pltpu.VMEM((2, 2, rows, width), bf16),
        pltpu.VMEM((2, block, units), bf16),
        pltpu.VMEM((2, block, columns), bf16),
        pltpu.VMEM((2, block, width), bf16),
        pltpu.VMEM((2, 2, 2, rows, width), bf16),
    ]
    scratch += reduce_scratch(rows, width)[1:]
    scratch += [pltpu.SemaphoreType.DMA((6,)), pltpu.SemaphoreType.DMA((4,)), pltpu.SemaphoreType.DMA((6,))]
    return moving(
        feed_kernel, 4, outs, (mid, cotangents, gu_zero, gu_one, down), scratch + wires(30, 2),
        out_specs=[ANY, ANY, ANY, VMEM],
        limit=62,
    )


def fold_y(wire, source, recv, passed, kept):
    y, x, h, l, c = coordinates()
    sent = [wire.send(source(1 - y, hh), recv.at[hh], 16) for hh in (1 - h, h)]

    def half(k, hh, target):
        sent[k].wait_recv()
        mine = source(y, hh)

        def body(r):
            target[r] = (wide(mine, r) + wide(recv.at[hh], r)).astype(target.dtype)

        each_rows(target.shape[0], body)

    return lambda: half(0, 1 - h, passed), lambda: half(1, h, kept)


def fold_h(wire, passed, kept, recv, out):
    sent = wire.send(passed, recv, 4)

    def finish():
        sent.wait_recv()

        def body(r):
            out[r] = (wide(kept, r) + wide(recv, r)).astype(out.dtype)

        each_rows(out.shape[0], body)

    return finish


def hand_back(wire, own, out):
    y, x, h, l, c = coordinates()
    rank = x * 4 + l * 2 + c
    mine = wire.local(own(rank), out.at[rank])
    sent = [wire.send(own(flip(rank, j)), out.at[rank], PLANE[j - 1]) for j in range(1, 8)]

    def finish():
        mine.wait()
        arrived(sent)

    return finish


def hand_back_halves(wire, own, out):
    y, x, h, l, c = coordinates()
    rank = x * 4 + l * 2 + c
    sent = {j: wire.later(own(flip(rank, j)), out.at[rank], PLANE[j - 1]) for j in range(1, 8)}
    mine = wire.later_local(own(rank), out.at[rank])

    def start(target):
        for side in (0, 1):

            @pl.when(x == side)
            def _(side=side):
                for j in range(1, 8):
                    if side ^ (j // 4) == target:
                        sent[j].start()
                if side == target:
                    mine.start()

    def finish():
        mine.wait()
        arrived(sent.values())

    return lambda: start(0), lambda: start(1), finish


def norm_back(value, gain, grad):
    scale = row_scale(value)
    weighted = gain * grad
    inner = scale * weighted - value * scale * scale * scale * jnp.mean(weighted * value, axis=-1, keepdims=True)
    return inner, grad * value * scale


def over_tokens(left, right):
    return lax.dot_general(left, right, (((0,), (0,)), ((), ())), preferred_element_type=f32).astype(bf16)


def branch_kernel(
    normed_grad, final_parts, middle, cotangent, gain, mid, hidden, gu_grads, cotangents,
    grad_middle, gain_grad, plane_branch, output, down_out, gu_passed, gu_kept, gu_one,
    kept, from_c, s1, r1, s2, r2, total, branch, wd_grad, wd_recv, wd_passed, wd_kept, wd_far, gu_zero, gu_recv,
    hidden_v, gu_v, tokens_v, load_sem, send_sem, recv_sem, local_sem,
):
    wire = Wire(send_sem, recv_sem, local_sem)
    loads = [
        pltpu.make_async_copy(source, target, load_sem.at[k])
        for k, (source, target) in enumerate(
            ((hidden, hidden_v), (cotangents, tokens_v), (gu_grads, gu_v), (mid, tokens_v))
        )
    ]
    for load in loads[:3]:
        load.start()
    greet(LINKS)
    size = middle.shape[0]
    gain_grad[...] = jnp.zeros_like(gain_grad)

    def norm(r):
        inner, outer = norm_back(middle[r], gain[...], normed_grad[r])
        value = cotangent[r].astype(f32) + inner
        grad_middle[r] = value
        branch[r] = value.astype(bf16)
        gain_grad[...] += jnp.sum(outer, axis=0, keepdims=True)

    each_rows(size, norm)
    passing, gathered = plane_gather(wire, branch, plane_branch, plane_branch.at[0, 0, 0], routes(size, 4, 2))
    give, arrive, steps, finish = plane_reduce(
        wire, final_parts, total, kept, from_c, s1, r1, s2, r2, routes(size, 4, 3)
    )
    each(give)
    landed(loads[:2])
    down_rows = wd_grad.shape[2]
    for k in range(4):
        wd_grad[k // 2, k % 2] = over_tokens(hidden_v[:, k * down_rows : (k + 1) * down_rows], tokens_v[...])
    down_passed, down_kept = fold_y(wire, lambda yy, hh: wd_grad.at[yy, hh], wd_recv, wd_passed, wd_kept)
    loads[3].start()
    each(arrive)
    landed(loads[2:])
    gu_rows = gu_one.shape[2]

    def columns(yy, xx, hh):
        start = (yy * 4 + xx * 2 + hh) * gu_rows
        return over_tokens(tokens_v[:, start : start + gu_rows], gu_v[...])

    for k in range(4):
        gu_zero[k // 2, k % 2] = columns(k // 2, 0, k % 2)
        passing[k]()
    gu_sums = fold_y(wire, lambda yy, hh: gu_zero.at[yy, hh], gu_recv, gu_passed, gu_kept)
    down_passed()
    down_h = fold_h(wire, wd_passed, wd_kept, wd_far, down_out)
    for k in range(4):
        steps[k]()
        gu_one[k // 2, k % 2] = columns(k // 2, 1, k % 2)
    gathered()
    finish()

    def emit(r):
        output[r] = (middle[r] + total[r]).astype(bf16)

    each_rows(size, emit)
    down_kept()
    do(gu_sums)
    down_h()
    wire.close()


def branch_step(normed_grad, final_parts, middle, cotangent, gain, mid, hidden, gu_grads, cotangents):
    rows, width = middle.shape
    columns = gu_grads.shape[1]
    down = (hidden.shape[1] // 4, width)
    gu = (width // 8, columns)
    outs = [
        shaped((rows, width), f32),
        shaped((1, width), f32),
        shaped(final_parts.shape),
        shaped((rows, width)),
        shaped(down, f32),
        shaped(gu),
        shaped(gu),
        shaped((2, 2) + gu),
    ]
    scratch = reduce_scratch(rows, width) + [pltpu.VMEM((rows, width), f32), pltpu.VMEM((rows, width), bf16)]
    scratch += [pltpu.VMEM((2, 2) + down, bf16), pltpu.VMEM((2,) + down, bf16)] + [pltpu.VMEM(down, bf16)] * 3
    scratch += [pltpu.VMEM((2, 2) + gu, bf16), pltpu.VMEM((2,) + gu, bf16)]
    scratch += [pltpu.VMEM(v.shape, bf16) for v in (hidden, gu_grads, mid)]
    operands = (normed_grad, final_parts, middle, cotangent, gain, mid, hidden, gu_grads, cotangents)
    return moving(
        branch_kernel, 5, outs, operands, scratch + [pltpu.SemaphoreType.DMA((4,))] + wires(60, 16),
        in_specs=[VMEM, ANY, VMEM, VMEM, VMEM, ANY, ANY, ANY, ANY],
        out_specs=[VMEM, VMEM, ANY, VMEM, VMEM, VMEM, VMEM, VMEM],
        limit=62,
    )


def attend_back_kernel(
    plane_set, plane_branch, queries, attended, lse, wq, wo, cosine, sine, key_index, query_index, first_index,
    gu_passed, gu_kept, gu_one,
    query_grad, back, gu_out, gu_passed_next, gu_kept_next, o_passed, o_kept,
    kv, branch, out_grad, heads, o_recv, staged, grad_keys, grad_values, from_c, s1, r1, s2, r2, gu_recv, gu_recv_y, mask,
    load_sem, send_sem, recv_sem, local_sem,
):
    wire = Wire(send_sem, recv_sem, local_sem)
    rank_dim = wq.shape[0]
    rows = kv.shape[3]
    block = 2 * rows
    load_kv = pltpu.make_async_copy(plane_set.at[:, :, :, :, pl.ds(rank_dim, 4 * HEAD_DIM)], kv, load_sem.at[0])
    load_kv.start()

    loads = [pltpu.make_async_copy(plane_branch.at[k], branch.at[k], load_sem.at[1 + n]) for n, k in enumerate(ARRIVAL)]
    for load in loads:
        load.start()
    greet(LINKS)
    gu_h = fold_h(wire, gu_passed, gu_kept, gu_recv, gu_out)
    gu_sums = fold_y(wire, lambda yy, hh: gu_one.at[yy, hh], gu_recv_y, gu_passed_next, gu_kept_next)
    buffers = (staged, back, staged.at[:, :, 0], from_c, s1, r1, s2, r2)

    def of(columns):
        every = slice(None)
        return [ref.at[(every,) * (len(ref.shape) - 1) + (columns,)] for ref in buffers]

    normed_sum = plane_reduce(wire, *of(pl.ds(0, rank_dim)), routes(rows, 2, 1), load=False)
    kv_sum = plane_reduce(wire, *of(pl.ds(rank_dim, 4 * HEAD_DIM)), routes(rows, 2, 1), load=False)
    load_kv.wait()

    def one(n):
        g, i = ARRIVAL[n]
        if n < 2:
            loads[n].wait()
        if n % 2 == 0:
            grad_keys[...] = jnp.zeros_like(grad_keys)
            grad_values[...] = jnp.zeros_like(grad_values)
        place = pl.ds((g * 2 + i) * block, block)
        grads = lax.dot_general(
            branch[g, i].reshape(block, -1), wo[...], (((1,), (1,)), ((), ())), preferred_element_type=f32
        ).astype(bf16)
        keys = jnp.concatenate(
            [kv[g, :, :, :, :HEAD_DIM].reshape(2 * block, HEAD_DIM), kv[g, :, :, :, 2 * HEAD_DIM : 3 * HEAD_DIM].reshape(2 * block, HEAD_DIM)]
        )
        values = jnp.concatenate(
            [kv[g, :, :, :, HEAD_DIM : 2 * HEAD_DIM].reshape(2 * block, HEAD_DIM), kv[g, :, :, :, 3 * HEAD_DIM :].reshape(2 * block, HEAD_DIM)]
        )
        query_parts = []
        mask[...] = mask_of(key_index[...], first_index[:, place], query_index[:, place])
        for a in range(2):
            span = slice(a * HEAD_DIM, (a + 1) * HEAD_DIM)
            query, grad = queries[place, span], grads[:, span]
            product = grad.astype(f32) * attended[place, span].astype(f32)
            delta = lax.dot_general(
                jnp.ones((8, HEAD_DIM), f32), product, (((1,), (1,)), ((), ())),
                precision=lax.Precision.HIGHEST, preferred_element_type=f32,
            )[:1]
            probs = jnp.exp(scores_of(keys, query) + mask[...] - lse[a, :, place])
            grad_values[...] += jnp.dot(probs.astype(bf16), grad, preferred_element_type=f32)
            grad_probs = lax.dot_general(values, grad, (((1,), (1,)), ((), ())), preferred_element_type=f32)
            grad_scores = (probs * (grad_probs - delta)).astype(bf16)
            grad_keys[...] += jnp.dot(grad_scores, query, preferred_element_type=f32)
            query_parts.append(
                lax.dot_general(grad_scores, keys, (((0,), (0,)), ((), ())), preferred_element_type=f32)
            )
        query_sum = turned(jnp.concatenate(query_parts, axis=1), cosine[place], sine[place], -1.0)
        query_sum = (query_sum * (1.0 / math.sqrt(HEAD_DIM))).astype(bf16)
        query_grad[place] = query_sum
        normed = lax.dot_general(query_sum, wq[...], (((1,), (1,)), ((), ())), preferred_element_type=f32)
        staged[g, i, :, :, :rank_dim] = normed.astype(bf16).reshape(2, rows, rank_dim)
        if n % 2 == 1:
            for number, (source, side) in enumerate(
                ((grad_keys, 0), (grad_values, 0), (grad_keys, 1), (grad_values, 1))
            ):
                column = rank_dim + number * HEAD_DIM
                half = source[side * 2 * block : (side + 1) * 2 * block].astype(bf16)
                staged[g, :, :, :, column : column + HEAD_DIM] = half.reshape(2, 2, rows, HEAD_DIM)

    one(0)
    normed_sum[0](ARRIVAL[0])
    one(1)
    kv_sum[0](ARRIVAL[0])
    kv_sum[0](ARRIVAL[1])
    normed_sum[0](ARRIVAL[1])
    normed_sum[1](ARRIVAL[0])
    kv_sum[1](ARRIVAL[0])
    kv_sum[1](ARRIVAL[1])
    normed_sum[1](ARRIVAL[1])
    landed(loads[2:])
    y, x, h, l, c = coordinates()
    head_rows = out_grad.shape[2]
    for k in range(4):
        part = attended[:, k * head_rows : (k + 1) * head_rows]
        out_grad[k // 2, k % 2] = over_tokens(part, branch[...].reshape(8 * rows, -1))
    swapped = wire.send(out_grad.at[:, 1 - c], heads.at[:, c], 1)
    stayed = wire.local(out_grad.at[:, c], heads.at[:, c])
    one(2)
    normed_sum[0](ARRIVAL[2])
    stayed.wait()
    swapped.wait_recv()
    o_sums = fold_y(wire, lambda yy, hh: heads.at[yy, hh], o_recv, o_passed, o_kept)
    gu_h()
    one(3)
    kv_sum[0](ARRIVAL[2])
    kv_sum[0](ARRIVAL[3])
    normed_sum[0](ARRIVAL[3])
    kv_sum[1](ARRIVAL[2])
    normed_sum[1](ARRIVAL[2])
    kv_sum[1](ARRIVAL[3])
    normed_sum[1](ARRIVAL[3])
    do(kv_sum[2])
    do(normed_sum[2])
    do(gu_sums)
    do(o_sums)
    kv_sum[3]()
    normed_sum[3]()
    wire.close()


def attend_back(
    plane_set, plane_branch, queries, attended, lse, wq, wo, cosine, sine, key_index, query_index, first_index,
    gu_passed, gu_kept, gu_one,
):
    rows = plane_set.shape[3]
    tokens = 8 * rows
    gu = gu_passed.shape
    width = wq.shape[0] + 4 * HEAD_DIM
    heads = (wo.shape[0] // 4, wo.shape[1])
    outs = [
        shaped((tokens, 2 * HEAD_DIM)),
        shaped((rows, width), f32),
        shaped(gu),
        shaped(gu),
        shaped(gu),
        shaped(heads),
        shaped(heads),
    ]
    scratch = [
        pltpu.VMEM((2, 2, 2, rows, 4 * HEAD_DIM), bf16),
        pltpu.VMEM((2, 2, 2, rows, wo.shape[1]), bf16),
        pltpu.VMEM((2, 2) + heads, bf16),
        pltpu.VMEM((2, 2) + heads, bf16),
        pltpu.VMEM((2,) + heads, bf16),
        pltpu.VMEM((2, 2, 2, rows, width), bf16),
        pltpu.VMEM((8 * rows, HEAD_DIM), f32),
        pltpu.VMEM((8 * rows, HEAD_DIM), f32),
    ]
    scratch += reduce_scratch(rows, width)[1:] + [pltpu.VMEM(gu, bf16)]
    scratch += [pltpu.VMEM((2,) + gu, bf16), pltpu.VMEM((tokens, 2 * rows), f32), pltpu.SemaphoreType.DMA((5,))]
    operands = (
        plane_set, plane_branch, queries, attended, lse, wq, wo, cosine, sine, key_index, query_index, first_index,
        gu_passed, gu_kept, gu_one,
    )
    return moving(
        attend_back_kernel, 6, outs, operands, scratch + wires(60, 12),
        in_specs=[ANY, ANY] + [VMEM] * 10 + [ANY, VMEM, VMEM],
        out_specs=[VMEM] * 7,
        limit=62,
    )


def tail_kernel(
    back, normed, compressed, tokens, grad_middle, first_weight, gain_in, gain_q, gain_mid_grad, cosine, sine,
    gu_total, gu_passed, gu_kept, o_passed, o_kept, plane_set, query_grad,
    grad_tokens, down_out, key_out, value_out, gains_out, gate_out, up_out, q_up_out, out_out,
    total, up_grad, normed_v, kv_send, kv_recv, mixed, normed_grad, gain_rows,
    blocks, acc, recv, core, gains, gains_recv,
    gu_far, gu_back, gu_wide, up_recv, up_passed, up_kept, up_far, up_own, up_back,
    o_far,
    send_sem, recv_sem, local_sem,
):
    y, x, h, l, c = coordinates()
    own = dict(zip("yxhlc", (y, x, h, l, c)))
    every = slice(None)
    wire = Wire(send_sem, recv_sem, local_sem)
    rows = back.shape[0]
    rank_dim = compressed.shape[1]
    split = rank_dim + 2 * HEAD_DIM
    load_normed = wire.local(plane_set.at[:, :, :, :, pl.ds(0, rank_dim)], normed_v)
    kv_send[...] = back[:, split:].astype(bf16)
    greet([16, 4] + PLANE)
    far = wire.send(kv_send, kv_recv, 4)
    gu_first = wire.local(gu_total, gu_wide.at[0])
    gu_first.wait()
    piece_rows = gu_back.shape[2]
    gu_piece = lambda k: gu_wide.at[k // 4, pl.ds(pl.multiple_of((k % 4) * piece_rows, piece_rows), piece_rows)]
    gu_begin, gu_rest, gu_done = hand_back_halves(wire, gu_piece, gu_back.at[0])
    gu_begin()
    inner, outer = norm_back(compressed[...], gain_q[...], back[:, :rank_dim])
    mixed[:, :rank_dim] = inner.astype(bf16)
    gain_rows[1:2, :rank_dim] = jnp.sum(outer, axis=0, keepdims=True)
    gain_rows[2:3, :] = gain_mid_grad[...]
    far.wait_recv()
    gu_h = fold_h(wire, gu_passed, gu_kept, gu_far, gu_wide.at[1])
    o_h = fold_h(wire, o_passed, o_kept, o_far, out_out)
    kv = back[:, rank_dim:split] + kv_recv[...].astype(f32)
    mixed[:, rank_dim : rank_dim + HEAD_DIM] = turned(kv[:, :HEAD_DIM], cosine[:rows], sine[:rows], -1.0).astype(bf16)
    mixed[:, rank_dim + HEAD_DIM :] = kv[:, HEAD_DIM:].astype(bf16)
    size = normed.shape[1] // 8
    cores = []
    for k in range(8):
        at = (k // 4, k // 2 % 2, k % 2)
        grad = lax.dot_general(
            normed[:, k * size : (k + 1) * size], mixed[...], (((0,), (0,)), ((), ())), preferred_element_type=f32
        )
        blocks[at] = grad.astype(bf16).reshape(blocks.shape[3:])
        cores.append(wire.send(blocks.at[at + (every, 1 - c)], core.at[at], 1))
    span = blocks.shape[5]
    width = blocks.shape[6]
    columns = thirds(width)
    orders = ["yxlh", "xylh", "lyxh"]
    sent = [None] * 3

    def index(fixed, block):
        free = [k for k in "yxhl" if k not in fixed]
        at = dict(fixed)
        for position, k in enumerate(reversed(free)):
            at[k] = (block // 2**position) % 2
        return tuple(at[k] for k in "yxhl")

    def over(fixed, body):
        @pl.loop(0, 2 ** (4 - len(fixed)))
        def _(i):
            body(index(fixed, i))

    def pass_on(p, step):
        order = orders[p]
        fixed = {k: own[k] for k in order[:step]}
        bit = order[step]
        src = {**fixed, bit: 1 - own[bit]}
        dst = {**fixed, bit: own[bit]}
        place = lambda at: tuple(at.get(k, every) for k in "yxhl") + (every, columns[p])
        mask = {"y": 16, "x": 8, "h": 4, "l": 2}[bit]
        sent[p] = wire.send(acc.at[place(src)], recv.at[place(dst)], mask)

    arrived(cores)
    for first_side in (True, False):
        for p in range(3):
            bit = orders[p][0]

            def body(at, p=p):
                value = wide(blocks, at + (c, every, columns[p])) + wide(core, at + (every, columns[p]))
                acc[at + (every, columns[p])] = value.astype(bf16)

            over({bit: 1 - own[bit] if first_side else own[bit]}, body)
            if first_side:
                pass_on(p, 0)
    load_normed.wait()
    up_size = up_grad.shape[3]
    for k in range(8):
        tokens_part = normed_v[:, :, :, :, k * up_size : (k + 1) * up_size].reshape(8 * rows, up_size)
        up_grad[k // 4, k // 2 % 2, k % 2] = over_tokens(tokens_part, query_grad[...])
    up_sums = [
        fold_y(wire, lambda yy, hh, k=k: up_grad.at[yy, k, hh], up_recv.at[k], up_passed.at[k], up_kept.at[k])
        for k in range(2)
    ]
    gu_h()
    gu_rest()
    wire.left(cores)
    wire.local(first_weight, blocks).wait()
    weight = blocks[...].reshape(-1, blocks.shape[6])
    normed_grad[...] = lax.dot_general(mixed[...], weight, (((1,), (1,)), ((), ())), preferred_element_type=f32)
    gain_rows[0:1, :] = jnp.zeros((1, gain_rows.shape[1]), f32)

    def norm(r):
        inner, outer = norm_back(tokens[r].astype(f32), gain_in[...], normed_grad[r])
        grad_tokens[r] = (grad_middle[r] + inner).astype(bf16)
        gain_rows[0:1, :] += jnp.sum(outer, axis=0, keepdims=True)

    each_rows(rows, norm)
    q_span = rank_dim // 32
    gains[...] = jnp.zeros_like(gains)
    for n in range(32):
        at = (n // 16, n // 8 % 2, n // 4 % 2, n // 2 % 2, n % 2, 0)
        gains[at + (slice(0, 128),)] = jnp.concatenate(
            [gain_rows[0, n * span : (n + 1) * span], gain_rows[2, n * span : (n + 1) * span]], axis=0
        )
        gains[at + (slice(128, 128 + q_span),)] = gain_rows[1, n * q_span : (n + 1) * q_span]

    def pass_gains(order, step):
        fixed = {k: own[k] for k in order[:step]}
        bit = order[step]
        place = lambda at: tuple(at.get(k, every) for k in "yxhlc")
        mask = {"y": 16, "x": 8, "h": 4, "l": 2, "c": 1}[bit]
        return wire.send(gains.at[place({**fixed, bit: 1 - own[bit]})], gains_recv.at[place({**fixed, bit: own[bit]})], mask)

    def add_gains(order, step):
        fixed = {k: own[k] for k in order[:step]}
        bit = order[step]
        place = lambda at: tuple(at.get(k, every) for k in "yxhlc")
        mine = place({**fixed, bit: own[bit]})
        gains[mine] = gains[mine] + gains_recv[place({**fixed, bit: 1 - own[bit]})]

    gain_order = "cyxlh"
    gain_sent = pass_gains(gain_order, 0)
    gain_step = 0
    for step in range(4):
        for p in range(3):
            order = orders[p]
            fixed = {k: own[k] for k in order[:step]}
            bit = order[step]
            sent[p].wait_recv()

            def body(at, p=p, bit=bit, last=step == 3):
                other = tuple(1 - own[k] if k == bit else v for k, v in zip("yxhl", at))
                value = wide(acc, at + (every, columns[p])) + wide(recv, other + (every, columns[p]))
                if last:
                    total[:, columns[p]] = value
                else:
                    acc[at + (every, columns[p])] = value.astype(bf16)

            if step < 3:
                over({**fixed, bit: own[bit], order[step + 1]: 1 - own[order[step + 1]]}, body)
                pass_on(p, step + 1)
                over({**fixed, bit: own[bit], order[step + 1]: own[order[step + 1]]}, body)
            else:
                over({**fixed, bit: own[bit]}, body)
        if gain_step < 5:
            gain_sent.wait_recv()
            add_gains(gain_order, gain_step)
            gain_step += 1
            if gain_step < 5:
                gain_sent = pass_gains(gain_order, gain_step)
        if step == 0:
            for k in range(2):
                do(up_sums[k])
            up_h = [fold_h(wire, up_passed.at[k], up_kept.at[k], up_far.at[k], up_own.at[k]) for k in range(2)]
        if step == 1:
            for k in range(2):
                up_h[k]()
            up_rows = up_back.shape[1]
            up_piece = lambda k: up_own.at[k // 4, pl.ds(pl.multiple_of((k % 4) * up_rows, up_rows), up_rows)]
            up_done = hand_back(wire, up_piece, up_back)
            gu_done()
            unit = gate_out.shape[1] // 32
            units = 4 * unit
            main = units // 128 * 128
            rest = units - main
            for source in range(8):
                tile = gu_back[0, source].astype(f32)
                halves = (
                    tile[:, : main + rest],
                    jnp.concatenate([tile[:, main + 2 * rest :], tile[:, main + rest : main + 2 * rest]], axis=1),
                )
                for half, target in zip(halves, (gate_out, up_out)):
                    for q in range(4):
                        n = q // 2 * 16 + source // 4 * 8 + q % 2 * 4 + source % 4
                        target[:, n * unit : (n + 1) * unit] = half[:, q * unit : (q + 1) * unit]
        if step == 3:
            o_h()
            up_done()
            for head in range(q_up_out.shape[1] // HEAD_DIM):
                hy, hx, hh, hl = head // 8, head // 4 % 2, head // 2 % 2, head % 2
                source = hx * 4 + hl * 2 + hh
                q_up_out[:, head * HEAD_DIM : (head + 1) * HEAD_DIM] = up_back[
                    source, :, hy * HEAD_DIM : (hy + 1) * HEAD_DIM
                ].astype(f32)
    while gain_step < 5:
        gain_sent.wait_recv()
        add_gains(gain_order, gain_step)
        gain_step += 1
        if gain_step < 5:
            gain_sent = pass_gains(gain_order, gain_step)
    gains_out[...] = gains[y, x, h, l, c]
    down_out[...] = total[:, :rank_dim]
    key_out[...] = total[:, rank_dim : rank_dim + HEAD_DIM]
    value_out[...] = total[:, rank_dim + HEAD_DIM :]
    wire.close()


def tail(
    back, normed, compressed, tokens, grad_middle, first_weight, gain_in, gain_q, gain_mid_grad, cosine, sine,
    gu_total, gu_passed, gu_kept, o_passed, o_kept, plane_set, query_grad,
):
    rows, width = tokens.shape
    rank_dim = compressed.shape[1]
    near = first_weight.shape[-1]
    span = width // 32
    gu = gu_total.shape
    units = gu[1] * 4
    up = (rank_dim // 8, query_grad.shape[1])
    heads = o_passed.shape
    outs = [
        shaped((rows, width)),
        shaped((span, rank_dim), f32),
        shaped((span, HEAD_DIM), f32),
        shaped((span, HEAD_DIM), f32),
        shaped((1, 256), f32),
        shaped((span, units), f32),
        shaped((span, units), f32),
        shaped((up[0] // 4, 8 * up[1]), f32),
        shaped(heads, f32),
    ]
    sums = (2, 2, 2, 2, span, near)
    scratch = [
        pltpu.VMEM((span, near), f32),
        pltpu.VMEM((2, 2, 2) + up, bf16),
        pltpu.VMEM(plane_set.shape[:4] + (rank_dim,), bf16),
        pltpu.VMEM((rows, 2 * HEAD_DIM), bf16),
        pltpu.VMEM((rows, 2 * HEAD_DIM), bf16),
        pltpu.VMEM((rows, near), bf16),
        pltpu.VMEM((rows, width), f32),
        pltpu.VMEM((8, width), f32),
        pltpu.VMEM((2, 2, 2, 2, 2, span, near), bf16),
        pltpu.VMEM(sums, bf16),
        pltpu.VMEM(sums, bf16),
        pltpu.VMEM(sums, bf16),
        pltpu.VMEM((2, 2, 2, 2, 2, 1, 256), f32),
        pltpu.VMEM((2, 2, 2, 2, 2, 1, 256), f32),
        pltpu.VMEM(gu, bf16),
        pltpu.VMEM((1, 8, span, gu[1]), bf16),
        pltpu.VMEM((2,) + gu, bf16),
        pltpu.VMEM((2, 2) + up, bf16),
        pltpu.VMEM((2,) + up, bf16),
        pltpu.VMEM((2,) + up, bf16),
        pltpu.VMEM((2,) + up, bf16),
        pltpu.VMEM((2,) + up, bf16),
        pltpu.VMEM((8, up[0] // 4, up[1]), bf16),
        pltpu.VMEM(heads, bf16),
    ]
    operands = (
        back, normed, compressed, tokens, grad_middle, first_weight, gain_in, gain_q, gain_mid_grad, cosine, sine,
        gu_total, gu_passed, gu_kept, o_passed, o_kept, plane_set, query_grad,
    )
    return moving(
        tail_kernel, 7, outs, operands, scratch + wires(100, 24),
        in_specs=[VMEM] * 5 + [ANY] + [VMEM] * 5 + [ANY, ANY, VMEM, ANY, VMEM, ANY, VMEM],
        out_specs=[VMEM] * 9,
        limit=62,
    )


def finish_kernel(*refs):
    count = (len(refs) - 2) // 3
    loads = [pltpu.make_async_copy(refs[k], refs[2 * count + k], refs[-2].at[k]) for k in range(count)]
    for load in loads:
        load.start()
    stores = []
    for k in range(count):
        loads[k].wait()
        stores.append(pltpu.make_async_copy(refs[2 * count + k], refs[count + k], refs[-1].at[k]))
        stores[-1].start()
    landed(stores)


def finish(arrays):
    count = len(arrays)
    return pl.pallas_call(
        finish_kernel,
        out_shape=[shaped(v.shape, v.dtype) for v in arrays],
        in_specs=[ANY] * count,
        out_specs=[ANY] * count,
        scratch_shapes=[pltpu.VMEM(v.shape, v.dtype) for v in arrays] + [pltpu.SemaphoreType.DMA((count,))] * 2,
        compiler_params=pltpu.CompilerParams(vmem_limit_bytes=62 * 1024 * 1024),
        name="finish",
    )(*arrays)


def plane_local(
    tokens,
    positions,
    cotangent,
    norm_in_gain,
    q_down,
    q_gain,
    q_up,
    key_proj,
    value_proj,
    out_proj,
    norm_mid_gain,
    w_gate,
    w_up,
    w_down,
):
    rows, width = tokens.shape
    rank_dim = q_down.shape[1]
    span, q_span = norm_in_gain.shape[0], q_gain.shape[0]

    gains = jnp.concatenate([norm_in_gain, norm_mid_gain, q_gain, jnp.zeros((256 - 2 * span - q_span,), f32)])
    gains = lax.reduce_precision(gains, 8, 7).reshape(1, 256)
    (
        first_weight, up_query, gu_pieces, wo_own, wo_far, wd_own, in_gain, mid_gain, query_gain,
        first_index, query_index, key_index, cosine, sine,
    ) = head(
        q_down, key_proj, value_proj, gains, q_up, w_gate, w_up, out_proj, w_down, positions.reshape(1, rows)
    )
    up_query = up_query.reshape(rank_dim, 2 * HEAD_DIM)

    plane_set, out_weight, gu_set, wd_far, normed, compressed = pack(
        tokens, in_gain, query_gain, first_weight.reshape(width, -1), cosine, sine, wo_own, wo_far, gu_pieces, wd_own
    )
    out_weight = out_weight.reshape(2 * HEAD_DIM, width)
    queries, attended, lse, middle, plane_mid, plane_cotangent, gu_zero, gu_one, down_weight = attend(
        plane_set, up_query, out_weight, cosine, sine, key_index, query_index, first_index, tokens, mid_gain, cotangent,
        gu_set, wd_own, wd_far,
    )
    hidden, gu_grads, final_parts, normed_grad = feed(plane_mid, plane_cotangent, gu_zero, gu_one, down_weight)
    flat = lambda blocks: blocks.reshape(8 * rows, -1)
    grad_middle, mid_gain_grad, plane_branch, output, grad_down, gu_passed, gu_kept, gu_one_grad = branch_step(
        normed_grad, final_parts.reshape(2, 2, 2, rows, width), middle, cotangent, mid_gain, flat(plane_mid), hidden,
        gu_grads, flat(plane_cotangent),
    )
    query_grad, back, gu_total, gu_passed, gu_kept, o_passed, o_kept = attend_back(
        plane_set, plane_branch, queries, attended, lse, up_query, out_weight, cosine, sine,
        key_index, query_index, first_index, gu_passed, gu_kept, gu_one_grad,
    )
    grad_tokens, grad_q_down, grad_key, grad_value, grad_gains, grad_gate, grad_up, grad_q_up, grad_out = tail(
        back, normed, compressed, tokens, grad_middle, first_weight, in_gain, query_gain, mid_gain_grad,
        cosine, sine, gu_total, gu_passed, gu_kept, o_passed, o_kept, plane_set, query_grad,
    )
    output, grad_tokens, grad_q_down, grad_q_up, grad_key, grad_value, grad_out, grad_gate, grad_up, grad_down = finish(
        (output, grad_tokens, grad_q_down, grad_q_up, grad_key, grad_value, grad_out, grad_gate, grad_up, grad_down)
    )
    return (
        output,
        grad_tokens,
        grad_gains[0, :span],
        grad_q_down,
        grad_gains[0, 2 * span : 2 * span + q_span],
        grad_q_up,
        grad_key,
        grad_value,
        grad_out,
        grad_gains[0, span : 2 * span],
        grad_gate,
        grad_up,
        grad_down,
    )


def solution(mesh):
    return jax.shard_map(
        plane_local if dict(mesh.shape) == {"dp": 4, "seq": 8} else local,
        mesh=mesh,
        in_specs=(
            P(("dp", "seq"), None),
            P(("dp", "seq")),
            P(("dp", "seq"), None),
            P(("dp", "seq")),
            P(("dp", "seq"), None),
            P(("dp", "seq")),
            P(("dp", "seq"), None),
            P(("dp", "seq"), None),
            P(("dp", "seq"), None),
            P(("dp", "seq"), None),
            P(("dp", "seq")),
            P(("dp", "seq"), None),
            P(("dp", "seq"), None),
            P(("dp", "seq"), None),
        ),
        out_specs=(
            P(("dp", "seq"), None),
            P(("dp", "seq"), None),
            P(("dp", "seq")),
            P(("dp", "seq"), None),
            P(("dp", "seq")),
            P(("dp", "seq"), None),
            P(("dp", "seq"), None),
            P(("dp", "seq"), None),
            P(("dp", "seq"), None),
            P(("dp", "seq")),
            P(("dp", "seq"), None),
            P(("dp", "seq"), None),
            P(("dp", "seq"), None),
        ),
        check_vma=False,
    )
```

```python
import math

import jax
import jax.numpy as jnp
from jax import lax
from jax.experimental import pallas as pl
from jax.experimental.pallas import tpu as pltpu
from jax.sharding import PartitionSpec as P

HEADS = 16
HEAD_DIM = 256


epsilon = 1e-05
rope_base = 10000.0
masked_score = -1e30


def rms_scale(values):
    return lax.rsqrt(jnp.mean(values * values, axis=-1, keepdims=True) + epsilon)


def rotary(values, places, sign):
    half = values.shape[-1] // 2
    freqs = rope_base ** (-(2.0 * jnp.arange(half).astype(jnp.float32)) / values.shape[-1])
    angles = places.astype(jnp.float32)[:, None] * freqs[None, :]
    cosine = jnp.cos(angles)[:, None, :]
    sine = jnp.sin(angles)[:, None, :]
    first = values[..., :half]
    second = values[..., half:]
    return jnp.concatenate(
        [first * cosine - sign * second * sine, sign * first * sine + second * cosine], axis=-1
    )


def norm_backward(inputs, scale, gain, grad_out):
    weighted = gain * grad_out
    grad_in = scale * weighted - inputs * scale * scale * scale * jnp.mean(
        weighted * inputs, axis=-1, keepdims=True
    )
    grad_gain = jnp.sum(grad_out * inputs * scale, axis=0)
    return (grad_in, grad_gain)


def add_rows(total, block, start):
    current = lax.dynamic_slice_in_dim(total, start, block.shape[0], 0)
    return lax.dynamic_update_slice_in_dim(total, current + block, start, 0)


def local(
    tokens,
    positions,
    cotangent,
    norm_in_gain,
    q_down,
    q_gain,
    q_up,
    key_proj,
    value_proj,
    out_proj,
    norm_mid_gain,
    w_gate,
    w_up,
    w_down,
):
    width = tokens.shape[0]
    scale = 1.0 / math.sqrt(HEAD_DIM)
    attention_set = (
        lax.all_gather(norm_in_gain.astype(jnp.bfloat16), ("dp", "seq"), axis=0, tiled=True),
        lax.all_gather(q_down.astype(jnp.bfloat16), ("dp", "seq"), axis=0, tiled=True),
        lax.all_gather(q_gain.astype(jnp.bfloat16), ("dp", "seq"), axis=0, tiled=True),
        lax.all_gather(q_up.astype(jnp.bfloat16), ("dp", "seq"), axis=0, tiled=True),
        lax.all_gather(key_proj.astype(jnp.bfloat16), ("dp", "seq"), axis=0, tiled=True),
        lax.all_gather(value_proj.astype(jnp.bfloat16), ("dp", "seq"), axis=0, tiled=True),
        lax.all_gather(out_proj.astype(jnp.bfloat16), ("dp", "seq"), axis=0, tiled=True),
    )
    feed_set = (
        lax.all_gather(norm_mid_gain.astype(jnp.bfloat16), ("dp", "seq"), axis=0, tiled=True),
        lax.all_gather(w_gate.astype(jnp.bfloat16), ("dp", "seq"), axis=0, tiled=True),
        lax.all_gather(w_up.astype(jnp.bfloat16), ("dp", "seq"), axis=0, tiled=True),
        lax.all_gather(w_down.astype(jnp.bfloat16), ("dp", "seq"), axis=0, tiled=True),
    )
    in_gain = attention_set[0].astype(jnp.float32)
    query_gain = attention_set[2].astype(jnp.float32)
    inputs = tokens.astype(jnp.float32)
    in_scale = rms_scale(inputs)
    normed = (inputs * in_scale * in_gain).astype(jnp.bfloat16)
    compressed = jnp.dot(normed, attention_set[1], preferred_element_type=jnp.float32)
    query_scale = rms_scale(compressed)
    compressed_normed = (compressed * query_scale * query_gain).astype(jnp.bfloat16)
    queries_raw = jnp.dot(
        compressed_normed, attention_set[3], preferred_element_type=jnp.float32
    ).reshape(width, HEADS, HEAD_DIM)
    queries = rotary(queries_raw, positions, 1.0).astype(jnp.bfloat16)
    keys_raw = jnp.dot(normed, attention_set[4], preferred_element_type=jnp.float32)
    keys = rotary(keys_raw[:, None, :], positions, 1.0)[:, 0, :].astype(jnp.bfloat16)
    values = jnp.dot(normed, attention_set[5], preferred_element_type=jnp.float32).astype(
        jnp.bfloat16
    )
    query_index = lax.axis_index("seq") * width + jnp.arange(width, dtype=jnp.int32)
    first_index = query_index - positions

    def visibility(key_start):
        key_index = key_start + jnp.arange(width, dtype=jnp.int32)
        seen = (key_index[None, :] >= first_index[:, None]) & (
            key_index[None, :] <= query_index[:, None]
        )
        return seen[:, None, :]

    start_state = (
        jnp.full((width, HEADS), masked_score, jnp.float32),
        jnp.zeros((width, HEADS), jnp.float32),
        jnp.zeros((width, HEADS, HEAD_DIM), jnp.float32),
    )
    carry = start_state
    piece = (
        lax.all_gather(keys, "seq", axis=0, tiled=True),
        lax.all_gather(values, "seq", axis=0, tiled=True),
    )
    blocks = piece[0].shape[0] // width
    key_blocks = piece[0].reshape(blocks, width, HEAD_DIM)
    value_blocks = piece[1].reshape(blocks, width, HEAD_DIM)

    def forward_one_block(state, item):
        key_block, value_block, number = item
        key_start = number * width
        top, total, accum = state
        seen = visibility(key_start)
        scores = (
            jnp.einsum("thd,kd->thk", queries, key_block, preferred_element_type=jnp.float32)
            * scale
        )
        scores = jnp.where(seen, scores, masked_score)
        new_top = jnp.maximum(top, jnp.max(scores, axis=-1))
        weights = jnp.where(seen, jnp.exp(scores - new_top[..., None]), 0.0)
        decay = jnp.exp(top - new_top)
        total = total * decay + jnp.sum(weights, axis=-1)
        accum = accum * decay[..., None] + jnp.einsum(
            "thk,kd->thd",
            weights.astype(jnp.bfloat16),
            value_block,
            preferred_element_type=jnp.float32,
        )
        state = (new_top, total, accum)
        return (state, None)

    carry, _ = lax.scan(
        forward_one_block, carry, (key_blocks, value_blocks, jnp.arange(blocks, dtype=jnp.int32))
    )
    top, total, accum = carry
    attended_full = accum / total[..., None]
    log_total = top + jnp.log(total)
    attended = attended_full.reshape(width, HEADS * HEAD_DIM).astype(jnp.bfloat16)
    middle = inputs + jnp.dot(attended, attention_set[6], preferred_element_type=jnp.float32)
    mid_gain = feed_set[0].astype(jnp.float32)
    mid_scale = rms_scale(middle)
    normed_mid = (middle * mid_scale * mid_gain).astype(jnp.bfloat16)
    gate = jnp.dot(normed_mid, feed_set[1], preferred_element_type=jnp.float32)
    upper = jnp.dot(normed_mid, feed_set[2], preferred_element_type=jnp.float32)
    sigmoid_gate = jax.nn.sigmoid(gate)
    silu_gate = gate * sigmoid_gate
    hidden = (silu_gate * upper).astype(jnp.bfloat16)
    output = (middle + jnp.dot(hidden, feed_set[3], preferred_element_type=jnp.float32)).astype(
        jnp.bfloat16
    )
    feed_back = (
        lax.all_gather(norm_mid_gain.astype(jnp.bfloat16), ("dp", "seq"), axis=0, tiled=True),
        lax.all_gather(w_gate.astype(jnp.bfloat16), ("dp", "seq"), axis=0, tiled=True),
        lax.all_gather(w_up.astype(jnp.bfloat16), ("dp", "seq"), axis=0, tiled=True),
        lax.all_gather(w_down.astype(jnp.bfloat16), ("dp", "seq"), axis=0, tiled=True),
    )
    grad_out_full = cotangent.astype(jnp.float32)
    grad_down = jnp.einsum("tf,td->fd", hidden, cotangent, preferred_element_type=jnp.float32)
    grad_hidden = jnp.einsum(
        "td,fd->tf", cotangent, feed_back[3], preferred_element_type=jnp.float32
    )
    grad_gate = (grad_hidden * upper * sigmoid_gate * (1.0 + gate * (1.0 - sigmoid_gate))).astype(
        jnp.bfloat16
    )
    grad_upper = (grad_hidden * silu_gate).astype(jnp.bfloat16)
    grad_gate_weight = jnp.einsum(
        "td,tf->df", normed_mid, grad_gate, preferred_element_type=jnp.float32
    )
    grad_up_weight = jnp.einsum(
        "td,tf->df", normed_mid, grad_upper, preferred_element_type=jnp.float32
    )
    grad_normed_mid = jnp.einsum(
        "tf,df->td", grad_gate, feed_back[1], preferred_element_type=jnp.float32
    ) + jnp.einsum("tf,df->td", grad_upper, feed_back[2], preferred_element_type=jnp.float32)
    grad_mid_norm, grad_mid_gain = norm_backward(
        middle, mid_scale, feed_back[0].astype(jnp.float32), grad_normed_mid
    )
    grad_middle = grad_out_full + grad_mid_norm
    feed_grads = (
        lax.psum_scatter(grad_mid_gain, ("dp", "seq"), scatter_dimension=0, tiled=True),
        lax.psum_scatter(grad_gate_weight, ("dp", "seq"), scatter_dimension=0, tiled=True),
        lax.psum_scatter(grad_up_weight, ("dp", "seq"), scatter_dimension=0, tiled=True),
        lax.psum_scatter(grad_down, ("dp", "seq"), scatter_dimension=0, tiled=True),
    )
    attention_back = (
        lax.all_gather(norm_in_gain.astype(jnp.bfloat16), ("dp", "seq"), axis=0, tiled=True),
        lax.all_gather(q_down.astype(jnp.bfloat16), ("dp", "seq"), axis=0, tiled=True),
        lax.all_gather(q_gain.astype(jnp.bfloat16), ("dp", "seq"), axis=0, tiled=True),
        lax.all_gather(q_up.astype(jnp.bfloat16), ("dp", "seq"), axis=0, tiled=True),
        lax.all_gather(key_proj.astype(jnp.bfloat16), ("dp", "seq"), axis=0, tiled=True),
        lax.all_gather(value_proj.astype(jnp.bfloat16), ("dp", "seq"), axis=0, tiled=True),
        lax.all_gather(out_proj.astype(jnp.bfloat16), ("dp", "seq"), axis=0, tiled=True),
    )
    branch_grad = grad_middle.astype(jnp.bfloat16)
    grad_output_weight = jnp.einsum(
        "ta,td->ad", attended, branch_grad, preferred_element_type=jnp.float32
    )
    grad_attended = (
        jnp.einsum("td,ad->ta", branch_grad, attention_back[6], preferred_element_type=jnp.float32)
        .reshape(width, HEADS, HEAD_DIM)
        .astype(jnp.bfloat16)
    )
    delta = jnp.sum(grad_attended.astype(jnp.float32) * attended_full, axis=-1)
    group_rows = width * lax.axis_size("seq")
    back_state = (
        jnp.zeros((width, HEADS, HEAD_DIM), jnp.float32),
        jnp.zeros((group_rows, HEAD_DIM), jnp.float32),
        jnp.zeros((group_rows, HEAD_DIM), jnp.float32),
    )
    carry = back_state
    piece = (
        lax.all_gather(keys, "seq", axis=0, tiled=True),
        lax.all_gather(values, "seq", axis=0, tiled=True),
    )
    blocks = piece[0].shape[0] // width
    key_blocks = piece[0].reshape(blocks, width, HEAD_DIM)
    value_blocks = piece[1].reshape(blocks, width, HEAD_DIM)

    def backward_one_block(state, item):
        key_block, value_block, number = item
        key_start = number * width
        grad_query, grad_keys, grad_values = state
        seen = visibility(key_start)
        scores = (
            jnp.einsum("thd,kd->thk", queries, key_block, preferred_element_type=jnp.float32)
            * scale
        )
        probs = jnp.where(seen, jnp.exp(scores - log_total[..., None]), 0.0)
        grad_value_block = jnp.einsum(
            "thk,thd->kd",
            probs.astype(jnp.bfloat16),
            grad_attended,
            preferred_element_type=jnp.float32,
        )
        grad_probs = jnp.einsum(
            "thd,kd->thk", grad_attended, value_block, preferred_element_type=jnp.float32
        )
        grad_scores = (probs * (grad_probs - delta[..., None]) * scale).astype(jnp.bfloat16)
        grad_query = grad_query + jnp.einsum(
            "thk,kd->thd", grad_scores, key_block, preferred_element_type=jnp.float32
        )
        grad_key_block = jnp.einsum(
            "thk,thd->kd", grad_scores, queries, preferred_element_type=jnp.float32
        )
        state = (
            grad_query,
            add_rows(grad_keys, grad_key_block, key_start),
            add_rows(grad_values, grad_value_block, key_start),
        )
        return (state, None)

    carry, _ = lax.scan(
        backward_one_block, carry, (key_blocks, value_blocks, jnp.arange(blocks, dtype=jnp.int32))
    )
    grad_query, grad_keys, grad_values = carry
    local_key_grad, local_value_grad = (
        lax.psum_scatter(
            grad_keys.astype(jnp.bfloat16), "seq", scatter_dimension=0, tiled=True
        ).astype(jnp.float32),
        lax.psum_scatter(
            grad_values.astype(jnp.bfloat16), "seq", scatter_dimension=0, tiled=True
        ).astype(jnp.float32),
    )
    grad_key_pre = rotary(local_key_grad[:, None, :], positions, -1.0)[:, 0, :].astype(jnp.bfloat16)
    grad_value_pre = local_value_grad.astype(jnp.bfloat16)
    grad_query_pre = (
        rotary(grad_query, positions, -1.0).reshape(width, HEADS * HEAD_DIM).astype(jnp.bfloat16)
    )
    grad_up_query = jnp.einsum(
        "tr,ta->ra", compressed_normed, grad_query_pre, preferred_element_type=jnp.float32
    )
    grad_compressed_normed = jnp.einsum(
        "ta,ra->tr", grad_query_pre, attention_back[3], preferred_element_type=jnp.float32
    )
    grad_compressed, grad_query_gain = norm_backward(
        compressed, query_scale, attention_back[2].astype(jnp.float32), grad_compressed_normed
    )
    grad_compressed = grad_compressed.astype(jnp.bfloat16)
    grad_down_weight = jnp.einsum(
        "td,tr->dr", normed, grad_compressed, preferred_element_type=jnp.float32
    )
    grad_key_weight = jnp.einsum(
        "td,te->de", normed, grad_key_pre, preferred_element_type=jnp.float32
    )
    grad_value_weight = jnp.einsum(
        "td,te->de", normed, grad_value_pre, preferred_element_type=jnp.float32
    )
    grad_normed = jnp.einsum(
        "tr,dr->td", grad_compressed, attention_back[1], preferred_element_type=jnp.float32
    )
    grad_normed = grad_normed + jnp.einsum(
        "te,de->td", grad_key_pre, attention_back[4], preferred_element_type=jnp.float32
    )
    grad_normed = grad_normed + jnp.einsum(
        "te,de->td", grad_value_pre, attention_back[5], preferred_element_type=jnp.float32
    )
    grad_in_norm, grad_in_gain = norm_backward(
        inputs, in_scale, attention_back[0].astype(jnp.float32), grad_normed
    )
    grad_tokens = (grad_middle + grad_in_norm).astype(jnp.bfloat16)
    attention_grads = (
        lax.psum_scatter(grad_in_gain, ("dp", "seq"), scatter_dimension=0, tiled=True),
        lax.psum_scatter(grad_down_weight, ("dp", "seq"), scatter_dimension=0, tiled=True),
        lax.psum_scatter(grad_query_gain, ("dp", "seq"), scatter_dimension=0, tiled=True),
        lax.psum_scatter(grad_up_query, ("dp", "seq"), scatter_dimension=0, tiled=True),
        lax.psum_scatter(grad_key_weight, ("dp", "seq"), scatter_dimension=0, tiled=True),
        lax.psum_scatter(grad_value_weight, ("dp", "seq"), scatter_dimension=0, tiled=True),
        lax.psum_scatter(grad_output_weight, ("dp", "seq"), scatter_dimension=0, tiled=True),
    )
    return (
        output,
        grad_tokens,
        attention_grads[0],
        attention_grads[1],
        attention_grads[2],
        attention_grads[3],
        attention_grads[4],
        attention_grads[5],
        attention_grads[6],
        feed_grads[0],
        feed_grads[1],
        feed_grads[2],
        feed_grads[3],
    )


bf16 = jnp.bfloat16
f32 = jnp.float32
ANY = pl.BlockSpec(memory_space=pl.ANY)
VMEM = pl.BlockSpec(memory_space=pltpu.VMEM)
PLANE = [j // 4 * 8 + j % 4 for j in range(1, 8)]
LINKS = [16, 8, 4, 2, 1]


def flip(number, bits):
    bit = 1
    while bit <= bits:
        if bits & bit:
            number = number + bit - 2 * bit * ((number // bit) % 2)
        bit *= 2
    return number


def coordinates():
    dp = lax.axis_index("dp")
    seq = lax.axis_index("seq")
    return dp // 2, dp % 2, seq // 4, (seq // 2) % 2, seq % 2


def partner(mask):
    return flip(lax.axis_index("dp"), mask // 8), flip(lax.axis_index("seq"), mask % 8)


PENDING = []


def greet(masks):
    barrier = pltpu.get_barrier_semaphore()
    for mask in masks:
        pl.semaphore_signal(barrier, inc=1, device_id=partner(mask), device_id_type=pl.DeviceIdType.MESH)
    pl.semaphore_wait(barrier, len(masks))
    while PENDING:
        PENDING.pop().wait()


class Wire:
    def __init__(self, send_sem, recv_sem, local_sem):
        self.send_sem, self.recv_sem, self.local_sem = send_sem, recv_sem, local_sem
        self.copies = []
        self.gone = []
        self.locals = 0

    def send(self, src, dst, mask):
        copy = self.later(src, dst, mask)
        copy.start()
        return copy

    def later(self, src, dst, mask):
        k = len(self.copies)
        copy = pltpu.make_async_remote_copy(
            src_ref=src,
            dst_ref=dst,
            send_sem=self.send_sem.at[k],
            recv_sem=self.recv_sem.at[k],
            device_id=partner(mask),
            device_id_type=pl.DeviceIdType.MESH,
        )
        self.copies.append(copy)
        return copy

    def local(self, src, dst):
        copy = self.later_local(src, dst)
        copy.start()
        return copy

    def later_local(self, src, dst):
        copy = pltpu.make_async_copy(src, dst, self.local_sem.at[self.locals])
        self.locals += 1
        return copy

    def left(self, copies):
        for copy in copies:
            copy.wait_send()
        self.gone += copies

    def close(self):
        for copy in self.copies:
            if not any(copy is other for other in self.gone):
                copy.wait_send()


def wires(remote, local):
    return [pltpu.SemaphoreType.DMA((remote,)), pltpu.SemaphoreType.DMA((remote,)), pltpu.SemaphoreType.DMA((local,))]


def arrived(copies):
    for copy in copies:
        copy.wait_recv()


def landed(copies):
    for copy in copies:
        copy.wait()


def moving(kernel, number, outs, operands, scratch, in_specs=None, out_specs=None, limit=56):
    in_specs = list(in_specs or [ANY] * len(operands))
    early = [k for k, spec in enumerate(in_specs) if spec is VMEM and operands[k].size >= 1 << 14]
    for k in early:
        in_specs[k] = ANY

    def whole(*refs):
        refs, buffers, sems = list(refs[: -len(early) - 1]), refs[-len(early) - 1 : -1], refs[-1]
        for n, (k, buffer) in enumerate(zip(early, buffers)):
            copy = pltpu.make_async_copy(refs[k], buffer, sems.at[n])
            copy.start()
            PENDING.append(copy)
            refs[k] = buffer
        kernel(*refs)

    if early:
        buffers = [pltpu.VMEM(operands[k].shape, operands[k].dtype) for k in early]
        scratch = list(scratch) + buffers + [pltpu.SemaphoreType.DMA((len(early),))]
    return pl.pallas_call(
        whole if early else kernel,
        out_shape=outs,
        in_specs=in_specs,
        out_specs=out_specs or [ANY] * len(outs),
        scratch_shapes=scratch,
        compiler_params=pltpu.CompilerParams(
            collective_id=number, has_side_effects=True, vmem_limit_bytes=limit * 1024 * 1024
        ),
        cost_estimate=pl.CostEstimate(flops=0, bytes_accessed=100_000_000, transcendentals=0),
        name=kernel.__name__,
    )(*operands)


def shaped(shape, dtype=bf16):
    return jax.ShapeDtypeStruct(tuple(shape), dtype)


def each_rows(rows, body, step=16):
    @pl.loop(0, rows // step)
    def _(i):
        body(pl.ds(pl.multiple_of(i * step, step), step))


def wide(ref, where):
    return ref[where].astype(f32)


def routes(rows, pieces, direct):
    size = rows // pieces
    return [(pl.ds(i * size, size), "xl" if i < direct else "lx") for i in range(pieces)]


def plane_gather(wire, block, out, own, ways):
    links = {"x": (out.at[1, 0, 0], out.at[1, 0, 1], 8), "l": (out.at[0, 1, 0], out.at[0, 1, 1], 2)}
    far, far_core = out.at[1, 1, 0], out.at[1, 1, 1]
    ordered = [k for k in range(len(ways)) if ways[k][1] == "xl"] + [k for k in range(len(ways)) if ways[k][1] == "lx"]
    came = {}
    for turn in (0, 1):
        for k in ordered:
            rows, way = ways[k]
            target, _, mask = links[way[turn]]
            came[way[turn], k] = wire.send(block.at[rows], target.at[rows], mask)
    cores = [wire.send(block, out.at[0, 0, 1], 1)]
    mine = wire.local(block, own) if own is not None else None
    diagonal = {}

    def step(k):
        rows, way = ways[k]
        target, core, _ = links[way[0]]
        came[way[0], k].wait_recv()
        diagonal[k] = wire.send(target.at[rows], far.at[rows], links[way[1]][2])
        cores.append(wire.send(target.at[rows], core.at[rows], 1))

    def finish():
        for k in ordered:
            rows, way = ways[k]
            target, core, _ = links[way[1]]
            came[way[1], k].wait_recv()
            cores.append(wire.send(target.at[rows], core.at[rows], 1))
        for k in ordered:
            rows, way = ways[k]
            diagonal[k].wait_recv()
            cores.append(wire.send(far.at[rows], far_core.at[rows], 1))
        if mine is not None:
            mine.wait()
        arrived(cores)

    return [lambda k=k: step(k) for k in ordered], finish


ARRIVAL = [(1, 1), (1, 0), (0, 1), (0, 0)]


def plane_reduce(wire, parts, out, kept, from_c, send_one, recv_one, send_two, recv_two, ways, load=True):
    cores = {}
    loads = {}
    masks = {"x": 8, "l": 2}
    beside = {"xl": (1, 0), "lx": (0, 1)}
    after = {"xl": (0, 1), "lx": (1, 0)}
    came = {}
    passed = {}

    def give(k):
        cores[k] = wire.send(parts.at[k[0], k[1], 1], from_c.at[k[0], k[1]], 1)
        if load:
            loads[k] = wire.local(parts.at[k[0], k[1], 0], kept.at[k[0], k[1]])

    def pair(k, r):
        return wide(kept.at[k[0], k[1]], r) + wide(from_c.at[k[0], k[1]], r)

    def within(rows, body):
        @pl.loop(0, rows.size // 16)
        def _(i):
            body(pl.ds(pl.multiple_of(rows.start + i * 16, 16), 16))

    def put(slot, k, j):
        rows, way = ways[j]

        def fill(r):
            send_one[slot, r] = pair(k, r).astype(bf16)

        within(rows, fill)
        came[slot, j] = wire.send(send_one.at[slot, rows], recv_one.at[slot, rows], masks[way[0]])

    def arrive(k):
        if load:
            loads[k].wait()
        cores[k].wait_recv()
        for j in range(len(ways)):
            if k == (1, 1):
                put(0, k, j)
            elif beside[ways[j][1]] == k:
                put(1, k, j)

    def step(j):
        rows, way = ways[j]
        came[0, j].wait_recv()

        def fill(r):
            send_two[r] = (pair(after[way], r) + wide(recv_one.at[0], r)).astype(bf16)

        within(rows, fill)
        passed[j] = wire.send(send_two.at[rows], recv_two.at[rows], masks[way[1]])

    def finish():
        for j, (rows, way) in enumerate(ways):
            came[1, j].wait_recv()
            passed[j].wait_recv()

            def fill(r):
                out[r] = pair((0, 0), r) + wide(recv_one.at[1], r) + wide(recv_two, r)

            within(rows, fill)

    return give, arrive, [lambda j=j: step(j) for j in range(len(ways))], finish


def each(action, items=ARRIVAL):
    for item in items:
        action(item)


def do(steps):
    for step in steps:
        step()


def reduce_scratch(rows, width):
    return [
        pltpu.VMEM((2, 2, rows, width), bf16),
        pltpu.VMEM((2, 2, rows, width), bf16),
        pltpu.VMEM((2, rows, width), bf16),
        pltpu.VMEM((2, rows, width), bf16),
        pltpu.VMEM((rows, width), bf16),
        pltpu.VMEM((rows, width), bf16),
    ]


def over_y(wire, block, place, side):
    y, x, h, l, c = coordinates()
    hh = h if side == 0 else 1 - h
    mine = wire.local(block, place(y, hh))
    sent = wire.send(block, place(y, hh), 16)

    def finish():
        mine.wait()
        sent.wait_recv()

    return finish


def thirds(width):
    main = (width * 5 // 12) // 128 * 128
    return [pl.ds(0, main), pl.ds(main, main), pl.ds(2 * main, width - 2 * main)]


def head_kernel(
    q_down, key, value, gains, q_up, gate, up, out_proj, w_down, places,
    first_out, upq_out, gu, wo_out, wo_far, wd_out, in_gain, mid_gain, q_gain, first_index, query_index, key_index,
    cosine, sine, first, upq, staged, gains_out, places_out, send_sem, recv_sem, local_sem,
):
    y, x, h, l, c = coordinates()
    rank = x * 4 + l * 2 + c
    wire = Wire(send_sem, recv_sem, local_sem)
    greet([16, 4] + PLANE)
    r1, r2 = q_down.shape[1], q_down.shape[1] + key.shape[1]
    first[:, :r1] = q_down[...].astype(bf16)
    first[:, r1:r2] = key[...].astype(bf16)
    first[:, r2:] = value[...].astype(bf16)
    width = first.shape[1]
    a, b, d = thirds(width)
    mine = [wire.local(first, first_out.at[y, x, h, l, c]), wire.local(gains, gains_out.at[y, x, h, l, c])]
    one = [wire.send(first.at[:, p], first_out.at[y, x, h, l, c, :, p], 4) for p in (a, b, d)]
    gain = wire.send(gains, gains_out.at[y, x, h, l, c], 4)
    place = [wire.send(places, places_out.at[j], PLANE[j - 1]) for j in range(1, 8)]
    place_mine = wire.local(places, places_out.at[0])
    heads = q_up.shape[1] // HEAD_DIM
    for head in range(heads):
        hy, hx, hh, hl = head // 8, head // 4 % 2, head // 2 % 2, head % 2
        target = hx * 4 + hl * 2 + hh
        upq[target, :, hy * HEAD_DIM : (hy + 1) * HEAD_DIM] = q_up[:, head * HEAD_DIM : (head + 1) * HEAD_DIM].astype(bf16)
    up_rows = upq.shape[1]
    up_place = lambda: upq_out.at[y, x, h, pl.ds((l * 2 + c) * up_rows, up_rows), :]
    up_mine = wire.local(upq.at[rank], up_place())
    up_sent = [wire.send(upq.at[flip(rank, j)], up_place(), PLANE[j - 1]) for j in range(1, 8)]
    wo_out[...] = out_proj[...].astype(bf16)
    piece = gate.shape[1] // 32
    size = 4 * piece
    main = size // 128 * 128
    for target in range(8):
        for where, weight in ((0, gate), (1, up)):
            for q in range(4):
                n = q // 2 * 16 + target // 4 * 8 + q % 2 * 4 + target % 4
                staged[where, :, q * piece : (q + 1) * piece] = weight[:, n * piece : (n + 1) * piece]
        gu[target, :, :main] = staged[0, :, :main].astype(bf16)
        rest = size - main
        both = jnp.concatenate([staged[0, :, main : main + rest], staged[1, :, main : main + rest]], axis=1)
        gu[target, :, main : main + 2 * rest] = both.astype(bf16)
        gu[target, :, main + 2 * rest :] = staged[1, :, :main].astype(bf16)
    wd_out[...] = w_down[...].astype(bf16)
    landed(mine)

    every = slice(None)

    def step(held, columns, mask):
        at = tuple(every if k in held else v for k, v in zip("yxhlc", (y, x, h, l, c)))
        if columns is None:
            return wire.send(gains_out.at[at], gains_out.at[at], mask)
        place = first_out.at[at + (every, columns)]
        return wire.send(place, place, mask)

    def last(held, bit, columns):
        at = {k: every if k in held else v for k, v in zip("yxhlc", (y, x, h, l, c))}
        at[bit] = 1 - dict(zip("yxhlc", (y, x, h, l, c)))[bit]
        place = first_out.at[tuple(at[k] for k in "yxhlc") + (every, columns)]
        return wire.send(place, place, 1)

    bits = {"y": 16, "x": 8, "h": 4, "l": 2}
    orders = [("hlxy", a), ("hlyx", b), ("hxyl", d)]
    sent = one
    for k in range(1, 4):
        following = []
        for (order, columns), copy in zip(orders, sent):
            copy.wait_recv()
            following.append(step(order[:k], columns, bits[order[k]]))
        sent = following
        gain.wait_recv()
        gain = step("hlxy"[:k], None, bits["hlxy"[k]])
        if k == 1:
            up_mine.wait()
            arrived(up_sent)
            up_h = wire.send(upq_out.at[y, :, h], upq_out.at[y, :, h], 4)
            up_y = [wire.send(upq_out.at[y, :, h], upq_out.at[y, :, h], 16)]
            wo_sent = wire.send(wo_out, wo_far, 4)
        if k == 3:
            five = [step(order[:3], columns, 1) for order, columns in orders]
    up_h.wait_recv()
    up_y += [wire.send(upq_out.at[y, :, 1 - h], upq_out.at[y, :, 1 - h], 16)]
    gain.wait_recv()
    gain = step("hlxy", None, 1)
    for (order, columns), copy in zip(orders, sent):
        copy.wait_recv()
        five.append(last(order[:3], order[3], columns))
    place_mine.wait()
    arrived(place)
    rows = places.shape[1]
    half = HEAD_DIM // 2
    powers = lax.broadcasted_iota(jnp.int32, (rows, half), 1).astype(f32)
    freqs = jnp.exp(powers * (-2.0 / HEAD_DIM * math.log(rope_base)))
    eye = lax.broadcasted_iota(jnp.int32, (rows, rows), 0) == lax.broadcasted_iota(jnp.int32, (rows, rows), 1)
    index = []
    for j in range(8):
        place = jnp.sum(jnp.where(eye, places_out[j].astype(f32), 0.0), axis=1, keepdims=True)
        angles = place * freqs
        cosine[j * rows : (j + 1) * rows] = jnp.cos(angles)
        sine[j * rows : (j + 1) * rows] = jnp.sin(angles)
        b, d = j // 2 % 2, j % 2
        block = (l + b - 2 * l * b) * 2 + (c + d - 2 * c * d)
        start = (h * 4 + block) * rows
        index.append(start + lax.broadcasted_iota(jnp.int32, (1, rows), 1))
        side = h if j < 4 else 1 - h
        key_index[j * rows : (j + 1) * rows] = (side * 4 + block) * rows + lax.broadcasted_iota(jnp.int32, (rows, 1), 0)
    index = jnp.concatenate(index, axis=1)
    query_index[...] = index
    first_index[...] = index - jnp.concatenate([places_out[j] for j in range(8)], axis=1)
    gain.wait_recv()
    span, q_span = in_gain.shape[1] // 32, q_gain.shape[1] // 32
    for n in range(32):
        row = gains_out[n // 16, n // 8 % 2, n // 4 % 2, n // 2 % 2, n % 2]
        in_gain[:, n * span : (n + 1) * span] = row[:, :span]
        mid_gain[:, n * span : (n + 1) * span] = row[:, span : 2 * span]
        q_gain[:, n * q_span : (n + 1) * q_span] = row[:, 2 * span : 2 * span + q_span]
    arrived(five + up_y + [wo_sent])
    wire.close()


def head(q_down, key, value, gains, q_up, gate, up, out_proj, w_down, places):
    rows = q_down.shape[0]
    count = 8 * places.shape[1]
    width = q_down.shape[1] + 2 * key.shape[1]
    columns = gate.shape[1] // 4
    slice_size = gate.shape[1] // 8
    outs = [
        shaped((2, 2, 2, 2, 2, rows, width)),
        shaped((2, 2, 2, 4 * q_up.shape[0], 2 * HEAD_DIM)),
        shaped((8, rows, columns)),
        shaped(out_proj.shape),
        shaped(out_proj.shape),
        shaped(w_down.shape),
        shaped((1, 32 * rows), f32),
        shaped((1, 32 * rows), f32),
        shaped((1, q_down.shape[1]), f32),
        shaped((1, count), jnp.int32),
        shaped((1, count), jnp.int32),
        shaped((count, 1), jnp.int32),
        shaped((count, HEAD_DIM // 2), f32),
        shaped((count, HEAD_DIM // 2), f32),
    ]
    scratch = [
        pltpu.VMEM((rows, width), bf16),
        pltpu.VMEM((8, q_up.shape[0], 2 * HEAD_DIM), bf16),
        pltpu.VMEM((2, rows, slice_size), f32),
        pltpu.VMEM((2, 2, 2, 2, 2) + gains.shape, f32),
        pltpu.VMEM((8,) + places.shape, jnp.int32),
    ]
    operands = (q_down, key, value, gains, q_up, gate, up, out_proj, w_down, places)
    return moving(
        head_kernel, 1, outs, operands, scratch + wires(100, 8),
        in_specs=[VMEM] * len(operands),
        out_specs=[ANY, ANY, VMEM, VMEM, ANY] + [VMEM] * 9,
    )


def turned(values, cosine, sine, sign):
    half = HEAD_DIM // 2
    out = []
    for start in range(0, values.shape[1], HEAD_DIM):
        one, two = values[:, start : start + half], values[:, start + half : start + HEAD_DIM]
        out += [one * cosine - sign * two * sine, sign * one * sine + two * cosine]
    return jnp.concatenate(out, axis=1)


def row_scale(values):
    return lax.rsqrt(jnp.mean(values * values, axis=-1, keepdims=True) + epsilon)


def pack_kernel(
    tokens, gain_in, gain_q, first_weight, cosine, sine, wo_own, wo_far, gu, wd_own,
    out, weight_out, gu_out, wd_far, normed, compressed,
    weight, block, weight_all, send_sem, recv_sem, local_sem,
):
    y, x, h, l, c = coordinates()
    wire = Wire(send_sem, recv_sem, local_sem)
    load = wire.local(first_weight, weight)
    greet([16, 4] + PLANE)
    rank = x * 4 + l * 2 + c
    gu_rows = gu.shape[1]
    gu_place = gu_out.at[x, pl.ds((l * 2 + c) * gu_rows, gu_rows), :]
    gu_mine = wire.local(gu.at[rank], gu_place)
    gu_sent = [wire.send(gu.at[flip(rank, j)], gu_place, PLANE[j - 1]) for j in range(1, 8)]
    weight_done = [over_y(wire, ref, lambda yy, hh: weight_all.at[yy, hh], k) for k, ref in enumerate((wo_own, wo_far))]
    rows = tokens.shape[0]
    inputs = tokens[...].astype(f32)
    normed[...] = (inputs * row_scale(inputs) * gain_in[...]).astype(bf16)
    load.wait()
    mixed = jnp.dot(normed[...], weight[...], preferred_element_type=f32)
    rank_dim = compressed.shape[1]
    query = mixed[:, :rank_dim]
    compressed[...] = query
    block[:, :rank_dim] = (query * row_scale(query) * gain_q[...]).astype(bf16)
    block[:, rank_dim : rank_dim + HEAD_DIM] = turned(
        mixed[:, rank_dim : rank_dim + HEAD_DIM], cosine[:rows], sine[:rows], 1.0
    ).astype(bf16)
    block[:, rank_dim + HEAD_DIM :] = mixed[:, rank_dim + HEAD_DIM :].astype(bf16)
    near = block.shape[1]
    far = 2 * HEAD_DIM
    columns, far_columns = pl.ds(0, near), pl.ds(near, far)
    from_h = wire.send(block.at[:, pl.ds(near - far, far)], out.at[0, 0, 0, :, far_columns], 4)
    near_out = out.at[:, :, :, :, columns]
    size = block.shape[0]
    steps, finish = plane_gather(wire, block, near_out, near_out.at[0, 0, 0], routes(size, 4, 1))
    from_h.wait_recv()
    wd_sent = wire.send(wd_own, wd_far, 4)
    far_out = out.at[:, :, :, :, far_columns]
    far_steps, far_finish = plane_gather(wire, far_out.at[0, 0, 0], far_out, None, routes(size, 2, 1))
    do(steps)
    do(far_steps)
    do(weight_done)
    swapped = wire.send(weight_all.at[:, 1 - c], weight_out.at[:, c], 1)
    kept = wire.local(weight_all.at[:, c], weight_out.at[:, c])
    finish()
    far_finish()
    kept.wait()
    gu_mine.wait()
    arrived([swapped, wd_sent] + gu_sent)
    wire.close()


def pack(tokens, gain_in, gain_q, first_weight, cosine, sine, wo_own, wo_far, gu, wd_own):
    rows, width = tokens.shape
    near = first_weight.shape[1]
    rank_dim = near - 2 * HEAD_DIM
    outs = [
        shaped((2, 2, 2, rows, near + 2 * HEAD_DIM)),
        shaped((2, 2) + wo_own.shape),
        shaped((2, 4 * gu.shape[1], gu.shape[2])),
        shaped(wd_own.shape),
        shaped((rows, width)),
        shaped((rows, rank_dim), f32),
    ]
    operands = (tokens, gain_in, gain_q, first_weight, cosine, sine, wo_own, wo_far, gu, wd_own)
    return moving(
        pack_kernel, 2, outs, operands,
        [pltpu.VMEM(first_weight.shape, bf16), pltpu.VMEM((rows, near), bf16), pltpu.VMEM((2, 2) + wo_own.shape, bf16)]
        + wires(60, 12),
        in_specs=[VMEM, VMEM, VMEM, ANY, VMEM, VMEM, VMEM, VMEM, VMEM, VMEM],
        out_specs=[ANY, VMEM, ANY, ANY, VMEM, VMEM],
    )


def mask_of(index, first, last):
    return jnp.where((index >= first) & (index <= last), 0.0, masked_score)


def scores_of(keys, queries):
    return lax.dot_general(keys, queries, (((1,), (1,)), ((), ())), preferred_element_type=f32)


def attend_kernel(
    plane_set, wq, wo, cosine, sine, key_index, query_index, first_index, tokens, gain, cotangent, gu_set, wd_own, wd_far,
    queries_out, attended, lse, middle, plane_mid, cotangents, gu_zero, gu_one, wd_out,
    kv, normed, staged, mask, from_c, s1, r1, s2, r2, mid, gu_far, gu_next, load_sem, send_sem, recv_sem, local_sem,
):
    wire = Wire(send_sem, recv_sem, local_sem)
    rank_dim = wq.shape[0]
    loads = [
        pltpu.make_async_copy(plane_set.at[:, :, :, :, pl.ds(rank_dim, 4 * HEAD_DIM)], kv, load_sem.at[0]),
        pltpu.make_async_copy(plane_set.at[:, :, :, :, pl.ds(0, rank_dim)], normed, load_sem.at[1]),
    ]
    for load in loads:
        load.start()
    greet(LINKS)
    places = [lambda yy, hh: gu_zero.at[yy, hh], lambda yy, hh: gu_one.at[yy, hh]]
    passing, gathered = plane_gather(
        wire, cotangent, cotangents, cotangents.at[0, 0, 0], routes(cotangent.shape[0], 4, 1)
    )
    far_sent = wire.send(gu_set.at[0], gu_far, 4)
    gu_done = [over_y(wire, ref, lambda yy, hh: wd_out.at[yy, hh], k) for k, ref in enumerate((wd_own, wd_far))]
    landed(loads)
    rows = kv.shape[3]
    block = 2 * rows

    def one(g, i):
        start = (g * 2 + i) * block
        place = pl.ds(start, block)
        raw = jnp.dot(normed[g, i].reshape(block, rank_dim), wq[...], preferred_element_type=f32)
        queries = (turned(raw, cosine[place], sine[place], 1.0) * (1.0 / math.sqrt(HEAD_DIM))).astype(bf16)
        queries_out[place] = queries
        mask[...] = mask_of(key_index[...], first_index[:, place], query_index[:, place])
        keys = jnp.concatenate(
            [kv[g, :, :, :, :HEAD_DIM].reshape(2 * block, HEAD_DIM), kv[g, :, :, :, 2 * HEAD_DIM : 3 * HEAD_DIM].reshape(2 * block, HEAD_DIM)]
        )
        values = jnp.concatenate(
            [kv[g, :, :, :, HEAD_DIM : 2 * HEAD_DIM].reshape(2 * block, HEAD_DIM), kv[g, :, :, :, 3 * HEAD_DIM :].reshape(2 * block, HEAD_DIM)]
        )
        merged = []
        for a in range(2):
            scores = scores_of(keys, queries[:, a * HEAD_DIM : (a + 1) * HEAD_DIM]) + mask[...]
            top = jnp.max(scores, axis=0, keepdims=True)
            weights = jnp.exp(scores - top)
            total = jnp.sum(weights, axis=0, keepdims=True)
            lse[a, :, place] = top + jnp.log(total)
            probs = (weights * (1.0 / total)).astype(bf16)
            merged.append(lax.dot_general(probs, values, (((0,), (0,)), ((), ())), preferred_element_type=f32).astype(bf16))
        merged = jnp.concatenate(merged, axis=1)
        attended[place] = merged
        staged[g, i] = jnp.dot(merged, wo[...], preferred_element_type=f32).astype(bf16).reshape(2, rows, -1)

    give, arrive, steps, finish = plane_reduce(
        wire, staged, middle, staged.at[:, :, 0], from_c, s1, r1, s2, r2, routes(rows, 4, 3), load=False
    )
    for number, k in enumerate(ARRIVAL):
        one(*k)
        give(k)
        if number == 0:
            arrive(k)
        elif number > 1:
            arrive(ARRIVAL[number - 1])
        if number == 1:
            do(passing[:2])
        if number == 2:
            do(passing[2:])
    arrive((0, 0))
    gu_done += [over_y(wire, gu_set.at[k], places[k], 0) for k in range(2)]
    do(steps)
    far_sent.wait_recv()
    next_sent = wire.send(gu_set.at[1], gu_next, 4)
    gu_done.append(over_y(wire, gu_far, places[0], 1))
    gathered()
    finish()

    def norm(r):
        value = tokens[r].astype(f32) + middle[r]
        middle[r] = value
        mid[r] = (value * row_scale(value) * gain[...]).astype(bf16)

    each_rows(rows, norm)
    steps, finish = plane_gather(wire, mid, plane_mid, plane_mid.at[0, 0, 0], routes(rows, 4, 2))
    do(steps)
    next_sent.wait_recv()
    gu_done.append(over_y(wire, gu_next, places[1], 1))
    finish()
    do(gu_done)
    wire.close()


def attend(plane_set, wq, wo, cosine, sine, key_index, query_index, first_index, tokens, gain, cotangent, gu_set, wd_own, wd_far):
    rows, width = tokens.shape
    count = 8 * rows
    rank_dim = wq.shape[0]
    gu = gu_set.shape[1:]
    outs = [
        shaped((count, 2 * HEAD_DIM)),
        shaped((count, 2 * HEAD_DIM)),
        shaped((2, 1, count), f32),
        shaped((rows, width), f32),
        shaped((2, 2, 2, rows, width)),
        shaped((2, 2, 2, rows, width)),
        shaped((2, 2) + gu),
        shaped((2, 2) + gu),
        shaped((2, 2) + wd_own.shape),
    ]
    scratch = [
        pltpu.VMEM((2, 2, 2, rows, 4 * HEAD_DIM), bf16),
        pltpu.VMEM((2, 2, 2, rows, rank_dim), bf16),
        pltpu.VMEM((2, 2, 2, rows, width), bf16),
        pltpu.VMEM((count, 2 * rows), f32),
    ]
    scratch += reduce_scratch(rows, width)[1:]
    scratch += [pltpu.VMEM((rows, width), bf16), pltpu.VMEM(gu, bf16), pltpu.VMEM(gu, bf16), pltpu.SemaphoreType.DMA((2,))]
    operands = (
        plane_set, wq, wo, cosine, sine, key_index, query_index, first_index, tokens, gain, cotangent, gu_set, wd_own, wd_far,
    )
    return moving(
        attend_kernel, 3, outs, operands, scratch + wires(80, 16),
        in_specs=[ANY] + [VMEM] * 13,
        out_specs=[VMEM, VMEM, VMEM, VMEM, ANY, ANY, ANY, ANY, ANY],
        limit=62,
    )


def feed_kernel(
    mid, cotangents, gu_zero, gu_one, down,
    hidden, grads, final_parts, normed_grad,
    gu, wd, mid_v, cot_v, hid_v, grads_v, final_v, staged, from_c, s1, r1, s2, r2,
    weight_sem, load_sem, store_sem, send_sem, recv_sem, local_sem,
):
    wire = Wire(send_sem, recv_sem, local_sem)
    main = gu.shape[4] // 2 // 128 * 128
    size = down.shape[2]
    units = 4 * size
    rows = staged.shape[3]
    block = 2 * rows
    copies = [
        pltpu.make_async_copy(gu_zero, gu.at[:, 0], weight_sem.at[0]),
        pltpu.make_async_copy(gu_one, gu.at[:, 1], weight_sem.at[1]),
    ]
    for k in range(4):
        copies.append(pltpu.make_async_copy(down.at[k // 2, k % 2], wd.at[pl.ds(k * size, size)], weight_sem.at[2 + k]))
    for copy in copies:
        copy.start()

    def load(n):
        k = ARRIVAL[n]
        pairs = [(mid.at[k[0], k[1]], mid_v.at[n % 2]), (cotangents.at[k[0], k[1]], cot_v.at[n % 2])]
        moves = [pltpu.make_async_copy(src, dst, load_sem.at[2 * (n % 2) + q]) for q, (src, dst) in enumerate(pairs)]
        for move in moves:
            move.start()
        return moves

    def store(n):
        k = ARRIVAL[n]
        place = pl.ds((k[0] * 2 + k[1]) * block, block)
        pairs = [(hid_v, hidden.at[place]), (grads_v, grads.at[place]), (final_v, final_parts.at[place])]
        moves = [
            pltpu.make_async_copy(src.at[n % 2], dst, store_sem.at[3 * (n % 2) + q]) for q, (src, dst) in enumerate(pairs)
        ]
        for move in moves:
            move.start()
        return moves

    moves = [load(0)]
    greet(LINKS)
    wd[units:] = jnp.zeros((wd.shape[0] - units, wd.shape[1]), bf16)
    landed(copies)
    give, arrive, steps, finish = plane_reduce(
        wire, staged, normed_grad, staged.at[:, :, 0], from_c, s1, r1, s2, r2, routes(rows, 4, 2), load=False
    )
    weight = lambda: gu[...].reshape(-1, gu.shape[4])
    stores = []
    for n, k in enumerate(ARRIVAL):
        landed(moves[n])
        if n < 3:
            moves.append(load(n + 1))
        if n > 1:
            landed(stores[n - 2])
        slot = n % 2
        both = jnp.dot(mid_v[slot].reshape(block, -1), weight(), preferred_element_type=f32)
        if n > 0:
            arrive(ARRIVAL[n - 1])
        if n > 2:
            do(steps)
        gate = both[:, : main + 128]
        upper = jnp.concatenate([both[:, main + 128 :], pltpu.roll(both[:, main : main + 128], 64, 1)], axis=1)
        cotangent = cot_v[slot].reshape(block, -1)
        grad = lax.dot_general(cotangent, wd[...], (((1,), (1,)), ((), ())), preferred_element_type=f32)
        sigmoid = 1.0 / (1.0 + jnp.exp(-gate))
        silu = gate * sigmoid
        hid = (silu * upper).astype(bf16)
        hid_v[slot] = hid[:, :units]
        grad_gate = grad * upper * sigmoid * (1.0 + gate * (1.0 - sigmoid))
        grad_upper = grad * silu
        joint = grad_gate[:, main:] + pltpu.roll(grad_upper[:, main:], 64, 1)
        out = jnp.concatenate([grad_gate[:, :main], joint, grad_upper[:, :main]], axis=1).astype(bf16)
        grads_v[slot] = out
        mid_grad = lax.dot_general(out, weight(), (((1,), (1,)), ((), ())), preferred_element_type=f32)
        staged[k] = mid_grad.astype(bf16).reshape(2, rows, -1)
        give(k)
        final_v[slot] = jnp.dot(hid, wd[...], preferred_element_type=f32).astype(bf16)
        stores.append(store(n))
    arrive((0, 0))
    finish()
    landed(stores[2] + stores[3])
    wire.close()


def feed(mid, cotangents, gu_zero, gu_one, down):
    rows, width = mid.shape[3:]
    count = 8 * rows
    columns = gu_zero.shape[-1]
    units = 4 * down.shape[2]
    padded = (units + 127) // 128 * 128
    block = 2 * rows
    outs = [shaped((count, units)), shaped((count, columns)), shaped((count, width)), shaped((rows, width), f32)]
    scratch = [
        pltpu.VMEM((2, 2, 2) + gu_one.shape[2:], bf16),
        pltpu.VMEM((padded, width), bf16),
        pltpu.VMEM((2, 2, rows, width), bf16),
        pltpu.VMEM((2, 2, rows, width), bf16),
        pltpu.VMEM((2, block, units), bf16),
        pltpu.VMEM((2, block, columns), bf16),
        pltpu.VMEM((2, block, width), bf16),
        pltpu.VMEM((2, 2, 2, rows, width), bf16),
    ]
    scratch += reduce_scratch(rows, width)[1:]
    scratch += [pltpu.SemaphoreType.DMA((6,)), pltpu.SemaphoreType.DMA((4,)), pltpu.SemaphoreType.DMA((6,))]
    return moving(
        feed_kernel, 4, outs, (mid, cotangents, gu_zero, gu_one, down), scratch + wires(30, 2),
        out_specs=[ANY, ANY, ANY, VMEM],
        limit=62,
    )


def fold_y(wire, source, recv, passed, kept):
    y, x, h, l, c = coordinates()
    sent = [wire.send(source(1 - y, hh), recv.at[hh], 16) for hh in (1 - h, h)]

    def half(k, hh, target):
        sent[k].wait_recv()
        mine = source(y, hh)

        def body(r):
            target[r] = (wide(mine, r) + wide(recv.at[hh], r)).astype(target.dtype)

        each_rows(target.shape[0], body)

    return lambda: half(0, 1 - h, passed), lambda: half(1, h, kept)


def fold_y_far(wire, source, recv, passed):
    y, x, h, l, c = coordinates()
    sent = wire.send(source(1 - y, 1 - h), recv, 16)

    def finish():
        sent.wait_recv()
        mine = source(y, 1 - h)

        def body(r):
            passed[r] = (wide(mine, r) + wide(recv, r)).astype(passed.dtype)

        each_rows(passed.shape[0], body)

    return finish


def fold_h(wire, passed, kept, recv, out):
    sent = wire.send(passed, recv, 4)

    def finish():
        sent.wait_recv()

        def body(r):
            out[r] = (wide(kept, r) + wide(recv, r)).astype(out.dtype)

        each_rows(out.shape[0], body)

    return finish


def hand_back(wire, own, out):
    y, x, h, l, c = coordinates()
    rank = x * 4 + l * 2 + c
    mine = wire.local(own(rank), out.at[rank])
    sent = [wire.send(own(flip(rank, j)), out.at[rank], PLANE[j - 1]) for j in range(1, 8)]

    def finish():
        mine.wait()
        arrived(sent)

    return finish


def hand_back_halves(wire, own, out):
    y, x, h, l, c = coordinates()
    rank = x * 4 + l * 2 + c
    sent = {j: wire.later(own(flip(rank, j)), out.at[rank], PLANE[j - 1]) for j in range(1, 8)}
    mine = wire.later_local(own(rank), out.at[rank])

    def start(target):
        for side in (0, 1):

            @pl.when(x == side)
            def _(side=side):
                for j in range(1, 8):
                    if side ^ (j // 4) == target:
                        sent[j].start()
                if side == target:
                    mine.start()

    def finish():
        mine.wait()
        arrived(sent.values())

    return lambda: start(0), lambda: start(1), finish


def norm_back(value, gain, grad):
    scale = row_scale(value)
    weighted = gain * grad
    inner = scale * weighted - value * scale * scale * scale * jnp.mean(weighted * value, axis=-1, keepdims=True)
    return inner, grad * value * scale


def over_tokens(left, right):
    return lax.dot_general(left, right, (((0,), (0,)), ((), ())), preferred_element_type=f32).astype(bf16)


def branch_kernel(
    normed_grad, final_parts, middle, cotangent, gain, mid, hidden, gu_grads, cotangents,
    grad_middle, gain_grad, plane_branch, output, down_out, gu_passed, gu_zero_out, gu_one_out,
    kept, from_c, s1, r1, s2, r2, total, branch, wd_grad, wd_recv, wd_passed, wd_kept, wd_far, gu_recv,
    hidden_v, gu_v, tokens_v, gu_zero, gu_one, load_sem, store_sem, send_sem, recv_sem, local_sem,
):
    wire = Wire(send_sem, recv_sem, local_sem)
    loads = [
        pltpu.make_async_copy(source, target, load_sem.at[k])
        for k, (source, target) in enumerate(
            ((hidden, hidden_v), (cotangents, tokens_v), (gu_grads, gu_v), (mid, tokens_v))
        )
    ]
    for load in loads[:3]:
        load.start()
    greet(LINKS)
    size = middle.shape[0]
    gain_grad[...] = jnp.zeros_like(gain_grad)

    def norm(r):
        inner, outer = norm_back(middle[r], gain[...], normed_grad[r])
        value = cotangent[r].astype(f32) + inner
        grad_middle[r] = value
        branch[r] = value.astype(bf16)
        gain_grad[...] += jnp.sum(outer, axis=0, keepdims=True)

    each_rows(size, norm)
    passing, gathered = plane_gather(wire, branch, plane_branch, plane_branch.at[0, 0, 0], routes(size, 4, 2))
    give, arrive, steps, finish = plane_reduce(
        wire, final_parts, total, kept, from_c, s1, r1, s2, r2, routes(size, 4, 3)
    )
    each(give)
    landed(loads[:2])
    down_rows = wd_grad.shape[2]
    for k in range(4):
        wd_grad[k // 2, k % 2] = over_tokens(hidden_v[:, k * down_rows : (k + 1) * down_rows], tokens_v[...])
    down_passed, down_kept = fold_y(wire, lambda yy, hh: wd_grad.at[yy, hh], wd_recv, wd_passed, wd_kept)
    loads[3].start()
    each(arrive)
    landed(loads[2:])
    gu_rows = gu_one.shape[2]

    def columns(yy, xx, hh):
        start = (yy * 4 + xx * 2 + hh) * gu_rows
        return over_tokens(tokens_v[:, start : start + gu_rows], gu_v[...])

    stores = [
        pltpu.make_async_copy(source.at[k // 2, k % 2], target.at[k // 2, k % 2], store_sem.at[side, k])
        for side, (source, target) in enumerate(((gu_zero, gu_zero_out), (gu_one, gu_one_out)))
        for k in range(4)
    ]
    for k in range(4):
        gu_zero[k // 2, k % 2] = columns(k // 2, 0, k % 2)
        stores[k].start()
        passing[k]()
    gu_sum = fold_y_far(wire, lambda yy, hh: gu_zero.at[yy, hh], gu_recv, gu_passed)
    down_passed()
    down_h = fold_h(wire, wd_passed, wd_kept, wd_far, down_out)
    for k in range(4):
        steps[k]()
        gu_one[k // 2, k % 2] = columns(k // 2, 1, k % 2)
        stores[4 + k].start()
    gathered()
    finish()

    def emit(r):
        output[r] = (middle[r] + total[r]).astype(bf16)

    each_rows(size, emit)
    down_kept()
    gu_sum()
    down_h()
    landed(stores)
    wire.close()


def branch_step(normed_grad, final_parts, middle, cotangent, gain, mid, hidden, gu_grads, cotangents):
    rows, width = middle.shape
    columns = gu_grads.shape[1]
    down = (hidden.shape[1] // 4, width)
    gu = (width // 8, columns)
    outs = [
        shaped((rows, width), f32),
        shaped((1, width), f32),
        shaped(final_parts.shape),
        shaped((rows, width)),
        shaped(down, f32),
        shaped(gu),
        shaped((2, 2) + gu),
        shaped((2, 2) + gu),
    ]
    scratch = reduce_scratch(rows, width) + [pltpu.VMEM((rows, width), f32), pltpu.VMEM((rows, width), bf16)]
    scratch += [pltpu.VMEM((2, 2) + down, bf16), pltpu.VMEM((2,) + down, bf16)] + [pltpu.VMEM(down, bf16)] * 3
    scratch += [pltpu.VMEM(gu, bf16)]
    scratch += [pltpu.VMEM(v.shape, bf16) for v in (hidden, gu_grads, mid)] + [pltpu.VMEM((2, 2) + gu, bf16)] * 2
    operands = (normed_grad, final_parts, middle, cotangent, gain, mid, hidden, gu_grads, cotangents)
    return moving(
        branch_kernel, 5, outs, operands, scratch + [pltpu.SemaphoreType.DMA((4,)), pltpu.SemaphoreType.DMA((2, 4))] + wires(60, 16),
        in_specs=[VMEM, ANY, VMEM, VMEM, VMEM, ANY, ANY, ANY, ANY],
        out_specs=[VMEM, VMEM, ANY, VMEM, VMEM, VMEM, ANY, ANY],
        limit=62,
    )


def attend_back_kernel(
    plane_set, plane_branch, queries, attended, lse, wq, wo, cosine, sine, key_index, query_index, first_index,
    gu_passed, gu_zero, gu_one,
    query_grad, back, gu_out, gu_passed_next, gu_kept_next, heads,
    kv, branch, out_grad, near_mine, near_recv, staged, grad_keys, grad_values, from_c, s1, r1, s2, r2, gu_recv, gu_recv_y, mask,
    load_sem, send_sem, recv_sem, local_sem,
):
    wire = Wire(send_sem, recv_sem, local_sem)
    rank_dim = wq.shape[0]
    rows = kv.shape[3]
    block = 2 * rows
    load_kv = pltpu.make_async_copy(plane_set.at[:, :, :, :, pl.ds(rank_dim, 4 * HEAD_DIM)], kv, load_sem.at[0])
    load_kv.start()

    loads = [pltpu.make_async_copy(plane_branch.at[k], branch.at[k], load_sem.at[1 + n]) for n, k in enumerate(ARRIVAL)]
    for load in loads:
        load.start()
    greet(LINKS)
    y, x, h, l, c = coordinates()
    far_sent = wire.send(gu_passed, gu_recv, 4)
    near_load = wire.local(gu_zero.at[y, h], near_mine)
    near_sent = wire.send(gu_zero.at[1 - y, h], near_recv, 16)
    gu_sums = fold_y(wire, lambda yy, hh: gu_one.at[yy, hh], gu_recv_y, gu_passed_next, gu_kept_next)
    buffers = (staged, back, staged.at[:, :, 0], from_c, s1, r1, s2, r2)

    def of(columns):
        every = slice(None)
        return [ref.at[(every,) * (len(ref.shape) - 1) + (columns,)] for ref in buffers]

    normed_sum = plane_reduce(wire, *of(pl.ds(0, rank_dim)), routes(rows, 2, 1), load=False)
    kv_sum = plane_reduce(wire, *of(pl.ds(rank_dim, 4 * HEAD_DIM)), routes(rows, 2, 1), load=False)
    load_kv.wait()

    def one(n):
        g, i = ARRIVAL[n]
        if n < 2:
            loads[n].wait()
        if n % 2 == 0:
            grad_keys[...] = jnp.zeros_like(grad_keys)
            grad_values[...] = jnp.zeros_like(grad_values)
        place = pl.ds((g * 2 + i) * block, block)
        grads = lax.dot_general(
            branch[g, i].reshape(block, -1), wo[...], (((1,), (1,)), ((), ())), preferred_element_type=f32
        ).astype(bf16)
        keys = jnp.concatenate(
            [kv[g, :, :, :, :HEAD_DIM].reshape(2 * block, HEAD_DIM), kv[g, :, :, :, 2 * HEAD_DIM : 3 * HEAD_DIM].reshape(2 * block, HEAD_DIM)]
        )
        values = jnp.concatenate(
            [kv[g, :, :, :, HEAD_DIM : 2 * HEAD_DIM].reshape(2 * block, HEAD_DIM), kv[g, :, :, :, 3 * HEAD_DIM :].reshape(2 * block, HEAD_DIM)]
        )
        query_parts = []
        mask[...] = mask_of(key_index[...], first_index[:, place], query_index[:, place])
        for a in range(2):
            span = slice(a * HEAD_DIM, (a + 1) * HEAD_DIM)
            query, grad = queries[place, span], grads[:, span]
            product = grad.astype(f32) * attended[place, span].astype(f32)
            delta = lax.dot_general(
                jnp.ones((8, HEAD_DIM), f32), product, (((1,), (1,)), ((), ())),
                precision=lax.Precision.HIGHEST, preferred_element_type=f32,
            )[:1]
            probs = jnp.exp(scores_of(keys, query) + mask[...] - lse[a, :, place])
            grad_values[...] += jnp.dot(probs.astype(bf16), grad, preferred_element_type=f32)
            grad_probs = lax.dot_general(values, grad, (((1,), (1,)), ((), ())), preferred_element_type=f32)
            grad_scores = (probs * (grad_probs - delta)).astype(bf16)
            grad_keys[...] += jnp.dot(grad_scores, query, preferred_element_type=f32)
            query_parts.append(
                lax.dot_general(grad_scores, keys, (((0,), (0,)), ((), ())), preferred_element_type=f32)
            )
        query_sum = turned(jnp.concatenate(query_parts, axis=1), cosine[place], sine[place], -1.0)
        query_sum = (query_sum * (1.0 / math.sqrt(HEAD_DIM))).astype(bf16)
        query_grad[place] = query_sum
        normed = lax.dot_general(query_sum, wq[...], (((1,), (1,)), ((), ())), preferred_element_type=f32)
        staged[g, i, :, :, :rank_dim] = normed.astype(bf16).reshape(2, rows, rank_dim)
        if n % 2 == 1:
            for number, (source, side) in enumerate(
                ((grad_keys, 0), (grad_values, 0), (grad_keys, 1), (grad_values, 1))
            ):
                column = rank_dim + number * HEAD_DIM
                half = source[side * 2 * block : (side + 1) * 2 * block].astype(bf16)
                staged[g, :, :, :, column : column + HEAD_DIM] = half.reshape(2, 2, rows, HEAD_DIM)

    one(0)
    normed_sum[0](ARRIVAL[0])
    one(1)
    kv_sum[0](ARRIVAL[0])
    kv_sum[0](ARRIVAL[1])
    normed_sum[0](ARRIVAL[1])
    normed_sum[1](ARRIVAL[0])
    kv_sum[1](ARRIVAL[0])
    kv_sum[1](ARRIVAL[1])
    normed_sum[1](ARRIVAL[1])
    landed(loads[2:])
    head_rows = out_grad.shape[2]
    for k in range(4):
        part = attended[:, k * head_rows : (k + 1) * head_rows]
        out_grad[k // 2, k % 2] = over_tokens(part, branch[...].reshape(8 * rows, -1))
    swapped = wire.send(out_grad.at[:, 1 - c], heads.at[:, c], 1)
    stayed = wire.local(out_grad.at[:, c], heads.at[:, c])
    one(2)
    normed_sum[0](ARRIVAL[2])
    stayed.wait()
    swapped.wait_recv()
    one(3)
    kv_sum[0](ARRIVAL[2])
    kv_sum[0](ARRIVAL[3])
    normed_sum[0](ARRIVAL[3])
    kv_sum[1](ARRIVAL[2])
    normed_sum[1](ARRIVAL[2])
    kv_sum[1](ARRIVAL[3])
    normed_sum[1](ARRIVAL[3])
    do(kv_sum[2])
    do(normed_sum[2])
    near_load.wait()
    arrived([near_sent, far_sent])

    def total(r):
        gu_out[r] = (wide(near_mine, r) + wide(near_recv, r) + wide(gu_recv, r)).astype(bf16)

    each_rows(gu_out.shape[0], total)
    do(gu_sums)
    kv_sum[3]()
    normed_sum[3]()
    wire.close()


def attend_back(
    plane_set, plane_branch, queries, attended, lse, wq, wo, cosine, sine, key_index, query_index, first_index,
    gu_passed, gu_zero, gu_one,
):
    rows = plane_set.shape[3]
    tokens = 8 * rows
    gu = gu_passed.shape
    width = wq.shape[0] + 4 * HEAD_DIM
    heads = (wo.shape[0] // 4, wo.shape[1])
    outs = [
        shaped((tokens, 2 * HEAD_DIM)),
        shaped((rows, width), f32),
        shaped(gu),
        shaped(gu),
        shaped(gu),
        shaped((2, 2) + heads),
    ]
    scratch = [
        pltpu.VMEM((2, 2, 2, rows, 4 * HEAD_DIM), bf16),
        pltpu.VMEM((2, 2, 2, rows, wo.shape[1]), bf16),
        pltpu.VMEM((2, 2) + heads, bf16),
        pltpu.VMEM(gu, bf16),
        pltpu.VMEM(gu, bf16),
        pltpu.VMEM((2, 2, 2, rows, width), bf16),
        pltpu.VMEM((8 * rows, HEAD_DIM), f32),
        pltpu.VMEM((8 * rows, HEAD_DIM), f32),
    ]
    scratch += reduce_scratch(rows, width)[1:] + [pltpu.VMEM(gu, bf16)]
    scratch += [pltpu.VMEM((2,) + gu, bf16), pltpu.VMEM((tokens, 2 * rows), f32), pltpu.SemaphoreType.DMA((5,))]
    operands = (
        plane_set, plane_branch, queries, attended, lse, wq, wo, cosine, sine, key_index, query_index, first_index,
        gu_passed, gu_zero, gu_one,
    )
    return moving(
        attend_back_kernel, 6, outs, operands, scratch + wires(60, 12),
        in_specs=[ANY, ANY] + [VMEM] * 10 + [ANY, ANY, VMEM],
        out_specs=[VMEM] * 6,
        limit=62,
    )


def tail_kernel(
    back, normed, compressed, tokens, grad_middle, first_weight, gain_in, gain_q, gain_mid_grad, cosine, sine,
    gu_total, gu_passed, gu_kept, heads, plane_set, query_grad,
    grad_tokens, down_out, key_out, value_out, gains_out, gate_out, up_out, q_up_out, out_out,
    total, up_grad, normed_v, kv_send, kv_recv, mixed, normed_grad, gain_rows,
    blocks, acc, recv, core, gains, gains_recv,
    gu_far, gu_back, gu_wide, up_recv, up_passed, up_kept, up_far, up_own, up_back,
    o_recv, o_passed, o_kept, o_far,
    send_sem, recv_sem, local_sem,
):
    y, x, h, l, c = coordinates()
    own = dict(zip("yxhlc", (y, x, h, l, c)))
    every = slice(None)
    wire = Wire(send_sem, recv_sem, local_sem)
    rows = back.shape[0]
    rank_dim = compressed.shape[1]
    split = rank_dim + 2 * HEAD_DIM
    load_normed = wire.local(plane_set.at[:, :, :, :, pl.ds(0, rank_dim)], normed_v)
    greet([16, 4] + PLANE)
    kv_send[...] = back[:, split:].astype(bf16)
    far = wire.send(kv_send, kv_recv, 4)
    gu_first = wire.local(gu_total, gu_wide.at[0])
    gu_first.wait()
    piece_rows = gu_back.shape[2]
    gu_piece = lambda k: gu_wide.at[k // 4, pl.ds(pl.multiple_of((k % 4) * piece_rows, piece_rows), piece_rows)]
    gu_begin, gu_rest, gu_done = hand_back_halves(wire, gu_piece, gu_back.at[0])
    gu_begin()
    o_sums = fold_y(wire, lambda yy, hh: heads.at[yy, hh], o_recv, o_passed, o_kept)
    inner, outer = norm_back(compressed[...], gain_q[...], back[:, :rank_dim])
    mixed[:, :rank_dim] = inner.astype(bf16)
    gain_rows[1:2, :rank_dim] = jnp.sum(outer, axis=0, keepdims=True)
    gain_rows[2:3, :] = gain_mid_grad[...]
    far.wait_recv()
    gu_h = fold_h(wire, gu_passed, gu_kept, gu_far, gu_wide.at[1])
    kv = back[:, rank_dim:split] + kv_recv[...].astype(f32)
    mixed[:, rank_dim : rank_dim + HEAD_DIM] = turned(kv[:, :HEAD_DIM], cosine[:rows], sine[:rows], -1.0).astype(bf16)
    mixed[:, rank_dim + HEAD_DIM :] = kv[:, HEAD_DIM:].astype(bf16)
    size = normed.shape[1] // 8
    cores = []
    for k in range(8):
        at = (k // 4, k // 2 % 2, k % 2)
        grad = lax.dot_general(
            normed[:, k * size : (k + 1) * size], mixed[...], (((0,), (0,)), ((), ())), preferred_element_type=f32
        )
        blocks[at] = grad.astype(bf16).reshape(blocks.shape[3:])
        cores.append(wire.send(blocks.at[at + (every, 1 - c)], core.at[at], 1))
    span = blocks.shape[5]
    width = blocks.shape[6]
    columns = thirds(width)
    orders = ["yxlh", "xylh", "lyxh"]
    sent = [None] * 3

    def index(fixed, block):
        free = [k for k in "yxhl" if k not in fixed]
        at = dict(fixed)
        for position, k in enumerate(reversed(free)):
            at[k] = (block // 2**position) % 2
        return tuple(at[k] for k in "yxhl")

    def over(fixed, body):
        @pl.loop(0, 2 ** (4 - len(fixed)))
        def _(i):
            body(index(fixed, i))

    def pass_on(p, step):
        order = orders[p]
        fixed = {k: own[k] for k in order[:step]}
        bit = order[step]
        src = {**fixed, bit: 1 - own[bit]}
        dst = {**fixed, bit: own[bit]}
        place = lambda at: tuple(at.get(k, every) for k in "yxhl") + (every, columns[p])
        mask = {"y": 16, "x": 8, "h": 4, "l": 2}[bit]
        sent[p] = wire.send(acc.at[place(src)], recv.at[place(dst)], mask)

    arrived(cores)
    for first_side in (True, False):
        for p in range(3):
            bit = orders[p][0]

            def body(at, p=p):
                value = wide(blocks, at + (c, every, columns[p])) + wide(core, at + (every, columns[p]))
                acc[at + (every, columns[p])] = value.astype(bf16)

            over({bit: 1 - own[bit] if first_side else own[bit]}, body)
            if first_side:
                pass_on(p, 0)
    load_normed.wait()
    up_size = up_grad.shape[3]
    for k in range(8):
        tokens_part = normed_v[:, :, :, :, k * up_size : (k + 1) * up_size].reshape(8 * rows, up_size)
        up_grad[k // 4, k // 2 % 2, k % 2] = over_tokens(tokens_part, query_grad[...])
    up_sums = [
        fold_y(wire, lambda yy, hh, k=k: up_grad.at[yy, k, hh], up_recv.at[k], up_passed.at[k], up_kept.at[k])
        for k in range(2)
    ]
    wire.left(cores)
    wire.local(first_weight, blocks).wait()
    weight = blocks[...].reshape(-1, blocks.shape[6])
    normed_grad[...] = lax.dot_general(mixed[...], weight, (((1,), (1,)), ((), ())), preferred_element_type=f32)
    gain_rows[0:1, :] = jnp.zeros((1, gain_rows.shape[1]), f32)

    def norm(r):
        inner, outer = norm_back(tokens[r].astype(f32), gain_in[...], normed_grad[r])
        grad_tokens[r] = (grad_middle[r] + inner).astype(bf16)
        gain_rows[0:1, :] += jnp.sum(outer, axis=0, keepdims=True)

    each_rows(rows, norm)
    q_span = rank_dim // 32
    gains[...] = jnp.zeros_like(gains)
    for n in range(32):
        at = (n // 16, n // 8 % 2, n // 4 % 2, n // 2 % 2, n % 2, 0)
        gains[at + (slice(0, 128),)] = jnp.concatenate(
            [gain_rows[0, n * span : (n + 1) * span], gain_rows[2, n * span : (n + 1) * span]], axis=0
        )
        gains[at + (slice(128, 128 + q_span),)] = gain_rows[1, n * q_span : (n + 1) * q_span]

    def pass_gains(order, step):
        fixed = {k: own[k] for k in order[:step]}
        bit = order[step]
        place = lambda at: tuple(at.get(k, every) for k in "yxhlc")
        mask = {"y": 16, "x": 8, "h": 4, "l": 2, "c": 1}[bit]
        return wire.send(gains.at[place({**fixed, bit: 1 - own[bit]})], gains_recv.at[place({**fixed, bit: own[bit]})], mask)

    def add_gains(order, step):
        fixed = {k: own[k] for k in order[:step]}
        bit = order[step]
        place = lambda at: tuple(at.get(k, every) for k in "yxhlc")
        mine = place({**fixed, bit: own[bit]})
        gains[mine] = gains[mine] + gains_recv[place({**fixed, bit: 1 - own[bit]})]

    gu_h()
    gu_rest()
    do(o_sums)
    o_h = fold_h(wire, o_passed, o_kept, o_far, out_out)
    gain_order = "cyxlh"
    gain_sent = pass_gains(gain_order, 0)
    gain_step = 0
    for step in range(4):
        for p in range(3):
            order = orders[p]
            fixed = {k: own[k] for k in order[:step]}
            bit = order[step]
            sent[p].wait_recv()

            def body(at, p=p, bit=bit, last=step == 3):
                other = tuple(1 - own[k] if k == bit else v for k, v in zip("yxhl", at))
                value = wide(acc, at + (every, columns[p])) + wide(recv, other + (every, columns[p]))
                if last:
                    total[:, columns[p]] = value
                else:
                    acc[at + (every, columns[p])] = value.astype(bf16)

            if step < 3:
                over({**fixed, bit: own[bit], order[step + 1]: 1 - own[order[step + 1]]}, body)
                pass_on(p, step + 1)
                over({**fixed, bit: own[bit], order[step + 1]: own[order[step + 1]]}, body)
            else:
                over({**fixed, bit: own[bit]}, body)
        if gain_step < 5:
            gain_sent.wait_recv()
            add_gains(gain_order, gain_step)
            gain_step += 1
            if gain_step < 5:
                gain_sent = pass_gains(gain_order, gain_step)
        if step == 0:
            for k in range(2):
                do(up_sums[k])
            up_h = [fold_h(wire, up_passed.at[k], up_kept.at[k], up_far.at[k], up_own.at[k]) for k in range(2)]
        if step == 1:
            for k in range(2):
                up_h[k]()
            up_rows = up_back.shape[1]
            up_piece = lambda k: up_own.at[k // 4, pl.ds(pl.multiple_of((k % 4) * up_rows, up_rows), up_rows)]
            up_done = hand_back(wire, up_piece, up_back)
            gu_done()
            unit = gate_out.shape[1] // 32
            units = 4 * unit
            main = units // 128 * 128
            rest = units - main
            for source in range(8):
                tile = gu_back[0, source].astype(f32)
                halves = (
                    tile[:, : main + rest],
                    jnp.concatenate([tile[:, main + 2 * rest :], tile[:, main + rest : main + 2 * rest]], axis=1),
                )
                for half, target in zip(halves, (gate_out, up_out)):
                    for q in range(4):
                        n = q // 2 * 16 + source // 4 * 8 + q % 2 * 4 + source % 4
                        target[:, n * unit : (n + 1) * unit] = half[:, q * unit : (q + 1) * unit]
        if step == 3:
            o_h()
            up_done()
            for head in range(q_up_out.shape[1] // HEAD_DIM):
                hy, hx, hh, hl = head // 8, head // 4 % 2, head // 2 % 2, head % 2
                source = hx * 4 + hl * 2 + hh
                q_up_out[:, head * HEAD_DIM : (head + 1) * HEAD_DIM] = up_back[
                    source, :, hy * HEAD_DIM : (hy + 1) * HEAD_DIM
                ].astype(f32)
    while gain_step < 5:
        gain_sent.wait_recv()
        add_gains(gain_order, gain_step)
        gain_step += 1
        if gain_step < 5:
            gain_sent = pass_gains(gain_order, gain_step)
    gains_out[...] = gains[y, x, h, l, c]
    down_out[...] = total[:, :rank_dim]
    key_out[...] = total[:, rank_dim : rank_dim + HEAD_DIM]
    value_out[...] = total[:, rank_dim + HEAD_DIM :]
    wire.close()


def tail(
    back, normed, compressed, tokens, grad_middle, first_weight, gain_in, gain_q, gain_mid_grad, cosine, sine,
    gu_total, gu_passed, gu_kept, heads, plane_set, query_grad,
):
    rows, width = tokens.shape
    rank_dim = compressed.shape[1]
    near = first_weight.shape[-1]
    span = width // 32
    gu = gu_total.shape
    units = gu[1] * 4
    up = (rank_dim // 8, query_grad.shape[1])
    out_size = heads.shape[2:]
    outs = [
        shaped((rows, width)),
        shaped((span, rank_dim), f32),
        shaped((span, HEAD_DIM), f32),
        shaped((span, HEAD_DIM), f32),
        shaped((1, 256), f32),
        shaped((span, units), f32),
        shaped((span, units), f32),
        shaped((up[0] // 4, 8 * up[1]), f32),
        shaped(out_size, f32),
    ]
    sums = (2, 2, 2, 2, span, near)
    scratch = [
        pltpu.VMEM((span, near), f32),
        pltpu.VMEM((2, 2, 2) + up, bf16),
        pltpu.VMEM(plane_set.shape[:4] + (rank_dim,), bf16),
        pltpu.VMEM((rows, 2 * HEAD_DIM), bf16),
        pltpu.VMEM((rows, 2 * HEAD_DIM), bf16),
        pltpu.VMEM((rows, near), bf16),
        pltpu.VMEM((rows, width), f32),
        pltpu.VMEM((8, width), f32),
        pltpu.VMEM((2, 2, 2, 2, 2, span, near), bf16),
        pltpu.VMEM(sums, bf16),
        pltpu.VMEM(sums, bf16),
        pltpu.VMEM(sums, bf16),
        pltpu.VMEM((2, 2, 2, 2, 2, 1, 256), f32),
        pltpu.VMEM((2, 2, 2, 2, 2, 1, 256), f32),
        pltpu.VMEM(gu, bf16),
        pltpu.VMEM((1, 8, span, gu[1]), bf16),
        pltpu.VMEM((2,) + gu, bf16),
        pltpu.VMEM((2, 2) + up, bf16),
        pltpu.VMEM((2,) + up, bf16),
        pltpu.VMEM((2,) + up, bf16),
        pltpu.VMEM((2,) + up, bf16),
        pltpu.VMEM((2,) + up, bf16),
        pltpu.VMEM((8, up[0] // 4, up[1]), bf16),
        pltpu.VMEM((2,) + out_size, bf16),
        pltpu.VMEM(out_size, bf16),
        pltpu.VMEM(out_size, bf16),
        pltpu.VMEM(out_size, bf16),
    ]
    operands = (
        back, normed, compressed, tokens, grad_middle, first_weight, gain_in, gain_q, gain_mid_grad, cosine, sine,
        gu_total, gu_passed, gu_kept, heads, plane_set, query_grad,
    )
    return moving(
        tail_kernel, 7, outs, operands, scratch + wires(100, 24),
        in_specs=[VMEM] * 5 + [ANY] + [VMEM] * 5 + [ANY, ANY, VMEM, VMEM, ANY, VMEM],
        out_specs=[VMEM] * 9,
        limit=62,
    )


def finish_kernel(*refs):
    count = (len(refs) - 2) // 3
    loads = [pltpu.make_async_copy(refs[k], refs[2 * count + k], refs[-2].at[k]) for k in range(count)]
    for load in loads:
        load.start()
    stores = []
    for k in range(count):
        loads[k].wait()
        stores.append(pltpu.make_async_copy(refs[2 * count + k], refs[count + k], refs[-1].at[k]))
        stores[-1].start()
    landed(stores)


def finish(arrays):
    count = len(arrays)
    return pl.pallas_call(
        finish_kernel,
        out_shape=[shaped(v.shape, v.dtype) for v in arrays],
        in_specs=[ANY] * count,
        out_specs=[ANY] * count,
        scratch_shapes=[pltpu.VMEM(v.shape, v.dtype) for v in arrays] + [pltpu.SemaphoreType.DMA((count,))] * 2,
        compiler_params=pltpu.CompilerParams(vmem_limit_bytes=62 * 1024 * 1024),
        name="finish",
    )(*arrays)


def plane_local(
    tokens,
    positions,
    cotangent,
    norm_in_gain,
    q_down,
    q_gain,
    q_up,
    key_proj,
    value_proj,
    out_proj,
    norm_mid_gain,
    w_gate,
    w_up,
    w_down,
):
    rows, width = tokens.shape
    rank_dim = q_down.shape[1]
    span, q_span = norm_in_gain.shape[0], q_gain.shape[0]

    gains = jnp.concatenate([norm_in_gain, norm_mid_gain, q_gain, jnp.zeros((256 - 2 * span - q_span,), f32)])
    gains = lax.reduce_precision(gains, 8, 7).reshape(1, 256)
    (
        first_weight, up_query, gu_pieces, wo_own, wo_far, wd_own, in_gain, mid_gain, query_gain,
        first_index, query_index, key_index, cosine, sine,
    ) = head(
        q_down, key_proj, value_proj, gains, q_up, w_gate, w_up, out_proj, w_down, positions.reshape(1, rows)
    )
    up_query = up_query.reshape(rank_dim, 2 * HEAD_DIM)

    plane_set, out_weight, gu_set, wd_far, normed, compressed = pack(
        tokens, in_gain, query_gain, first_weight.reshape(width, -1), cosine, sine, wo_own, wo_far, gu_pieces, wd_own
    )
    out_weight = out_weight.reshape(2 * HEAD_DIM, width)
    queries, attended, lse, middle, plane_mid, plane_cotangent, gu_zero, gu_one, down_weight = attend(
        plane_set, up_query, out_weight, cosine, sine, key_index, query_index, first_index, tokens, mid_gain, cotangent,
        gu_set, wd_own, wd_far,
    )
    hidden, gu_grads, final_parts, normed_grad = feed(plane_mid, plane_cotangent, gu_zero, gu_one, down_weight)
    flat = lambda blocks: blocks.reshape(8 * rows, -1)
    grad_middle, mid_gain_grad, plane_branch, output, grad_down, gu_passed, gu_zero_grad, gu_one_grad = branch_step(
        normed_grad, final_parts.reshape(2, 2, 2, rows, width), middle, cotangent, mid_gain, flat(plane_mid), hidden,
        gu_grads, flat(plane_cotangent),
    )
    query_grad, back, gu_total, gu_passed, gu_kept, out_grad = attend_back(
        plane_set, plane_branch, queries, attended, lse, up_query, out_weight, cosine, sine,
        key_index, query_index, first_index, gu_passed, gu_zero_grad, gu_one_grad,
    )
    grad_tokens, grad_q_down, grad_key, grad_value, grad_gains, grad_gate, grad_up, grad_q_up, grad_out = tail(
        back, normed, compressed, tokens, grad_middle, first_weight, in_gain, query_gain, mid_gain_grad,
        cosine, sine, gu_total, gu_passed, gu_kept, out_grad, plane_set, query_grad,
    )
    output, grad_tokens, grad_q_down, grad_q_up, grad_key, grad_value, grad_out, grad_gate, grad_up, grad_down = finish(
        (output, grad_tokens, grad_q_down, grad_q_up, grad_key, grad_value, grad_out, grad_gate, grad_up, grad_down)
    )
    return (
        output,
        grad_tokens,
        grad_gains[0, :span],
        grad_q_down,
        grad_gains[0, 2 * span : 2 * span + q_span],
        grad_q_up,
        grad_key,
        grad_value,
        grad_out,
        grad_gains[0, span : 2 * span],
        grad_gate,
        grad_up,
        grad_down,
    )


def solution(mesh):
    return jax.shard_map(
        plane_local if dict(mesh.shape) == {"dp": 4, "seq": 8} else local,
        mesh=mesh,
        in_specs=(
            P(("dp", "seq"), None),
            P(("dp", "seq")),
            P(("dp", "seq"), None),
            P(("dp", "seq")),
            P(("dp", "seq"), None),
            P(("dp", "seq")),
            P(("dp", "seq"), None),
            P(("dp", "seq"), None),
            P(("dp", "seq"), None),
            P(("dp", "seq"), None),
            P(("dp", "seq")),
            P(("dp", "seq"), None),
            P(("dp", "seq"), None),
            P(("dp", "seq"), None),
        ),
        out_specs=(
            P(("dp", "seq"), None),
            P(("dp", "seq"), None),
            P(("dp", "seq")),
            P(("dp", "seq"), None),
            P(("dp", "seq")),
            P(("dp", "seq"), None),
            P(("dp", "seq"), None),
            P(("dp", "seq"), None),
            P(("dp", "seq"), None),
            P(("dp", "seq")),
            P(("dp", "seq"), None),
            P(("dp", "seq"), None),
            P(("dp", "seq"), None),
        ),
        check_vma=False,
    )
```

```python
import math

import jax
import jax.numpy as jnp
from jax import lax
from jax.experimental import pallas as pl
from jax.experimental.pallas import tpu as pltpu
from jax.sharding import PartitionSpec as P

HEADS = 16
HEAD_DIM = 256


epsilon = 1e-05
rope_base = 10000.0
masked_score = -1e30


def rms_scale(values):
    return lax.rsqrt(jnp.mean(values * values, axis=-1, keepdims=True) + epsilon)


def rotary(values, places, sign):
    half = values.shape[-1] // 2
    freqs = rope_base ** (-(2.0 * jnp.arange(half).astype(jnp.float32)) / values.shape[-1])
    angles = places.astype(jnp.float32)[:, None] * freqs[None, :]
    cosine = jnp.cos(angles)[:, None, :]
    sine = jnp.sin(angles)[:, None, :]
    first = values[..., :half]
    second = values[..., half:]
    return jnp.concatenate(
        [first * cosine - sign * second * sine, sign * first * sine + second * cosine], axis=-1
    )


def norm_backward(inputs, scale, gain, grad_out):
    weighted = gain * grad_out
    grad_in = scale * weighted - inputs * scale * scale * scale * jnp.mean(
        weighted * inputs, axis=-1, keepdims=True
    )
    grad_gain = jnp.sum(grad_out * inputs * scale, axis=0)
    return (grad_in, grad_gain)


def add_rows(total, block, start):
    current = lax.dynamic_slice_in_dim(total, start, block.shape[0], 0)
    return lax.dynamic_update_slice_in_dim(total, current + block, start, 0)


def local(
    tokens,
    positions,
    cotangent,
    norm_in_gain,
    q_down,
    q_gain,
    q_up,
    key_proj,
    value_proj,
    out_proj,
    norm_mid_gain,
    w_gate,
    w_up,
    w_down,
):
    width = tokens.shape[0]
    scale = 1.0 / math.sqrt(HEAD_DIM)
    attention_set = (
        lax.all_gather(norm_in_gain.astype(jnp.bfloat16), ("dp", "seq"), axis=0, tiled=True),
        lax.all_gather(q_down.astype(jnp.bfloat16), ("dp", "seq"), axis=0, tiled=True),
        lax.all_gather(q_gain.astype(jnp.bfloat16), ("dp", "seq"), axis=0, tiled=True),
        lax.all_gather(q_up.astype(jnp.bfloat16), ("dp", "seq"), axis=0, tiled=True),
        lax.all_gather(key_proj.astype(jnp.bfloat16), ("dp", "seq"), axis=0, tiled=True),
        lax.all_gather(value_proj.astype(jnp.bfloat16), ("dp", "seq"), axis=0, tiled=True),
        lax.all_gather(out_proj.astype(jnp.bfloat16), ("dp", "seq"), axis=0, tiled=True),
    )
    feed_set = (
        lax.all_gather(norm_mid_gain.astype(jnp.bfloat16), ("dp", "seq"), axis=0, tiled=True),
        lax.all_gather(w_gate.astype(jnp.bfloat16), ("dp", "seq"), axis=0, tiled=True),
        lax.all_gather(w_up.astype(jnp.bfloat16), ("dp", "seq"), axis=0, tiled=True),
        lax.all_gather(w_down.astype(jnp.bfloat16), ("dp", "seq"), axis=0, tiled=True),
    )
    in_gain = attention_set[0].astype(jnp.float32)
    query_gain = attention_set[2].astype(jnp.float32)
    inputs = tokens.astype(jnp.float32)
    in_scale = rms_scale(inputs)
    normed = (inputs * in_scale * in_gain).astype(jnp.bfloat16)
    compressed = jnp.dot(normed, attention_set[1], preferred_element_type=jnp.float32)
    query_scale = rms_scale(compressed)
    compressed_normed = (compressed * query_scale * query_gain).astype(jnp.bfloat16)
    queries_raw = jnp.dot(
        compressed_normed, attention_set[3], preferred_element_type=jnp.float32
    ).reshape(width, HEADS, HEAD_DIM)
    queries = rotary(queries_raw, positions, 1.0).astype(jnp.bfloat16)
    keys_raw = jnp.dot(normed, attention_set[4], preferred_element_type=jnp.float32)
    keys = rotary(keys_raw[:, None, :], positions, 1.0)[:, 0, :].astype(jnp.bfloat16)
    values = jnp.dot(normed, attention_set[5], preferred_element_type=jnp.float32).astype(
        jnp.bfloat16
    )
    query_index = lax.axis_index("seq") * width + jnp.arange(width, dtype=jnp.int32)
    first_index = query_index - positions

    def visibility(key_start):
        key_index = key_start + jnp.arange(width, dtype=jnp.int32)
        seen = (key_index[None, :] >= first_index[:, None]) & (
            key_index[None, :] <= query_index[:, None]
        )
        return seen[:, None, :]

    start_state = (
        jnp.full((width, HEADS), masked_score, jnp.float32),
        jnp.zeros((width, HEADS), jnp.float32),
        jnp.zeros((width, HEADS, HEAD_DIM), jnp.float32),
    )
    carry = start_state
    piece = (
        lax.all_gather(keys, "seq", axis=0, tiled=True),
        lax.all_gather(values, "seq", axis=0, tiled=True),
    )
    blocks = piece[0].shape[0] // width
    key_blocks = piece[0].reshape(blocks, width, HEAD_DIM)
    value_blocks = piece[1].reshape(blocks, width, HEAD_DIM)

    def forward_one_block(state, item):
        key_block, value_block, number = item
        key_start = number * width
        top, total, accum = state
        seen = visibility(key_start)
        scores = (
            jnp.einsum("thd,kd->thk", queries, key_block, preferred_element_type=jnp.float32)
            * scale
        )
        scores = jnp.where(seen, scores, masked_score)
        new_top = jnp.maximum(top, jnp.max(scores, axis=-1))
        weights = jnp.where(seen, jnp.exp(scores - new_top[..., None]), 0.0)
        decay = jnp.exp(top - new_top)
        total = total * decay + jnp.sum(weights, axis=-1)
        accum = accum * decay[..., None] + jnp.einsum(
            "thk,kd->thd",
            weights.astype(jnp.bfloat16),
            value_block,
            preferred_element_type=jnp.float32,
        )
        state = (new_top, total, accum)
        return (state, None)

    carry, _ = lax.scan(
        forward_one_block, carry, (key_blocks, value_blocks, jnp.arange(blocks, dtype=jnp.int32))
    )
    top, total, accum = carry
    attended_full = accum / total[..., None]
    log_total = top + jnp.log(total)
    attended = attended_full.reshape(width, HEADS * HEAD_DIM).astype(jnp.bfloat16)
    middle = inputs + jnp.dot(attended, attention_set[6], preferred_element_type=jnp.float32)
    mid_gain = feed_set[0].astype(jnp.float32)
    mid_scale = rms_scale(middle)
    normed_mid = (middle * mid_scale * mid_gain).astype(jnp.bfloat16)
    gate = jnp.dot(normed_mid, feed_set[1], preferred_element_type=jnp.float32)
    upper = jnp.dot(normed_mid, feed_set[2], preferred_element_type=jnp.float32)
    sigmoid_gate = jax.nn.sigmoid(gate)
    silu_gate = gate * sigmoid_gate
    hidden = (silu_gate * upper).astype(jnp.bfloat16)
    output = (middle + jnp.dot(hidden, feed_set[3], preferred_element_type=jnp.float32)).astype(
        jnp.bfloat16
    )
    feed_back = (
        lax.all_gather(norm_mid_gain.astype(jnp.bfloat16), ("dp", "seq"), axis=0, tiled=True),
        lax.all_gather(w_gate.astype(jnp.bfloat16), ("dp", "seq"), axis=0, tiled=True),
        lax.all_gather(w_up.astype(jnp.bfloat16), ("dp", "seq"), axis=0, tiled=True),
        lax.all_gather(w_down.astype(jnp.bfloat16), ("dp", "seq"), axis=0, tiled=True),
    )
    grad_out_full = cotangent.astype(jnp.float32)
    grad_down = jnp.einsum("tf,td->fd", hidden, cotangent, preferred_element_type=jnp.float32)
    grad_hidden = jnp.einsum(
        "td,fd->tf", cotangent, feed_back[3], preferred_element_type=jnp.float32
    )
    grad_gate = (grad_hidden * upper * sigmoid_gate * (1.0 + gate * (1.0 - sigmoid_gate))).astype(
        jnp.bfloat16
    )
    grad_upper = (grad_hidden * silu_gate).astype(jnp.bfloat16)
    grad_gate_weight = jnp.einsum(
        "td,tf->df", normed_mid, grad_gate, preferred_element_type=jnp.float32
    )
    grad_up_weight = jnp.einsum(
        "td,tf->df", normed_mid, grad_upper, preferred_element_type=jnp.float32
    )
    grad_normed_mid = jnp.einsum(
        "tf,df->td", grad_gate, feed_back[1], preferred_element_type=jnp.float32
    ) + jnp.einsum("tf,df->td", grad_upper, feed_back[2], preferred_element_type=jnp.float32)
    grad_mid_norm, grad_mid_gain = norm_backward(
        middle, mid_scale, feed_back[0].astype(jnp.float32), grad_normed_mid
    )
    grad_middle = grad_out_full + grad_mid_norm
    feed_grads = (
        lax.psum_scatter(grad_mid_gain, ("dp", "seq"), scatter_dimension=0, tiled=True),
        lax.psum_scatter(grad_gate_weight, ("dp", "seq"), scatter_dimension=0, tiled=True),
        lax.psum_scatter(grad_up_weight, ("dp", "seq"), scatter_dimension=0, tiled=True),
        lax.psum_scatter(grad_down, ("dp", "seq"), scatter_dimension=0, tiled=True),
    )
    attention_back = (
        lax.all_gather(norm_in_gain.astype(jnp.bfloat16), ("dp", "seq"), axis=0, tiled=True),
        lax.all_gather(q_down.astype(jnp.bfloat16), ("dp", "seq"), axis=0, tiled=True),
        lax.all_gather(q_gain.astype(jnp.bfloat16), ("dp", "seq"), axis=0, tiled=True),
        lax.all_gather(q_up.astype(jnp.bfloat16), ("dp", "seq"), axis=0, tiled=True),
        lax.all_gather(key_proj.astype(jnp.bfloat16), ("dp", "seq"), axis=0, tiled=True),
        lax.all_gather(value_proj.astype(jnp.bfloat16), ("dp", "seq"), axis=0, tiled=True),
        lax.all_gather(out_proj.astype(jnp.bfloat16), ("dp", "seq"), axis=0, tiled=True),
    )
    branch_grad = grad_middle.astype(jnp.bfloat16)
    grad_output_weight = jnp.einsum(
        "ta,td->ad", attended, branch_grad, preferred_element_type=jnp.float32
    )
    grad_attended = (
        jnp.einsum("td,ad->ta", branch_grad, attention_back[6], preferred_element_type=jnp.float32)
        .reshape(width, HEADS, HEAD_DIM)
        .astype(jnp.bfloat16)
    )
    delta = jnp.sum(grad_attended.astype(jnp.float32) * attended_full, axis=-1)
    group_rows = width * lax.axis_size("seq")
    back_state = (
        jnp.zeros((width, HEADS, HEAD_DIM), jnp.float32),
        jnp.zeros((group_rows, HEAD_DIM), jnp.float32),
        jnp.zeros((group_rows, HEAD_DIM), jnp.float32),
    )
    carry = back_state
    piece = (
        lax.all_gather(keys, "seq", axis=0, tiled=True),
        lax.all_gather(values, "seq", axis=0, tiled=True),
    )
    blocks = piece[0].shape[0] // width
    key_blocks = piece[0].reshape(blocks, width, HEAD_DIM)
    value_blocks = piece[1].reshape(blocks, width, HEAD_DIM)

    def backward_one_block(state, item):
        key_block, value_block, number = item
        key_start = number * width
        grad_query, grad_keys, grad_values = state
        seen = visibility(key_start)
        scores = (
            jnp.einsum("thd,kd->thk", queries, key_block, preferred_element_type=jnp.float32)
            * scale
        )
        probs = jnp.where(seen, jnp.exp(scores - log_total[..., None]), 0.0)
        grad_value_block = jnp.einsum(
            "thk,thd->kd",
            probs.astype(jnp.bfloat16),
            grad_attended,
            preferred_element_type=jnp.float32,
        )
        grad_probs = jnp.einsum(
            "thd,kd->thk", grad_attended, value_block, preferred_element_type=jnp.float32
        )
        grad_scores = (probs * (grad_probs - delta[..., None]) * scale).astype(jnp.bfloat16)
        grad_query = grad_query + jnp.einsum(
            "thk,kd->thd", grad_scores, key_block, preferred_element_type=jnp.float32
        )
        grad_key_block = jnp.einsum(
            "thk,thd->kd", grad_scores, queries, preferred_element_type=jnp.float32
        )
        state = (
            grad_query,
            add_rows(grad_keys, grad_key_block, key_start),
            add_rows(grad_values, grad_value_block, key_start),
        )
        return (state, None)

    carry, _ = lax.scan(
        backward_one_block, carry, (key_blocks, value_blocks, jnp.arange(blocks, dtype=jnp.int32))
    )
    grad_query, grad_keys, grad_values = carry
    local_key_grad, local_value_grad = (
        lax.psum_scatter(
            grad_keys.astype(jnp.bfloat16), "seq", scatter_dimension=0, tiled=True
        ).astype(jnp.float32),
        lax.psum_scatter(
            grad_values.astype(jnp.bfloat16), "seq", scatter_dimension=0, tiled=True
        ).astype(jnp.float32),
    )
    grad_key_pre = rotary(local_key_grad[:, None, :], positions, -1.0)[:, 0, :].astype(jnp.bfloat16)
    grad_value_pre = local_value_grad.astype(jnp.bfloat16)
    grad_query_pre = (
        rotary(grad_query, positions, -1.0).reshape(width, HEADS * HEAD_DIM).astype(jnp.bfloat16)
    )
    grad_up_query = jnp.einsum(
        "tr,ta->ra", compressed_normed, grad_query_pre, preferred_element_type=jnp.float32
    )
    grad_compressed_normed = jnp.einsum(
        "ta,ra->tr", grad_query_pre, attention_back[3], preferred_element_type=jnp.float32
    )
    grad_compressed, grad_query_gain = norm_backward(
        compressed, query_scale, attention_back[2].astype(jnp.float32), grad_compressed_normed
    )
    grad_compressed = grad_compressed.astype(jnp.bfloat16)
    grad_down_weight = jnp.einsum(
        "td,tr->dr", normed, grad_compressed, preferred_element_type=jnp.float32
    )
    grad_key_weight = jnp.einsum(
        "td,te->de", normed, grad_key_pre, preferred_element_type=jnp.float32
    )
    grad_value_weight = jnp.einsum(
        "td,te->de", normed, grad_value_pre, preferred_element_type=jnp.float32
    )
    grad_normed = jnp.einsum(
        "tr,dr->td", grad_compressed, attention_back[1], preferred_element_type=jnp.float32
    )
    grad_normed = grad_normed + jnp.einsum(
        "te,de->td", grad_key_pre, attention_back[4], preferred_element_type=jnp.float32
    )
    grad_normed = grad_normed + jnp.einsum(
        "te,de->td", grad_value_pre, attention_back[5], preferred_element_type=jnp.float32
    )
    grad_in_norm, grad_in_gain = norm_backward(
        inputs, in_scale, attention_back[0].astype(jnp.float32), grad_normed
    )
    grad_tokens = (grad_middle + grad_in_norm).astype(jnp.bfloat16)
    attention_grads = (
        lax.psum_scatter(grad_in_gain, ("dp", "seq"), scatter_dimension=0, tiled=True),
        lax.psum_scatter(grad_down_weight, ("dp", "seq"), scatter_dimension=0, tiled=True),
        lax.psum_scatter(grad_query_gain, ("dp", "seq"), scatter_dimension=0, tiled=True),
        lax.psum_scatter(grad_up_query, ("dp", "seq"), scatter_dimension=0, tiled=True),
        lax.psum_scatter(grad_key_weight, ("dp", "seq"), scatter_dimension=0, tiled=True),
        lax.psum_scatter(grad_value_weight, ("dp", "seq"), scatter_dimension=0, tiled=True),
        lax.psum_scatter(grad_output_weight, ("dp", "seq"), scatter_dimension=0, tiled=True),
    )
    return (
        output,
        grad_tokens,
        attention_grads[0],
        attention_grads[1],
        attention_grads[2],
        attention_grads[3],
        attention_grads[4],
        attention_grads[5],
        attention_grads[6],
        feed_grads[0],
        feed_grads[1],
        feed_grads[2],
        feed_grads[3],
    )


bf16 = jnp.bfloat16
f32 = jnp.float32
ANY = pl.BlockSpec(memory_space=pl.ANY)
VMEM = pl.BlockSpec(memory_space=pltpu.VMEM)
PLANE = [j // 4 * 8 + j % 4 for j in range(1, 8)]
LINKS = [16, 8, 4, 2, 1]


def flip(number, bits):
    bit = 1
    while bit <= bits:
        if bits & bit:
            number = number + bit - 2 * bit * ((number // bit) % 2)
        bit *= 2
    return number


def coordinates():
    dp = lax.axis_index("dp")
    seq = lax.axis_index("seq")
    return dp // 2, dp % 2, seq // 4, (seq // 2) % 2, seq % 2


def partner(mask):
    return flip(lax.axis_index("dp"), mask // 8), flip(lax.axis_index("seq"), mask % 8)


PENDING = []


def greet(masks):
    barrier = pltpu.get_barrier_semaphore()
    for mask in masks:
        pl.semaphore_signal(barrier, inc=1, device_id=partner(mask), device_id_type=pl.DeviceIdType.MESH)
    pl.semaphore_wait(barrier, len(masks))
    while PENDING:
        PENDING.pop().wait()


class Wire:
    def __init__(self, send_sem, recv_sem, local_sem):
        self.send_sem, self.recv_sem, self.local_sem = send_sem, recv_sem, local_sem
        self.copies = []
        self.gone = []
        self.locals = 0

    def send(self, src, dst, mask):
        copy = self.later(src, dst, mask)
        copy.start()
        return copy

    def later(self, src, dst, mask):
        k = len(self.copies)
        copy = pltpu.make_async_remote_copy(
            src_ref=src,
            dst_ref=dst,
            send_sem=self.send_sem.at[k],
            recv_sem=self.recv_sem.at[k],
            device_id=partner(mask),
            device_id_type=pl.DeviceIdType.MESH,
        )
        self.copies.append(copy)
        return copy

    def local(self, src, dst):
        copy = self.later_local(src, dst)
        copy.start()
        return copy

    def later_local(self, src, dst):
        copy = pltpu.make_async_copy(src, dst, self.local_sem.at[self.locals])
        self.locals += 1
        return copy

    def left(self, copies):
        for copy in copies:
            copy.wait_send()
        self.gone += copies

    def close(self):
        for copy in self.copies:
            if not any(copy is other for other in self.gone):
                copy.wait_send()


def wires(remote, local):
    return [pltpu.SemaphoreType.DMA((remote,)), pltpu.SemaphoreType.DMA((remote,)), pltpu.SemaphoreType.DMA((local,))]


def arrived(copies):
    for copy in copies:
        copy.wait_recv()


def landed(copies):
    for copy in copies:
        copy.wait()


def moving(kernel, number, outs, operands, scratch, in_specs=None, out_specs=None, limit=56):
    in_specs = list(in_specs or [ANY] * len(operands))
    early = [k for k, spec in enumerate(in_specs) if spec is VMEM and operands[k].size >= 1 << 14]
    for k in early:
        in_specs[k] = ANY

    def whole(*refs):
        refs, buffers, sems = list(refs[: -len(early) - 1]), refs[-len(early) - 1 : -1], refs[-1]
        for n, (k, buffer) in enumerate(zip(early, buffers)):
            copy = pltpu.make_async_copy(refs[k], buffer, sems.at[n])
            copy.start()
            PENDING.append(copy)
            refs[k] = buffer
        kernel(*refs)

    if early:
        buffers = [pltpu.VMEM(operands[k].shape, operands[k].dtype) for k in early]
        scratch = list(scratch) + buffers + [pltpu.SemaphoreType.DMA((len(early),))]
    return pl.pallas_call(
        whole if early else kernel,
        out_shape=outs,
        in_specs=in_specs,
        out_specs=out_specs or [ANY] * len(outs),
        scratch_shapes=scratch,
        compiler_params=pltpu.CompilerParams(
            collective_id=number, has_side_effects=True, vmem_limit_bytes=limit * 1024 * 1024
        ),
        cost_estimate=pl.CostEstimate(flops=0, bytes_accessed=100_000_000, transcendentals=0),
        name=kernel.__name__,
    )(*operands)


def shaped(shape, dtype=bf16):
    return jax.ShapeDtypeStruct(tuple(shape), dtype)


def each_rows(rows, body, step=16):
    @pl.loop(0, rows // step)
    def _(i):
        body(pl.ds(pl.multiple_of(i * step, step), step))


def wide(ref, where):
    return ref[where].astype(f32)


def routes(rows, pieces, direct):
    size = rows // pieces
    return [(pl.ds(i * size, size), "xl" if i < direct else "lx") for i in range(pieces)]


def plane_gather(wire, block, out, own, ways):
    links = {"x": (out.at[1, 0, 0], out.at[1, 0, 1], 8), "l": (out.at[0, 1, 0], out.at[0, 1, 1], 2)}
    far, far_core = out.at[1, 1, 0], out.at[1, 1, 1]
    ordered = [k for k in range(len(ways)) if ways[k][1] == "xl"] + [k for k in range(len(ways)) if ways[k][1] == "lx"]
    came = {}
    for turn in (0, 1):
        for k in ordered:
            rows, way = ways[k]
            target, _, mask = links[way[turn]]
            came[way[turn], k] = wire.send(block.at[rows], target.at[rows], mask)
    cores = [wire.send(block, out.at[0, 0, 1], 1)]
    mine = wire.local(block, own) if own is not None else None
    diagonal = {}

    def step(k):
        rows, way = ways[k]
        target, core, _ = links[way[0]]
        came[way[0], k].wait_recv()
        diagonal[k] = wire.send(target.at[rows], far.at[rows], links[way[1]][2])
        cores.append(wire.send(target.at[rows], core.at[rows], 1))

    def finish():
        for k in ordered:
            rows, way = ways[k]
            target, core, _ = links[way[1]]
            came[way[1], k].wait_recv()
            cores.append(wire.send(target.at[rows], core.at[rows], 1))
        for k in ordered:
            rows, way = ways[k]
            diagonal[k].wait_recv()
            cores.append(wire.send(far.at[rows], far_core.at[rows], 1))
        if mine is not None:
            mine.wait()
        arrived(cores)

    return [lambda k=k: step(k) for k in ordered], finish


ARRIVAL = [(1, 1), (1, 0), (0, 1), (0, 0)]


def plane_reduce(wire, parts, out, kept, from_c, send_one, recv_one, send_two, recv_two, ways, load=True):
    cores = {}
    loads = {}
    masks = {"x": 8, "l": 2}
    beside = {"xl": (1, 0), "lx": (0, 1)}
    after = {"xl": (0, 1), "lx": (1, 0)}
    came = {}
    passed = {}

    def give(k):
        cores[k] = wire.send(parts.at[k[0], k[1], 1], from_c.at[k[0], k[1]], 1)
        if load:
            loads[k] = wire.local(parts.at[k[0], k[1], 0], kept.at[k[0], k[1]])

    def pair(k, r):
        return wide(kept.at[k[0], k[1]], r) + wide(from_c.at[k[0], k[1]], r)

    def within(rows, body):
        @pl.loop(0, rows.size // 16)
        def _(i):
            body(pl.ds(pl.multiple_of(rows.start + i * 16, 16), 16))

    def put(slot, k, j):
        rows, way = ways[j]

        def fill(r):
            send_one[slot, r] = pair(k, r).astype(bf16)

        within(rows, fill)
        came[slot, j] = wire.send(send_one.at[slot, rows], recv_one.at[slot, rows], masks[way[0]])

    def arrive(k):
        if load:
            loads[k].wait()
        cores[k].wait_recv()
        for j in range(len(ways)):
            if k == (1, 1):
                put(0, k, j)
            elif beside[ways[j][1]] == k:
                put(1, k, j)

    def step(j):
        rows, way = ways[j]
        came[0, j].wait_recv()

        def fill(r):
            send_two[r] = (pair(after[way], r) + wide(recv_one.at[0], r)).astype(bf16)

        within(rows, fill)
        passed[j] = wire.send(send_two.at[rows], recv_two.at[rows], masks[way[1]])

    def finish():
        for j, (rows, way) in enumerate(ways):
            came[1, j].wait_recv()
            passed[j].wait_recv()

            def fill(r):
                out[r] = pair((0, 0), r) + wide(recv_one.at[1], r) + wide(recv_two, r)

            within(rows, fill)

    return give, arrive, [lambda j=j: step(j) for j in range(len(ways))], finish


def each(action, items=ARRIVAL):
    for item in items:
        action(item)


def do(steps):
    for step in steps:
        step()


def reduce_scratch(rows, width):
    return [
        pltpu.VMEM((2, 2, rows, width), bf16),
        pltpu.VMEM((2, 2, rows, width), bf16),
        pltpu.VMEM((2, rows, width), bf16),
        pltpu.VMEM((2, rows, width), bf16),
        pltpu.VMEM((rows, width), bf16),
        pltpu.VMEM((rows, width), bf16),
    ]


def over_y(wire, block, place, side):
    y, x, h, l, c = coordinates()
    hh = h if side == 0 else 1 - h
    mine = wire.local(block, place(y, hh))
    sent = wire.send(block, place(y, hh), 16)

    def finish():
        mine.wait()
        sent.wait_recv()

    return finish


def thirds(width):
    main = (width * 5 // 12) // 128 * 128
    return [pl.ds(0, main), pl.ds(main, main), pl.ds(2 * main, width - 2 * main)]


def head_kernel(
    q_down, key, value, gains, q_up, gate, up, out_proj, w_down, places,
    first_out, upq_out, gu, wo_out, wo_far, wd_out, in_gain, mid_gain, q_gain, first_index, query_index, key_index,
    cosine, sine, first, upq, staged, gains_out, places_out, send_sem, recv_sem, local_sem,
):
    y, x, h, l, c = coordinates()
    rank = x * 4 + l * 2 + c
    wire = Wire(send_sem, recv_sem, local_sem)
    greet([16, 4] + PLANE)
    r1, r2 = q_down.shape[1], q_down.shape[1] + key.shape[1]
    first[:, :r1] = q_down[...].astype(bf16)
    first[:, r1:r2] = key[...].astype(bf16)
    first[:, r2:] = value[...].astype(bf16)
    width = first.shape[1]
    a, b, d = thirds(width)
    mine = [wire.local(first, first_out.at[y, x, h, l, c]), wire.local(gains, gains_out.at[y, x, h, l, c])]
    one = [wire.send(first.at[:, p], first_out.at[y, x, h, l, c, :, p], 4) for p in (a, b, d)]
    gain = wire.send(gains, gains_out.at[y, x, h, l, c], 4)
    place = [wire.send(places, places_out.at[j], PLANE[j - 1]) for j in range(1, 8)]
    place_mine = wire.local(places, places_out.at[0])
    heads = q_up.shape[1] // HEAD_DIM
    for head in range(heads):
        hy, hx, hh, hl = head // 8, head // 4 % 2, head // 2 % 2, head % 2
        target = hx * 4 + hl * 2 + hh
        upq[target, :, hy * HEAD_DIM : (hy + 1) * HEAD_DIM] = q_up[:, head * HEAD_DIM : (head + 1) * HEAD_DIM].astype(bf16)
    up_rows = upq.shape[1]
    up_place = lambda: upq_out.at[y, x, h, pl.ds((l * 2 + c) * up_rows, up_rows), :]
    up_mine = wire.local(upq.at[rank], up_place())
    up_sent = [wire.send(upq.at[flip(rank, j)], up_place(), PLANE[j - 1]) for j in range(1, 8)]
    wo_out[...] = out_proj[...].astype(bf16)
    piece = gate.shape[1] // 32
    size = 4 * piece
    main = size // 128 * 128
    for target in range(8):
        for where, weight in ((0, gate), (1, up)):
            for q in range(4):
                n = q // 2 * 16 + target // 4 * 8 + q % 2 * 4 + target % 4
                staged[where, :, q * piece : (q + 1) * piece] = weight[:, n * piece : (n + 1) * piece]
        gu[target, :, :main] = staged[0, :, :main].astype(bf16)
        rest = size - main
        both = jnp.concatenate([staged[0, :, main : main + rest], staged[1, :, main : main + rest]], axis=1)
        gu[target, :, main : main + 2 * rest] = both.astype(bf16)
        gu[target, :, main + 2 * rest :] = staged[1, :, :main].astype(bf16)
    wd_out[...] = w_down[...].astype(bf16)
    landed(mine)

    every = slice(None)

    def step(held, columns, mask):
        at = tuple(every if k in held else v for k, v in zip("yxhlc", (y, x, h, l, c)))
        if columns is None:
            return wire.send(gains_out.at[at], gains_out.at[at], mask)
        place = first_out.at[at + (every, columns)]
        return wire.send(place, place, mask)

    def last(held, bit, columns):
        at = {k: every if k in held else v for k, v in zip("yxhlc", (y, x, h, l, c))}
        at[bit] = 1 - dict(zip("yxhlc", (y, x, h, l, c)))[bit]
        place = first_out.at[tuple(at[k] for k in "yxhlc") + (every, columns)]
        return wire.send(place, place, 1)

    bits = {"y": 16, "x": 8, "h": 4, "l": 2}
    orders = [("hlxy", a), ("hlyx", b), ("hxyl", d)]
    sent = one
    for k in range(1, 4):
        following = []
        for (order, columns), copy in zip(orders, sent):
            copy.wait_recv()
            following.append(step(order[:k], columns, bits[order[k]]))
        sent = following
        gain.wait_recv()
        gain = step("hlxy"[:k], None, bits["hlxy"[k]])
        if k == 1:
            up_mine.wait()
            arrived(up_sent)
            up_h = wire.send(upq_out.at[y, :, h], upq_out.at[y, :, h], 4)
            up_y = [wire.send(upq_out.at[y, :, h], upq_out.at[y, :, h], 16)]
            wo_sent = wire.send(wo_out, wo_far, 4)
        if k == 3:
            five = [step(order[:3], columns, 1) for order, columns in orders]
    place_mine.wait()
    arrived(place)
    rows = places.shape[1]
    half = HEAD_DIM // 2
    powers = lax.broadcasted_iota(jnp.int32, (rows, half), 1).astype(f32)
    freqs = jnp.exp(powers * (-2.0 / HEAD_DIM * math.log(rope_base)))
    eye = lax.broadcasted_iota(jnp.int32, (rows, rows), 0) == lax.broadcasted_iota(jnp.int32, (rows, rows), 1)
    index = []
    for j in range(8):
        place = jnp.sum(jnp.where(eye, places_out[j].astype(f32), 0.0), axis=1, keepdims=True)
        angles = place * freqs
        cosine[j * rows : (j + 1) * rows] = jnp.cos(angles)
        sine[j * rows : (j + 1) * rows] = jnp.sin(angles)
        b, d = j // 2 % 2, j % 2
        block = (l + b - 2 * l * b) * 2 + (c + d - 2 * c * d)
        start = (h * 4 + block) * rows
        index.append(start + lax.broadcasted_iota(jnp.int32, (1, rows), 1))
        side = h if j < 4 else 1 - h
        key_index[j * rows : (j + 1) * rows] = (side * 4 + block) * rows + lax.broadcasted_iota(jnp.int32, (rows, 1), 0)
    index = jnp.concatenate(index, axis=1)
    query_index[...] = index
    first_index[...] = index - jnp.concatenate([places_out[j] for j in range(8)], axis=1)
    up_h.wait_recv()
    up_y += [wire.send(upq_out.at[y, :, 1 - h], upq_out.at[y, :, 1 - h], 16)]
    gain.wait_recv()
    gain = step("hlxy", None, 1)
    for (order, columns), copy in zip(orders, sent):
        copy.wait_recv()
        five.append(last(order[:3], order[3], columns))
    gain.wait_recv()
    span, q_span = in_gain.shape[1] // 32, q_gain.shape[1] // 32
    for n in range(32):
        row = gains_out[n // 16, n // 8 % 2, n // 4 % 2, n // 2 % 2, n % 2]
        in_gain[:, n * span : (n + 1) * span] = row[:, :span]
        mid_gain[:, n * span : (n + 1) * span] = row[:, span : 2 * span]
        q_gain[:, n * q_span : (n + 1) * q_span] = row[:, 2 * span : 2 * span + q_span]
    arrived(five + up_y + [wo_sent])
    wire.close()


def head(q_down, key, value, gains, q_up, gate, up, out_proj, w_down, places):
    rows = q_down.shape[0]
    count = 8 * places.shape[1]
    width = q_down.shape[1] + 2 * key.shape[1]
    columns = gate.shape[1] // 4
    slice_size = gate.shape[1] // 8
    outs = [
        shaped((2, 2, 2, 2, 2, rows, width)),
        shaped((2, 2, 2, 4 * q_up.shape[0], 2 * HEAD_DIM)),
        shaped((8, rows, columns)),
        shaped(out_proj.shape),
        shaped(out_proj.shape),
        shaped(w_down.shape),
        shaped((1, 32 * rows), f32),
        shaped((1, 32 * rows), f32),
        shaped((1, q_down.shape[1]), f32),
        shaped((1, count), jnp.int32),
        shaped((1, count), jnp.int32),
        shaped((count, 1), jnp.int32),
        shaped((count, HEAD_DIM // 2), f32),
        shaped((count, HEAD_DIM // 2), f32),
    ]
    scratch = [
        pltpu.VMEM((rows, width), bf16),
        pltpu.VMEM((8, q_up.shape[0], 2 * HEAD_DIM), bf16),
        pltpu.VMEM((2, rows, slice_size), f32),
        pltpu.VMEM((2, 2, 2, 2, 2) + gains.shape, f32),
        pltpu.VMEM((8,) + places.shape, jnp.int32),
    ]
    operands = (q_down, key, value, gains, q_up, gate, up, out_proj, w_down, places)
    return moving(
        head_kernel, 1, outs, operands, scratch + wires(100, 8),
        in_specs=[VMEM] * len(operands),
        out_specs=[ANY, ANY, VMEM, VMEM, ANY] + [VMEM] * 9,
    )


def turned(values, cosine, sine, sign):
    half = HEAD_DIM // 2
    out = []
    for start in range(0, values.shape[1], HEAD_DIM):
        one, two = values[:, start : start + half], values[:, start + half : start + HEAD_DIM]
        out += [one * cosine - sign * two * sine, sign * one * sine + two * cosine]
    return jnp.concatenate(out, axis=1)


def row_scale(values):
    return lax.rsqrt(jnp.mean(values * values, axis=-1, keepdims=True) + epsilon)


def pack_kernel(
    tokens, gain_in, gain_q, first_weight, cosine, sine, wo_own, wo_far, gu, wd_own,
    out, weight_out, gu_out, wd_far, normed, compressed,
    weight, block, weight_all, send_sem, recv_sem, local_sem,
):
    y, x, h, l, c = coordinates()
    wire = Wire(send_sem, recv_sem, local_sem)
    load = wire.local(first_weight, weight)
    greet([16, 4] + PLANE)
    rank = x * 4 + l * 2 + c
    gu_rows = gu.shape[1]
    gu_place = gu_out.at[x, pl.ds((l * 2 + c) * gu_rows, gu_rows), :]
    gu_mine = wire.local(gu.at[rank], gu_place)
    gu_sent = [wire.send(gu.at[flip(rank, j)], gu_place, PLANE[j - 1]) for j in range(1, 8)]
    weight_done = [over_y(wire, ref, lambda yy, hh: weight_all.at[yy, hh], k) for k, ref in enumerate((wo_own, wo_far))]
    rows = tokens.shape[0]
    inputs = tokens[...].astype(f32)
    normed[...] = (inputs * row_scale(inputs) * gain_in[...]).astype(bf16)
    load.wait()
    mixed = jnp.dot(normed[...], weight[...], preferred_element_type=f32)
    rank_dim = compressed.shape[1]
    query = mixed[:, :rank_dim]
    compressed[...] = query
    block[:, :rank_dim] = (query * row_scale(query) * gain_q[...]).astype(bf16)
    block[:, rank_dim : rank_dim + HEAD_DIM] = turned(
        mixed[:, rank_dim : rank_dim + HEAD_DIM], cosine[:rows], sine[:rows], 1.0
    ).astype(bf16)
    block[:, rank_dim + HEAD_DIM :] = mixed[:, rank_dim + HEAD_DIM :].astype(bf16)
    near = block.shape[1]
    far = 2 * HEAD_DIM
    columns, far_columns = pl.ds(0, near), pl.ds(near, far)
    from_h = wire.send(block.at[:, pl.ds(near - far, far)], out.at[0, 0, 0, :, far_columns], 4)
    near_out = out.at[:, :, :, :, columns]
    size = block.shape[0]
    steps, finish = plane_gather(wire, block, near_out, near_out.at[0, 0, 0], routes(size, 4, 1))
    from_h.wait_recv()
    wd_sent = wire.send(wd_own, wd_far, 4)
    far_out = out.at[:, :, :, :, far_columns]
    far_steps, far_finish = plane_gather(wire, far_out.at[0, 0, 0], far_out, None, routes(size, 2, 1))
    do(steps)
    do(far_steps)
    do(weight_done)
    swapped = wire.send(weight_all.at[:, 1 - c], weight_out.at[:, c], 1)
    kept = wire.local(weight_all.at[:, c], weight_out.at[:, c])
    finish()
    far_finish()
    kept.wait()
    gu_mine.wait()
    arrived([swapped, wd_sent] + gu_sent)
    wire.close()


def pack(tokens, gain_in, gain_q, first_weight, cosine, sine, wo_own, wo_far, gu, wd_own):
    rows, width = tokens.shape
    near = first_weight.shape[1]
    rank_dim = near - 2 * HEAD_DIM
    outs = [
        shaped((2, 2, 2, rows, near + 2 * HEAD_DIM)),
        shaped((2, 2) + wo_own.shape),
        shaped((2, 4 * gu.shape[1], gu.shape[2])),
        shaped(wd_own.shape),
        shaped((rows, width)),
        shaped((rows, rank_dim), f32),
    ]
    operands = (tokens, gain_in, gain_q, first_weight, cosine, sine, wo_own, wo_far, gu, wd_own)
    return moving(
        pack_kernel, 2, outs, operands,
        [pltpu.VMEM(first_weight.shape, bf16), pltpu.VMEM((rows, near), bf16), pltpu.VMEM((2, 2) + wo_own.shape, bf16)]
        + wires(60, 12),
        in_specs=[VMEM, VMEM, VMEM, ANY, VMEM, VMEM, VMEM, VMEM, VMEM, VMEM],
        out_specs=[ANY, VMEM, ANY, ANY, VMEM, VMEM],
    )


def mask_of(index, first, last):
    return jnp.where((index >= first) & (index <= last), 0.0, masked_score)


def scores_of(keys, queries):
    return lax.dot_general(keys, queries, (((1,), (1,)), ((), ())), preferred_element_type=f32)


def attend_kernel(
    plane_set, wq, wo, cosine, sine, key_index, query_index, first_index, tokens, gain, cotangent, gu_set, wd_own, wd_far,
    queries_out, attended, lse, middle, plane_mid, cotangents, gu_zero, gu_one, wd_out,
    kv, normed, staged, mask, from_c, s1, r1, s2, r2, mid, gu_far, gu_next, load_sem, send_sem, recv_sem, local_sem,
):
    wire = Wire(send_sem, recv_sem, local_sem)
    rank_dim = wq.shape[0]
    loads = [
        pltpu.make_async_copy(plane_set.at[:, :, :, :, pl.ds(rank_dim, 4 * HEAD_DIM)], kv, load_sem.at[0]),
        pltpu.make_async_copy(plane_set.at[:, :, :, :, pl.ds(0, rank_dim)], normed, load_sem.at[1]),
    ]
    for load in loads:
        load.start()
    greet(LINKS)
    places = [lambda yy, hh: gu_zero.at[yy, hh], lambda yy, hh: gu_one.at[yy, hh]]
    passing, gathered = plane_gather(
        wire, cotangent, cotangents, cotangents.at[0, 0, 0], routes(cotangent.shape[0], 4, 0)
    )
    far_sent = wire.send(gu_set.at[0], gu_far, 4)
    gu_done = [over_y(wire, ref, lambda yy, hh: wd_out.at[yy, hh], k) for k, ref in enumerate((wd_own, wd_far))]
    landed(loads)
    rows = kv.shape[3]
    block = 2 * rows

    def one(g, i):
        start = (g * 2 + i) * block
        place = pl.ds(start, block)
        raw = jnp.dot(normed[g, i].reshape(block, rank_dim), wq[...], preferred_element_type=f32)
        queries = (turned(raw, cosine[place], sine[place], 1.0) * (1.0 / math.sqrt(HEAD_DIM))).astype(bf16)
        queries_out[place] = queries
        mask[...] = mask_of(key_index[...], first_index[:, place], query_index[:, place])
        keys = jnp.concatenate(
            [kv[g, :, :, :, :HEAD_DIM].reshape(2 * block, HEAD_DIM), kv[g, :, :, :, 2 * HEAD_DIM : 3 * HEAD_DIM].reshape(2 * block, HEAD_DIM)]
        )
        values = jnp.concatenate(
            [kv[g, :, :, :, HEAD_DIM : 2 * HEAD_DIM].reshape(2 * block, HEAD_DIM), kv[g, :, :, :, 3 * HEAD_DIM :].reshape(2 * block, HEAD_DIM)]
        )
        merged = []
        for a in range(2):
            scores = scores_of(keys, queries[:, a * HEAD_DIM : (a + 1) * HEAD_DIM]) + mask[...]
            top = jnp.max(scores, axis=0, keepdims=True)
            weights = jnp.exp(scores - top)
            total = jnp.sum(weights, axis=0, keepdims=True)
            lse[a, :, place] = top + jnp.log(total)
            probs = (weights * (1.0 / total)).astype(bf16)
            merged.append(lax.dot_general(probs, values, (((0,), (0,)), ((), ())), preferred_element_type=f32).astype(bf16))
        merged = jnp.concatenate(merged, axis=1)
        attended[place] = merged
        staged[g, i] = jnp.dot(merged, wo[...], preferred_element_type=f32).astype(bf16).reshape(2, rows, -1)

    give, arrive, steps, finish = plane_reduce(
        wire, staged, middle, staged.at[:, :, 0], from_c, s1, r1, s2, r2, routes(rows, 4, 4), load=False
    )
    for number, k in enumerate(ARRIVAL):
        one(*k)
        give(k)
        if number == 0:
            arrive(k)
        elif number > 1:
            arrive(ARRIVAL[number - 1])
        if number == 1:
            do(passing[:2])
        if number == 2:
            do(passing[2:])
    arrive((0, 0))
    gu_done += [over_y(wire, gu_set.at[k], places[k], 0) for k in range(2)]
    do(steps)
    far_sent.wait_recv()
    next_sent = wire.send(gu_set.at[1], gu_next, 4)
    gu_done.append(over_y(wire, gu_far, places[0], 1))
    gathered()
    finish()

    def norm(r):
        value = tokens[r].astype(f32) + middle[r]
        middle[r] = value
        mid[r] = (value * row_scale(value) * gain[...]).astype(bf16)

    each_rows(rows, norm)
    steps, finish = plane_gather(wire, mid, plane_mid, plane_mid.at[0, 0, 0], routes(rows, 4, 2))
    do(steps)
    next_sent.wait_recv()
    gu_done.append(over_y(wire, gu_next, places[1], 1))
    finish()
    do(gu_done)
    wire.close()


def attend(plane_set, wq, wo, cosine, sine, key_index, query_index, first_index, tokens, gain, cotangent, gu_set, wd_own, wd_far):
    rows, width = tokens.shape
    count = 8 * rows
    rank_dim = wq.shape[0]
    gu = gu_set.shape[1:]
    outs = [
        shaped((count, 2 * HEAD_DIM)),
        shaped((count, 2 * HEAD_DIM)),
        shaped((2, 1, count), f32),
        shaped((rows, width), f32),
        shaped((2, 2, 2, rows, width)),
        shaped((2, 2, 2, rows, width)),
        shaped((2, 2) + gu),
        shaped((2, 2) + gu),
        shaped((2, 2) + wd_own.shape),
    ]
    scratch = [
        pltpu.VMEM((2, 2, 2, rows, 4 * HEAD_DIM), bf16),
        pltpu.VMEM((2, 2, 2, rows, rank_dim), bf16),
        pltpu.VMEM((2, 2, 2, rows, width), bf16),
        pltpu.VMEM((count, 2 * rows), f32),
    ]
    scratch += reduce_scratch(rows, width)[1:]
    scratch += [pltpu.VMEM((rows, width), bf16), pltpu.VMEM(gu, bf16), pltpu.VMEM(gu, bf16), pltpu.SemaphoreType.DMA((2,))]
    operands = (
        plane_set, wq, wo, cosine, sine, key_index, query_index, first_index, tokens, gain, cotangent, gu_set, wd_own, wd_far,
    )
    return moving(
        attend_kernel, 3, outs, operands, scratch + wires(80, 16),
        in_specs=[ANY] + [VMEM] * 13,
        out_specs=[VMEM, VMEM, VMEM, VMEM, ANY, ANY, ANY, ANY, ANY],
        limit=62,
    )


def feed_kernel(
    mid, cotangents, gu_zero, gu_one, down,
    hidden, grads, final_parts, normed_grad,
    gu, wd, mid_v, cot_v, hid_v, grads_v, final_v, staged, from_c, s1, r1, s2, r2,
    weight_sem, load_sem, store_sem, send_sem, recv_sem, local_sem,
):
    wire = Wire(send_sem, recv_sem, local_sem)
    main = gu.shape[4] // 2 // 128 * 128
    size = down.shape[2]
    units = 4 * size
    rows = staged.shape[3]
    block = 2 * rows
    copies = [
        pltpu.make_async_copy(gu_zero, gu.at[:, 0], weight_sem.at[0]),
        pltpu.make_async_copy(gu_one, gu.at[:, 1], weight_sem.at[1]),
    ]
    for k in range(4):
        copies.append(pltpu.make_async_copy(down.at[k // 2, k % 2], wd.at[pl.ds(k * size, size)], weight_sem.at[2 + k]))
    for copy in copies:
        copy.start()

    def load(n):
        k = ARRIVAL[n]
        pairs = [(mid.at[k[0], k[1]], mid_v.at[n % 2]), (cotangents.at[k[0], k[1]], cot_v.at[n % 2])]
        moves = [pltpu.make_async_copy(src, dst, load_sem.at[2 * (n % 2) + q]) for q, (src, dst) in enumerate(pairs)]
        for move in moves:
            move.start()
        return moves

    def store(n):
        k = ARRIVAL[n]
        place = pl.ds((k[0] * 2 + k[1]) * block, block)
        pairs = [(hid_v, hidden.at[place]), (grads_v, grads.at[place]), (final_v, final_parts.at[place])]
        moves = [
            pltpu.make_async_copy(src.at[n % 2], dst, store_sem.at[3 * (n % 2) + q]) for q, (src, dst) in enumerate(pairs)
        ]
        for move in moves:
            move.start()
        return moves

    moves = [load(0)]
    greet(LINKS)
    wd[units:] = jnp.zeros((wd.shape[0] - units, wd.shape[1]), bf16)
    landed(copies)
    give, arrive, steps, finish = plane_reduce(
        wire, staged, normed_grad, staged.at[:, :, 0], from_c, s1, r1, s2, r2, routes(rows, 4, 2), load=False
    )
    weight = lambda: gu[...].reshape(-1, gu.shape[4])
    stores = []
    for n, k in enumerate(ARRIVAL):
        landed(moves[n])
        if n < 3:
            moves.append(load(n + 1))
        if n > 1:
            landed(stores[n - 2])
        slot = n % 2
        both = jnp.dot(mid_v[slot].reshape(block, -1), weight(), preferred_element_type=f32)
        if n > 0:
            arrive(ARRIVAL[n - 1])
        if n > 2:
            do(steps)
        gate = both[:, : main + 128]
        upper = jnp.concatenate([both[:, main + 128 :], pltpu.roll(both[:, main : main + 128], 64, 1)], axis=1)
        cotangent = cot_v[slot].reshape(block, -1)
        grad = lax.dot_general(cotangent, wd[...], (((1,), (1,)), ((), ())), preferred_element_type=f32)
        sigmoid = 1.0 / (1.0 + jnp.exp(-gate))
        silu = gate * sigmoid
        hid = (silu * upper).astype(bf16)
        hid_v[slot] = hid[:, :units]
        grad_gate = grad * upper * sigmoid * (1.0 + gate * (1.0 - sigmoid))
        grad_upper = grad * silu
        joint = grad_gate[:, main:] + pltpu.roll(grad_upper[:, main:], 64, 1)
        out = jnp.concatenate([grad_gate[:, :main], joint, grad_upper[:, :main]], axis=1).astype(bf16)
        grads_v[slot] = out
        mid_grad = lax.dot_general(out, weight(), (((1,), (1,)), ((), ())), preferred_element_type=f32)
        staged[k] = mid_grad.astype(bf16).reshape(2, rows, -1)
        give(k)
        final_v[slot] = jnp.dot(hid, wd[...], preferred_element_type=f32).astype(bf16)
        stores.append(store(n))
    arrive((0, 0))
    finish()
    landed(stores[2] + stores[3])
    wire.close()


def feed(mid, cotangents, gu_zero, gu_one, down):
    rows, width = mid.shape[3:]
    count = 8 * rows
    columns = gu_zero.shape[-1]
    units = 4 * down.shape[2]
    padded = (units + 127) // 128 * 128
    block = 2 * rows
    outs = [shaped((count, units)), shaped((count, columns)), shaped((count, width)), shaped((rows, width), f32)]
    scratch = [
        pltpu.VMEM((2, 2, 2) + gu_one.shape[2:], bf16),
        pltpu.VMEM((padded, width), bf16),
        pltpu.VMEM((2, 2, rows, width), bf16),
        pltpu.VMEM((2, 2, rows, width), bf16),
        pltpu.VMEM((2, block, units), bf16),
        pltpu.VMEM((2, block, columns), bf16),
        pltpu.VMEM((2, block, width), bf16),
        pltpu.VMEM((2, 2, 2, rows, width), bf16),
    ]
    scratch += reduce_scratch(rows, width)[1:]
    scratch += [pltpu.SemaphoreType.DMA((6,)), pltpu.SemaphoreType.DMA((4,)), pltpu.SemaphoreType.DMA((6,))]
    return moving(
        feed_kernel, 4, outs, (mid, cotangents, gu_zero, gu_one, down), scratch + wires(30, 2),
        out_specs=[ANY, ANY, ANY, VMEM],
        limit=62,
    )


def fold_y(wire, source, recv, passed, kept):
    y, x, h, l, c = coordinates()
    sent = [wire.send(source(1 - y, hh), recv.at[hh], 16) for hh in (1 - h, h)]

    def half(k, hh, target):
        sent[k].wait_recv()
        mine = source(y, hh)

        def body(r):
            target[r] = (wide(mine, r) + wide(recv.at[hh], r)).astype(target.dtype)

        each_rows(target.shape[0], body)

    return lambda: half(0, 1 - h, passed), lambda: half(1, h, kept)


def fold_y_far(wire, source, recv, passed):
    y, x, h, l, c = coordinates()
    sent = wire.send(source(1 - y, 1 - h), recv, 16)

    def finish():
        sent.wait_recv()
        mine = source(y, 1 - h)

        def body(r):
            passed[r] = (wide(mine, r) + wide(recv, r)).astype(passed.dtype)

        each_rows(passed.shape[0], body)

    return finish


def fold_h(wire, passed, kept, recv, out):
    sent = wire.send(passed, recv, 4)

    def finish():
        sent.wait_recv()

        def body(r):
            out[r] = (wide(kept, r) + wide(recv, r)).astype(out.dtype)

        each_rows(out.shape[0], body)

    return finish


def hand_back(wire, own, out):
    y, x, h, l, c = coordinates()
    rank = x * 4 + l * 2 + c
    mine = wire.local(own(rank), out.at[rank])
    sent = [wire.send(own(flip(rank, j)), out.at[rank], PLANE[j - 1]) for j in range(1, 8)]

    def finish():
        mine.wait()
        arrived(sent)

    return finish


def hand_back_halves(wire, own, out):
    y, x, h, l, c = coordinates()
    rank = x * 4 + l * 2 + c
    sent = {j: wire.later(own(flip(rank, j)), out.at[rank], PLANE[j - 1]) for j in range(1, 8)}
    mine = wire.later_local(own(rank), out.at[rank])

    def start(target):
        for side in (0, 1):

            @pl.when(x == side)
            def _(side=side):
                for j in range(1, 8):
                    if side ^ (j // 4) == target:
                        sent[j].start()
                if side == target:
                    mine.start()

    def finish():
        mine.wait()
        arrived(sent.values())

    return lambda: start(0), lambda: start(1), finish


def norm_back(value, gain, grad):
    scale = row_scale(value)
    weighted = gain * grad
    inner = scale * weighted - value * scale * scale * scale * jnp.mean(weighted * value, axis=-1, keepdims=True)
    return inner, grad * value * scale


def over_tokens(left, right):
    return lax.dot_general(left, right, (((0,), (0,)), ((), ())), preferred_element_type=f32).astype(bf16)


def branch_kernel(
    normed_grad, final_parts, middle, cotangent, gain, mid, hidden, gu_grads, cotangents,
    grad_middle, gain_grad, plane_branch, output, down_out, gu_passed, gu_zero_out, gu_one_out,
    kept, from_c, s1, r1, s2, r2, total, branch, wd_grad, wd_recv, wd_passed, wd_kept, wd_far, gu_recv,
    hidden_v, gu_v, tokens_v, gu_zero, gu_one, load_sem, store_sem, send_sem, recv_sem, local_sem,
):
    wire = Wire(send_sem, recv_sem, local_sem)
    loads = [
        pltpu.make_async_copy(source, target, load_sem.at[k])
        for k, (source, target) in enumerate(
            ((hidden, hidden_v), (cotangents, tokens_v), (gu_grads, gu_v), (mid, tokens_v))
        )
    ]
    for load in loads[:3]:
        load.start()
    greet(LINKS)
    size = middle.shape[0]
    gain_grad[...] = jnp.zeros_like(gain_grad)

    def norm(r):
        inner, outer = norm_back(middle[r], gain[...], normed_grad[r])
        value = cotangent[r].astype(f32) + inner
        grad_middle[r] = value
        branch[r] = value.astype(bf16)
        gain_grad[...] += jnp.sum(outer, axis=0, keepdims=True)

    each_rows(size, norm)
    passing, gathered = plane_gather(wire, branch, plane_branch, plane_branch.at[0, 0, 0], routes(size, 4, 2))
    give, arrive, steps, finish = plane_reduce(
        wire, final_parts, total, kept, from_c, s1, r1, s2, r2, routes(size, 4, 3)
    )
    each(give)
    landed(loads[:2])
    down_rows = wd_grad.shape[2]
    for k in range(4):
        wd_grad[k // 2, k % 2] = over_tokens(hidden_v[:, k * down_rows : (k + 1) * down_rows], tokens_v[...])
    down_passed, down_kept = fold_y(wire, lambda yy, hh: wd_grad.at[yy, hh], wd_recv, wd_passed, wd_kept)
    loads[3].start()
    each(arrive)
    landed(loads[2:])
    gu_rows = gu_one.shape[2]

    def columns(yy, xx, hh):
        start = (yy * 4 + xx * 2 + hh) * gu_rows
        return over_tokens(tokens_v[:, start : start + gu_rows], gu_v[...])

    stores = [
        pltpu.make_async_copy(source.at[k // 2, k % 2], target.at[k // 2, k % 2], store_sem.at[side, k])
        for side, (source, target) in enumerate(((gu_zero, gu_zero_out), (gu_one, gu_one_out)))
        for k in range(4)
    ]
    for k in range(4):
        gu_zero[k // 2, k % 2] = columns(k // 2, 0, k % 2)
        stores[k].start()
        passing[k]()
    gu_sum = fold_y_far(wire, lambda yy, hh: gu_zero.at[yy, hh], gu_recv, gu_passed)
    down_passed()
    down_h = fold_h(wire, wd_passed, wd_kept, wd_far, down_out)
    for k in range(4):
        steps[k]()
        gu_one[k // 2, k % 2] = columns(k // 2, 1, k % 2)
        stores[4 + k].start()
    gathered()
    finish()

    def emit(r):
        output[r] = (middle[r] + total[r]).astype(bf16)

    each_rows(size, emit)
    down_kept()
    gu_sum()
    down_h()
    landed(stores)
    wire.close()


def branch_step(normed_grad, final_parts, middle, cotangent, gain, mid, hidden, gu_grads, cotangents):
    rows, width = middle.shape
    columns = gu_grads.shape[1]
    down = (hidden.shape[1] // 4, width)
    gu = (width // 8, columns)
    outs = [
        shaped((rows, width), f32),
        shaped((1, width), f32),
        shaped(final_parts.shape),
        shaped((rows, width)),
        shaped(down, f32),
        shaped(gu),
        shaped((2, 2) + gu),
        shaped((2, 2) + gu),
    ]
    scratch = reduce_scratch(rows, width) + [pltpu.VMEM((rows, width), f32), pltpu.VMEM((rows, width), bf16)]
    scratch += [pltpu.VMEM((2, 2) + down, bf16), pltpu.VMEM((2,) + down, bf16)] + [pltpu.VMEM(down, bf16)] * 3
    scratch += [pltpu.VMEM(gu, bf16)]
    scratch += [pltpu.VMEM(v.shape, bf16) for v in (hidden, gu_grads, mid)] + [pltpu.VMEM((2, 2) + gu, bf16)] * 2
    operands = (normed_grad, final_parts, middle, cotangent, gain, mid, hidden, gu_grads, cotangents)
    return moving(
        branch_kernel, 5, outs, operands, scratch + [pltpu.SemaphoreType.DMA((4,)), pltpu.SemaphoreType.DMA((2, 4))] + wires(60, 16),
        in_specs=[VMEM, ANY, VMEM, VMEM, VMEM, ANY, ANY, ANY, ANY],
        out_specs=[VMEM, VMEM, ANY, VMEM, VMEM, VMEM, ANY, ANY],
        limit=62,
    )


def attend_back_kernel(
    plane_set, plane_branch, queries, attended, lse, wq, wo, cosine, sine, key_index, query_index, first_index,
    gu_passed, gu_zero, gu_one,
    query_grad, back, gu_out, gu_passed_next, gu_kept_next, heads,
    kv, branch, out_grad, near_mine, near_recv, staged, grad_keys, grad_values, from_c, s1, r1, s2, r2, gu_recv, gu_recv_y, mask,
    load_sem, send_sem, recv_sem, local_sem,
):
    wire = Wire(send_sem, recv_sem, local_sem)
    rank_dim = wq.shape[0]
    rows = kv.shape[3]
    block = 2 * rows
    load_kv = pltpu.make_async_copy(plane_set.at[:, :, :, :, pl.ds(rank_dim, 4 * HEAD_DIM)], kv, load_sem.at[0])
    load_kv.start()

    loads = [pltpu.make_async_copy(plane_branch.at[k], branch.at[k], load_sem.at[1 + n]) for n, k in enumerate(ARRIVAL)]
    for load in loads:
        load.start()
    greet(LINKS)
    y, x, h, l, c = coordinates()
    far_sent = wire.send(gu_passed, gu_recv, 4)
    near_load = wire.local(gu_zero.at[y, h], near_mine)
    near_sent = wire.send(gu_zero.at[1 - y, h], near_recv, 16)
    gu_sums = fold_y(wire, lambda yy, hh: gu_one.at[yy, hh], gu_recv_y, gu_passed_next, gu_kept_next)
    buffers = (staged, back, staged.at[:, :, 0], from_c, s1, r1, s2, r2)

    def of(columns):
        every = slice(None)
        return [ref.at[(every,) * (len(ref.shape) - 1) + (columns,)] for ref in buffers]

    normed_sum = plane_reduce(wire, *of(pl.ds(0, rank_dim)), routes(rows, 2, 1), load=False)
    kv_sum = plane_reduce(wire, *of(pl.ds(rank_dim, 4 * HEAD_DIM)), routes(rows, 2, 1), load=False)
    load_kv.wait()

    def one(n):
        g, i = ARRIVAL[n]
        if n < 2:
            loads[n].wait()
        if n % 2 == 0:
            grad_keys[...] = jnp.zeros_like(grad_keys)
            grad_values[...] = jnp.zeros_like(grad_values)
        place = pl.ds((g * 2 + i) * block, block)
        grads = lax.dot_general(
            branch[g, i].reshape(block, -1), wo[...], (((1,), (1,)), ((), ())), preferred_element_type=f32
        ).astype(bf16)
        keys = jnp.concatenate(
            [kv[g, :, :, :, :HEAD_DIM].reshape(2 * block, HEAD_DIM), kv[g, :, :, :, 2 * HEAD_DIM : 3 * HEAD_DIM].reshape(2 * block, HEAD_DIM)]
        )
        values = jnp.concatenate(
            [kv[g, :, :, :, HEAD_DIM : 2 * HEAD_DIM].reshape(2 * block, HEAD_DIM), kv[g, :, :, :, 3 * HEAD_DIM :].reshape(2 * block, HEAD_DIM)]
        )
        query_parts = []
        mask[...] = mask_of(key_index[...], first_index[:, place], query_index[:, place])
        for a in range(2):
            span = slice(a * HEAD_DIM, (a + 1) * HEAD_DIM)
            query, grad = queries[place, span], grads[:, span]
            product = grad.astype(f32) * attended[place, span].astype(f32)
            delta = lax.dot_general(
                jnp.ones((8, HEAD_DIM), f32), product, (((1,), (1,)), ((), ())),
                precision=lax.Precision.HIGHEST, preferred_element_type=f32,
            )[:1]
            probs = jnp.exp(scores_of(keys, query) + mask[...] - lse[a, :, place])
            grad_values[...] += jnp.dot(probs.astype(bf16), grad, preferred_element_type=f32)
            grad_probs = lax.dot_general(values, grad, (((1,), (1,)), ((), ())), preferred_element_type=f32)
            grad_scores = (probs * (grad_probs - delta)).astype(bf16)
            grad_keys[...] += jnp.dot(grad_scores, query, preferred_element_type=f32)
            query_parts.append(
                lax.dot_general(grad_scores, keys, (((0,), (0,)), ((), ())), preferred_element_type=f32)
            )
        query_sum = turned(jnp.concatenate(query_parts, axis=1), cosine[place], sine[place], -1.0)
        query_sum = (query_sum * (1.0 / math.sqrt(HEAD_DIM))).astype(bf16)
        query_grad[place] = query_sum
        normed = lax.dot_general(query_sum, wq[...], (((1,), (1,)), ((), ())), preferred_element_type=f32)
        staged[g, i, :, :, :rank_dim] = normed.astype(bf16).reshape(2, rows, rank_dim)
        if n % 2 == 1:
            for number, (source, side) in enumerate(
                ((grad_keys, 0), (grad_values, 0), (grad_keys, 1), (grad_values, 1))
            ):
                column = rank_dim + number * HEAD_DIM
                half = source[side * 2 * block : (side + 1) * 2 * block].astype(bf16)
                staged[g, :, :, :, column : column + HEAD_DIM] = half.reshape(2, 2, rows, HEAD_DIM)

    one(0)
    normed_sum[0](ARRIVAL[0])
    one(1)
    kv_sum[0](ARRIVAL[0])
    kv_sum[0](ARRIVAL[1])
    normed_sum[0](ARRIVAL[1])
    normed_sum[1](ARRIVAL[0])
    kv_sum[1](ARRIVAL[0])
    kv_sum[1](ARRIVAL[1])
    normed_sum[1](ARRIVAL[1])
    landed(loads[2:])
    head_rows = out_grad.shape[2]
    for k in range(4):
        part = attended[:, k * head_rows : (k + 1) * head_rows]
        out_grad[k // 2, k % 2] = over_tokens(part, branch[...].reshape(8 * rows, -1))
    swapped = wire.send(out_grad.at[:, 1 - c], heads.at[:, c], 1)
    stayed = wire.local(out_grad.at[:, c], heads.at[:, c])
    one(2)
    normed_sum[0](ARRIVAL[2])
    stayed.wait()
    swapped.wait_recv()
    one(3)
    kv_sum[0](ARRIVAL[2])
    kv_sum[0](ARRIVAL[3])
    normed_sum[0](ARRIVAL[3])
    kv_sum[1](ARRIVAL[2])
    normed_sum[1](ARRIVAL[2])
    kv_sum[1](ARRIVAL[3])
    normed_sum[1](ARRIVAL[3])
    do(kv_sum[2])
    do(normed_sum[2])
    near_load.wait()
    arrived([near_sent, far_sent])

    def total(r):
        gu_out[r] = (wide(near_mine, r) + wide(near_recv, r) + wide(gu_recv, r)).astype(bf16)

    each_rows(gu_out.shape[0], total)
    do(gu_sums)
    kv_sum[3]()
    normed_sum[3]()
    wire.close()


def attend_back(
    plane_set, plane_branch, queries, attended, lse, wq, wo, cosine, sine, key_index, query_index, first_index,
    gu_passed, gu_zero, gu_one,
):
    rows = plane_set.shape[3]
    tokens = 8 * rows
    gu = gu_passed.shape
    width = wq.shape[0] + 4 * HEAD_DIM
    heads = (wo.shape[0] // 4, wo.shape[1])
    outs = [
        shaped((tokens, 2 * HEAD_DIM)),
        shaped((rows, width), f32),
        shaped(gu),
        shaped(gu),
        shaped(gu),
        shaped((2, 2) + heads),
    ]
    scratch = [
        pltpu.VMEM((2, 2, 2, rows, 4 * HEAD_DIM), bf16),
        pltpu.VMEM((2, 2, 2, rows, wo.shape[1]), bf16),
        pltpu.VMEM((2, 2) + heads, bf16),
        pltpu.VMEM(gu, bf16),
        pltpu.VMEM(gu, bf16),
        pltpu.VMEM((2, 2, 2, rows, width), bf16),
        pltpu.VMEM((8 * rows, HEAD_DIM), f32),
        pltpu.VMEM((8 * rows, HEAD_DIM), f32),
    ]
    scratch += reduce_scratch(rows, width)[1:] + [pltpu.VMEM(gu, bf16)]
    scratch += [pltpu.VMEM((2,) + gu, bf16), pltpu.VMEM((tokens, 2 * rows), f32), pltpu.SemaphoreType.DMA((5,))]
    operands = (
        plane_set, plane_branch, queries, attended, lse, wq, wo, cosine, sine, key_index, query_index, first_index,
        gu_passed, gu_zero, gu_one,
    )
    return moving(
        attend_back_kernel, 6, outs, operands, scratch + wires(60, 12),
        in_specs=[ANY, ANY] + [VMEM] * 10 + [ANY, ANY, VMEM],
        out_specs=[VMEM] * 6,
        limit=62,
    )


def tail_kernel(
    back, normed, compressed, tokens, grad_middle, first_weight, gain_in, gain_q, gain_mid_grad, cosine, sine,
    gu_total, gu_passed, gu_kept, heads, plane_set, query_grad,
    grad_tokens, down_out, key_out, value_out, gains_out, gate_out, up_out, q_up_out, out_out,
    total, up_grad, normed_v, kv_send, kv_recv, mixed, normed_grad, gain_rows,
    blocks, acc, recv, core, gains, gains_recv,
    gu_far, gu_back, gu_wide, up_recv, up_passed, up_kept, up_far, up_own, up_back,
    o_recv, o_passed, o_kept, o_far,
    send_sem, recv_sem, local_sem,
):
    y, x, h, l, c = coordinates()
    own = dict(zip("yxhlc", (y, x, h, l, c)))
    every = slice(None)
    wire = Wire(send_sem, recv_sem, local_sem)
    rows = back.shape[0]
    rank_dim = compressed.shape[1]
    split = rank_dim + 2 * HEAD_DIM
    load_normed = wire.local(plane_set.at[:, :, :, :, pl.ds(0, rank_dim)], normed_v)
    greet([16, 4] + PLANE)
    kv_send[...] = back[:, split:].astype(bf16)
    far = wire.send(kv_send, kv_recv, 4)
    gu_first = wire.local(gu_total, gu_wide.at[0])
    gu_first.wait()
    piece_rows = gu_back.shape[2]
    gu_piece = lambda k: gu_wide.at[k // 4, pl.ds(pl.multiple_of((k % 4) * piece_rows, piece_rows), piece_rows)]
    gu_begin, gu_rest, gu_done = hand_back_halves(wire, gu_piece, gu_back.at[0])
    gu_begin()
    o_sums = fold_y(wire, lambda yy, hh: heads.at[yy, hh], o_recv, o_passed, o_kept)
    inner, outer = norm_back(compressed[...], gain_q[...], back[:, :rank_dim])
    mixed[:, :rank_dim] = inner.astype(bf16)
    gain_rows[1:2, :rank_dim] = jnp.sum(outer, axis=0, keepdims=True)
    gain_rows[2:3, :] = gain_mid_grad[...]
    far.wait_recv()
    gu_h = fold_h(wire, gu_passed, gu_kept, gu_far, gu_wide.at[1])
    kv = back[:, rank_dim:split] + kv_recv[...].astype(f32)
    mixed[:, rank_dim : rank_dim + HEAD_DIM] = turned(kv[:, :HEAD_DIM], cosine[:rows], sine[:rows], -1.0).astype(bf16)
    mixed[:, rank_dim + HEAD_DIM :] = kv[:, HEAD_DIM:].astype(bf16)
    size = normed.shape[1] // 8
    cores = []
    for k in range(8):
        at = (k // 4, k // 2 % 2, k % 2)
        grad = lax.dot_general(
            normed[:, k * size : (k + 1) * size], mixed[...], (((0,), (0,)), ((), ())), preferred_element_type=f32
        )
        blocks[at] = grad.astype(bf16).reshape(blocks.shape[3:])
        cores.append(wire.send(blocks.at[at + (every, 1 - c)], core.at[at], 1))
    span = blocks.shape[5]
    width = blocks.shape[6]
    columns = thirds(width)
    orders = ["yxlh", "xylh", "lyxh"]
    sent = [None] * 3

    def index(fixed, block):
        free = [k for k in "yxhl" if k not in fixed]
        at = dict(fixed)
        for position, k in enumerate(reversed(free)):
            at[k] = (block // 2**position) % 2
        return tuple(at[k] for k in "yxhl")

    def over(fixed, body):
        @pl.loop(0, 2 ** (4 - len(fixed)))
        def _(i):
            body(index(fixed, i))

    def pass_on(p, step):
        order = orders[p]
        fixed = {k: own[k] for k in order[:step]}
        bit = order[step]
        src = {**fixed, bit: 1 - own[bit]}
        dst = {**fixed, bit: own[bit]}
        place = lambda at: tuple(at.get(k, every) for k in "yxhl") + (every, columns[p])
        mask = {"y": 16, "x": 8, "h": 4, "l": 2}[bit]
        sent[p] = wire.send(acc.at[place(src)], recv.at[place(dst)], mask)

    arrived(cores)
    for first_side in (True, False):
        for p in range(3):
            bit = orders[p][0]

            def body(at, p=p):
                value = wide(blocks, at + (c, every, columns[p])) + wide(core, at + (every, columns[p]))
                acc[at + (every, columns[p])] = value.astype(bf16)

            over({bit: 1 - own[bit] if first_side else own[bit]}, body)
            if first_side:
                pass_on(p, 0)
    load_normed.wait()
    up_size = up_grad.shape[3]
    for k in range(8):
        tokens_part = normed_v[:, :, :, :, k * up_size : (k + 1) * up_size].reshape(8 * rows, up_size)
        up_grad[k // 4, k // 2 % 2, k % 2] = over_tokens(tokens_part, query_grad[...])
    up_sums = [
        fold_y(wire, lambda yy, hh, k=k: up_grad.at[yy, k, hh], up_recv.at[k], up_passed.at[k], up_kept.at[k])
        for k in range(2)
    ]
    wire.left(cores)
    wire.local(first_weight, blocks).wait()
    weight = blocks[...].reshape(-1, blocks.shape[6])
    normed_grad[...] = lax.dot_general(mixed[...], weight, (((1,), (1,)), ((), ())), preferred_element_type=f32)
    gain_rows[0:1, :] = jnp.zeros((1, gain_rows.shape[1]), f32)

    def norm(r):
        inner, outer = norm_back(tokens[r].astype(f32), gain_in[...], normed_grad[r])
        grad_tokens[r] = (grad_middle[r] + inner).astype(bf16)
        gain_rows[0:1, :] += jnp.sum(outer, axis=0, keepdims=True)

    each_rows(rows, norm)
    q_span = rank_dim // 32
    gains[...] = jnp.zeros_like(gains)
    for n in range(32):
        at = (n // 16, n // 8 % 2, n // 4 % 2, n // 2 % 2, n % 2, 0)
        gains[at + (slice(0, 128),)] = jnp.concatenate(
            [gain_rows[0, n * span : (n + 1) * span], gain_rows[2, n * span : (n + 1) * span]], axis=0
        )
        gains[at + (slice(128, 128 + q_span),)] = gain_rows[1, n * q_span : (n + 1) * q_span]

    def pass_gains(order, step):
        fixed = {k: own[k] for k in order[:step]}
        bit = order[step]
        place = lambda at: tuple(at.get(k, every) for k in "yxhlc")
        mask = {"y": 16, "x": 8, "h": 4, "l": 2, "c": 1}[bit]
        return wire.send(gains.at[place({**fixed, bit: 1 - own[bit]})], gains_recv.at[place({**fixed, bit: own[bit]})], mask)

    def add_gains(order, step):
        fixed = {k: own[k] for k in order[:step]}
        bit = order[step]
        place = lambda at: tuple(at.get(k, every) for k in "yxhlc")
        mine = place({**fixed, bit: own[bit]})
        gains[mine] = gains[mine] + gains_recv[place({**fixed, bit: 1 - own[bit]})]

    gu_h()
    gu_rest()
    do(o_sums)
    o_h = fold_h(wire, o_passed, o_kept, o_far, out_out)
    gain_order = "cyxlh"
    gain_sent = pass_gains(gain_order, 0)
    gain_step = 0
    for step in range(4):
        for p in range(3):
            order = orders[p]
            fixed = {k: own[k] for k in order[:step]}
            bit = order[step]
            sent[p].wait_recv()

            def body(at, p=p, bit=bit, last=step == 3):
                other = tuple(1 - own[k] if k == bit else v for k, v in zip("yxhl", at))
                value = wide(acc, at + (every, columns[p])) + wide(recv, other + (every, columns[p]))
                if last:
                    total[:, columns[p]] = value
                else:
                    acc[at + (every, columns[p])] = value.astype(bf16)

            if step < 3:
                over({**fixed, bit: own[bit], order[step + 1]: 1 - own[order[step + 1]]}, body)
                pass_on(p, step + 1)
                over({**fixed, bit: own[bit], order[step + 1]: own[order[step + 1]]}, body)
            else:
                over({**fixed, bit: own[bit]}, body)
        if gain_step < 5:
            gain_sent.wait_recv()
            add_gains(gain_order, gain_step)
            gain_step += 1
            if gain_step < 5:
                gain_sent = pass_gains(gain_order, gain_step)
        if step == 0:
            for k in range(2):
                do(up_sums[k])
            up_h = [fold_h(wire, up_passed.at[k], up_kept.at[k], up_far.at[k], up_own.at[k]) for k in range(2)]
        if step == 1:
            for k in range(2):
                up_h[k]()
            up_rows = up_back.shape[1]
            up_piece = lambda k: up_own.at[k // 4, pl.ds(pl.multiple_of((k % 4) * up_rows, up_rows), up_rows)]
            up_done = hand_back(wire, up_piece, up_back)
            gu_done()
            unit = gate_out.shape[1] // 32
            units = 4 * unit
            main = units // 128 * 128
            rest = units - main
            for source in range(8):
                tile = gu_back[0, source].astype(f32)
                halves = (
                    tile[:, : main + rest],
                    jnp.concatenate([tile[:, main + 2 * rest :], tile[:, main + rest : main + 2 * rest]], axis=1),
                )
                for half, target in zip(halves, (gate_out, up_out)):
                    for q in range(4):
                        n = q // 2 * 16 + source // 4 * 8 + q % 2 * 4 + source % 4
                        target[:, n * unit : (n + 1) * unit] = half[:, q * unit : (q + 1) * unit]
        if step == 3:
            o_h()
            up_done()
            for head in range(q_up_out.shape[1] // HEAD_DIM):
                hy, hx, hh, hl = head // 8, head // 4 % 2, head // 2 % 2, head % 2
                source = hx * 4 + hl * 2 + hh
                q_up_out[:, head * HEAD_DIM : (head + 1) * HEAD_DIM] = up_back[
                    source, :, hy * HEAD_DIM : (hy + 1) * HEAD_DIM
                ].astype(f32)
    while gain_step < 5:
        gain_sent.wait_recv()
        add_gains(gain_order, gain_step)
        gain_step += 1
        if gain_step < 5:
            gain_sent = pass_gains(gain_order, gain_step)
    gains_out[...] = gains[y, x, h, l, c]
    down_out[...] = total[:, :rank_dim]
    key_out[...] = total[:, rank_dim : rank_dim + HEAD_DIM]
    value_out[...] = total[:, rank_dim + HEAD_DIM :]
    wire.close()


def tail(
    back, normed, compressed, tokens, grad_middle, first_weight, gain_in, gain_q, gain_mid_grad, cosine, sine,
    gu_total, gu_passed, gu_kept, heads, plane_set, query_grad,
):
    rows, width = tokens.shape
    rank_dim = compressed.shape[1]
    near = first_weight.shape[-1]
    span = width // 32
    gu = gu_total.shape
    units = gu[1] * 4
    up = (rank_dim // 8, query_grad.shape[1])
    out_size = heads.shape[2:]
    outs = [
        shaped((rows, width)),
        shaped((span, rank_dim), f32),
        shaped((span, HEAD_DIM), f32),
        shaped((span, HEAD_DIM), f32),
        shaped((1, 256), f32),
        shaped((span, units), f32),
        shaped((span, units), f32),
        shaped((up[0] // 4, 8 * up[1]), f32),
        shaped(out_size, f32),
    ]
    sums = (2, 2, 2, 2, span, near)
    scratch = [
        pltpu.VMEM((span, near), f32),
        pltpu.VMEM((2, 2, 2) + up, bf16),
        pltpu.VMEM(plane_set.shape[:4] + (rank_dim,), bf16),
        pltpu.VMEM((rows, 2 * HEAD_DIM), bf16),
        pltpu.VMEM((rows, 2 * HEAD_DIM), bf16),
        pltpu.VMEM((rows, near), bf16),
        pltpu.VMEM((rows, width), f32),
        pltpu.VMEM((8, width), f32),
        pltpu.VMEM((2, 2, 2, 2, 2, span, near), bf16),
        pltpu.VMEM(sums, bf16),
        pltpu.VMEM(sums, bf16),
        pltpu.VMEM(sums, bf16),
        pltpu.VMEM((2, 2, 2, 2, 2, 1, 256), f32),
        pltpu.VMEM((2, 2, 2, 2, 2, 1, 256), f32),
        pltpu.VMEM(gu, bf16),
        pltpu.VMEM((1, 8, span, gu[1]), bf16),
        pltpu.VMEM((2,) + gu, bf16),
        pltpu.VMEM((2, 2) + up, bf16),
        pltpu.VMEM((2,) + up, bf16),
        pltpu.VMEM((2,) + up, bf16),
        pltpu.VMEM((2,) + up, bf16),
        pltpu.VMEM((2,) + up, bf16),
        pltpu.VMEM((8, up[0] // 4, up[1]), bf16),
        pltpu.VMEM((2,) + out_size, bf16),
        pltpu.VMEM(out_size, bf16),
        pltpu.VMEM(out_size, bf16),
        pltpu.VMEM(out_size, bf16),
    ]
    operands = (
        back, normed, compressed, tokens, grad_middle, first_weight, gain_in, gain_q, gain_mid_grad, cosine, sine,
        gu_total, gu_passed, gu_kept, heads, plane_set, query_grad,
    )
    return moving(
        tail_kernel, 7, outs, operands, scratch + wires(100, 24),
        in_specs=[VMEM] * 5 + [ANY] + [VMEM] * 5 + [ANY, ANY, VMEM, VMEM, ANY, VMEM],
        out_specs=[VMEM] * 9,
        limit=62,
    )


def finish_kernel(*refs):
    count = (len(refs) - 2) // 3
    loads = [pltpu.make_async_copy(refs[k], refs[2 * count + k], refs[-2].at[k]) for k in range(count)]
    for load in loads:
        load.start()
    stores = []
    for k in range(count):
        loads[k].wait()
        stores.append(pltpu.make_async_copy(refs[2 * count + k], refs[count + k], refs[-1].at[k]))
        stores[-1].start()
    landed(stores)


def finish(arrays):
    count = len(arrays)
    return pl.pallas_call(
        finish_kernel,
        out_shape=[shaped(v.shape, v.dtype) for v in arrays],
        in_specs=[ANY] * count,
        out_specs=[ANY] * count,
        scratch_shapes=[pltpu.VMEM(v.shape, v.dtype) for v in arrays] + [pltpu.SemaphoreType.DMA((count,))] * 2,
        compiler_params=pltpu.CompilerParams(vmem_limit_bytes=62 * 1024 * 1024),
        name="finish",
    )(*arrays)


def plane_local(
    tokens,
    positions,
    cotangent,
    norm_in_gain,
    q_down,
    q_gain,
    q_up,
    key_proj,
    value_proj,
    out_proj,
    norm_mid_gain,
    w_gate,
    w_up,
    w_down,
):
    rows, width = tokens.shape
    rank_dim = q_down.shape[1]
    span, q_span = norm_in_gain.shape[0], q_gain.shape[0]

    gains = jnp.concatenate([norm_in_gain, norm_mid_gain, q_gain, jnp.zeros((256 - 2 * span - q_span,), f32)])
    gains = lax.reduce_precision(gains, 8, 7).reshape(1, 256)
    (
        first_weight, up_query, gu_pieces, wo_own, wo_far, wd_own, in_gain, mid_gain, query_gain,
        first_index, query_index, key_index, cosine, sine,
    ) = head(
        q_down, key_proj, value_proj, gains, q_up, w_gate, w_up, out_proj, w_down, positions.reshape(1, rows)
    )
    up_query = up_query.reshape(rank_dim, 2 * HEAD_DIM)

    plane_set, out_weight, gu_set, wd_far, normed, compressed = pack(
        tokens, in_gain, query_gain, first_weight.reshape(width, -1), cosine, sine, wo_own, wo_far, gu_pieces, wd_own
    )
    out_weight = out_weight.reshape(2 * HEAD_DIM, width)
    queries, attended, lse, middle, plane_mid, plane_cotangent, gu_zero, gu_one, down_weight = attend(
        plane_set, up_query, out_weight, cosine, sine, key_index, query_index, first_index, tokens, mid_gain, cotangent,
        gu_set, wd_own, wd_far,
    )
    hidden, gu_grads, final_parts, normed_grad = feed(plane_mid, plane_cotangent, gu_zero, gu_one, down_weight)
    flat = lambda blocks: blocks.reshape(8 * rows, -1)
    grad_middle, mid_gain_grad, plane_branch, output, grad_down, gu_passed, gu_zero_grad, gu_one_grad = branch_step(
        normed_grad, final_parts.reshape(2, 2, 2, rows, width), middle, cotangent, mid_gain, flat(plane_mid), hidden,
        gu_grads, flat(plane_cotangent),
    )
    query_grad, back, gu_total, gu_passed, gu_kept, out_grad = attend_back(
        plane_set, plane_branch, queries, attended, lse, up_query, out_weight, cosine, sine,
        key_index, query_index, first_index, gu_passed, gu_zero_grad, gu_one_grad,
    )
    grad_tokens, grad_q_down, grad_key, grad_value, grad_gains, grad_gate, grad_up, grad_q_up, grad_out = tail(
        back, normed, compressed, tokens, grad_middle, first_weight, in_gain, query_gain, mid_gain_grad,
        cosine, sine, gu_total, gu_passed, gu_kept, out_grad, plane_set, query_grad,
    )
    output, grad_tokens, grad_q_down, grad_q_up, grad_key, grad_value, grad_out, grad_gate, grad_up, grad_down = finish(
        (output, grad_tokens, grad_q_down, grad_q_up, grad_key, grad_value, grad_out, grad_gate, grad_up, grad_down)
    )
    return (
        output,
        grad_tokens,
        grad_gains[0, :span],
        grad_q_down,
        grad_gains[0, 2 * span : 2 * span + q_span],
        grad_q_up,
        grad_key,
        grad_value,
        grad_out,
        grad_gains[0, span : 2 * span],
        grad_gate,
        grad_up,
        grad_down,
    )


def solution(mesh):
    return jax.shard_map(
        plane_local if dict(mesh.shape) == {"dp": 4, "seq": 8} else local,
        mesh=mesh,
        in_specs=(
            P(("dp", "seq"), None),
            P(("dp", "seq")),
            P(("dp", "seq"), None),
            P(("dp", "seq")),
            P(("dp", "seq"), None),
            P(("dp", "seq")),
            P(("dp", "seq"), None),
            P(("dp", "seq"), None),
            P(("dp", "seq"), None),
            P(("dp", "seq"), None),
            P(("dp", "seq")),
            P(("dp", "seq"), None),
            P(("dp", "seq"), None),
            P(("dp", "seq"), None),
        ),
        out_specs=(
            P(("dp", "seq"), None),
            P(("dp", "seq"), None),
            P(("dp", "seq")),
            P(("dp", "seq"), None),
            P(("dp", "seq")),
            P(("dp", "seq"), None),
            P(("dp", "seq"), None),
            P(("dp", "seq"), None),
            P(("dp", "seq"), None),
            P(("dp", "seq")),
            P(("dp", "seq"), None),
            P(("dp", "seq"), None),
            P(("dp", "seq"), None),
        ),
        check_vma=False,
    )
```
